32 devices in a mesh: dp: 8 (over z, y), state: 4 (over x, core).
Axes of the slice: x: 2, y: 2, z: 4, core: 2. Of those that a mesh axis runs over, the one named last changes fastest.
Arguments:
- inputs: float32 [8, 512, 1024], P('dp', 'state'), may hold values from -50 to 50
- lengths: int32 [8], P('dp'), may hold values from 1 to 1024, 6144 in all
- cotangent: float32 [8, 512, 1024], P('dp', 'state'), may hold values from -6 to 6
- bn_gain: float32 [2, 512], P(None, 'state'), may hold values from 0.25 to 1.75
- bn_bias: float32 [2, 512], P(None, 'state'), may hold values from -3 to 3
- b_weight: bfloat16 [2, 2, 256, 512], P(None, None, 'state'), may hold values from -0.1875 to 0.1875
- c_weight: bfloat16 [2, 2, 256, 512], P(None, None, 'state'), may hold values from -0.375 to 0.375
- nu_log: float32 [2, 256], P(None, 'state'), may hold values from -9 to -3
- theta_log: float32 [2, 256], P(None, 'state'), may hold values from -4.6 to 1.1
- gamma_log: float32 [2, 256], P(None, 'state'), may hold values from -5 to 0
- skip_weight: float32 [2, 512], P(None, 'state'), may hold values from -4 to 4
- glu_weight: bfloat16 [2, 2, 512, 512], P(None, None, 'state'), may hold values from -0.5 to 0.5
- glu_bias: float32 [2, 2, 512], P(None, None, 'state'), may hold values from -2 to 2
Outputs:
- result: float32 [8, 512, 1024], P('dp', 'state')
- grad_inputs: float32 [8, 512, 1024], P('dp', 'state')
- grad_bn_gain: float32 [2, 512], P(None, 'state')
- grad_bn_bias: float32 [2, 512], P(None, 'state')
- grad_b: float32 [2, 2, 256, 512], P(None, None, 'state')
- grad_c: float32 [2, 2, 256, 512], P(None, None, 'state')
- grad_nu: float32 [2, 256], P(None, 'state')
- grad_theta: float32 [2, 256], P(None, 'state')
- grad_gamma: float32 [2, 256], P(None, 'state')
- grad_skip: float32 [2, 512], P(None, 'state')
- grad_glu_weight: float32 [2, 2, 512, 512], P(None, None, 'state')
- grad_glu_bias: float32 [2, 2, 512], P(None, None, 'state')
The draws below stay inside these ranges and needn't reach their ends.
Inputs may be any that keep to these rules, and one draw needn't show every extreme that they name: A sequence's valid tokens are its first lengths[s] positions, and some sequence has all 1024.
All inputs are finite; a program needn't handle non-finite values. No bound on the sum of `lengths` on one device may be relied on, other than what follows from the above.
Results may differ from the reference program's by a relative error of at most 0.03.
Values may be sent and summed in bfloat16 or wider, within the bound.
No kernel may reach another device: no remote copies, remote signals or barrier semaphores. Data moves between devices by JAX's collectives and lax.ppermute only.
A program may use at most 64 MiB of HBM per device.

```python
import math
import jax
import jax.numpy as jnp
import numpy as np
from jax import lax

D = 512
NS = 256
LAYERS = 2
LEN = 1024
SEQS = 8


def decay_span(key, shortest, longest):
    return jax.random.uniform(key, (LAYERS, NS), jnp.float32, math.log(shortest), math.log(longest))


def draw_nu_log(key, part):
    spans = decay_span(key, 30.0, 2.0 * LEN)
    return -spans


def draw_gamma_log(key, part):
    spans = decay_span(key, 30.0, 2.0 * LEN)
    key = jax.random.fold_in(key, 22)
    jitter = jax.random.uniform(key, (LAYERS, NS), jnp.float32, -0.4, 0.4)
    return 0.5 * jnp.log(-jnp.expm1(-2.0 * jnp.exp(-spans))) + jitter


def draw_inputs(key, part):
    key = jax.random.fold_in(key, 23)
    noise_key, scale_key, centre_key, feature_key = jax.random.split(key, 4)
    seq_order = jnp.arange(SEQS).astype(jnp.float32) / max(SEQS - 1, 1)
    seq_ramp = 1.0 + 2.0 * seq_order
    noise_draw = jnp.clip(jax.random.normal(noise_key, (SEQS, D, LEN), jnp.float32), -5.0, 5.0)
    spread = jnp.sqrt(seq_ramp) * jnp.exp(jax.random.uniform(scale_key, (SEQS,), jnp.float32, -0.3, 0.3))
    centre = 0.7 * jax.random.uniform(centre_key, (D,), jnp.float32, -1.0, 1.0)
    feature = jnp.exp(jax.random.uniform(feature_key, (D,), jnp.float32, -0.7, 0.7))
    return centre[None, :, None] * seq_ramp[:, None, None] + spread[:, None, None] * feature[None, :, None] * noise_draw


def shard_levels(key, shape, cuts, least, top_value):
    loudness = 1.0
    for position, shards_of in cuts:
        heights = jax.random.uniform(jax.random.fold_in(jax.random.fold_in(key, 6), position), (shards_of,), jnp.float32, least / len(cuts), top_value / len(cuts))
        loudness = loudness * jnp.repeat(jnp.exp(heights), shape[position] // shards_of).reshape((-1,) + (1,) * (len(shape) - 1 - position))
    return loudness


def split_up(count, total, limit, slope):
    portions = [(1 << 20) // math.isqrt(standing ** slope) + 1 for standing in range(2, count + 1)]
    spare, holding = total - limit - (count - 1), [1] * (count - 1)
    while spare > 0:
        free = [i for i in range(count - 1) if holding[i] < limit]
        whole, budget = sum([portions[i] for i in free]), spare
        for i in free:
            more = min(limit - holding[i], max(1, budget * portions[i] // whole), spare)
            holding[i] = holding[i] + more
            spare = spare - more
    return np.array([limit] + holding)


def ragged(stream_key, amount, total, reach, lean):
    if amount == 2:
        one = jax.random.randint(stream_key, (), max(1, total - reach), min(reach, total - 1) + 1)
        return jnp.stack([one, total - one])
    sizes = jnp.asarray(split_up(amount, total, reach, lean), jnp.int32)
    couples = (amount - 1) // 2
    donor, sink = sizes[1:1 + 2 * couples:2], sizes[2:2 + 2 * couples:2]
    slack = jnp.minimum(donor - 1, reach - sink)
    shifted = jax.random.randint(jax.random.fold_in(stream_key, 1), (couples,), 0, 1 << 20) % (slack + 1)
    sizes = sizes.at[1:1 + 2 * couples:2].set(donor - shifted).at[2:2 + 2 * couples:2].set(sink + shifted)
    return sizes[jax.random.permutation(jax.random.fold_in(stream_key, 2), amount)]


def normal_values(key, extent, deviation, bound, cuts=(), kind=jnp.bfloat16):
    values = jax.random.normal(key, extent, jnp.float32) * deviation
    if len(cuts) > 0:
        values = shard_levels(key, extent, cuts, -0.22, 0.18) * values
    return jnp.clip(values, min=-bound, max=bound).astype(kind)


def setup_inputs(seed: int = 0) -> dict:
    arg_keys = jax.random.split(jax.random.key(seed), 14)
    inputs = draw_inputs(jax.random.fold_in(arg_keys[13], 71), 0)
    lengths = ragged(arg_keys[1], SEQS, 3 * SEQS * LEN // 4, LEN, 2).astype(jnp.int32)
    cotangent = normal_values(arg_keys[2], (SEQS, D, LEN), 1.0, 6.0, ((0, 8), (1, 4)), jnp.float32)
    bn_gain = jnp.clip(1.0 + 0.15 * jax.random.normal(arg_keys[3], (LAYERS, D), jnp.float32), 0.25, 1.75)
    bn_bias = normal_values(arg_keys[4], (LAYERS, D), 0.5, 3.0, ((1, 4),), jnp.float32)
    b_weight = normal_values(arg_keys[5], (LAYERS, 2, NS, D), (2 * D) ** -0.5, 0.1875, ((2, 4),))
    c_weight = normal_values(arg_keys[6], (LAYERS, 2, NS, D), NS ** -0.5, 0.375, ((2, 4),))
    nu_log = draw_nu_log(jax.random.fold_in(arg_keys[13], 71), 0)
    theta_log = jnp.clip(-4.6 + 5.7 * jax.random.uniform(arg_keys[8], (LAYERS, NS), jnp.float32) ** shard_levels(arg_keys[8], (LAYERS, NS), ((1, 4),), -0.2, 0.2), -4.6, 1.1)
    gamma_log = draw_gamma_log(jax.random.fold_in(arg_keys[13], 71), 0)
    skip_weight = normal_values(arg_keys[10], (LAYERS, D), 1.0, 4.0, ((1, 4),), jnp.float32)
    glu_weight = normal_values(arg_keys[11], (LAYERS, 2, D, D), (D // 4) ** -0.5, 0.5, ((2, 4),))
    glu_bias = normal_values(arg_keys[12], (LAYERS, 2, D), 0.3, 2.0, ((2, 4),), jnp.float32)
    return dict(inputs=inputs, lengths=lengths, cotangent=cotangent, bn_gain=bn_gain, bn_bias=bn_bias, b_weight=b_weight, c_weight=c_weight, nu_log=nu_log, theta_log=theta_log, gamma_log=gamma_log, skip_weight=skip_weight, glu_weight=glu_weight, glu_bias=glu_bias)


epsilon = 1e-05
highest_precision = lax.Precision.HIGHEST

@jax.custom_vjp
def low(v):
    return lax.optimization_barrier(v.astype(jnp.bfloat16)).astype(jnp.float32)

@jax.custom_vjp
def lowered_backward(v):
    return v

def low_keep(v):
    return (low(v), None)

def low_pass(kept, grad):
    return (grad,)

def back_keep(v):
    return (v, None)

def back_low(kept, grad):
    return (low(grad),)
low.defvjp(low_keep, low_pass)
lowered_backward.defvjp(back_keep, back_low)

def recurrence(drive_re, drive_im, valid_rows, rate_re, rate_im, backward):

    def advance(carried, step_item):
        state_real, state_imaginary = carried
        push_re, push_im, keep_row = step_item
        new_re = keep_row[:, None] * (rate_re * state_real - rate_im * state_imaginary + push_re)
        new_im = keep_row[:, None] * (rate_re * state_imaginary + rate_im * state_real + push_im)
        return ((new_re, new_im), (new_re, new_im))
    zero_state = jnp.zeros((drive_re.shape[0], drive_re.shape[2]), jnp.float32)
    sequence_items = (jnp.swapaxes(drive_re, 0, 1), jnp.swapaxes(drive_im, 0, 1), jnp.swapaxes(valid_rows, 0, 1))
    final_pair, (states_re, states_im) = lax.scan(jax.checkpoint(advance), (zero_state, zero_state), sequence_items, reverse=backward)
    return (jnp.swapaxes(states_re, 0, 1), jnp.swapaxes(states_im, 0, 1))

def apply_layer(stream, valid_rows, gain_here, shift_here, input_matrix_layer, output_matrix_layer, nu_here, theta_here, gamma_log_here, skip_here, gate_weight_layer, gate_bias_layer, backward):
    valid3 = valid_rows[..., None]
    counted = jnp.sum(valid_rows)
    centre = lax.optimization_barrier(jnp.sum(stream * valid3, axis=(0, 1))) / counted
    meansq = lax.optimization_barrier(jnp.sum(stream * stream * valid3, axis=(0, 1))) / counted
    inv_dev = lax.rsqrt(meansq - centre * centre + epsilon)
    normalized_input = low(valid3 * ((stream - centre) * inv_dev * gain_here + shift_here))
    driven_input = lowered_backward(jnp.einsum('eqy,bry->eqbr', normalized_input, input_matrix_layer, precision=highest_precision))
    gamma_here = jnp.exp(gamma_log_here)
    modulus = jnp.exp(-jnp.exp(nu_here))
    rotation = jnp.exp(theta_here)
    rate_re = modulus * jnp.cos(rotation)
    rate_im = modulus * jnp.sin(rotation)
    state_real, state_imaginary = recurrence(gamma_here * driven_input[:, :, 0], gamma_here * driven_input[:, :, 1], valid_rows, rate_re, rate_im, backward)
    state_real = low(state_real)
    state_imaginary = low(state_imaginary)
    preactivation = jnp.einsum('cmt,th->cmh', state_real, output_matrix_layer[0], precision=highest_precision)
    preactivation = preactivation - jnp.einsum('cmt,th->cmh', state_imaginary, output_matrix_layer[1], precision=highest_precision)
    preactivation = lowered_backward(preactivation + skip_here * normalized_input)
    active_mask = low(jax.nn.gelu(preactivation, approximate=False))
    gated_output = lowered_backward(jnp.einsum('xbw,ucw->xbuc', active_mask, gate_weight_layer, precision=highest_precision) + gate_bias_layer)
    return stream + valid3 * (gated_output[:, :, 0] * jax.nn.sigmoid(gated_output[:, :, 1]))

def reference(inputs, lengths, cotangent, bn_gain, bn_bias, b_weight, c_weight, nu_log, theta_log, gamma_log, skip_weight, glu_weight, glu_bias):
    positions = jnp.arange(LEN).astype(jnp.int32)
    valid_rows = (positions[None, :] < lengths.astype(jnp.int32)[:, None]).astype(jnp.float32)

    def forward(stream_in, gain_all, shift_all, b_all, c_all, nu_all, theta_all, gamma_all, skip_all, glu_w_all, glu_b_all):
        stream = jnp.swapaxes(stream_in, 1, 2)
        for layer_index in range(LAYERS):
            stream = apply_layer(stream, valid_rows, gain_all[layer_index], shift_all[layer_index], b_all[layer_index], c_all[layer_index], nu_all[layer_index], theta_all[layer_index], gamma_all[layer_index], skip_all[layer_index], glu_w_all[layer_index], glu_b_all[layer_index], layer_index % 2 == 1)
        return jnp.swapaxes(stream, 1, 2)
    result, pullback = jax.vjp(forward, inputs, bn_gain, bn_bias, b_weight.astype(jnp.float32), c_weight.astype(jnp.float32), nu_log, theta_log, gamma_log, skip_weight, glu_weight.astype(jnp.float32), glu_bias)
    gradients = pullback(cotangent)
    return (result, gradients[0], gradients[1], gradients[2], gradients[3], gradients[4], gradients[5], gradients[6], gradients[7], gradients[8], gradients[9], gradients[10])
```

```python
import functools

import jax
import jax.numpy as jnp
from jax import lax
from jax.experimental import pallas as pl
from jax.experimental.pallas import tpu as pltpu
from jax.sharding import PartitionSpec as P

LAYERS = 2
CHUNKS = 16
EPSILON = 1e-05
F32 = jnp.float32
LOW = jnp.bfloat16
PARAM_ROWS = 16
VMEM_BYTES = 56 * 1024 * 1024

GAIN, SHIFT, SKIP, BIAS_LINEAR, BIAS_GATE = range(5)
RATE_RE, RATE_IM, GAMMA = range(3)

NN = (((1,), (0,)), ((), ()))
NT = (((1,), (1,)), ((), ()))
TN = (((0,), (0,)), ((), ()))


def dot(left, right, dims):
    return lax.dot_general(left, right, dims, preferred_element_type=F32)


def rows_at(index, size):
    return pl.ds(pl.multiple_of(index * size, size), size)


def lanes_at(quarter, width):
    return pl.ds(pl.multiple_of(quarter * width, width), width)


def for_rows(total, size, body, init=None, unroll=1):
    def step(index, carry):
        return body(rows_at(index, size), index, carry)

    return lax.fori_loop(0, total // size, step, init, unroll=unroll)


def keep_rows(first_step, rows, steps, length):
    row = lax.broadcasted_iota(jnp.int32, (rows, 1), 0)
    position = (row % CHUNKS) * steps + row // CHUNKS + first_step
    return position < length


def gelu_parts(value):
    size = jnp.abs(value)
    below = 1.0 + size * (0.3275911 * 0.7071067811865476)
    guess = pl.reciprocal(below, approx=True)
    inverse = guess * (2.0 - below * guess)
    bell = jnp.exp(value * value * -0.5)
    tail = inverse * (
        0.5 * 0.254829592
        + inverse
        * (
            0.5 * -0.284496736
            + inverse * (0.5 * 1.421413741 + inverse * (0.5 * -1.453152027 + inverse * (0.5 * 1.061405429)))
        )
    )
    tail = tail * bell
    return jnp.where(value >= 0.0, 1.0 - tail, tail), bell * 0.3989422804014327


def sigmoid(value):
    return 0.5 * jnp.tanh(0.5 * value) + 0.5


def squared(re, im, times):
    for _ in range(times):
        re, im = re * re - im * im, 2.0 * re * im
    return re, im


def chunk_starts(re, im, rate_re, rate_im, reverse):
    row = lax.broadcasted_iota(jnp.int32, re.shape, 0)

    def moved(value, by):
        if reverse:
            return jnp.where(row < CHUNKS - by, pltpu.roll(value, CHUNKS - by, 0), 0.0)
        return jnp.where(row >= by, pltpu.roll(value, by, 0), 0.0)

    by = 1
    while by < CHUNKS:
        past_re, past_im = moved(re, by), moved(im, by)
        re, im = (
            re + rate_re * past_re - rate_im * past_im,
            im + rate_re * past_im + rate_im * past_re,
        )
        rate_re, rate_im = squared(rate_re, rate_im, 1)
        by *= 2
    return moved(re, 1), moved(im, 1)


def sweep(drive_ref, rate_re, rate_im, steps, reverse, emit, extra, unroll=4):
    states = rate_re.shape[1]
    shape = (CHUNKS, states)
    wide_re = jnp.broadcast_to(rate_re, shape)
    wide_im = jnp.broadcast_to(rate_im, shape)

    def advance(index, re, im):
        place = steps - 1 - index if reverse else index
        rows = rows_at(place, CHUNKS)
        drive_re = drive_ref[rows, :states]
        drive_im = drive_ref[rows, states:]
        new_re = (wide_re * re + drive_re) - wide_im * im
        new_im = (wide_re * im + drive_im) + wide_im * re
        return rows, place, new_re, new_im, drive_re, drive_im

    def first(index, carry):
        _, _, re, im, _, _ = advance(index, *carry)
        return re, im

    def second(index, carry):
        re, im, held = carry
        rows, place, re, im, drive_re, drive_im = advance(index, re, im)
        return re, im, emit(rows, place, re, im, drive_re, drive_im, held)

    zero = jnp.zeros(shape, F32)
    re, im = lax.fori_loop(0, steps, first, (zero, zero), unroll=unroll)
    far_re, far_im = rate_re, rate_im
    power = 1
    while power < steps:
        far_re, far_im = squared(far_re, far_im, 1)
        power *= 2
    re, im = chunk_starts(re, im, far_re, far_im, reverse)
    return lax.fori_loop(0, steps, second, (re, im, extra), unroll=unroll)[2]


def from_feature_rows(source_ref, held_ref, steps, emit):
    length = source_ref.shape[1]
    for block in range(length // 128):
        held_ref[block * 128 : (block + 1) * 128, :] = source_ref[:, block * 128 : (block + 1) * 128].T

    def step(index, carry):
        emit(rows_at(index, CHUNKS), index, held_ref[pl.ds(index, CHUNKS, stride=steps), :])
        return carry

    lax.fori_loop(0, steps, step, 0, unroll=4)


def to_feature_rows(load, held_ref, out_ref, steps):
    length = out_ref.shape[1]

    def step(index, carry):
        held_ref[pl.ds(index, CHUNKS, stride=steps), :] = load(rows_at(index, CHUNKS), index)
        return carry

    lax.fori_loop(0, steps, step, 0, unroll=4)
    for block in range(length // 128):
        out_ref[:, block * 128 : (block + 1) * 128] = held_ref[block * 128 : (block + 1) * 128, :].T


def enter_kernel(meta_ref, x_ref, params_ref, out_ref, sums_ref, held_ref):
    length = meta_ref[0]
    total = x_ref.shape[1]
    steps = total // CHUNKS
    out_ref[total:, :] = params_ref[...]
    sums_ref[...] = jnp.zeros_like(sums_ref)

    def emit(rows, index, value):
        out_ref[rows, :] = value
        kept = jnp.where(keep_rows(index, CHUNKS, steps, length), value, 0.0)
        sums_ref[0:16, :] += kept
        sums_ref[16:32, :] += kept * kept

    from_feature_rows(x_ref, held_ref, steps, emit)
    plain = jnp.sum(sums_ref[0:16, :], axis=0, keepdims=True)
    square = jnp.sum(sums_ref[16:32, :], axis=0, keepdims=True)
    sums_ref[0:1, :] = plain
    sums_ref[1:2, :] = square
    sums_ref[2:3, :] = jnp.full((1, 128), length, jnp.int32).astype(F32)


def cotangent_kernel(x_ref, out_ref, low_ref, held_ref):
    steps = x_ref.shape[1] // CHUNKS

    def emit(rows, index, value):
        out_ref[rows, :] = value
        low_ref[rows, :] = value.astype(LOW)

    from_feature_rows(x_ref, held_ref, steps, emit)


def assemble_states(parts, whole_ref):
    half = parts[0].shape[0] // 2
    states = half * len(parts)
    for place, part in enumerate(parts):
        whole_ref[place * half : (place + 1) * half, :] = part[:half, :]
        whole_ref[states + place * half : states + (place + 1) * half, :] = part[half:, :]


def assemble_output(parts, whole_ref):
    half = parts[0].shape[0] // 2
    states = half * len(parts)
    for place, part in enumerate(parts):
        whole_ref[place * half : (place + 1) * half, :] = part[:half, :]
        whole_ref[states + place * half : states + (place + 1) * half, :] = -part[half:, :]


def assemble_glu(parts, whole_ref, quarter):
    half = parts[0].shape[0] // 2
    width = half * len(parts)
    for place, part in enumerate(parts):
        whole_ref[lanes_at(quarter ^ place, half), :] = part[:half, :]
        whole_ref[pl.ds(pl.multiple_of(width + (quarter ^ place) * half, half), half), :] = part[half:, :]


def norm_rows(sums, counted):
    centre = sums[0:1, :] / counted
    meansq = sums[1:2, :] / counted
    return centre, lax.rsqrt(meansq - centre * centre + EPSILON)


def drive_phase(normed_ref, b_ref, drive_ref, gamma, part):
    total = normed_ref.shape[0]
    both = jnp.concatenate([gamma, gamma], axis=1)

    def body(rows, index, carry):
        drive_ref[rows, :] = dot(normed_ref[rows, :], b_ref[...], NT) * both
        return carry

    for_rows(total, part, body, 0)


def pre_phase(low_ref, c_ref, normed_ref, skip, active_ref, slope_ref, held_ref, part):
    total = normed_ref.shape[0]

    def body(rows, index, carry):
        held_ref[...] = dot(low_ref[rows, :], c_ref[...], NN)
        base = index * part

        def inner(local, place, carry):
            here = pl.ds(pl.multiple_of(base + place * 16, 16), 16)
            value = held_ref[local, :] + skip * normed_ref[here, :].astype(F32)
            cdf, density = gelu_parts(value)
            active_ref[here, :] = (value * cdf).astype(LOW)
            slope_ref[here, :] = (cdf + value * density).astype(slope_ref.dtype)
            return carry

        for_rows(part, 16, inner, 0, unroll=2)
        return carry

    for_rows(total, part, body, 0)


def start_kernel(
    meta_ref, x0, x1, x2, x3, sums_ref, b0, b1, b2, b3, c0, c1, c2, c3,
    normed_ref, drive_own_ref, low_ref, slope_ref, active_ref, b_ref, c_ref, feature_ref, state_ref, norm_ref,
    drive_ref, held_ref, stats_ref, part,
):
    length, quarter = meta_ref[0], meta_ref[1]
    parts = (x0, x1, x2, x3)
    total = normed_ref.shape[0]
    steps = total // CHUNKS
    width = x0.shape[1]
    assemble_states((b0, b1, b2, b3), b_ref)
    assemble_output((c0, c1, c2, c3), c_ref)
    lane = lax.broadcasted_iota(jnp.int32, (8, width), 1)
    for place, value in enumerate(parts):
        feature_ref[:, lanes_at(quarter ^ place, width)] = value[total:, :]
    for pair in range(2):
        early, late = parts[2 * pair][total + 8 :, :], parts[2 * pair + 1][total + 8 :, :]
        state_ref[:, pair * 128 : (pair + 1) * 128] = jnp.where(lane < 64, early, pltpu.roll(late, 64, 1))
    groups = sums_ref.shape[0] // 8
    for place in range(4):
        value = sums_ref[place * 8 : place * 8 + 8, :]
        for other in range(1, groups // 4):
            value += sums_ref[(other * 4 + place) * 8 : (other * 4 + place) * 8 + 8, :]
        stats_ref[:, place * width : (place + 1) * width] = value
    centre, inv_dev = norm_rows(stats_ref[0:2, :], stats_ref[2:3, :])
    norm_ref[...] = jnp.zeros_like(norm_ref)
    norm_ref[0:1, :] = centre
    norm_ref[1:2, :] = inv_dev
    norm_ref[2:3, :] = stats_ref[2:3, :]

    def normal(rows, index, carry):
        keep = keep_rows(index * 2, 32, steps, length)
        for place, value in enumerate(parts):
            lanes = lanes_at(quarter ^ place, width)
            z = (value[rows, :] - norm_ref[0:1, lanes]) * norm_ref[1:2, lanes]
            z = z * feature_ref[GAIN : GAIN + 1, lanes] + feature_ref[SHIFT : SHIFT + 1, lanes]
            normed_ref[rows, lanes] = jnp.where(keep, z, 0.0).astype(LOW)
        return carry

    for_rows(total, 32, normal, 0)
    state = state_ref[...]
    states = state.shape[1]
    drive_phase(normed_ref, b_ref, drive_ref, state[2 + GAMMA : 3 + GAMMA, :], part)

    def emit(rows, step, re, im, drive_re, drive_im, held):
        low_ref[rows, :states] = re.astype(LOW)
        low_ref[rows, states:] = im.astype(LOW)
        drive_own_ref[rows, :128] = drive_re[:, :128]
        drive_own_ref[rows, 128:] = drive_im[:, :128]
        return held

    sweep(drive_ref, state[2:3, :], state[3:4, :], steps, False, emit, 0)
    pre_phase(low_ref, c_ref, normed_ref, feature_ref[SKIP : SKIP + 1, :], active_ref, slope_ref, held_ref, part)


def glu_kernel(
    meta_ref, x0, x1, x2, x3, active_ref, w0, w1, w2, w3, feature_ref,
    stream_ref, linear_ref, gate_ref, w_ref, sums_ref,
    held_ref, part,
):
    length, quarter = meta_ref[0], meta_ref[1]
    parts = (x0, x1, x2, x3)
    total, full = active_ref.shape
    steps = total // CHUNKS
    width = x0.shape[1]
    assemble_glu((w0, w1, w2, w3), w_ref, quarter)
    sums_ref[...] = jnp.zeros_like(sums_ref)

    def body(rows, index, carry):
        held_ref[...] = dot(active_ref[rows, :], w_ref[...], NT)
        base = index * part

        def inner(local, place_index, carry):
            here = pl.ds(pl.multiple_of(base + place_index * 16, 16), 16)
            keep = keep_rows(index * (part // CHUNKS) + place_index, 16, steps, length)
            for place, value in enumerate(parts):
                lanes = lanes_at(quarter ^ place, width)
                far = pl.ds(pl.multiple_of(full + (quarter ^ place) * width, width), width)
                linear = held_ref[local, lanes] + feature_ref[BIAS_LINEAR : BIAS_LINEAR + 1, lanes]
                gate = sigmoid(held_ref[local, far] + feature_ref[BIAS_GATE : BIAS_GATE + 1, lanes])
                mixed = linear * gate
                gate_ref[here, lanes] = gate.astype(gate_ref.dtype)
                linear_ref[here, lanes] = (mixed * (1.0 - gate)).astype(linear_ref.dtype)
                moved = value[here, :] + jnp.where(keep, mixed, 0.0)
                stream_ref[here, lanes] = moved
                kept = jnp.where(keep, moved, 0.0)
                sums_ref[0:16, lanes] += kept
                sums_ref[16:32, lanes] += kept * kept
            return carry

        for_rows(part, 16, inner, 0, unroll=2)
        return carry

    for_rows(total, part, body, 0)
    plain = jnp.sum(sums_ref[0:16, :], axis=0, keepdims=True)
    square = jnp.sum(sums_ref[16:32, :], axis=0, keepdims=True)
    sums_ref[0:1, :] = plain
    sums_ref[1:2, :] = square


def total_rows(sums_ref, count):
    groups = sums_ref.shape[0] // 8
    value = sums_ref[0:8, :]
    for other in range(1, groups):
        value += sums_ref[other * 8 : other * 8 + 8, :]
    return value


def adjoint_phase(
    grad_gated_ref, w_ref, slope_ref, normed_ref, c_ref, low_ref, drive_own_ref, state, first_row, quarter, length,
    pre_grad_ref, held_ref, grad_state_ref, grad_driven_ref, small_ref, sum_ref, reverse, part,
):
    total, full = normed_ref.shape
    steps = total // CHUNKS
    width = 128
    states = state.shape[1]
    own = lanes_at(quarter, width)
    sum_ref[...] = jnp.zeros_like(sum_ref)

    def body(rows, index, carry):
        held_ref[:, :full] = dot(grad_gated_ref[rows, :], w_ref[...], NN)
        base = index * part

        def inner(local, place, carry):
            here = pl.ds(pl.multiple_of(base + place * 16, 16), 16)
            pre_grad_ref[here, :] = (held_ref[local, :full] * slope_ref[here, :].astype(F32)).astype(LOW)
            sum_ref[...] += pre_grad_ref[here, own].astype(F32) * normed_ref[here, own].astype(F32)
            return carry

        for_rows(part, 16, inner, 0, unroll=2)
        grad_state_ref[rows, :] = dot(pre_grad_ref[rows, :], c_ref[...], NT)
        return carry

    for_rows(total, part, body, 0)
    rate_re = state[first_row : first_row + 1, :]
    rate_im = state[first_row + 1 : first_row + 2, :]
    gamma = jnp.broadcast_to(state[first_row + 2 : first_row + 3, :], (CHUNKS, states))

    def emit(rows, step, re, im, drive_re, drive_im, held):
        out_re, out_im = gamma * re, gamma * im
        if not reverse:
            keep = keep_rows(step, CHUNKS, steps, length)
            out_re, out_im = jnp.where(keep, out_re, 0.0), jnp.where(keep, out_im, 0.0)
        grad_driven_ref[rows, :states] = out_re.astype(LOW)
        grad_driven_ref[rows, states:] = out_im.astype(LOW)
        one, two, three = held
        own_re, own_im = re[:, :128], im[:, :128]
        late_re, late_im = own_re - drive_re[:, :128], own_im - drive_im[:, :128]
        low_re = low_ref[rows, :128].astype(F32)
        low_im = low_ref[rows, states : states + 128].astype(F32)
        one = one + late_re * low_re + late_im * low_im
        two = two + late_im * low_re - late_re * low_im
        three = three + own_re * drive_own_ref[rows, :128] + own_im * drive_own_ref[rows, 128:]
        return one, two, three

    zero = jnp.zeros((CHUNKS, 128), F32)
    one, two, three = sweep(grad_state_ref, rate_re, -rate_im, steps, reverse, emit, (zero, zero, zero))
    small_ref[0:1, 0:128] = jnp.sum(one, axis=0, keepdims=True)
    small_ref[1:2, 0:128] = jnp.sum(two, axis=0, keepdims=True)
    small_ref[2:3, 0:128] = jnp.sum(three, axis=0, keepdims=True)
    small_ref[3:4, 0:128] = jnp.sum(sum_ref[...], axis=0, keepdims=True)


def weight_grads(grads_ref, grad_driven_ref, normed_ref, low_ref, pre_grad_ref, grad_gated_ref, active_ref, quarter, states):
    full = normed_ref.shape[1]
    half = states // 4
    for place in range(2):
        lanes = slice(place * states, place * states + 128)
        got = dot(grad_driven_ref[:, lanes], normed_ref[...], TN)[:half, :]
        grads_ref[place * half : (place + 1) * half, :] = got.astype(LOW)
        got = dot(low_ref[:, lanes], pre_grad_ref[...], TN)[:half, :]
        got = got if place == 0 else -got
        grads_ref[128 + place * half : 128 + (place + 1) * half, :] = got.astype(LOW)
        lanes = pl.ds(pl.multiple_of(place * full + quarter * 128, 128), 128)
        got = dot(grad_gated_ref[:, lanes], active_ref[...], TN)
        grads_ref[256 + place * 128 : 256 + (place + 1) * 128, :] = got.astype(LOW)


def middle_kernel(
    meta_ref, stream_ref, sums_ref, b0, b1, b2, b3, c0, c1, c2, c3, w0, w1, w2, w3, feature_ref, state_ref, norm0_ref,
    t0, t1, t2, t3,
    result_ref, base_ref, bn_ref, grads_ref, small_ref, norm_ref,
    b_ref, c_ref, w_ref, normed_ref, drive_ref, drive_own_ref, low_ref, slope_ref, active_ref, held_ref, own_ref,
    order_ref, grad_gated_ref, pre_grad_ref, grad_driven_ref, sum_ref, bias_ref, part,
):
    length, quarter = meta_ref[0], meta_ref[1]
    total, full = stream_ref.shape
    steps = total // CHUNKS
    width = 128
    own = lanes_at(quarter, width)
    assemble_states((b0, b1, b2, b3), b_ref)
    assemble_output((c0, c1, c2, c3), c_ref)
    assemble_glu((w0, w1, w2, w3), w_ref, quarter)
    counted = norm0_ref[2:3, :]
    centre, inv_dev = norm_rows(total_rows(sums_ref, 2), counted)
    norm_ref[...] = jnp.zeros_like(norm_ref)
    norm_ref[0:1, :] = centre
    norm_ref[1:2, :] = inv_dev
    norm_ref[2:3, :] = counted
    gain = feature_ref[5 + GAIN : 6 + GAIN, :]
    shift = feature_ref[5 + SHIFT : 6 + SHIFT, :]
    skip = feature_ref[5 + SKIP : 6 + SKIP, :]

    def normal(rows, index, carry):
        keep = keep_rows(index, 16, steps, length)
        z = (stream_ref[rows, :] - centre) * inv_dev
        normed_ref[rows, :] = jnp.where(keep, z * gain + shift, 0.0).astype(LOW)
        return carry

    for_rows(total, 16, normal, 0, unroll=2)
    state = state_ref[...]
    states = state.shape[1]
    drive_phase(normed_ref, b_ref, drive_ref, state[5 + GAMMA : 6 + GAMMA, :], part)

    def emit(rows, step, re, im, drive_re, drive_im, held):
        low_ref[rows, :states] = re.astype(LOW)
        low_ref[rows, states:] = im.astype(LOW)
        drive_own_ref[rows, :128] = drive_re[:, :128]
        drive_own_ref[rows, 128:] = drive_im[:, :128]
        return held

    sweep(drive_ref, state[5:6, :], state[6:7, :], steps, True, emit, 0)
    pre_phase(low_ref, c_ref, normed_ref, skip, active_ref, slope_ref, held_ref.at[:, :full], part)
    bias_ref[...] = jnp.zeros_like(bias_ref)

    def body(rows, index, carry):
        held_ref[...] = dot(active_ref[rows, :], w_ref[...], NT)
        base = index * part

        def inner(local, place_index, carry):
            here = pl.ds(pl.multiple_of(base + place_index * 16, 16), 16)
            keep = keep_rows(index * (part // CHUNKS) + place_index, 16, steps, length)
            for place, value in enumerate((t0, t1, t2, t3)):
                lanes = lanes_at(quarter ^ place, width)
                far = pl.ds(pl.multiple_of(full + (quarter ^ place) * width, width), width)
                linear = held_ref[local, lanes] + feature_ref[5 + BIAS_LINEAR : 6 + BIAS_LINEAR, lanes]
                gate = sigmoid(held_ref[local, far] + feature_ref[5 + BIAS_GATE : 6 + BIAS_GATE, lanes])
                mixed = linear * gate
                up = jnp.where(keep, value[here, :].astype(F32), 0.0)
                grad_linear = (up * gate).astype(LOW)
                grad_gate = (up * mixed * (1.0 - gate)).astype(LOW)
                grad_gated_ref[here, lanes] = grad_linear
                grad_gated_ref[here, far] = grad_gate
                if place == 0:
                    own_ref[here, :] = stream_ref[here, lanes] + jnp.where(keep, mixed, 0.0)
                    bias_ref[0:16, :] += grad_linear.astype(F32)
                    bias_ref[16:32, :] += grad_gate.astype(F32)
            return carry

        for_rows(part, 16, inner, 0, unroll=2)
        return carry

    for_rows(total, part, body, 0)
    to_feature_rows(lambda rows, index: own_ref[rows, :], order_ref, result_ref, steps)
    small_ref[...] = jnp.zeros_like(small_ref)
    adjoint_phase(
        grad_gated_ref, w_ref, slope_ref, normed_ref, c_ref, low_ref, drive_own_ref, state, 5, quarter, length,
        pre_grad_ref, held_ref, drive_ref, grad_driven_ref, small_ref, sum_ref, False, part,
    )
    small_ref[4:5, 0:128] = jnp.sum(bias_ref[0:16, :], axis=0, keepdims=True)
    small_ref[5:6, 0:128] = jnp.sum(bias_ref[16:32, :], axis=0, keepdims=True)
    weight_grads(
        grads_ref, grad_driven_ref, normed_ref, low_ref, pre_grad_ref, grad_gated_ref, active_ref, quarter, states
    )
    bn_ref[...] = jnp.zeros_like(bn_ref)
    scale = inv_dev * gain

    def back(rows, index, carry):
        held_ref[:, :full] = dot(grad_driven_ref[rows, :], b_ref[...], NN)
        base = index * part

        def inner(local, place_index, carry):
            here = pl.ds(pl.multiple_of(base + place_index * 16, 16), 16)
            grad = held_ref[local, :full] + skip * pre_grad_ref[here, :].astype(F32)
            z = (stream_ref[here, :] - centre) * inv_dev
            bn_ref[0:16, :] += grad
            bn_ref[16:32, :] += grad * z
            base_ref[here, :] = scale * grad
            return carry

        for_rows(part, 16, inner, 0, unroll=2)
        return carry

    for_rows(total, part, back, 0)

    def add(rows, index, carry):
        for place, value in enumerate((t0, t1, t2, t3)):
            lanes = lanes_at(quarter ^ place, width)
            base_ref[rows, lanes] += value[rows, :].astype(F32)
        return carry

    for_rows(total, 16, add, 0, unroll=2)
    plain = jnp.sum(bn_ref[0:16, :], axis=0, keepdims=True)
    scaled = jnp.sum(bn_ref[16:32, :], axis=0, keepdims=True)
    bn_ref[0:1, :] = plain
    bn_ref[1:2, :] = scaled


def last_kernel(
    meta_ref, stream_ref, base_ref, sums_ref, norm1_ref, gate_ref, linear_ref, slope_ref, active_ref, normed_ref, low_ref,
    drive_own_ref, b_ref, c_ref, w_ref, feature_ref, state_ref, x_ref, norm0_ref, grads1_ref, small1_ref,
    send_ref, up_ref, grad_ref,
    held_ref, grad_state_ref, grad_gated_ref, pre_grad_ref, grad_driven_ref, sum_ref, bias_ref, small_ref, bn_ref,
    grads_ref, row_ref, part,
):
    length, quarter = meta_ref[0], meta_ref[1]
    total, full = stream_ref.shape
    steps = total // CHUNKS
    width = 128
    own = lanes_at(quarter, width)
    counted = norm0_ref[2:3, :]
    whole = total_rows(sums_ref, 2)
    centre, inv_dev = norm1_ref[0:1, :], norm1_ref[1:2, :]
    gain = feature_ref[5 + GAIN : 6 + GAIN, :]
    scale = inv_dev * gain
    level = scale * whole[0:1, :] / counted
    tilt = scale * inv_dev * whole[1:2, :] / counted
    bias_ref[...] = jnp.zeros_like(bias_ref)

    def top(rows, index, carry):
        keep = keep_rows(index, 16, steps, length)
        up = base_ref[rows, :] - jnp.where(keep, level + (stream_ref[rows, :] - centre) * tilt, 0.0)
        row_ref[...] = up
        up_ref[rows, :] = row_ref[:, own]
        up = jnp.where(keep, up, 0.0)
        grad_gated_ref[rows, :full] = (up * gate_ref[rows, :].astype(F32)).astype(LOW)
        grad_gated_ref[rows, full:] = (up * linear_ref[rows, :].astype(F32)).astype(LOW)
        bias_ref[0:16, :] += grad_gated_ref[rows, own].astype(F32)
        bias_ref[16:32, :] += grad_gated_ref[rows, pl.ds(pl.multiple_of(full + quarter * width, width), width)].astype(F32)
        return carry

    for_rows(total, 16, top, 0, unroll=2)
    small_ref[...] = jnp.zeros_like(small_ref)
    state = state_ref[...]
    states = state.shape[1]
    adjoint_phase(
        grad_gated_ref, w_ref, slope_ref, normed_ref, c_ref, low_ref, drive_own_ref, state, 2, quarter, length,
        pre_grad_ref, held_ref, grad_state_ref, grad_driven_ref, small_ref, sum_ref, True, part,
    )
    small_ref[4:5, 0:128] = jnp.sum(bias_ref[0:16, :], axis=0, keepdims=True)
    small_ref[5:6, 0:128] = jnp.sum(bias_ref[16:32, :], axis=0, keepdims=True)
    weight_grads(
        grads_ref, grad_driven_ref, normed_ref, low_ref, pre_grad_ref, grad_gated_ref, active_ref, quarter, states
    )
    bn_ref[...] = jnp.zeros_like(bn_ref)
    centre0, inv_dev0 = norm0_ref[0:1, own], norm0_ref[1:2, own]
    skip = feature_ref[SKIP : SKIP + 1, own]

    def back(rows, index, carry):
        held_ref[:, :width] = dot(grad_driven_ref[rows, :], b_ref[:, own], NN)
        base = index * part

        def inner(local, place_index, carry):
            here = pl.ds(pl.multiple_of(base + place_index * 16, 16), 16)
            grad = held_ref[local, :width] + skip * pre_grad_ref[here, own].astype(F32)
            grad_ref[here, :] = grad
            z = (x_ref[here, :] - centre0) * inv_dev0
            bn_ref[0:16, :] += grad
            bn_ref[16:32, :] += grad * z
            return carry

        for_rows(part, 16, inner, 0, unroll=2)
        return carry

    for_rows(total, part, back, 0)
    groups = send_ref.shape[0]
    share = send_ref.shape[1] - 32
    row_ref[0:8, :] = small_ref[...]
    row_ref[8:16, :] = small1_ref[...]
    row_ref[6:7, 0:width] = jnp.sum(bn_ref[0:16, :], axis=0, keepdims=True)
    row_ref[7:8, 0:width] = jnp.sum(bn_ref[16:32, :], axis=0, keepdims=True)
    exact = row_ref[...]
    high = exact.astype(LOW)
    rest = (exact - high.astype(F32)).astype(LOW)
    sections = ((grads_ref, 0), (grads1_ref, 0), (grads_ref, 128), (grads1_ref, 128),
                (grads_ref, 256), (grads_ref, 384), (grads1_ref, 256), (grads1_ref, 384))
    for group in range(groups):
        source, start = sections[group * share // 128]
        start += group * share % 128
        send_ref[group, :share, :] = source[start : start + share, :]
    for group in range(groups):
        send_ref[group, share : share + 16, :] = high
        send_ref[group, share + 16 :, :] = rest


def finish_kernel(
    meta_ref, got_ref, up_ref, grad_ref, x_ref, norm0_ref, feature_ref, nu_ref, theta_ref, bn1_ref,
    send_ref, nu_out, theta_out, gamma_out, skip_out, bias_out, gain_out, shift_out, out_ref,
    held_ref, row_ref, order_ref,
):
    length, quarter = meta_ref[0], meta_ref[1]
    groups = got_ref.shape[0]
    share = got_ref.shape[1] - 32
    total, width = x_ref.shape[0] - PARAM_ROWS, x_ref.shape[1]
    steps = total // CHUNKS
    own = lanes_at(quarter, width)
    small = jnp.zeros((16, got_ref.shape[2]), F32)
    for group in range(groups):
        small += got_ref[group, share : share + 16, :].astype(F32) + got_ref[group, share + 16 :, :].astype(F32)
    row_ref[...] = small
    for piece in range(0, share, 16):
        value = got_ref[0, piece : piece + 16, :].astype(F32)
        for group in range(1, groups):
            value += got_ref[group, piece : piece + 16, :].astype(F32)
        value = value.astype(LOW)
        for group in range(groups):
            send_ref[group, piece : piece + 16, :] = value
    states = nu_out.shape[1]
    bn1 = total_rows(bn1_ref, 2)
    held_ref[0:8, :] = bn1
    for layer, first in ((0, 0), (1, 8)):
        nu_out[layer : layer + 1, :] = -jnp.exp(nu_ref[layer : layer + 1, :]) * row_ref[first : first + 1, :states]
        theta_out[layer : layer + 1, :] = jnp.exp(theta_ref[layer : layer + 1, :]) * row_ref[first + 1 : first + 2, :states]
        gamma_out[layer : layer + 1, :] = row_ref[first + 2 : first + 3, :states]
        skip_out[layer : layer + 1, :] = row_ref[first + 3 : first + 4, :width]
        bias_out[layer, 0:1, :] = row_ref[first + 4 : first + 5, :width]
        bias_out[layer, 1:2, :] = row_ref[first + 5 : first + 6, :width]
    shift_out[0:1, :] = row_ref[6:7, :width]
    gain_out[0:1, :] = row_ref[7:8, :width]
    shift_out[1:2, :] = held_ref[0:1, own]
    gain_out[1:2, :] = held_ref[1:2, own]
    counted = norm0_ref[2:3, own]
    centre, inv_dev = norm0_ref[0:1, own], norm0_ref[1:2, own]
    level = row_ref[6:7, :width] / counted
    tilt = row_ref[7:8, :width] * inv_dev / counted
    scale = inv_dev * feature_ref[GAIN : GAIN + 1, own]

    def load(rows, index):
        keep = keep_rows(index, CHUNKS, steps, length)
        inner = grad_ref[rows, :] - level - (x_ref[rows, :] - centre) * tilt
        return up_ref[rows, :] + jnp.where(keep, scale * inner, 0.0)

    to_feature_rows(load, order_ref, out_ref, steps)


def call(kernel, outs, scratch, args, smem=1, flops=0, name=None):
    specs = [
        pl.BlockSpec(memory_space=pltpu.SMEM if place < smem else pltpu.VMEM) for place in range(len(args))
    ]
    moved = sum(a.size * a.dtype.itemsize for a in args) + sum(o.size * o.dtype.itemsize for o in outs)
    return pl.pallas_call(
        kernel,
        out_shape=tuple(outs),
        in_specs=specs,
        out_specs=tuple(pl.BlockSpec(memory_space=pltpu.VMEM) for _ in outs),
        scratch_shapes=scratch,
        compiler_params=pltpu.CompilerParams(vmem_limit_bytes=VMEM_BYTES),
        cost_estimate=pl.CostEstimate(flops=int(flops), bytes_accessed=int(moved), transcendentals=0),
        name=name,
    )(*args)


def shape(*dims, dtype=F32):
    return jax.ShapeDtypeStruct(dims, dtype)


def swap(value, bit, sharers):
    pairs = [(q * sharers + r, (q ^ bit) * sharers + r) for q in range(4) for r in range(sharers)]
    return lax.ppermute(value, "state", pairs)


def gather(value, sharers):
    across = swap(value, 2, sharers)
    return value, swap(value, 1, sharers), across, swap(across, 1, sharers)


def spread(value, axes, count):
    whole = jnp.broadcast_to(value[None], (count,) + value.shape)
    return lax.all_to_all(whole, axes, 0, 0, tiled=True).reshape((-1,) + value.shape[1:])


def local(
    inputs, lengths, cotangent, bn_gain, bn_bias, b_weight, c_weight, nu_log, theta_log, gamma_log, skip_weight,
    glu_weight, glu_bias, dp_size, state_size,
):
    sharers = state_size // 4
    place = lax.axis_index("state").astype(jnp.int32)
    quarter = place // sharers

    def joined(value, axis):
        if sharers == 1:
            return value
        groups = [[q * sharers + r for r in range(sharers)] for q in range(4)]
        return lax.all_gather(value, "state", axis=axis, axis_index_groups=groups, tiled=True)

    def own(value, axis):
        if sharers == 1:
            return value
        size = value.shape[axis] // sharers
        return lax.dynamic_slice_in_dim(value, place % sharers * size, size, axis)

    inputs, cotangent = joined(inputs, 1), joined(cotangent, 1)
    bn_gain, bn_bias, skip_weight = joined(bn_gain, 1), joined(bn_bias, 1), joined(skip_weight, 1)
    nu_log, theta_log, gamma_log = joined(nu_log, 1), joined(theta_log, 1), joined(gamma_log, 1)
    b_weight, c_weight = joined(b_weight, 2), joined(c_weight, 2)
    glu_weight, glu_bias = joined(glu_weight, 2), joined(glu_bias, 2)
    width, total = inputs.shape[1:]
    full = b_weight.shape[3]
    states = b_weight.shape[2] * 4
    own_states = b_weight.shape[2]
    part = 256
    meta = jnp.stack([lengths[0], quarter])
    modulus = jnp.exp(-jnp.exp(nu_log))
    angle = jnp.exp(theta_log)
    rates = jnp.stack([modulus * jnp.cos(angle), modulus * jnp.sin(angle), jnp.exp(gamma_log)], 1)
    rates = jnp.pad(rates.reshape(6, own_states), ((0, 0), (0, width - own_states)))
    features = jnp.concatenate(
        [jnp.stack([bn_gain, bn_bias, skip_weight], 1), glu_bias], 1
    ).reshape(10, width)
    params = jnp.concatenate([features, rates], 0)

    b_parts = [gather(b_weight[layer].reshape(2 * own_states, full), sharers) for layer in range(LAYERS)]
    c_parts = [gather(c_weight[layer].reshape(2 * own_states, full), sharers) for layer in range(LAYERS)]
    w_parts = [gather(glu_weight[layer].reshape(2 * width, full), sharers) for layer in range(LAYERS)]

    packed, sums = call(
        enter_kernel,
        (shape(total + PARAM_ROWS, width), shape(32, width)),
        [pltpu.VMEM((total, width), F32)],
        (meta, inputs[0], params),
        name="enter",
    )
    x_parts = gather(packed, sharers)
    sums = spread(sums[:8], ("dp", "state"), dp_size * state_size)
    if sharers > 1:
        sums = sums.reshape(dp_size * 4, sharers, 8, width)[:, 0].reshape(-1, width)
    cotangent_own, cotangent_low = call(
        cotangent_kernel,
        (shape(total, width), shape(total, width, dtype=LOW)),
        [pltpu.VMEM((total, width), F32)],
        (cotangent[0],),
        smem=0,
        name="cotangent",
    )
    cotangent_parts = (cotangent_own,) + gather(cotangent_low, sharers)[1:]
    (normed0, drive0, low0, slope0, active0, b_all, c_all, feature, state, norm0) = call(
        functools.partial(start_kernel, part=part),
        (
            shape(total, full, dtype=LOW),
            shape(total, 256),
            shape(total, 2 * states, dtype=LOW),
            shape(total, full, dtype=LOW),
            shape(total, full, dtype=LOW),
            shape(2 * states, full, dtype=LOW),
            shape(2 * states, full, dtype=LOW),
            shape(PARAM_ROWS, full),
            shape(8, states),
            shape(8, full),
        ),
        [pltpu.VMEM((total, 2 * states), F32), pltpu.VMEM((part, full), F32), pltpu.VMEM((8, full), F32)],
        (meta, *x_parts, sums, *b_parts[0], *c_parts[0]),
        flops=4e9,
        name="start",
    )
    stream1, linear0, gate0, w_all, sums1 = call(
        functools.partial(glu_kernel, part=part),
        (
            shape(total, full),
            shape(total, full, dtype=LOW),
            shape(total, full, dtype=LOW),
            shape(2 * full, full, dtype=LOW),
            shape(32, full),
        ),
        [pltpu.VMEM((part, 2 * full), F32)],
        (meta, *x_parts, active0, *w_parts[0], feature),
        flops=3e9,
        name="glu",
    )
    sums1 = spread(sums1[:8], "dp", dp_size)
    result, base, bn1, grads1, small1, norm1 = call(
        functools.partial(middle_kernel, part=part),
        (
            shape(width, total),
            shape(total, full),
            shape(32, full),
            shape(4 * width, full, dtype=LOW),
            shape(8, full),
            shape(8, full),
        ),
        [
            pltpu.VMEM((2 * states, full), LOW),
            pltpu.VMEM((2 * states, full), LOW),
            pltpu.VMEM((2 * full, full), LOW),
            pltpu.VMEM((total, full), LOW),
            pltpu.VMEM((total, 2 * states), F32),
            pltpu.VMEM((total, 256), F32),
            pltpu.VMEM((total, 2 * states), LOW),
            pltpu.VMEM((total, full), F32),
            pltpu.VMEM((total, full), LOW),
            pltpu.VMEM((part, 2 * full), F32),
            pltpu.VMEM((total, width), F32),
            pltpu.VMEM((total, width), F32),
            pltpu.VMEM((total, 2 * full), LOW),
            pltpu.VMEM((total, full), LOW),
            pltpu.VMEM((total, 2 * states), LOW),
            pltpu.VMEM((16, width), F32),
            pltpu.VMEM((32, width), F32),
        ],
        (meta, stream1, sums1, *b_parts[1], *c_parts[1], *w_parts[1], feature, state, norm0, *cotangent_parts),
        flops=2e10,
        name="middle",
    )
    bn1 = spread(bn1[:8], "dp", dp_size)
    share = 8 * width // dp_size
    send, up0, grad0 = call(
        functools.partial(last_kernel, part=part),
        (shape(dp_size, share + 32, full, dtype=LOW), shape(total, width), shape(total, width)),
        [
            pltpu.VMEM((part, 2 * full), F32),
            pltpu.VMEM((total, 2 * states), F32),
            pltpu.VMEM((total, 2 * full), LOW),
            pltpu.VMEM((total, full), LOW),
            pltpu.VMEM((total, 2 * states), LOW),
            pltpu.VMEM((16, width), F32),
            pltpu.VMEM((32, width), F32),
            pltpu.VMEM((8, full), F32),
            pltpu.VMEM((32, width), F32),
            pltpu.VMEM((4 * width, full), LOW),
            pltpu.VMEM((16, full), F32),
        ],
        (meta, stream1, base, bn1, norm1, gate0, linear0, slope0, active0, normed0, low0, drive0, b_all, c_all, w_all,
         feature, state, packed, norm0, grads1, small1),
        flops=1e10,
        name="last",
    )
    got = lax.all_to_all(send, "dp", 0, 0, tiled=True)
    back, grad_nu, grad_theta, grad_gamma, grad_skip, grad_bias, grad_gain, grad_shift, grad_inputs = call(
        finish_kernel,
        (
            shape(dp_size, share, full, dtype=LOW),
            shape(LAYERS, own_states),
            shape(LAYERS, own_states),
            shape(LAYERS, own_states),
            shape(LAYERS, width),
            shape(LAYERS, 2, width),
            shape(LAYERS, width),
            shape(LAYERS, width),
            shape(width, total),
        ),
        [pltpu.VMEM((8, full), F32), pltpu.VMEM((16, full), F32), pltpu.VMEM((total, width), F32)],
        (meta, got, up0, grad0, packed, norm0, feature, nu_log, theta_log, bn1),
        name="finish",
    )
    whole = lax.all_to_all(back, "dp", 0, 0, tiled=True).reshape(8 * width, full).astype(F32)
    grad_b = whole[: 2 * width].reshape(LAYERS, 2, own_states, full)
    grad_c = whole[2 * width : 4 * width].reshape(LAYERS, 2, own_states, full)
    grad_glu = whole[4 * width :].reshape(LAYERS, 2, width, full)
    return (
        own(result[None], 1),
        own(grad_inputs[None], 1),
        own(grad_gain, 1),
        own(grad_shift, 1),
        own(grad_b, 2),
        own(grad_c, 2),
        own(grad_nu, 1),
        own(grad_theta, 1),
        own(grad_gamma, 1),
        own(grad_skip, 1),
        own(grad_glu, 2),
        own(grad_bias, 2),
    )


def solution(mesh):
    in_specs = (
        P("dp", "state", None),
        P("dp"),
        P("dp", "state", None),
        P(None, "state"),
        P(None, "state"),
        P(None, None, "state", None),
        P(None, None, "state", None),
        P(None, "state"),
        P(None, "state"),
        P(None, "state"),
        P(None, "state"),
        P(None, None, "state", None),
        P(None, None, "state"),
    )
    out_specs = (
        P("dp", "state", None),
        P("dp", "state", None),
        P(None, "state"),
        P(None, "state"),
        P(None, None, "state", None),
        P(None, None, "state", None),
        P(None, "state"),
        P(None, "state"),
        P(None, "state"),
        P(None, "state"),
        P(None, None, "state", None),
        P(None, None, "state"),
    )
    step = functools.partial(local, dp_size=mesh.shape["dp"], state_size=mesh.shape["state"])
    return jax.shard_map(step, mesh=mesh, in_specs=in_specs, out_specs=out_specs, check_vma=False)
```

```python
import functools

import jax
import jax.numpy as jnp
from jax import lax
from jax.experimental import pallas as pl
from jax.experimental.pallas import tpu as pltpu
from jax.sharding import PartitionSpec as P

LAYERS = 2
CHUNKS = 16
EPSILON = 1e-05
F32 = jnp.float32
LOW = jnp.bfloat16
PARAM_ROWS = 16
VMEM_BYTES = 56 * 1024 * 1024

GAIN, SHIFT, SKIP, BIAS_LINEAR, BIAS_GATE = range(5)
RATE_RE, RATE_IM, GAMMA = range(3)

NN = (((1,), (0,)), ((), ()))
NT = (((1,), (1,)), ((), ()))
TN = (((0,), (0,)), ((), ()))


def dot(left, right, dims):
    return lax.dot_general(left, right, dims, preferred_element_type=F32)


def rows_at(index, size):
    return pl.ds(pl.multiple_of(index * size, size), size)


def lanes_at(quarter, width):
    return pl.ds(pl.multiple_of(quarter * width, width), width)


def for_rows(total, size, body, init=None, unroll=1):
    def step(index, carry):
        return body(rows_at(index, size), index, carry)

    return lax.fori_loop(0, total // size, step, init, unroll=unroll)


def own_quarter():
    return (lax.axis_index("state") // (lax.axis_size("state") // 4)).astype(jnp.int32)


def keep_rows(first_step, rows, steps, length):
    row = lax.broadcasted_iota(jnp.int32, (rows, 1), 0)
    position = (row % CHUNKS) * steps + row // CHUNKS + first_step
    return position < length


def gelu_parts(value):
    size = jnp.abs(value)
    below = 1.0 + size * (0.3275911 * 0.7071067811865476)
    guess = pl.reciprocal(below, approx=True)
    inverse = guess * (2.0 - below * guess)
    bell = jnp.exp(value * value * -0.5)
    tail = inverse * (
        0.5 * 0.254829592
        + inverse
        * (
            0.5 * -0.284496736
            + inverse * (0.5 * 1.421413741 + inverse * (0.5 * -1.453152027 + inverse * (0.5 * 1.061405429)))
        )
    )
    tail = tail * bell
    return jnp.where(value >= 0.0, 1.0 - tail, tail), bell * 0.3989422804014327


def sigmoid(value):
    return 0.5 * jnp.tanh(0.5 * value) + 0.5


def squared(re, im, times):
    for _ in range(times):
        re, im = re * re - im * im, 2.0 * re * im
    return re, im


def chunk_starts(re, im, rate_re, rate_im, reverse):
    row = lax.broadcasted_iota(jnp.int32, re.shape, 0)

    def moved(value, by):
        if reverse:
            return jnp.where(row < CHUNKS - by, pltpu.roll(value, CHUNKS - by, 0), 0.0)
        return jnp.where(row >= by, pltpu.roll(value, by, 0), 0.0)

    by = 1
    while by < CHUNKS:
        past_re, past_im = moved(re, by), moved(im, by)
        re, im = (
            re + rate_re * past_re - rate_im * past_im,
            im + rate_re * past_im + rate_im * past_re,
        )
        rate_re, rate_im = squared(rate_re, rate_im, 1)
        by *= 2
    return moved(re, 1), moved(im, 1)


def sweep(drive_ref, rate_re, rate_im, steps, reverse, emit, extra, unroll=4):
    states = rate_re.shape[1]
    shape = (CHUNKS, states)
    wide_re = jnp.broadcast_to(rate_re, shape)
    wide_im = jnp.broadcast_to(rate_im, shape)

    def advance(index, re, im):
        place = steps - 1 - index if reverse else index
        rows = rows_at(place, CHUNKS)
        drive_re = drive_ref[rows, :states]
        drive_im = drive_ref[rows, states:]
        new_re = (wide_re * re + drive_re) - wide_im * im
        new_im = (wide_re * im + drive_im) + wide_im * re
        return rows, place, new_re, new_im, drive_re, drive_im

    def first(index, carry):
        _, _, re, im, _, _ = advance(index, *carry)
        return re, im

    def second(index, carry):
        re, im, held = carry
        rows, place, re, im, drive_re, drive_im = advance(index, re, im)
        return re, im, emit(rows, place, re, im, drive_re, drive_im, held)

    zero = jnp.zeros(shape, F32)
    re, im = lax.fori_loop(0, steps, first, (zero, zero), unroll=unroll)
    far_re, far_im = rate_re, rate_im
    power = 1
    while power < steps:
        far_re, far_im = squared(far_re, far_im, 1)
        power *= 2
    re, im = chunk_starts(re, im, far_re, far_im, reverse)
    return lax.fori_loop(0, steps, second, (re, im, extra), unroll=unroll)[2]


def from_feature_rows(source_ref, held_ref, steps, emit):
    length = source_ref.shape[1]
    for block in range(length // 128):
        held_ref[block * 128 : (block + 1) * 128, :] = source_ref[:, block * 128 : (block + 1) * 128].T

    def step(index, carry):
        emit(rows_at(index, CHUNKS), index, held_ref[pl.ds(index, CHUNKS, stride=steps), :])
        return carry

    lax.fori_loop(0, steps, step, 0, unroll=4)


def to_feature_rows(load, held_ref, out_ref, steps):
    length = out_ref.shape[1]

    def step(index, carry):
        held_ref[pl.ds(index, CHUNKS, stride=steps), :] = load(rows_at(index, CHUNKS), index)
        return carry

    lax.fori_loop(0, steps, step, 0, unroll=4)
    for block in range(length // 128):
        out_ref[:, block * 128 : (block + 1) * 128] = held_ref[block * 128 : (block + 1) * 128, :].T


def spread_rows(sums_ref, spread_ref):
    for group in range(spread_ref.shape[0]):
        spread_ref[group, :, :] = sums_ref[0:8, :]


def total_rows(sums_ref):
    value = sums_ref[0, :, :]
    for other in range(1, sums_ref.shape[0]):
        value += sums_ref[other, :, :]
    return value


def enter_kernel(
    length_ref, x_ref, gain_ref, shift_ref, skip_ref, bias_ref, nu_ref, theta_ref, gamma_ref, b_ref, c_ref, w_ref,
    out_ref, spread_ref, b0_ref, cw0_ref, later_ref,
    held_ref, sums_ref, stage_b, stage_c, stage_w, arrived, copied,
):
    length = length_ref[0]
    total = x_ref.shape[1]
    steps = total // CHUNKS
    own_states = nu_ref.shape[1]
    half, full = b_ref.shape[1], w_ref.shape[1]
    stages = ((b_ref, stage_b), (c_ref, stage_c), (w_ref, stage_w))
    arrivals = [pltpu.make_async_copy(*move, arrived.at[place]) for place, move in enumerate(stages)]
    for copy in arrivals:
        copy.start()
    moves = (
        (stage_b.at[0], b0_ref),
        (stage_c.at[0], cw0_ref.at[0:half]),
        (stage_w.at[0], cw0_ref.at[half:]),
        (stage_b.at[1], later_ref.at[0:half]),
        (stage_c.at[1], later_ref.at[half : 2 * half]),
        (stage_w.at[1], later_ref.at[2 * half :]),
    )
    copies = [pltpu.make_async_copy(*move, copied.at[place]) for place, move in enumerate(moves)]
    out_ref[total:, :] = jnp.zeros((PARAM_ROWS, x_ref.shape[0]), F32)
    for layer in range(LAYERS):
        first = total + 5 * layer
        out_ref[first + GAIN : first + GAIN + 1, :] = gain_ref[layer : layer + 1, :]
        out_ref[first + SHIFT : first + SHIFT + 1, :] = shift_ref[layer : layer + 1, :]
        out_ref[first + SKIP : first + SKIP + 1, :] = skip_ref[layer : layer + 1, :]
        out_ref[first + BIAS_LINEAR : first + BIAS_GATE + 1, :] = bias_ref[layer, :, :]
        first = total + 10 + 3 * layer
        for row, source in enumerate((nu_ref, theta_ref, gamma_ref)):
            out_ref[first + row : first + row + 1, :own_states] = source[layer : layer + 1, :]
    sums_ref[...] = jnp.zeros_like(sums_ref)
    for copy in arrivals:
        copy.wait()
    for copy in copies:
        copy.start()

    def emit(rows, index, value):
        out_ref[rows, :] = value
        kept = jnp.where(keep_rows(index, CHUNKS, steps, length), value, 0.0)
        sums_ref[0:16, :] += kept
        sums_ref[16:32, :] += kept * kept

    from_feature_rows(x_ref, held_ref, steps, emit)
    plain = jnp.sum(sums_ref[0:16, :], axis=0, keepdims=True)
    square = jnp.sum(sums_ref[16:32, :], axis=0, keepdims=True)
    sums_ref[0:1, :] = plain
    sums_ref[1:2, :] = square
    sums_ref[2:3, :] = jnp.full((1, x_ref.shape[0]), length, jnp.int32).astype(F32)
    spread_rows(sums_ref, spread_ref)
    for copy in copies:
        copy.wait()


def cotangent_kernel(x_ref, out_ref, low_ref, held_ref):
    steps = x_ref.shape[1] // CHUNKS

    def emit(rows, index, value):
        out_ref[rows, :] = value
        low_ref[rows, :] = value.astype(LOW)

    from_feature_rows(x_ref, held_ref, steps, emit)


def assemble_states(parts, whole_ref):
    half = parts[0].shape[0] // 2
    states = half * len(parts)
    for place, part in enumerate(parts):
        whole_ref[place * half : (place + 1) * half, :] = part[:half, :]
        whole_ref[states + place * half : states + (place + 1) * half, :] = part[half:, :]


def assemble_output(parts, whole_ref):
    half = parts[0].shape[0] // 2
    states = half * len(parts)
    for place, part in enumerate(parts):
        whole_ref[place * half : (place + 1) * half, :] = part[:half, :]
        whole_ref[states + place * half : states + (place + 1) * half, :] = -part[half:, :]


def assemble_glu(parts, whole_ref, quarter):
    half = parts[0].shape[0] // 2
    width = half * len(parts)
    for place, part in enumerate(parts):
        whole_ref[lanes_at(quarter ^ place, half), :] = part[:half, :]
        whole_ref[pl.ds(pl.multiple_of(width + (quarter ^ place) * half, half), half), :] = part[half:, :]


def norm_rows(sums, counted):
    centre = sums[0:1, :] / counted
    meansq = sums[1:2, :] / counted
    return centre, lax.rsqrt(meansq - centre * centre + EPSILON)


def drive_phase(normed_ref, b_ref, drive_ref, gamma, part):
    total = normed_ref.shape[0]
    both = jnp.concatenate([gamma, gamma], axis=1)

    def body(rows, index, carry):
        drive_ref[rows, :] = dot(normed_ref[rows, :], b_ref[...], NT) * both
        return carry

    for_rows(total, part, body, 0)


def pre_phase(low_ref, c_ref, normed_ref, skip, active_ref, slope_ref, held_ref, part):
    total = normed_ref.shape[0]

    def body(rows, index, carry):
        held_ref[...] = dot(low_ref[rows, :], c_ref[...], NN)
        base = index * part

        def inner(local, place, carry):
            here = pl.ds(pl.multiple_of(base + place * 16, 16), 16)
            value = held_ref[local, :] + skip * normed_ref[here, :].astype(F32)
            cdf, density = gelu_parts(value)
            active_ref[here, :] = (value * cdf).astype(LOW)
            slope_ref[here, :] = (cdf + value * density).astype(slope_ref.dtype)
            return carry

        for_rows(part, 16, inner, 0, unroll=2)
        return carry

    for_rows(total, part, body, 0)


def drive_kernel(
    length_ref, x0, x1, x2, x3, sums_ref, b0, b1, b2, b3,
    normed_ref, drive_own_ref, low_ref, b_ref, feature_ref, state_ref, norm_ref,
    drive_ref, stats_ref, part,
):
    length, quarter = length_ref[0], own_quarter()
    parts = (x0, x1, x2, x3)
    total = normed_ref.shape[0]
    steps = total // CHUNKS
    width = x0.shape[1]
    assemble_states((b0, b1, b2, b3), b_ref)
    lane = lax.broadcasted_iota(jnp.int32, (8, width), 1)
    for place, value in enumerate(parts):
        feature_ref[:, lanes_at(quarter ^ place, width)] = value[total:, :]
    for pair in range(2):
        early, late = parts[2 * pair][total + 8 :, :], parts[2 * pair + 1][total + 8 :, :]
        logs = jnp.where(lane < 64, early, pltpu.roll(late, 64, 1))
        lanes = slice(pair * width, (pair + 1) * width)
        for layer in range(LAYERS):
            first = 2 + 3 * layer
            modulus = jnp.exp(-jnp.exp(logs[first : first + 1, :]))
            angle = jnp.exp(logs[first + 1 : first + 2, :])
            state_ref[first : first + 1, lanes] = modulus * jnp.cos(angle)
            state_ref[first + 1 : first + 2, lanes] = modulus * jnp.sin(angle)
            state_ref[first + 2 : first + 3, lanes] = jnp.exp(logs[first + 2 : first + 3, :])
    for place in range(4):
        value = sums_ref[place, :, :]
        for other in range(1, sums_ref.shape[0] // 4):
            value += sums_ref[other * 4 + place, :, :]
        stats_ref[:, place * width : (place + 1) * width] = value
    centre, inv_dev = norm_rows(stats_ref[0:2, :], stats_ref[2:3, :])
    norm_ref[...] = jnp.zeros_like(norm_ref)
    norm_ref[0:1, :] = centre
    norm_ref[1:2, :] = inv_dev
    norm_ref[2:3, :] = stats_ref[2:3, :]

    def normal(rows, index, carry):
        keep = keep_rows(index * 2, 32, steps, length)
        for place, value in enumerate(parts):
            lanes = lanes_at(quarter ^ place, width)
            z = (value[rows, :] - norm_ref[0:1, lanes]) * norm_ref[1:2, lanes]
            z = z * feature_ref[GAIN : GAIN + 1, lanes] + feature_ref[SHIFT : SHIFT + 1, lanes]
            normed_ref[rows, lanes] = jnp.where(keep, z, 0.0).astype(LOW)
        return carry

    for_rows(total, 32, normal, 0)
    state = state_ref[...]
    states = state.shape[1]
    drive_phase(normed_ref, b_ref, drive_ref, state[2 + GAMMA : 3 + GAMMA, :], part)

    def emit(rows, step, re, im, drive_re, drive_im, held):
        low_ref[rows, :states] = re.astype(LOW)
        low_ref[rows, states:] = im.astype(LOW)
        drive_own_ref[rows, :128] = drive_re[:, :128]
        drive_own_ref[rows, 128:] = drive_im[:, :128]
        return held

    sweep(drive_ref, state[2:3, :], state[3:4, :], steps, False, emit, 0)


def glu_kernel(
    length_ref, x0, x1, x2, x3, normed_ref, low_ref, cw0, cw1, cw2, cw3, feature_ref,
    stream_ref, linear_ref, gate_ref, slope_ref, active_ref, c_ref, w_ref, spread_ref,
    held_ref, sums_ref, part,
):
    length, quarter = length_ref[0], own_quarter()
    parts = (x0, x1, x2, x3)
    total, full = active_ref.shape
    steps = total // CHUNKS
    width = x0.shape[1]
    weights = (cw0, cw1, cw2, cw3)
    assemble_output([part_ref.at[0:width] for part_ref in weights], c_ref)
    assemble_glu([part_ref.at[width : 3 * width] for part_ref in weights], w_ref, quarter)
    pre_phase(
        low_ref, c_ref, normed_ref, feature_ref[SKIP : SKIP + 1, :], active_ref, slope_ref, held_ref.at[:, :full], part
    )
    sums_ref[...] = jnp.zeros_like(sums_ref)

    def body(rows, index, carry):
        held_ref[...] = dot(active_ref[rows, :], w_ref[...], NT)
        base = index * part

        def inner(local, place_index, carry):
            here = pl.ds(pl.multiple_of(base + place_index * 16, 16), 16)
            keep = keep_rows(index * (part // CHUNKS) + place_index, 16, steps, length)
            for place, value in enumerate(parts):
                lanes = lanes_at(quarter ^ place, width)
                far = pl.ds(pl.multiple_of(full + (quarter ^ place) * width, width), width)
                linear = held_ref[local, lanes] + feature_ref[BIAS_LINEAR : BIAS_LINEAR + 1, lanes]
                gate = sigmoid(held_ref[local, far] + feature_ref[BIAS_GATE : BIAS_GATE + 1, lanes])
                mixed = linear * gate
                gate_ref[here, lanes] = gate.astype(gate_ref.dtype)
                linear_ref[here, lanes] = (mixed * (1.0 - gate)).astype(linear_ref.dtype)
                moved = value[here, :] + jnp.where(keep, mixed, 0.0)
                stream_ref[here, lanes] = moved
                kept = jnp.where(keep, moved, 0.0)
                sums_ref[0:16, lanes] += kept
                sums_ref[16:32, lanes] += kept * kept
            return carry

        for_rows(part, 16, inner, 0, unroll=2)
        return carry

    for_rows(total, part, body, 0)
    plain = jnp.sum(sums_ref[0:16, :], axis=0, keepdims=True)
    square = jnp.sum(sums_ref[16:32, :], axis=0, keepdims=True)
    sums_ref[0:1, :] = plain
    sums_ref[1:2, :] = square
    spread_rows(sums_ref, spread_ref)


def pre_grad_phase(grad_gated_ref, w_ref, slope_ref, normed_ref, quarter, pre_grad_ref, held_ref, small_ref, sum_ref, part):
    total, full = normed_ref.shape
    width = 128
    own = lanes_at(quarter, width)
    sum_ref[...] = jnp.zeros_like(sum_ref)

    def body(rows, index, carry):
        held_ref[:, :full] = dot(grad_gated_ref[rows, :], w_ref[...], NN)
        base = index * part

        def inner(local, place, carry):
            here = pl.ds(pl.multiple_of(base + place * 16, 16), 16)
            pre_grad_ref[here, :] = (held_ref[local, :full] * slope_ref[here, :].astype(F32)).astype(LOW)
            sum_ref[...] += pre_grad_ref[here, own].astype(F32) * normed_ref[here, own].astype(F32)
            return carry

        for_rows(part, 16, inner, 0, unroll=2)
        return carry

    for_rows(total, part, body, 0)
    small_ref[3:4, 0:128] = jnp.sum(sum_ref[...], axis=0, keepdims=True)


def adjoint_phase(
    pre_grad_ref, c_ref, low_ref, drive_own_ref, state, first_row, length,
    grad_state_ref, grad_driven_ref, small_ref, reverse, part,
):
    total = pre_grad_ref.shape[0]
    steps = total // CHUNKS
    states = state.shape[1]

    def body(rows, index, carry):
        grad_state_ref[rows, :] = dot(pre_grad_ref[rows, :], c_ref[...], NT)
        return carry

    for_rows(total, part, body, 0)
    rate_re = state[first_row : first_row + 1, :]
    rate_im = state[first_row + 1 : first_row + 2, :]
    gamma = jnp.broadcast_to(state[first_row + 2 : first_row + 3, :], (CHUNKS, states))

    def emit(rows, step, re, im, drive_re, drive_im, held):
        out_re, out_im = gamma * re, gamma * im
        if not reverse:
            keep = keep_rows(step, CHUNKS, steps, length)
            out_re, out_im = jnp.where(keep, out_re, 0.0), jnp.where(keep, out_im, 0.0)
        grad_driven_ref[rows, :states] = out_re.astype(LOW)
        grad_driven_ref[rows, states:] = out_im.astype(LOW)
        one, two, three = held
        own_re, own_im = re[:, :128], im[:, :128]
        late_re, late_im = own_re - drive_re[:, :128], own_im - drive_im[:, :128]
        low_re = low_ref[rows, :128].astype(F32)
        low_im = low_ref[rows, states : states + 128].astype(F32)
        one = one + late_re * low_re + late_im * low_im
        two = two + late_im * low_re - late_re * low_im
        three = three + own_re * drive_own_ref[rows, :128] + own_im * drive_own_ref[rows, 128:]
        return one, two, three

    zero = jnp.zeros((CHUNKS, 128), F32)
    one, two, three = sweep(grad_state_ref, rate_re, -rate_im, steps, reverse, emit, (zero, zero, zero))
    small_ref[0:1, 0:128] = jnp.sum(one, axis=0, keepdims=True)
    small_ref[1:2, 0:128] = jnp.sum(two, axis=0, keepdims=True)
    small_ref[2:3, 0:128] = jnp.sum(three, axis=0, keepdims=True)


def glu_grads(grads_ref, first, grad_gated_ref, active_ref, quarter):
    full = active_ref.shape[1]
    for place in range(2):
        lanes = pl.ds(pl.multiple_of(place * full + quarter * 128, 128), 128)
        got = dot(grad_gated_ref[:, lanes], active_ref[...], TN)
        grads_ref[first + place * 128 : first + (place + 1) * 128, :] = got.astype(LOW)


def state_grads(grads_ref, grad_driven_ref, normed_ref, low_ref, pre_grad_ref, states):
    half = states // 4
    for place in range(2):
        lanes = slice(place * states, place * states + 128)
        got = dot(grad_driven_ref[:, lanes], normed_ref[...], TN)[:half, :]
        grads_ref[place * half : (place + 1) * half, :] = got.astype(LOW)
        got = dot(low_ref[:, lanes], pre_grad_ref[...], TN)[:half, :]
        got = got if place == 0 else -got
        grads_ref[2 * half + place * half : 2 * half + (place + 1) * half, :] = got.astype(LOW)


def middle_kernel(
    length_ref, stream_ref, sums_ref, parts, ups, feature_ref, state_ref, norm0_ref,
    result_ref, base_ref, spread_ref, norm_ref, grads_ref,
    bn_ref, small_ref,
    b_ref, c_ref, w_ref, normed_ref, drive_ref, drive_own_ref, low_ref, slope_ref, active_ref, held_ref, own_ref,
    order_ref, grad_gated_ref, pre_grad_ref, grad_driven_ref, sum_ref, bias_ref, part,
):
    length, quarter = length_ref[0], own_quarter()
    total, full = stream_ref.shape
    steps = total // CHUNKS
    width = 128
    own = lanes_at(quarter, width)
    assemble_states([part_ref.at[0:128] for part_ref in parts], b_ref)
    assemble_output([part_ref.at[128:256] for part_ref in parts], c_ref)
    assemble_glu([part_ref.at[256:512] for part_ref in parts], w_ref, quarter)
    counted = norm0_ref[2:3, :]
    centre, inv_dev = norm_rows(total_rows(sums_ref), counted)
    norm_ref[...] = jnp.zeros_like(norm_ref)
    norm_ref[0:1, :] = centre
    norm_ref[1:2, :] = inv_dev
    norm_ref[2:3, :] = counted
    gain = feature_ref[5 + GAIN : 6 + GAIN, :]
    shift = feature_ref[5 + SHIFT : 6 + SHIFT, :]
    skip = feature_ref[5 + SKIP : 6 + SKIP, :]

    def normal(rows, index, carry):
        keep = keep_rows(index, 16, steps, length)
        z = (stream_ref[rows, :] - centre) * inv_dev
        normed_ref[rows, :] = jnp.where(keep, z * gain + shift, 0.0).astype(LOW)
        return carry

    for_rows(total, 16, normal, 0, unroll=2)
    state = state_ref[...]
    states = state.shape[1]
    drive_phase(normed_ref, b_ref, drive_ref, state[5 + GAMMA : 6 + GAMMA, :], part)

    def emit(rows, step, re, im, drive_re, drive_im, held):
        low_ref[rows, :states] = re.astype(LOW)
        low_ref[rows, states:] = im.astype(LOW)
        drive_own_ref[rows, :128] = drive_re[:, :128]
        drive_own_ref[rows, 128:] = drive_im[:, :128]
        return held

    sweep(drive_ref, state[5:6, :], state[6:7, :], steps, True, emit, 0)
    pre_phase(low_ref, c_ref, normed_ref, skip, active_ref, slope_ref, held_ref.at[:, :full], part)
    bias_ref[...] = jnp.zeros_like(bias_ref)

    def body(rows, index, carry):
        held_ref[...] = dot(active_ref[rows, :], w_ref[...], NT)
        base = index * part

        def inner(local, place_index, carry):
            here = pl.ds(pl.multiple_of(base + place_index * 16, 16), 16)
            keep = keep_rows(index * (part // CHUNKS) + place_index, 16, steps, length)
            for place, value in enumerate(ups):
                lanes = lanes_at(quarter ^ place, width)
                far = pl.ds(pl.multiple_of(full + (quarter ^ place) * width, width), width)
                linear = held_ref[local, lanes] + feature_ref[5 + BIAS_LINEAR : 6 + BIAS_LINEAR, lanes]
                gate = sigmoid(held_ref[local, far] + feature_ref[5 + BIAS_GATE : 6 + BIAS_GATE, lanes])
                mixed = linear * gate
                up = jnp.where(keep, value[here, :].astype(F32), 0.0)
                grad_linear = (up * gate).astype(LOW)
                grad_gate = (up * mixed * (1.0 - gate)).astype(LOW)
                grad_gated_ref[here, lanes] = grad_linear
                grad_gated_ref[here, far] = grad_gate
                if place == 0:
                    own_ref[here, :] = stream_ref[here, lanes] + jnp.where(keep, mixed, 0.0)
                    bias_ref[0:16, :] += grad_linear.astype(F32)
                    bias_ref[16:32, :] += grad_gate.astype(F32)
            return carry

        for_rows(part, 16, inner, 0, unroll=2)
        return carry

    for_rows(total, part, body, 0)
    to_feature_rows(lambda rows, index: own_ref[rows, :], order_ref, result_ref, steps)
    small_ref[...] = jnp.zeros_like(small_ref)
    pre_grad_phase(
        grad_gated_ref, w_ref, slope_ref, normed_ref, quarter, pre_grad_ref, held_ref, small_ref, sum_ref, part
    )
    adjoint_phase(
        pre_grad_ref, c_ref, low_ref, drive_own_ref, state, 5, length,
        drive_ref, grad_driven_ref, small_ref, False, part,
    )
    small_ref[4:5, 0:128] = jnp.sum(bias_ref[0:16, :], axis=0, keepdims=True)
    small_ref[5:6, 0:128] = jnp.sum(bias_ref[16:32, :], axis=0, keepdims=True)
    glu_grads(grads_ref, 2 * width, grad_gated_ref, active_ref, quarter)
    state_grads(grads_ref, grad_driven_ref, normed_ref, low_ref, pre_grad_ref, states)
    bn_ref[...] = jnp.zeros_like(bn_ref)
    scale = inv_dev * gain

    def back(rows, index, carry):
        held_ref[:, :full] = dot(grad_driven_ref[rows, :], b_ref[...], NN)
        base = index * part

        def inner(local, place_index, carry):
            here = pl.ds(pl.multiple_of(base + place_index * 16, 16), 16)
            grad = held_ref[local, :full] + skip * pre_grad_ref[here, :].astype(F32)
            z = (stream_ref[here, :] - centre) * inv_dev
            bn_ref[0:16, :] += grad
            bn_ref[16:32, :] += grad * z
            base_ref[here, :] = scale * grad
            return carry

        for_rows(part, 16, inner, 0, unroll=2)
        return carry

    for_rows(total, part, back, 0)

    def add(rows, index, carry):
        for place, value in enumerate(ups):
            lanes = lanes_at(quarter ^ place, width)
            base_ref[rows, lanes] += value[rows, :].astype(F32)
        return carry

    for_rows(total, 16, add, 0, unroll=2)
    plain = jnp.sum(bn_ref[0:16, :], axis=0, keepdims=True)
    scaled = jnp.sum(bn_ref[16:32, :], axis=0, keepdims=True)
    bn_ref[0:1, :] = plain
    bn_ref[1:2, :] = scaled
    bn_ref[2:8, :] = small_ref[0:6, :]
    spread_rows(bn_ref, spread_ref)


def last_glu_kernel(
    length_ref, stream_ref, base_ref, sums_ref, norm_ref, gate_ref, linear_ref, slope_ref, active_ref, normed_ref, w_ref,
    feature_ref,
    up_ref, pre_grad_ref, grads_ref, small_ref,
    held_ref, grad_gated_ref, sum_ref, bias_ref, row_ref, part,
):
    length, quarter = length_ref[0], own_quarter()
    total, full = stream_ref.shape
    steps = total // CHUNKS
    width = 128
    own = lanes_at(quarter, width)
    counted = norm_ref[2:3, :]
    whole = total_rows(sums_ref)
    centre, inv_dev = norm_ref[0:1, :], norm_ref[1:2, :]
    gain = feature_ref[5 + GAIN : 6 + GAIN, :]
    scale = inv_dev * gain
    level = scale * whole[0:1, :] / counted
    tilt = scale * inv_dev * whole[1:2, :] / counted
    bias_ref[...] = jnp.zeros_like(bias_ref)

    def top(rows, index, carry):
        keep = keep_rows(index, 16, steps, length)
        up = base_ref[rows, :] - jnp.where(keep, level + (stream_ref[rows, :] - centre) * tilt, 0.0)
        row_ref[...] = up
        up_ref[rows, :] = row_ref[:, own]
        up = jnp.where(keep, up, 0.0)
        grad_gated_ref[rows, :full] = (up * gate_ref[rows, :].astype(F32)).astype(LOW)
        grad_gated_ref[rows, full:] = (up * linear_ref[rows, :].astype(F32)).astype(LOW)
        bias_ref[0:16, :] += grad_gated_ref[rows, own].astype(F32)
        bias_ref[16:32, :] += grad_gated_ref[rows, pl.ds(pl.multiple_of(full + quarter * width, width), width)].astype(F32)
        return carry

    for_rows(total, 16, top, 0, unroll=2)
    small_ref[...] = jnp.zeros_like(small_ref)
    pre_grad_phase(
        grad_gated_ref, w_ref, slope_ref, normed_ref, quarter, pre_grad_ref, held_ref, small_ref, sum_ref, part
    )
    small_ref[4:5, 0:128] = jnp.sum(bias_ref[0:16, :], axis=0, keepdims=True)
    small_ref[5:6, 0:128] = jnp.sum(bias_ref[16:32, :], axis=0, keepdims=True)
    glu_grads(grads_ref, 0, grad_gated_ref, active_ref, quarter)


def last_state_kernel(
    length_ref, pre_grad_ref, normed_ref, low_ref, drive_own_ref, b_ref, c_ref, glu_grads_ref, small_in_ref, feature_ref,
    state_ref, x_ref, norm0_ref,
    send_ref, grad_ref,
    held_ref, grad_state_ref, grad_driven_ref, small_ref, bn_ref, grads_ref, row_ref, part,
):
    length, quarter = length_ref[0], own_quarter()
    total, full = normed_ref.shape
    width = 128
    own = lanes_at(quarter, width)
    small_ref[...] = small_in_ref[...]
    state = state_ref[...]
    adjoint_phase(
        pre_grad_ref, c_ref, low_ref, drive_own_ref, state, 2, length,
        grad_state_ref, grad_driven_ref, small_ref, True, part,
    )
    state_grads(grads_ref, grad_driven_ref, normed_ref, low_ref, pre_grad_ref, state.shape[1])
    grads_ref[2 * width :, :] = glu_grads_ref[...]
    bn_ref[...] = jnp.zeros_like(bn_ref)
    centre0, inv_dev0 = norm0_ref[0:1, own], norm0_ref[1:2, own]
    skip = feature_ref[SKIP : SKIP + 1, own]

    def back(rows, index, carry):
        held_ref[:, :width] = dot(grad_driven_ref[rows, :], b_ref[:, own], NN)
        base = index * part

        def inner(local, place_index, carry):
            here = pl.ds(pl.multiple_of(base + place_index * 16, 16), 16)
            grad = held_ref[local, :width] + skip * pre_grad_ref[here, own].astype(F32)
            grad_ref[here, :] = grad
            z = (x_ref[here, :] - centre0) * inv_dev0
            bn_ref[0:16, :] += grad
            bn_ref[16:32, :] += grad * z
            return carry

        for_rows(part, 16, inner, 0, unroll=2)
        return carry

    for_rows(total, part, back, 0)
    small_ref[6:7, 0:width] = jnp.sum(bn_ref[0:16, :], axis=0, keepdims=True)
    small_ref[7:8, 0:width] = jnp.sum(bn_ref[16:32, :], axis=0, keepdims=True)
    row_ref[...] = jnp.zeros_like(row_ref)
    for place in range(8):
        row_ref[place // 4 : place // 4 + 1, place % 4 * width : (place % 4 + 1) * width] = small_ref[place : place + 1, 0:width]
    exact = row_ref[0:8, :]
    row_ref[8:16, :] = exact - exact.astype(LOW).astype(F32)
    groups = send_ref.shape[0]
    share = send_ref.shape[1] - 16
    for group in range(groups):
        send_ref[group, :share, :] = grads_ref[group * share : (group + 1) * share, :]
        send_ref[group, share:, :] = row_ref[...].astype(LOW)


def add_kernel(got_ref, send_ref):
    groups, share = got_ref.shape[:2]
    for piece in range(0, share, 16):
        value = got_ref[0, piece : piece + 16, :].astype(F32)
        for group in range(1, groups):
            value += got_ref[group, piece : piece + 16, :].astype(F32)
        value = value.astype(LOW)
        for group in range(groups):
            send_ref[group, piece : piece + 16, :] = value


def share_kernel(got_ref, send_ref, small_ref):
    groups = got_ref.shape[0]
    share = got_ref.shape[1] - 16
    for piece in range(0, share, 16):
        value = got_ref[0, piece : piece + 16, :].astype(F32)
        for group in range(1, groups):
            value += got_ref[group, piece : piece + 16, :].astype(F32)
        value = value.astype(LOW)
        for group in range(groups):
            send_ref[group, piece : piece + 16, :] = value
    small = got_ref[0, share:, :].astype(F32)
    for group in range(1, groups):
        small += got_ref[group, share:, :].astype(F32)
    small_ref[...] = small[0:8, :] + small[8:16, :]


def finish_kernel(
    length_ref, up_ref, grad_ref, x_ref, norm0_ref, feature_ref, nu_ref, theta_ref, bn1_ref, small0_ref,
    nu_out, theta_out, gamma_out, skip_out, bias_out, gain_out, shift_out, out_ref,
    held_ref, order_ref,
):
    length, quarter = length_ref[0], own_quarter()
    total, width = up_ref.shape
    steps = total // CHUNKS
    own = lanes_at(quarter, width)
    states = nu_out.shape[1]
    held_ref[0:8, :] = total_rows(bn1_ref)
    for place in range(8):
        held_ref[8 + place : 9 + place, :width] = small0_ref[place // 4 : place // 4 + 1, place % 4 * width : (place % 4 + 1) * width]
    for layer, first in ((0, 8), (1, 2)):
        nu_out[layer : layer + 1, :] = -jnp.exp(nu_ref[layer : layer + 1, :]) * held_ref[first : first + 1, :states]
        theta_out[layer : layer + 1, :] = jnp.exp(theta_ref[layer : layer + 1, :]) * held_ref[first + 1 : first + 2, :states]
        gamma_out[layer : layer + 1, :] = held_ref[first + 2 : first + 3, :states]
        skip_out[layer : layer + 1, :] = held_ref[first + 3 : first + 4, :width]
        bias_out[layer, 0:1, :] = held_ref[first + 4 : first + 5, :width]
        bias_out[layer, 1:2, :] = held_ref[first + 5 : first + 6, :width]
    shift_out[0:1, :] = held_ref[14:15, :width]
    gain_out[0:1, :] = held_ref[15:16, :width]
    shift_out[1:2, :] = held_ref[0:1, own]
    gain_out[1:2, :] = held_ref[1:2, own]
    counted = norm0_ref[2:3, own]
    centre, inv_dev = norm0_ref[0:1, own], norm0_ref[1:2, own]
    level = held_ref[14:15, :width] / counted
    tilt = held_ref[15:16, :width] * inv_dev / counted
    scale = inv_dev * feature_ref[GAIN : GAIN + 1, own]

    def load(rows, index):
        keep = keep_rows(index, CHUNKS, steps, length)
        inner = grad_ref[rows, :] - level - (x_ref[rows, :] - centre) * tilt
        return up_ref[rows, :] + jnp.where(keep, scale * inner, 0.0)

    to_feature_rows(load, order_ref, out_ref, steps)


def widen_kernel(grads0_ref, grads1_ref, b_ref, c_ref, w_ref):
    half = b_ref.shape[1]
    for layer, source in enumerate((grads0_ref, grads1_ref)):
        b_ref[layer, :, :] = source[0:half, :].astype(F32)
        c_ref[layer, :, :] = source[half : 2 * half, :].astype(F32)
        w_ref[layer, :, :] = source[2 * half :, :].astype(F32)


def call(kernel, outs, scratch, args, smem=1, name=None, any_args=(), any_outs=()):
    def space(place):
        return pltpu.SMEM if place < smem else pl.ANY if place in any_args else pltpu.VMEM

    return pl.pallas_call(
        kernel,
        out_shape=tuple(outs),
        in_specs=[pl.BlockSpec(memory_space=space(place)) for place in range(len(args))],
        out_specs=tuple(
            pl.BlockSpec(memory_space=pl.ANY if place in any_outs else pltpu.VMEM) for place in range(len(outs))
        ),
        scratch_shapes=scratch,
        compiler_params=pltpu.CompilerParams(vmem_limit_bytes=VMEM_BYTES),
        cost_estimate=pl.CostEstimate(flops=0, bytes_accessed=0, transcendentals=0),
        name=name,
    )(*args)


def shape(*dims, dtype=F32):
    return jax.ShapeDtypeStruct(dims, dtype)


def swap(value, bit, sharers):
    pairs = [(q * sharers + r, (q ^ bit) * sharers + r) for q in range(4) for r in range(sharers)]
    return lax.ppermute(value, "state", pairs)


def gather(value, sharers):
    across = swap(value, 2, sharers)
    return value, swap(value, 1, sharers), across, swap(across, 1, sharers)


def local(
    inputs, lengths, cotangent, bn_gain, bn_bias, b_weight, c_weight, nu_log, theta_log, gamma_log, skip_weight,
    glu_weight, glu_bias, dp_size, state_size,
):
    sharers = state_size // 4
    place = lax.axis_index("state").astype(jnp.int32)
    quarter = place // sharers

    def joined(value, axis):
        if sharers == 1:
            return value
        groups = [[q * sharers + r for r in range(sharers)] for q in range(4)]
        return lax.all_gather(value, "state", axis=axis, axis_index_groups=groups, tiled=True)

    def own(value, axis):
        if sharers == 1:
            return value
        size = value.shape[axis] // sharers
        return lax.dynamic_slice_in_dim(value, place % sharers * size, size, axis)

    inputs, cotangent = joined(inputs, 1), joined(cotangent, 1)
    bn_gain, bn_bias, skip_weight = joined(bn_gain, 1), joined(bn_bias, 1), joined(skip_weight, 1)
    nu_log, theta_log, gamma_log = joined(nu_log, 1), joined(theta_log, 1), joined(gamma_log, 1)
    b_weight, c_weight = joined(b_weight, 2), joined(c_weight, 2)
    glu_weight, glu_bias = joined(glu_weight, 2), joined(glu_bias, 2)
    width, total = inputs.shape[1:]
    full = b_weight.shape[3]
    states = b_weight.shape[2] * 4
    own_states = b_weight.shape[2]
    part = 256
    meta = jnp.stack([lengths[0], quarter])

    def across(value, axes):
        return lax.all_to_all(value, axes, 0, 0, tiled=True)

    packed, sums, b0, cw0, later = call(
        enter_kernel,
        (
            shape(total + PARAM_ROWS, width),
            shape(dp_size * state_size, 8, width),
            shape(width, full, dtype=LOW),
            shape(3 * width, full, dtype=LOW),
            shape(4 * width, full, dtype=LOW),
        ),
        [
            pltpu.VMEM((total, width), F32),
            pltpu.VMEM((32, width), F32),
            pltpu.VMEM((LAYERS, width, full), LOW),
            pltpu.VMEM((LAYERS, width, full), LOW),
            pltpu.VMEM((LAYERS, 2 * width, full), LOW),
            pltpu.SemaphoreType.DMA((3,)),
            pltpu.SemaphoreType.DMA((6,)),
        ],
        (lengths, inputs[0], bn_gain, bn_bias, skip_weight, glu_bias, nu_log, theta_log, gamma_log,
         b_weight.reshape(LAYERS, width, full), c_weight.reshape(LAYERS, width, full),
         glu_weight.reshape(LAYERS, 2 * width, full)),
        any_args=(9, 10, 11),
        any_outs=(2, 3, 4),
        name="enter",
    )
    near = [swap(value, 1, sharers) for value in (packed, b0, cw0)]
    far = [swap(value, 2, sharers) for value in (packed, b0, cw0)]
    sums = across(sums, ("dp", "state"))
    if sharers > 1:
        sums = sums.reshape(dp_size * 4, sharers, 8, width)[:, 0]
    cotangent, packed = lax.optimization_barrier((cotangent, packed))
    up_own, up_low = call(
        cotangent_kernel,
        (shape(total, width), shape(total, width, dtype=LOW)),
        [pltpu.VMEM((total, width), F32)],
        (cotangent[0],),
        smem=0,
        name="cotangent",
    )
    far[0], far[1], sums, up_low = lax.optimization_barrier((far[0], far[1], sums, up_low))
    x_parts = (packed, near[0], far[0], swap(far[0], 1, sharers))
    b_parts = (b0, near[1], far[1], swap(far[1], 1, sharers))
    normed0, drive0, low0, b_all, feature, state, norm0 = call(
        functools.partial(drive_kernel, part=part),
        (
            shape(total, full, dtype=LOW),
            shape(total, 256),
            shape(total, 2 * states, dtype=LOW),
            shape(2 * states, full, dtype=LOW),
            shape(PARAM_ROWS, full),
            shape(8, states),
            shape(8, full),
        ),
        [pltpu.VMEM((total, 2 * states), F32), pltpu.VMEM((8, full), F32)],
        (lengths, *x_parts, sums, *b_parts),
        name="drive",
    )
    far[2], norm0 = lax.optimization_barrier((far[2], norm0))
    cw_parts = (cw0, near[2], far[2], swap(far[2], 1, sharers))
    later, up_low, *_ = lax.optimization_barrier((later, up_low, far[2]))
    far += [swap(value, 2, sharers) for value in (later, up_low)]
    stream1, linear0, gate0, slope0, active0, c_all, w_all, sums1 = call(
        functools.partial(glu_kernel, part=part),
        (
            shape(total, full),
            shape(total, full, dtype=LOW),
            shape(total, full, dtype=LOW),
            shape(total, full, dtype=LOW),
            shape(total, full, dtype=LOW),
            shape(2 * states, full, dtype=LOW),
            shape(2 * full, full, dtype=LOW),
            shape(dp_size, 8, full),
        ),
        [pltpu.VMEM((part, 2 * full), F32), pltpu.VMEM((32, full), F32)],
        (lengths, *x_parts, normed0, low0, *cw_parts, feature),
        name="glu",
    )
    sums1 = across(sums1, "dp")
    far[3], far[4], *_ = lax.optimization_barrier((far[3], far[4], stream1))
    later_parts, up_parts = (
        (own_part, swap(value, 1, sharers), far_part, swap(far_part, 1, sharers))
        for own_part, value, far_part in ((later, later, far[3]), (up_own, up_low, far[4]))
    )
    share = 4 * width // dp_size

    def middle(*refs):
        length_ref, stream_ref, sums_ref = refs[:3]
        parts, ups, refs = refs[3:7], refs[7:11], refs[11:]
        middle_kernel(length_ref, stream_ref, sums_ref, parts, ups, *refs, part=part)

    result, base, bn1, norm1, grads1 = call(
        middle,
        (
            shape(width, total),
            shape(total, full),
            shape(dp_size, 8, full),
            shape(8, full),
            shape(4 * width, full, dtype=LOW),
        ),
        [
            pltpu.VMEM((32, full), F32),
            pltpu.VMEM((8, full), F32),
            pltpu.VMEM((2 * states, full), LOW),
            pltpu.VMEM((2 * states, full), LOW),
            pltpu.VMEM((2 * full, full), LOW),
            pltpu.VMEM((total, full), LOW),
            pltpu.VMEM((total, 2 * states), F32),
            pltpu.VMEM((total, 256), F32),
            pltpu.VMEM((total, 2 * states), LOW),
            pltpu.VMEM((total, full), F32),
            pltpu.VMEM((total, full), LOW),
            pltpu.VMEM((part, 2 * full), F32),
            pltpu.VMEM((total, width), F32),
            pltpu.VMEM((total, width), F32),
            pltpu.VMEM((total, 2 * full), LOW),
            pltpu.VMEM((total, full), LOW),
            pltpu.VMEM((total, 2 * states), LOW),
            pltpu.VMEM((16, width), F32),
            pltpu.VMEM((32, width), F32),
        ],
        (lengths, stream1, sums1, *later_parts, *up_parts, feature, state, norm0),
        name="middle",
    )
    bn1 = across(bn1, "dp")
    grads1 = across(grads1.reshape(dp_size, share, full), "dp")
    up0, pre_grad0, glu_grads0, small0 = call(
        functools.partial(last_glu_kernel, part=part),
        (
            shape(total, width),
            shape(total, full, dtype=LOW),
            shape(2 * width, full, dtype=LOW),
            shape(8, full),
        ),
        [
            pltpu.VMEM((part, 2 * full), F32),
            pltpu.VMEM((total, 2 * full), LOW),
            pltpu.VMEM((16, width), F32),
            pltpu.VMEM((32, width), F32),
            pltpu.VMEM((16, full), F32),
        ],
        (lengths, stream1, base, bn1, norm1, gate0, linear0, slope0, active0, normed0, w_all, feature),
        name="last_glu",
    )
    grads1, pre_grad0 = lax.optimization_barrier((grads1, pre_grad0))
    (grads1,) = call(add_kernel, (shape(dp_size, share, full, dtype=LOW),), [], (grads1,), smem=0, name="add")
    pre_grad0, grads1 = lax.optimization_barrier((pre_grad0, grads1))
    grads1 = across(grads1, "dp")
    send, grad0 = call(
        functools.partial(last_state_kernel, part=part),
        (shape(dp_size, share + 16, full, dtype=LOW), shape(total, width)),
        [
            pltpu.VMEM((part, 2 * full), F32),
            pltpu.VMEM((total, 2 * states), F32),
            pltpu.VMEM((total, 2 * states), LOW),
            pltpu.VMEM((8, full), F32),
            pltpu.VMEM((32, width), F32),
            pltpu.VMEM((4 * width, full), LOW),
            pltpu.VMEM((16, full), F32),
        ],
        (lengths, pre_grad0, normed0, low0, drive0, b_all, c_all, glu_grads0, small0, feature, state, packed, norm0),
        name="last_state",
    )
    send, grads1 = lax.optimization_barrier((send, grads1))
    back, small0 = call(
        share_kernel,
        (shape(dp_size, share, full, dtype=LOW), shape(8, full)),
        [],
        (across(send, "dp"),),
        smem=0,
        name="share",
    )
    grad_nu, grad_theta, grad_gamma, grad_skip, grad_bias, grad_gain, grad_shift, grad_inputs = call(
        finish_kernel,
        (
            shape(LAYERS, own_states),
            shape(LAYERS, own_states),
            shape(LAYERS, own_states),
            shape(LAYERS, width),
            shape(LAYERS, 2, width),
            shape(LAYERS, width),
            shape(LAYERS, width),
            shape(width, total),
        ),
        [pltpu.VMEM((16, full), F32), pltpu.VMEM((total, width), F32)],
        (lengths, up0, grad0, packed, norm0, feature, nu_log, theta_log, bn1, small0),
        name="finish",
    )
    grads0 = across(back, "dp").reshape(4 * width, full)

    grad_b, grad_c, grad_glu = call(
        widen_kernel,
        (shape(LAYERS, width, full), shape(LAYERS, width, full), shape(LAYERS, 2 * width, full)),
        [],
        (grads0, grads1.reshape(4 * width, full)),
        smem=0,
        name="widen",
    )
    grad_b = grad_b.reshape(LAYERS, 2, own_states, full)
    grad_c = grad_c.reshape(LAYERS, 2, own_states, full)
    grad_glu = grad_glu.reshape(LAYERS, 2, width, full)
    return (
        own(result[None], 1),
        own(grad_inputs[None], 1),
        own(grad_gain, 1),
        own(grad_shift, 1),
        own(grad_b, 2),
        own(grad_c, 2),
        own(grad_nu, 1),
        own(grad_theta, 1),
        own(grad_gamma, 1),
        own(grad_skip, 1),
        own(grad_glu, 2),
        own(grad_bias, 2),
    )


def solution(mesh):
    in_specs = (
        P("dp", "state", None),
        P("dp"),
        P("dp", "state", None),
        P(None, "state"),
        P(None, "state"),
        P(None, None, "state", None),
        P(None, None, "state", None),
        P(None, "state"),
        P(None, "state"),
        P(None, "state"),
        P(None, "state"),
        P(None, None, "state", None),
        P(None, None, "state"),
    )
    out_specs = (
        P("dp", "state", None),
        P("dp", "state", None),
        P(None, "state"),
        P(None, "state"),
        P(None, None, "state", None),
        P(None, None, "state", None),
        P(None, "state"),
        P(None, "state"),
        P(None, "state"),
        P(None, "state"),
        P(None, None, "state", None),
        P(None, None, "state"),
    )
    step = functools.partial(local, dp_size=mesh.shape["dp"], state_size=mesh.shape["state"])
    return jax.shard_map(step, mesh=mesh, in_specs=in_specs, out_specs=out_specs, check_vma=False)
```

```python
import functools

import jax
import jax.numpy as jnp
from jax import lax
from jax.experimental import pallas as pl
from jax.experimental.pallas import tpu as pltpu
from jax.sharding import PartitionSpec as P

LAYERS = 2
CHUNKS = 16
PIECES = 4
EPSILON = 1e-05
F32 = jnp.float32
LOW = jnp.bfloat16
PARAM_ROWS = 16
VMEM_BYTES = 64 * 1024 * 1024
ENTER_FLOPS = 1e10

GAIN, SHIFT, SKIP, BIAS_LINEAR, BIAS_GATE = range(5)
RATE_RE, RATE_IM, GAMMA = range(3)

NN = (((1,), (0,)), ((), ()))
NT = (((1,), (1,)), ((), ()))
TN = (((0,), (0,)), ((), ()))


def dot(left, right, dims):
    return lax.dot_general(left, right, dims, preferred_element_type=F32)


def rows_at(index, size):
    return pl.ds(pl.multiple_of(index * size, size), size)


def lanes_at(quarter, width):
    return pl.ds(pl.multiple_of(quarter * width, width), width)


def for_rows(first, last, size, body, init=0, unroll=2):
    def step(index, carry):
        return body(rows_at(index, size), index, carry)

    return lax.fori_loop(first // size, last // size, step, init, unroll=unroll)


def own_quarter():
    return (lax.axis_index("state") // (lax.axis_size("state") // 4)).astype(jnp.int32)


def keep_rows(first_step, rows, steps, length):
    row = lax.broadcasted_iota(jnp.int32, (rows, 1), 0)
    position = (row % CHUNKS) * steps + row // CHUNKS + first_step
    return position < length


def gelu_parts(value):
    return 0.5 + 0.5 * lax.erf(value * 0.7071067811865476), jnp.exp(value * value * -0.5) * 0.3989422804014327


def squared(re, im, times):
    for _ in range(times):
        re, im = re * re - im * im, 2.0 * re * im
    return re, im


def folded(value):
    return value[0:8, :] + value[8:16, :]


def column_sum(value):
    return jnp.sum(value, axis=0, keepdims=True)


def chunk_starts(re, im, rate_re, rate_im, reverse):
    row = lax.broadcasted_iota(jnp.int32, re.shape, 0)

    def moved(value, by):
        if reverse:
            return jnp.where(row < CHUNKS - by, pltpu.roll(value, CHUNKS - by, 0), 0.0)
        return jnp.where(row >= by, pltpu.roll(value, by, 0), 0.0)

    by = 1
    while by < CHUNKS:
        past_re, past_im = moved(re, by), moved(im, by)
        re, im = (
            re + rate_re * past_re - rate_im * past_im,
            im + rate_re * past_im + rate_im * past_re,
        )
        rate_re, rate_im = squared(rate_re, rate_im, 1)
        by *= 2
    return moved(re, 1), moved(im, 1)


def sweep(drive_ref, rate_re, rate_im, steps, reverse, emit, extra, after=None, unroll=4):
    states = rate_re.shape[1]
    shape = (CHUNKS, states)
    wide_re = jnp.broadcast_to(rate_re, shape)
    wide_im = jnp.broadcast_to(rate_im, shape)

    def advance(index, re, im):
        place = steps - 1 - index if reverse else index
        rows = rows_at(place, CHUNKS)
        drive_re = drive_ref[rows, :states]
        drive_im = drive_ref[rows, states:]
        new_re = (wide_re * re + drive_re) - wide_im * im
        new_im = (wide_re * im + drive_im) + wide_im * re
        return rows, place, new_re, new_im, drive_re, drive_im

    def first(index, carry):
        _, _, re, im, _, _ = advance(index, *carry)
        return re, im

    def second(index, carry):
        re, im, held = carry
        rows, place, re, im, drive_re, drive_im = advance(index, re, im)
        return re, im, emit(rows, place, re, im, drive_re, drive_im, held)

    zero = jnp.zeros(shape, F32)
    re, im = lax.fori_loop(0, steps, first, (zero, zero), unroll=unroll)
    far_re, far_im = rate_re, rate_im
    power = 1
    while power < steps:
        far_re, far_im = squared(far_re, far_im, 1)
        power *= 2
    re, im = chunk_starts(re, im, far_re, far_im, reverse)
    carry = (re, im, extra)
    for piece in range(PIECES):
        size = steps // PIECES
        carry = lax.fori_loop(piece * size, (piece + 1) * size, second, carry, unroll=unroll)
        if after is not None:
            after(PIECES - 1 - piece if reverse else piece)
    return carry[2]


class Arrival:
    def __init__(self, source, ref, done, first, size, axis):
        self.ref = ref
        self.copies = []
        whole = ref.shape[axis]
        for piece, start in enumerate(range(0, whole, size)):
            where = (slice(None),) * axis + (pl.ds(start, min(size, whole - start)),)
            self.copies.append(
                pltpu.make_async_copy(source.at[where], ref.at[where], done.at[first + piece])
                if size < whole
                else pltpu.make_async_copy(source, ref, done.at[first])
            )
        self.short = whole % size > 0
        self.waited = set()

    def start(self, piece):
        last = len(self.copies) - self.short
        if piece < 0 and self.short:
            self.copies[-1].start()
        if 0 <= piece < last:
            self.copies[piece].start()

    def wait(self, piece=None):
        for place in range(len(self.copies)) if piece is None else (piece,):
            if place not in self.waited:
                self.copies[place].wait()
                self.waited.add(place)
        return self.ref


class Departure:
    def __init__(self, target, ref, done, first):
        self.target, self.ref, self.done, self.first = target, ref, done, first
        self.copies = []

    def send(self, start=None, size=None, source=None):
        place = self.done.at[self.first + len(self.copies)]
        where = self.target if start is None else self.target.at[pl.ds(start, size)]
        if source is None:
            source = self.ref if start is None else self.ref.at[pl.ds(start, size)]
        self.copies.append(pltpu.make_async_copy(source, where, place))
        self.copies[-1].start()

    def send_piece(self, piece):
        size = self.target.shape[0] // PIECES
        self.send(piece * size, size)

    def finish(self):
        if not self.copies:
            self.send()
        for copy in self.copies:
            copy.wait()


def call(kernel, outs, scratch, args, name, pieces=None, axes=None, bare=(), flops=0):
    pieces, axes = pieces or {}, axes or {}
    along = [axes.get(place, 0) for place in range(1, len(args))]
    sizes = [pieces.get(place, args[place].shape[axis]) for place, axis in enumerate(along, 1)]
    counts = [-(-args[place].shape[axis] // size) for place, (axis, size) in enumerate(zip(along, sizes), 1)]
    slots = 6
    copies_in = [pltpu.VMEM(a.shape, a.dtype) for a in args[1:]]
    copies_out = [pltpu.VMEM((8, 128) if place in bare else o.shape, o.dtype if place not in bare else F32) for place, o in enumerate(outs)]

    def body(*refs):
        refs = list(refs)

        def take(count):
            got = refs[:count]
            del refs[:count]
            return got

        (length_ref,) = take(1)
        sources = take(len(args) - 1)
        targets = take(len(outs))
        in_refs, out_refs = take(len(args) - 1), take(len(outs))
        arrived, sent = take(2)
        arrivals, first = [], 0
        for source, ref, size, count, axis in zip(sources, in_refs, sizes, counts, along):
            arrivals.append(Arrival(source, ref, arrived, first, size, axis))
            first += count
        for piece in range(-1, max(counts)):
            for arrival in arrivals:
                arrival.start(piece)
        departures = [
            Departure(target, ref, sent, place * slots) for place, (target, ref) in enumerate(zip(targets, out_refs))
        ]
        kernel(length_ref, arrivals, departures, *refs)
        for arrival in arrivals:
            arrival.wait()
        for departure in departures:
            departure.finish()

    return pl.pallas_call(
        body,
        out_shape=tuple(outs),
        in_specs=[pl.BlockSpec(memory_space=pltpu.SMEM if place == 0 else pl.ANY) for place in range(len(args))],
        out_specs=tuple(pl.BlockSpec(memory_space=pl.ANY) for _ in outs),
        scratch_shapes=[
            *copies_in,
            *copies_out,
            pltpu.SemaphoreType.DMA((sum(counts),)),
            pltpu.SemaphoreType.DMA((slots * len(outs),)),
            *scratch,
        ],
        compiler_params=pltpu.CompilerParams(vmem_limit_bytes=VMEM_BYTES),
        cost_estimate=pl.CostEstimate(flops=int(flops), bytes_accessed=0, transcendentals=0),
        name=name,
    )(*args)


def from_feature_rows(source, held_ref, steps, emit, init, after):
    length = source.ref.shape[1]
    blocks = length // 128
    for block in range(blocks):
        if block % (blocks // PIECES) == 0:
            source.wait(block // (blocks // PIECES))
        lanes = slice(block * 128, (block + 1) * 128)
        held_ref[lanes, :] = source.ref[:, lanes].T

    def step(index, carry):
        return emit(rows_at(index, CHUNKS), index, held_ref[pl.ds(index, CHUNKS, stride=steps), :], carry)

    carry = init
    for piece in range(PIECES):
        size = steps // PIECES
        carry = lax.fori_loop(piece * size, (piece + 1) * size, step, carry, unroll=4)
        after(piece)
    return carry


def to_feature_rows(load, held_ref, out, steps):
    length = out.ref.shape[1]

    def step(index, carry):
        held_ref[pl.ds(index, CHUNKS, stride=steps), :] = load(rows_at(index, CHUNKS), index)
        return carry

    lax.fori_loop(0, steps, step, 0, unroll=4)
    for block in range(length // 128):
        lanes = slice(block * 128, (block + 1) * 128)
        out.ref[:, lanes] = held_ref[lanes, :].T
    out.send()


def spread_rows(value, out):
    for group in range(out.ref.shape[0]):
        out.ref[group, :, :] = value
    out.send()


def narrowed(values, width):
    return jnp.concatenate([v[:, at : at + width] for v in values for at in range(0, v.shape[1], width)], axis=0)


def widened(rows, first, count):
    return jnp.concatenate([rows[first + place : first + place + 1, :] for place in range(count)], axis=1)


def total_rows(sums_ref):
    value = sums_ref[0, :, :]
    for other in range(1, sums_ref.shape[0]):
        value += sums_ref[other, :, :]
    return value


def assemble_states(parts, whole_ref):
    half = parts[0].shape[0] // 2
    states = half * len(parts)
    for place, part in enumerate(parts):
        whole_ref[place * half : (place + 1) * half, :] = part[:half, :]
        whole_ref[states + place * half : states + (place + 1) * half, :] = part[half:, :]


def assemble_output(parts, whole_ref):
    half = parts[0].shape[0] // 2
    states = half * len(parts)
    for place, part in enumerate(parts):
        whole_ref[place * half : (place + 1) * half, :] = part[:half, :]
        whole_ref[states + place * half : states + (place + 1) * half, :] = -part[half:, :]


def assemble_glu(parts, whole_ref, quarter):
    half = parts[0].shape[0] // 2
    width = half * len(parts)
    for place, part in enumerate(parts):
        whole_ref[lanes_at(quarter ^ place, half), :] = part[:half, :]
        whole_ref[pl.ds(pl.multiple_of(width + (quarter ^ place) * half, half), half), :] = part[half:, :]


def norm_rows(sums, counted):
    centre = sums[0:1, :] / counted
    meansq = sums[1:2, :] / counted
    return centre, lax.rsqrt(meansq - centre * centre + EPSILON)


def drive_phase(normed_ref, b_ref, drive_ref, gamma):
    drive_ref[...] = dot(normed_ref[...], b_ref[...], NT) * jnp.concatenate([gamma, gamma], axis=1)


def store_states(low_ref, drive_own_ref):
    def emit(rows, step, re, im, drive_re, drive_im, held):
        states = re.shape[1]
        low_ref[rows, :states] = re.astype(LOW)
        low_ref[rows, states:] = im.astype(LOW)
        drive_own_ref[rows, :128] = drive_re[:, :128].astype(drive_own_ref.dtype)
        drive_own_ref[rows, 128:] = drive_im[:, :128].astype(drive_own_ref.dtype)
        return held

    return emit


def pre_phase(low_ref, c_ref, normed_ref, skip, active_ref, slope_ref, held_ref, after=None):
    total, full = normed_ref.shape
    held_ref[:, :full] = dot(low_ref[...], c_ref[...], NN)

    def inner(rows, index, carry):
        value = held_ref[rows, :full] + skip * normed_ref[rows, :].astype(F32)
        cdf, density = gelu_parts(value)
        active_ref[rows, :] = (value * cdf).astype(LOW)
        slope_ref[rows, :] = (cdf + value * density).astype(slope_ref.dtype)
        return carry

    for piece in range(PIECES):
        for_rows(piece * total // PIECES, (piece + 1) * total // PIECES, 16, inner, unroll=4)
        if after is not None:
            after(piece)


def pre_grad_phase(grad_gated_ref, w_ref, slope_ref, normed_ref, quarter, pre_grad_ref, held_ref, small_ref):
    total, full = normed_ref.shape
    own = lanes_at(quarter, 128)
    held_ref[:, :full] = dot(grad_gated_ref[...], w_ref[...], NN)

    def inner(rows, index, carry):
        pre_grad_ref[rows, :] = (held_ref[rows, :full] * slope_ref[rows, :].astype(F32)).astype(LOW)
        return carry + folded(pre_grad_ref[rows, own].astype(F32) * normed_ref[rows, own].astype(F32))

    small_ref[3:4, 0:128] = column_sum(for_rows(0, total, 16, inner, jnp.zeros((8, 128), F32), unroll=4))


def adjoint_phase(pre_grad_ref, c_ref, low_ref, im_lane, drive_own_ref, state, first_row, length, grad_state_ref, grad_driven_ref, small_ref, reverse):
    total = pre_grad_ref.shape[0]
    steps = total // CHUNKS
    states = state.shape[1]
    grad_state_ref[...] = dot(pre_grad_ref[...], c_ref[...], NT)
    rate_re = state[first_row : first_row + 1, :]
    rate_im = state[first_row + 1 : first_row + 2, :]
    gamma = jnp.broadcast_to(state[first_row + 2 : first_row + 3, :], (CHUNKS, states))

    def emit(rows, step, re, im, drive_re, drive_im, held):
        out_re, out_im = gamma * re, gamma * im
        if not reverse:
            keep = keep_rows(step, CHUNKS, steps, length)
            out_re, out_im = jnp.where(keep, out_re, 0.0), jnp.where(keep, out_im, 0.0)
        grad_driven_ref[rows, :states] = out_re.astype(LOW)
        grad_driven_ref[rows, states:] = out_im.astype(LOW)
        one, two, three = held
        own_re, own_im = re[:, :128], im[:, :128]
        late_re, late_im = own_re - drive_re[:, :128], own_im - drive_im[:, :128]
        low_re = low_ref[rows, :128].astype(F32)
        low_im = low_ref[rows, im_lane : im_lane + 128].astype(F32)
        one = one + folded(late_re * low_re + late_im * low_im)
        two = two + folded(late_im * low_re - late_re * low_im)
        three = three + folded(
            own_re * drive_own_ref[rows, :128].astype(F32) + own_im * drive_own_ref[rows, 128:].astype(F32)
        )
        return one, two, three

    zero = jnp.zeros((8, 128), F32)
    one, two, three = sweep(grad_state_ref, rate_re, -rate_im, steps, reverse, emit, (zero, zero, zero))
    small_ref[0:1, 0:128] = column_sum(one)
    small_ref[1:2, 0:128] = column_sum(two)
    small_ref[2:3, 0:128] = column_sum(three)


def glu_grads(grads_ref, first, grad_gated_ref, active_ref, quarter):
    full = active_ref.shape[1]
    for place in range(2):
        lanes = pl.ds(pl.multiple_of(place * full + quarter * 128, 128), 128)
        got = dot(grad_gated_ref[:, lanes], active_ref[...], TN)
        grads_ref[first + place * 128 : first + (place + 1) * 128, :] = got.astype(LOW)


def state_grads(grads_ref, grad_driven_ref, normed_ref, low_re, low_im, pre_grad_ref, states):
    half = states // 4
    for place, low in enumerate((low_re, low_im)):
        lanes = slice(place * states, place * states + 128)
        got = dot(grad_driven_ref[:, lanes], normed_ref[...], TN)[:half, :]
        grads_ref[place * half : (place + 1) * half, :] = got.astype(LOW)
        got = dot(low, pre_grad_ref[...], TN)[:half, :]
        got = got if place == 0 else -got
        grads_ref[2 * half + place * half : 2 * half + (place + 1) * half, :] = got.astype(LOW)


def enter_kernel(length_ref, ins, outs, held_ref):
    x, b, c, w, gain, shift, skip, bias, nu, theta, gamma = ins
    tokens, spread, params, weights = outs
    length = length_ref[0]
    width, total = x.ref.shape
    steps = total // CHUNKS

    def emit(rows, index, value, carry):
        tokens.ref[rows, :] = value
        kept = jnp.where(keep_rows(index, CHUNKS, steps, length), value, 0.0)
        return carry[0] + folded(kept), carry[1] + folded(kept * kept)

    def after(piece):
        tokens.send_piece(piece)
        if piece == 1:
            b.wait()
            weights.send(0, width, source=b.ref.at[0])
            c.wait()
            weights.send(width, width, source=c.ref.at[0])
            w.wait()
            weights.send(2 * width, 2 * width, source=w.ref.at[0])

    zero = jnp.zeros((8, width), F32)
    plain, square = from_feature_rows(x, held_ref, steps, emit, (zero, zero), after)
    counted = jnp.full((1, width), length, jnp.int32).astype(F32)
    spread_rows(jnp.concatenate([column_sum(plain), column_sum(square), counted, jnp.zeros((5, width), F32)], axis=0), spread)
    for value in (gain, shift, skip, bias, nu, theta, gamma):
        value.wait()
    params.ref[...] = jnp.zeros((PARAM_ROWS, width), F32)
    for layer in range(LAYERS):
        first = 5 * layer
        params.ref[first + GAIN : first + GAIN + 1, :] = gain.ref[layer : layer + 1, :]
        params.ref[first + SHIFT : first + SHIFT + 1, :] = shift.ref[layer : layer + 1, :]
        params.ref[first + SKIP : first + SKIP + 1, :] = skip.ref[layer : layer + 1, :]
        params.ref[first + BIAS_LINEAR : first + BIAS_GATE + 1, :] = bias.ref[layer, :, :]
        first = 10 + 3 * layer
        for row, source in enumerate((nu, theta, gamma)):
            params.ref[first + row : first + row + 1, : source.ref.shape[1]] = source.ref[layer : layer + 1, :]


def cotangent_kernel(length_ref, ins, outs, held_ref):
    x, b, c, w = ins
    whole, later = outs
    width, total = x.ref.shape
    steps = total // CHUNKS
    each = steps // PIECES

    def emit(rows, index, value, carry):
        whole.ref[rows, :] = value
        place = pl.ds(pl.multiple_of(4 * width + index % each * CHUNKS, CHUNKS), CHUNKS)
        later.ref[place, lanes_at(index // each, width)] = value.astype(LOW)
        return carry

    def after(piece):
        whole.send_piece(piece)
        if piece == 1:
            b.wait()
            later.send(0, width, source=b.ref.at[1])
            c.wait()
            later.send(width, width, source=c.ref.at[1])
            w.wait()
            later.send(2 * width, 2 * width, source=w.ref.at[1])

    from_feature_rows(x, held_ref, steps, emit, 0, after)
    later.send(4 * width, total // PIECES)


def normal_kernel(length_ref, ins, outs, held_ref, stats_ref):
    sums, own_tokens = ins[:2]
    params, raws = ins[2:6], ins[6:]
    normed, stream, feature, state_out, norm = outs
    length, quarter = length_ref[0], own_quarter()
    total = normed.ref.shape[0]
    steps = total // CHUNKS
    width = own_tokens.ref.shape[1]
    lane = lax.broadcasted_iota(jnp.int32, (8, width), 1)
    tails = [part.wait() for part in params]
    for place, value in enumerate(tails):
        feature.ref[:, lanes_at(quarter ^ place, width)] = value[...]
    for pair in range(2):
        early, late = (value[8:16, :] for value in tails[2 * pair : 2 * pair + 2])
        logs = jnp.where(lane < 64, early, pltpu.roll(late, 64, 1))
        lanes = slice(pair * width, (pair + 1) * width)
        for layer in range(LAYERS):
            first = 2 + 3 * layer
            modulus = jnp.exp(-jnp.exp(logs[first : first + 1, :]))
            angle = jnp.exp(logs[first + 1 : first + 2, :])
            state_out.ref[first : first + 1, lanes] = modulus * jnp.cos(angle)
            state_out.ref[first + 1 : first + 2, lanes] = modulus * jnp.sin(angle)
            state_out.ref[first + 2 : first + 3, lanes] = jnp.exp(logs[first + 2 : first + 3, :])
    sums_ref = sums.wait()
    for place in range(4):
        value = sums_ref[place, :, :]
        for other in range(1, sums_ref.shape[0] // 4):
            value += sums_ref[other * 4 + place, :, :]
        stats_ref[:, place * width : (place + 1) * width] = value
    centre, inv_dev = norm_rows(stats_ref[0:2, :], stats_ref[2:3, :])
    norm.ref[...] = jnp.zeros_like(norm.ref)
    norm.ref[0:1, :] = centre
    norm.ref[1:2, :] = inv_dev
    norm.ref[2:3, :] = stats_ref[2:3, :]
    for out in (feature, state_out, norm):
        out.send()

    def normalized(place):
        lanes = lanes_at(quarter ^ place, width)

        def emit(rows, index, value, carry):
            stream.ref[rows, lanes] = value
            z = (value - norm.ref[0:1, lanes]) * norm.ref[1:2, lanes]
            z = z * feature.ref[GAIN : GAIN + 1, lanes] + feature.ref[SHIFT : SHIFT + 1, lanes]
            normed.ref[rows, lanes] = jnp.where(keep_rows(index, CHUNKS, steps, length), z, 0.0).astype(LOW)
            return carry

        return emit

    first = normalized(0)
    own_tokens.wait()
    for_rows(0, total, CHUNKS, lambda rows, index, carry: first(rows, index, own_tokens.ref[rows, :], carry), unroll=4)

    def after(piece):
        stream.send_piece(piece)
        normed.send_piece(piece)

    for place, raw in enumerate(raws, 1):
        from_feature_rows(raw, held_ref, steps, normalized(place), 0, after if place == 3 else lambda piece: None)


def start_kernel(length_ref, ins, outs, drive_ref, held_ref, b_ref, c_ref, w_ref, low_ref):
    feature_in, state_in, normed = ins[:3]
    weights, stream0 = ins[3:7], ins[7]
    drive_own, low_own, stream, linear_out, gate_out, slope, active, b_out, c_out, w_out, spread = outs
    length, quarter = length_ref[0], own_quarter()
    total, full = active.ref.shape
    steps = total // CHUNKS
    width = full // 4
    feature, state = feature_in.wait(), state_in.wait()[...]
    states = state.shape[1]
    normed.wait()
    for part in weights:
        part.wait()
    assemble_states([part.ref.at[0:width] for part in weights], b_ref)
    drive_phase(normed.ref, b_ref, drive_ref, state[2 + GAMMA : 3 + GAMMA, :])
    assemble_output([part.ref.at[width : 2 * width] for part in weights], c_ref)
    assemble_glu([part.ref.at[2 * width : 4 * width] for part in weights], w_ref, quarter)
    for out, source in ((b_out, b_ref), (c_out, c_ref), (w_out, w_ref)):
        out.send(source=source)
    store = store_states(low_ref, drive_own.ref)

    def emit(rows, step, re, im, drive_re, drive_im, held):
        low_own.ref[rows, :128] = re[:, :128].astype(LOW)
        low_own.ref[rows, 128:] = im[:, :128].astype(LOW)
        return store(rows, step, re, im, drive_re, drive_im, held)

    sweep(drive_ref, state[2:3, :], state[3:4, :], steps, False, emit, 0)
    drive_own.send()
    low_own.send()

    def after(piece):
        active.send_piece(piece)
        slope.send_piece(piece)

    pre_phase(low_ref, c_ref, normed.ref, feature[SKIP : SKIP + 1, :], active.ref, slope.ref, held_ref, after)
    held_ref[...] = dot(active.ref[...], w_ref[...], NT)

    def inner(rows, index, carry):
        keep = keep_rows(index, 16, steps, length)
        linear = held_ref[rows, :full] + feature[BIAS_LINEAR : BIAS_LINEAR + 1, :]
        gate = jax.nn.sigmoid(held_ref[rows, full:] + feature[BIAS_GATE : BIAS_GATE + 1, :])
        mixed = linear * gate
        gate_out.ref[rows, :] = gate.astype(LOW)
        linear_out.ref[rows, :] = (mixed * (1.0 - gate)).astype(LOW)
        moved = stream0.ref[rows, :] + jnp.where(keep, mixed, 0.0)
        stream.ref[rows, :] = moved
        kept = jnp.where(keep, moved, 0.0)
        return carry[0] + folded(kept), carry[1] + folded(kept * kept)

    zero = jnp.zeros((8, full), F32)
    carry = (zero, zero)
    for piece in range(PIECES):
        stream0.wait(piece)
        carry = for_rows(piece * total // PIECES, (piece + 1) * total // PIECES, 16, inner, carry)
        for out in (stream, linear_out, gate_out):
            out.send_piece(piece)
    spread_rows(narrowed([column_sum(carry[0]), column_sum(carry[1])], width), spread)


def middle_kernel(
    length_ref, ins, outs,
    small_ref, b_ref, c_ref, w_ref, normed_ref, drive_ref, drive_own_ref, low_ref, slope_ref, active_ref, held_ref,
    order_ref, up_ref, grad_gated_ref, pre_grad_ref, grad_driven_ref, grads_ref,
):
    sums, norm0, feature_in, state_in, stream, up_own = ins[:6]
    weights = ins[6:]
    result, base, spread, norm, *shares = outs
    length, quarter = length_ref[0], own_quarter()
    total, full = stream.ref.shape
    steps = total // CHUNKS
    width = 128
    counted = norm0.wait()[2:3, :]
    feature = feature_in.wait()
    state = state_in.wait()[...]
    states = state.shape[1]
    whole = total_rows(sums.wait())
    whole = jnp.concatenate([widened(whole, 0, 4), widened(whole, 4, 4)], axis=0)
    centre, inv_dev = norm_rows(whole, counted)
    norm.ref[...] = jnp.zeros_like(norm.ref)
    norm.ref[0:1, :] = centre
    norm.ref[1:2, :] = inv_dev
    norm.ref[2:3, :] = counted
    norm.send()
    gain = feature[5 + GAIN : 6 + GAIN, :]
    shift = feature[5 + SHIFT : 6 + SHIFT, :]
    skip = feature[5 + SKIP : 6 + SKIP, :]

    def normal(rows, index, carry):
        keep = keep_rows(index, 16, steps, length)
        z = (stream.ref[rows, :] - centre) * inv_dev
        normed_ref[rows, :] = jnp.where(keep, z * gain + shift, 0.0).astype(LOW)
        return carry

    for piece in range(PIECES):
        stream.wait(piece)
        for_rows(piece * total // PIECES, (piece + 1) * total // PIECES, 16, normal, unroll=4)
    for part in weights:
        part.wait()
    assemble_states([part.ref.at[0:width] for part in weights], b_ref)
    assemble_output([part.ref.at[width : 2 * width] for part in weights], c_ref)
    assemble_glu([part.ref.at[2 * width : 4 * width] for part in weights], w_ref, quarter)
    drive_phase(normed_ref, b_ref, drive_ref, state[5 + GAMMA : 6 + GAMMA, :])
    sweep(drive_ref, state[5:6, :], state[6:7, :], steps, True, store_states(low_ref, drive_own_ref), 0)
    pre_phase(low_ref, c_ref, normed_ref, skip, active_ref, slope_ref, held_ref)
    held_ref[...] = dot(active_ref[...], w_ref[...], NT)
    up_own.wait()
    own, own_far = lanes_at(quarter, width), lanes_at(quarter + 4, width)

    def spread_up(rows, index, carry):
        up_ref[rows, own] = up_own.ref[rows, :]
        return carry

    for_rows(0, total, 16, spread_up, unroll=4)
    for piece in range(PIECES):
        for place, part in enumerate(weights[1:], 1):
            lanes = lanes_at(quarter ^ place, width)
            size = total // PIECES
            up_ref[piece * size : (piece + 1) * size, lanes] = part.ref[4 * width :, piece * width : (piece + 1) * width].astype(F32)

    def inner(rows, index, carry):
        keep = keep_rows(index, 16, steps, length)
        linear = held_ref[rows, :full] + feature[5 + BIAS_LINEAR : 6 + BIAS_LINEAR, :]
        gate = jax.nn.sigmoid(held_ref[rows, full:] + feature[5 + BIAS_GATE : 6 + BIAS_GATE, :])
        mixed = linear * gate
        up = jnp.where(keep, up_ref[rows, :], 0.0)
        grad_gated_ref[rows, :full] = (up * gate).astype(LOW)
        grad_gated_ref[rows, full:] = (up * mixed * (1.0 - gate)).astype(LOW)
        held_ref[rows, :full] = jnp.where(keep, mixed, 0.0)
        return (
            carry[0] + folded(grad_gated_ref[rows, own].astype(F32)),
            carry[1] + folded(grad_gated_ref[rows, own_far].astype(F32)),
        )

    zero = jnp.zeros((8, width), F32)
    one, two = for_rows(0, total, 16, inner, (zero, zero))
    small_ref[...] = jnp.zeros_like(small_ref)
    small_ref[4:5, 0:128] = column_sum(one)
    small_ref[5:6, 0:128] = column_sum(two)
    to_feature_rows(lambda rows, index: stream.ref[rows, own] + held_ref[rows, own], order_ref, result, steps)
    pre_grad_phase(grad_gated_ref, w_ref, slope_ref, normed_ref, quarter, pre_grad_ref, held_ref, small_ref)
    adjoint_phase(
        pre_grad_ref, c_ref, low_ref, states, drive_own_ref, state, 5, length, drive_ref, grad_driven_ref, small_ref, False
    )
    held_ref[:, :full] = dot(grad_driven_ref[...], b_ref[...], NN)
    scale = inv_dev * gain

    def back(rows, index, carry):
        grad = held_ref[rows, :full] + skip * pre_grad_ref[rows, :].astype(F32)
        z = (stream.ref[rows, :] - centre) * inv_dev
        base.ref[rows, :] = scale * grad + up_ref[rows, :]
        return carry[0] + folded(grad), carry[1] + folded(grad * z)

    zero = jnp.zeros((8, full), F32)
    carry = (zero, zero)
    for piece in range(PIECES):
        carry = for_rows(piece * total // PIECES, (piece + 1) * total // PIECES, 16, back, carry)
        base.send_piece(piece)
    sent = narrowed([column_sum(carry[0]), column_sum(carry[1])], width)
    spread_rows(jnp.concatenate([sent, small_ref[:, 0:width]], axis=0), spread)
    glu_grads(grads_ref, 2 * width, grad_gated_ref, active_ref, quarter)
    state_grads(grads_ref, grad_driven_ref, normed_ref, low_ref[:, 0:128], low_ref[:, states : states + 128], pre_grad_ref, states)
    share = grads_ref.shape[0] // len(shares)
    for place, out in enumerate(shares):
        out.send(source=grads_ref.at[rows_at(lax.axis_index("dp") ^ place, share)])


def last_kernel(
    length_ref, ins, outs, held_ref, grad_state_ref, grad_gated_ref, pre_grad_ref, grad_driven_ref, small_ref, row_ref, grads_ref, pack_ref
):
    (sums, norm1, feature_in, state_in, norm0, stream, base, gate, linear, w, slope, normed, active, c, low, drive_own, b, x) = ins
    send, up_out, grad_out = outs
    length, quarter = length_ref[0], own_quarter()
    total, full = stream.ref.shape
    steps = total // CHUNKS
    width = 128
    own = lanes_at(quarter, width)
    feature, norm_ref = feature_in.wait(), norm1.wait()
    state = state_in.wait()[...]
    counted = norm_ref[2:3, :]
    whole = total_rows(sums.wait())
    whole = jnp.concatenate([widened(whole, 0, 4), widened(whole, 4, 4)], axis=0)
    centre, inv_dev = norm_ref[0:1, :], norm_ref[1:2, :]
    scale = inv_dev * feature[5 + GAIN : 6 + GAIN, :]
    level = scale * whole[0:1, :] / counted
    tilt = scale * inv_dev * whole[1:2, :] / counted

    def top(rows, index, carry):
        keep = keep_rows(index, 16, steps, length)
        up = base.ref[rows, :] - jnp.where(keep, level + (stream.ref[rows, :] - centre) * tilt, 0.0)
        row_ref[...] = up
        up_out.ref[rows, :] = row_ref[:, own]
        up = jnp.where(keep, up, 0.0)
        grad_gated_ref[rows, :full] = (up * gate.ref[rows, :].astype(F32)).astype(LOW)
        grad_gated_ref[rows, full:] = (up * linear.ref[rows, :].astype(F32)).astype(LOW)
        far = pl.ds(pl.multiple_of(full + quarter * width, width), width)
        return (
            carry[0] + folded(grad_gated_ref[rows, own].astype(F32)),
            carry[1] + folded(grad_gated_ref[rows, far].astype(F32)),
        )

    zero = jnp.zeros((8, width), F32)
    carry = (zero, zero)
    for piece in range(PIECES):
        for value in (stream, base, gate, linear):
            value.wait(piece)
        carry = for_rows(piece * total // PIECES, (piece + 1) * total // PIECES, 16, top, carry)
        up_out.send_piece(piece)
    small_ref[...] = jnp.zeros_like(small_ref)
    small_ref[4:5, 0:128] = column_sum(carry[0])
    small_ref[5:6, 0:128] = column_sum(carry[1])
    for value in (w, slope, normed):
        value.wait()
    pre_grad_phase(grad_gated_ref, w.ref, slope.ref, normed.ref, quarter, pre_grad_ref, held_ref, small_ref)
    for value in (active, c, low, drive_own):
        value.wait()
    glu_grads(grads_ref, 2 * width, grad_gated_ref, active.ref, quarter)
    adjoint_phase(
        pre_grad_ref, c.ref, low.ref, 128, drive_own.ref, state, 2, length, grad_state_ref, grad_driven_ref, small_ref, True
    )
    b.wait()
    x.wait()
    held_ref[:, :width] = dot(grad_driven_ref[...], b.ref[:, own], NN)
    centre0, inv_dev0 = norm0.wait()[0:1, own], norm0.ref[1:2, own]
    skip = feature[SKIP : SKIP + 1, own]

    def back(rows, index, carry):
        grad = held_ref[rows, :width] + skip * pre_grad_ref[rows, own].astype(F32)
        grad_out.ref[rows, :] = grad
        z = (x.ref[rows, :] - centre0) * inv_dev0
        return carry[0] + folded(grad), carry[1] + folded(grad * z)

    plain, scaled = for_rows(0, total, 16, back, (zero, zero), unroll=4)
    grad_out.send()
    small_ref[6:7, 0:width] = column_sum(plain)
    small_ref[7:8, 0:width] = column_sum(scaled)
    state_grads(grads_ref, grad_driven_ref, normed.ref, low.ref[:, :128], low.ref[:, 128:], pre_grad_ref, state.shape[1])
    pack_ref[...] = jnp.zeros_like(pack_ref)
    for place in range(8):
        pack_ref[place // 4 : place // 4 + 1, place % 4 * width : (place % 4 + 1) * width] = small_ref[place : place + 1, 0:width]
    exact = pack_ref[0:8, :]
    pack_ref[8:16, :] = exact - exact.astype(LOW).astype(F32)
    groups = send.ref.shape[0]
    share = send.ref.shape[1] - 16
    for group in range(groups):
        send.ref[group, :share, :] = grads_ref[group * share : (group + 1) * share, :]
        send.ref[group, share:, :] = pack_ref[...].astype(LOW)


def sum_shares(got, out, share):
    groups = got.ref.shape[0]
    for piece in range(0, share, 16):
        value = got.ref[0, piece : piece + 16, :].astype(F32)
        for group in range(1, groups):
            value += got.ref[group, piece : piece + 16, :].astype(F32)
        value = value.astype(LOW)
        for group in range(groups):
            out.ref[group, piece : piece + 16, :] = value


def add_kernel(length_ref, ins, outs):
    (out,) = outs
    for value in ins:
        value.wait()
    for piece in range(0, out.ref.shape[0], 16):
        at = slice(piece, piece + 16)
        total = ins[0].ref[at, :].astype(F32)
        for value in ins[1:]:
            total += value.ref[at, :].astype(F32)
        out.ref[at, :] = total.astype(LOW)


def share_kernel(length_ref, ins, outs):
    (got,) = ins
    out, small = outs
    got.wait()
    groups, share = got.ref.shape[0], got.ref.shape[1] - 16
    sum_shares(got, out, share)
    value = got.ref[0, share:, :].astype(F32)
    for group in range(1, groups):
        value += got.ref[group, share:, :].astype(F32)
    small.ref[...] = value[0:8, :] + value[8:16, :]


def finish_kernel(length_ref, ins, outs, held_ref, order_ref):
    small0, bn1, norm0, feature, nu, theta, up, grad, x = ins
    nu_out, theta_out, gamma_out, skip_out, bias_out, gain_out, shift_out, out = outs
    length, quarter = length_ref[0], own_quarter()
    total, width = up.ref.shape
    steps = total // CHUNKS
    own = lanes_at(quarter, width)
    states = nu_out.ref.shape[1]
    for value in ins:
        value.wait()
    whole = total_rows(bn1.ref)
    held_ref[0:1, :] = widened(whole, 0, 4)
    held_ref[1:2, :] = widened(whole, 4, 4)
    held_ref[16:32, :width] = whole
    for place in range(8):
        held_ref[8 + place : 9 + place, :width] = small0.ref[place // 4 : place // 4 + 1, place % 4 * width : (place % 4 + 1) * width]
    for layer, first in ((0, 8), (1, 24)):
        at = slice(layer, layer + 1)
        nu_out.ref[at, :] = -jnp.exp(nu.ref[at, :]) * held_ref[first : first + 1, :states]
        theta_out.ref[at, :] = jnp.exp(theta.ref[at, :]) * held_ref[first + 1 : first + 2, :states]
        gamma_out.ref[at, :] = held_ref[first + 2 : first + 3, :states]
        skip_out.ref[at, :] = held_ref[first + 3 : first + 4, :width]
        bias_out.ref[layer, 0:1, :] = held_ref[first + 4 : first + 5, :width]
        bias_out.ref[layer, 1:2, :] = held_ref[first + 5 : first + 6, :width]
    shift_out.ref[0:1, :] = held_ref[14:15, :width]
    gain_out.ref[0:1, :] = held_ref[15:16, :width]
    shift_out.ref[1:2, :] = held_ref[0:1, own]
    gain_out.ref[1:2, :] = held_ref[1:2, own]
    counted = norm0.ref[2:3, own]
    centre, inv_dev = norm0.ref[0:1, own], norm0.ref[1:2, own]
    level = held_ref[14:15, :width] / counted
    tilt = held_ref[15:16, :width] * inv_dev / counted
    scale = inv_dev * feature.ref[GAIN : GAIN + 1, own]

    def load(rows, index):
        keep = keep_rows(index, CHUNKS, steps, length)
        inner = grad.ref[rows, :] - level - (x.ref[rows, :] - centre) * tilt
        return up.ref[rows, :] + jnp.where(keep, scale * inner, 0.0)

    to_feature_rows(load, order_ref, out, steps)


def widen_kernel(length_ref, ins, outs, held_ref):
    b, c, w = outs
    half = b.ref.shape[1]
    grads0, *shares = ins
    share = shares[0].ref.shape[0]
    for place, value in enumerate(shares):
        held_ref[rows_at(lax.axis_index("dp") ^ place, share), :] = value.wait()[...]
    for layer, source_ref in ((1, held_ref), (0, grads0.ref)):
        if layer == 0:
            grads0.wait()
        for out, first, size in ((b, 0, half), (c, half, half), (w, 2 * half, 2 * half)):
            out.ref[layer, :, :] = source_ref[first : first + size, :].astype(F32)
            out.send(layer, 1)


def shape(*dims, dtype=F32):
    return jax.ShapeDtypeStruct(dims, dtype)


def swap(value, bit, sharers):
    pairs = [(q * sharers + r, (q ^ bit) * sharers + r) for q in range(4) for r in range(sharers)]
    return lax.ppermute(value, "state", pairs)


def across(value, axes):
    return lax.all_to_all(value, axes, 0, 0, tiled=True)


def local(
    inputs, lengths, cotangent, bn_gain, bn_bias, b_weight, c_weight, nu_log, theta_log, gamma_log, skip_weight,
    glu_weight, glu_bias, dp_size, state_size,
):
    sharers = state_size // 4
    place = lax.axis_index("state").astype(jnp.int32)

    def joined(value, axis):
        if sharers == 1:
            return value
        groups = [[q * sharers + r for r in range(sharers)] for q in range(4)]
        return lax.all_gather(value, "state", axis=axis, axis_index_groups=groups, tiled=True)

    def own(value, axis):
        if sharers == 1:
            return value
        size = value.shape[axis] // sharers
        return lax.dynamic_slice_in_dim(value, place % sharers * size, size, axis)

    inputs, cotangent = joined(inputs, 1), joined(cotangent, 1)
    bn_gain, bn_bias, skip_weight = joined(bn_gain, 1), joined(bn_bias, 1), joined(skip_weight, 1)
    nu_log, theta_log, gamma_log = joined(nu_log, 1), joined(theta_log, 1), joined(gamma_log, 1)
    b_weight, c_weight = joined(b_weight, 2), joined(c_weight, 2)
    glu_weight, glu_bias = joined(glu_weight, 2), joined(glu_bias, 2)
    width, total = inputs.shape[1:]
    full = b_weight.shape[3]
    states = b_weight.shape[2] * 4
    own_states = b_weight.shape[2]
    share = 4 * width // dp_size
    piece = total // PIECES

    def exchange(value, bit):
        return lax.ppermute(value, "dp", [(i, i ^ bit) for i in range(dp_size)])


    b_weight, c_weight = b_weight.reshape(LAYERS, width, full), c_weight.reshape(LAYERS, width, full)
    glu_weight = glu_weight.reshape(LAYERS, 2 * width, full)
    raw = inputs[0]
    raw_near, raw_far = swap(raw, 1, sharers), swap(raw, 2, sharers)
    tokens, sums, params, weights0 = call(
        enter_kernel,
        (
            shape(total, width),
            shape(dp_size * state_size, 8, width),
            shape(PARAM_ROWS, width),
            shape(4 * width, full, dtype=LOW),
        ),
        [pltpu.VMEM((total, width), F32)],
        (lengths, raw, b_weight, c_weight, glu_weight, bn_gain, bn_bias, skip_weight, glu_bias, nu_log, theta_log, gamma_log),
        "enter",
        pieces={1: piece},
        axes={1: 1},
        bare=(3,),
        flops=ENTER_FLOPS,
    )
    params_near, params_far = swap(params, 1, sharers), swap(params, 2, sharers)
    near0, far0 = swap(weights0, 1, sharers), swap(weights0, 2, sharers)
    sums = across(sums, ("dp", "state"))
    if sharers > 1:
        sums = sums.reshape(dp_size * 4, sharers, 8, width)[:, 0]
    cotangent, tokens = lax.optimization_barrier((cotangent, tokens))
    up_own, later = call(
        cotangent_kernel,
        (shape(total, width), shape(6 * width, full, dtype=LOW)),
        [pltpu.VMEM((total, width), F32)],
        (lengths, cotangent[0], b_weight, c_weight, glu_weight),
        "cotangent",
        pieces={1: piece},
        axes={1: 1},
    )
    raw_far, params_far, sums = lax.optimization_barrier((raw_far, params_far, sums))
    normed0, stream0, feature, state, norm0 = call(
        normal_kernel,
        (shape(total, full, dtype=LOW), shape(total, full), shape(PARAM_ROWS, full), shape(8, states), shape(8, full)),
        [pltpu.VMEM((total, width), F32), pltpu.VMEM((8, full), F32)],
        (lengths, sums, tokens, params, params_near, params_far, swap(params_far, 1, sharers),
         raw_near, raw_far, swap(raw_far, 1, sharers)),
        "normal",
        pieces={7: piece, 8: piece, 9: piece},
        axes={7: 1, 8: 1, 9: 1},
    )
    far0, normed0, later = lax.optimization_barrier((far0, normed0, later))
    later_far = swap(later, 2, sharers)
    drive0, low0, stream1, linear0, gate0, slope0, active0, b_all, c_all, w_all, sums1 = call(
        start_kernel,
        (
            shape(total, 256),
            shape(total, 256, dtype=LOW),
            shape(total, full),
            shape(total, full, dtype=LOW),
            shape(total, full, dtype=LOW),
            shape(total, full, dtype=LOW),
            shape(total, full, dtype=LOW),
            shape(2 * states, full, dtype=LOW),
            shape(2 * states, full, dtype=LOW),
            shape(2 * full, full, dtype=LOW),
            shape(dp_size, 8, width),
        ),
        [
            pltpu.VMEM((total, 2 * states), F32),
            pltpu.VMEM((total, 2 * full), F32),
            pltpu.VMEM((2 * states, full), LOW),
            pltpu.VMEM((2 * states, full), LOW),
            pltpu.VMEM((2 * full, full), LOW),
            pltpu.VMEM((total, 2 * states), LOW),
        ],
        (lengths, feature, state, normed0, weights0, near0, far0, swap(far0, 1, sharers), stream0),
        "start",
        pieces={8: piece},
        bare=(7, 8, 9),
    )
    sums1 = across(sums1, "dp")
    later_far, sums1 = lax.optimization_barrier((later_far, sums1))
    result, base, bn1, norm1, *shares1 = call(
        middle_kernel,
        (
            shape(width, total),
            shape(total, full),
            shape(dp_size, 16, width),
            shape(8, full),
            *(shape(share, full, dtype=LOW) for _ in range(dp_size)),
        ),
        [
            pltpu.VMEM((8, full), F32),
            pltpu.VMEM((2 * states, full), LOW),
            pltpu.VMEM((2 * states, full), LOW),
            pltpu.VMEM((2 * full, full), LOW),
            pltpu.VMEM((total, full), LOW),
            pltpu.VMEM((total, 2 * states), F32),
            pltpu.VMEM((total, 256), F32),
            pltpu.VMEM((total, 2 * states), LOW),
            pltpu.VMEM((total, full), F32),
            pltpu.VMEM((total, full), LOW),
            pltpu.VMEM((total, 2 * full), F32),
            pltpu.VMEM((total, width), F32),
            pltpu.VMEM((total, full), F32),
            pltpu.VMEM((total, 2 * full), LOW),
            pltpu.VMEM((total, full), LOW),
            pltpu.VMEM((total, 2 * states), LOW),
            pltpu.VMEM((4 * width, full), LOW),
        ],
        (lengths, sums1, norm0, feature, state, stream1, up_own, later, swap(later, 1, sharers), later_far,
         swap(later_far, 1, sharers)),
        "middle",
        pieces={5: piece},
        bare=tuple(range(4, 4 + dp_size)),
    )
    bn1 = across(bn1, "dp")
    shares1 = [shares1[0]] + [exchange(shares1[bit], bit) for bit in range(1, dp_size)]
    send, up0, grad0 = call(
        last_kernel,
        (shape(dp_size, share + 16, full, dtype=LOW), shape(total, width), shape(total, width)),
        [
            pltpu.VMEM((total, full), F32),
            pltpu.VMEM((total, 2 * states), F32),
            pltpu.VMEM((total, 2 * full), LOW),
            pltpu.VMEM((total, full), LOW),
            pltpu.VMEM((total, 2 * states), LOW),
            pltpu.VMEM((8, full), F32),
            pltpu.VMEM((16, full), F32),
            pltpu.VMEM((4 * width, full), LOW),
            pltpu.VMEM((16, full), F32),
        ],
        (lengths, bn1, norm1, feature, state, norm0, stream1, base, gate0, linear0, w_all, slope0, normed0, active0, c_all, low0,
         drive0, b_all, tokens),
        "last",
        pieces={6: piece, 7: piece, 8: piece, 9: piece},
    )
    *shares1, send = lax.optimization_barrier((*shares1, send))
    (share1,) = call(add_kernel, (shape(share, full, dtype=LOW),), [], (lengths, *shares1), "add")
    shares1 = [share1] + [exchange(share1, bit) for bit in range(1, dp_size)]
    got = across(send, "dp")
    *shares1, got = lax.optimization_barrier((*shares1, got))
    back, small0 = call(
        share_kernel,
        (shape(dp_size, share, full, dtype=LOW), shape(8, full)),
        [],
        (lengths, got),
        "share",
    )
    grad_nu, grad_theta, grad_gamma, grad_skip, grad_bias, grad_gain, grad_shift, grad_inputs = call(
        finish_kernel,
        (
            shape(LAYERS, own_states),
            shape(LAYERS, own_states),
            shape(LAYERS, own_states),
            shape(LAYERS, width),
            shape(LAYERS, 2, width),
            shape(LAYERS, width),
            shape(LAYERS, width),
            shape(width, total),
        ),
        [pltpu.VMEM((32, full), F32), pltpu.VMEM((total, width), F32)],
        (lengths, small0, bn1, norm0, feature, nu_log, theta_log, up0, grad0, tokens),
        "finish",
    )
    grads0 = across(back, "dp").reshape(4 * width, full)
    grad_b, grad_c, grad_glu = call(
        widen_kernel,
        (shape(LAYERS, width, full), shape(LAYERS, width, full), shape(LAYERS, 2 * width, full)),
        [pltpu.VMEM((4 * width, full), LOW)],
        (lengths, grads0, *shares1),
        "widen",
    )
    grad_b = grad_b.reshape(LAYERS, 2, own_states, full)
    grad_c = grad_c.reshape(LAYERS, 2, own_states, full)
    grad_glu = grad_glu.reshape(LAYERS, 2, width, full)
    return (
        own(result[None], 1),
        own(grad_inputs[None], 1),
        own(grad_gain, 1),
        own(grad_shift, 1),
        own(grad_b, 2),
        own(grad_c, 2),
        own(grad_nu, 1),
        own(grad_theta, 1),
        own(grad_gamma, 1),
        own(grad_skip, 1),
        own(grad_glu, 2),
        own(grad_bias, 2),
    )


def solution(mesh):
    in_specs = (
        P("dp", "state", None),
        P("dp"),
        P("dp", "state", None),
        P(None, "state"),
        P(None, "state"),
        P(None, None, "state", None),
        P(None, None, "state", None),
        P(None, "state"),
        P(None, "state"),
        P(None, "state"),
        P(None, "state"),
        P(None, None, "state", None),
        P(None, None, "state"),
    )
    out_specs = (
        P("dp", "state", None),
        P("dp", "state", None),
        P(None, "state"),
        P(None, "state"),
        P(None, None, "state", None),
        P(None, None, "state", None),
        P(None, "state"),
        P(None, "state"),
        P(None, "state"),
        P(None, "state"),
        P(None, None, "state", None),
        P(None, None, "state"),
    )
    step = functools.partial(local, dp_size=mesh.shape["dp"], state_size=mesh.shape["state"])
    return jax.shard_map(step, mesh=mesh, in_specs=in_specs, out_specs=out_specs, check_vma=False)
```

```python
import functools

import jax
import jax.numpy as jnp
from jax import lax
from jax.experimental import pallas as pl
from jax.experimental.pallas import tpu as pltpu
from jax.sharding import PartitionSpec as P

LAYERS = 2
CHUNKS = 16
PIECES = 4
EPSILON = 1e-05
F32 = jnp.float32
LOW = jnp.bfloat16
PARAM_ROWS = 24
OWN_MEAN = 16
VMEM_BYTES = 64 * 1024 * 1024

GAIN, SHIFT, SKIP, BIAS_LINEAR, BIAS_GATE = range(5)
RATE_RE, RATE_IM, GAMMA = range(3)

NN = (((1,), (0,)), ((), ()))
NT = (((1,), (1,)), ((), ()))
TN = (((0,), (0,)), ((), ()))


def dot(left, right, dims):
    return lax.dot_general(left, right, dims, preferred_element_type=F32)


def rows_at(index, size):
    return pl.ds(pl.multiple_of(index * size, size), size)


def lanes_at(quarter, width):
    return pl.ds(pl.multiple_of(quarter * width, width), width)


def for_rows(first, last, size, body, init=0, unroll=2):
    def step(index, carry):
        return body(rows_at(index, size), index, carry)

    return lax.fori_loop(first // size, last // size, step, init, unroll=unroll)


def own_quarter():
    return (lax.axis_index("state") // (lax.axis_size("state") // 4)).astype(jnp.int32)


def keep_rows(first_step, rows, steps, length):
    row = lax.broadcasted_iota(jnp.int32, (rows, 1), 0)
    position = (row % CHUNKS) * steps + row // CHUNKS + first_step
    return position < length


def gelu_parts(value):
    return 0.5 + 0.5 * lax.erf(value * 0.7071067811865476), jnp.exp(value * value * -0.5) * 0.3989422804014327


def squared(re, im, times):
    for _ in range(times):
        re, im = re * re - im * im, 2.0 * re * im
    return re, im


def folded(value):
    return value[0:8, :] + value[8:16, :]


def column_sum(value):
    return jnp.sum(value, axis=0, keepdims=True)


def chunk_starts(re, im, rate_re, rate_im, reverse):
    row = lax.broadcasted_iota(jnp.int32, re.shape, 0)

    def moved(value, by):
        if reverse:
            return jnp.where(row < CHUNKS - by, pltpu.roll(value, CHUNKS - by, 0), 0.0)
        return jnp.where(row >= by, pltpu.roll(value, by, 0), 0.0)

    by = 1
    while by < CHUNKS:
        past_re, past_im = moved(re, by), moved(im, by)
        re, im = (
            re + rate_re * past_re - rate_im * past_im,
            im + rate_re * past_im + rate_im * past_re,
        )
        rate_re, rate_im = squared(rate_re, rate_im, 1)
        by *= 2
    return moved(re, 1), moved(im, 1)


def sweep(drive_ref, rate_re, rate_im, steps, reverse, emit, extra, after=None, unroll=4):
    states = rate_re.shape[1]
    shape = (CHUNKS, states)
    wide_re = jnp.broadcast_to(rate_re, shape)
    wide_im = jnp.broadcast_to(rate_im, shape)

    def advance(index, re, im):
        place = steps - 1 - index if reverse else index
        rows = rows_at(place, CHUNKS)
        drive_re = drive_ref[rows, :states]
        drive_im = drive_ref[rows, states:]
        new_re = (wide_re * re + drive_re) - wide_im * im
        new_im = (wide_re * im + drive_im) + wide_im * re
        return rows, place, new_re, new_im, drive_re, drive_im

    def first(index, carry):
        _, _, re, im, _, _ = advance(index, *carry)
        return re, im

    def second(index, carry):
        re, im, held = carry
        rows, place, re, im, drive_re, drive_im = advance(index, re, im)
        return re, im, emit(rows, place, re, im, drive_re, drive_im, held)

    zero = jnp.zeros(shape, F32)
    re, im = lax.fori_loop(0, steps, first, (zero, zero), unroll=unroll)
    far_re, far_im = rate_re, rate_im
    power = 1
    while power < steps:
        far_re, far_im = squared(far_re, far_im, 1)
        power *= 2
    re, im = chunk_starts(re, im, far_re, far_im, reverse)
    carry = (re, im, extra)
    for piece in range(PIECES):
        size = steps // PIECES
        carry = lax.fori_loop(piece * size, (piece + 1) * size, second, carry, unroll=unroll)
        if after is not None:
            after(PIECES - 1 - piece if reverse else piece)
    return carry[2]


class Arrival:
    def __init__(self, source, ref, done, first, size, axis):
        self.ref = ref
        self.copies = []
        whole = ref.shape[axis]
        for piece, start in enumerate(range(0, whole, size)):
            where = (slice(None),) * axis + (pl.ds(start, min(size, whole - start)),)
            self.copies.append(
                pltpu.make_async_copy(source.at[where], ref.at[where], done.at[first + piece])
                if size < whole
                else pltpu.make_async_copy(source, ref, done.at[first])
            )
        self.short = whole % size > 0
        self.waited = set()

    def start(self, piece):
        last = len(self.copies) - self.short
        if piece < 0 and self.short:
            self.copies[-1].start()
        if 0 <= piece < last:
            self.copies[piece].start()

    def wait(self, piece=None):
        for place in range(len(self.copies)) if piece is None else (piece,):
            if place not in self.waited:
                self.copies[place].wait()
                self.waited.add(place)
        return self.ref


class Departure:
    def __init__(self, target, ref, done, first):
        self.target, self.ref, self.done, self.first = target, ref, done, first
        self.copies = []

    def send(self, start=None, size=None, source=None):
        place = self.done.at[self.first + len(self.copies)]
        where = self.target if start is None else self.target.at[pl.ds(start, size)]
        if source is None:
            source = self.ref if start is None else self.ref.at[pl.ds(start, size)]
        self.copies.append(pltpu.make_async_copy(source, where, place))
        self.copies[-1].start()

    def send_piece(self, piece):
        size = self.target.shape[0] // PIECES
        self.send(piece * size, size)

    def send_unsent(self):
        if not self.copies:
            self.send()

    def finish(self):
        for copy in self.copies:
            copy.wait()


def call(kernel, outs, scratch, args, name, pieces=None, axes=None, bare=(), late=(), order=None, flops=0):
    pieces, axes = pieces or {}, axes or {}
    along = [axes.get(place, 0) for place in range(1, len(args))]
    sizes = [pieces.get(place, args[place].shape[axis]) for place, axis in enumerate(along, 1)]
    counts = [-(-args[place].shape[axis] // size) for place, (axis, size) in enumerate(zip(along, sizes), 1)]
    slots = 6
    copies_in = [pltpu.VMEM(a.shape, a.dtype) for a in args[1:]]
    copies_out = [pltpu.VMEM((8, 128) if place in bare else o.shape, o.dtype if place not in bare else F32) for place, o in enumerate(outs)]

    def body(*refs):
        refs = list(refs)

        def take(count):
            got = refs[:count]
            del refs[:count]
            return got

        (length_ref,) = take(1)
        sources = take(len(args) - 1)
        targets = take(len(outs))
        in_refs, out_refs = take(len(args) - 1), take(len(outs))
        arrived, sent = take(2)
        arrivals, first = [], 0
        for source, ref, size, count, axis in zip(sources, in_refs, sizes, counts, along):
            arrivals.append(Arrival(source, ref, arrived, first, size, axis))
            first += count
        for group in (False, True):
            for piece in (-1, *(order or ()), *(piece for piece in range(max(counts)) if piece not in (order or ()))):
                for place, arrival in enumerate(arrivals, 1):
                    if (place in late) is group:
                        arrival.start(piece)
        departures = [
            Departure(target, ref, sent, place * slots) for place, (target, ref) in enumerate(zip(targets, out_refs))
        ]
        kernel(length_ref, arrivals, departures, *refs)
        for arrival in arrivals:
            arrival.wait()
        for departure in departures:
            departure.send_unsent()
        for departure in departures:
            departure.finish()

    return pl.pallas_call(
        body,
        out_shape=tuple(outs),
        in_specs=[pl.BlockSpec(memory_space=pltpu.SMEM if place == 0 else pl.ANY) for place in range(len(args))],
        out_specs=tuple(pl.BlockSpec(memory_space=pl.ANY) for _ in outs),
        scratch_shapes=[
            *copies_in,
            *copies_out,
            pltpu.SemaphoreType.DMA((sum(counts),)),
            pltpu.SemaphoreType.DMA((slots * len(outs),)),
            *scratch,
        ],
        compiler_params=pltpu.CompilerParams(vmem_limit_bytes=VMEM_BYTES),
        cost_estimate=pl.CostEstimate(flops=int(flops), bytes_accessed=0, transcendentals=0),
        name=name,
    )(*args)


def from_feature_rows(source, held_ref, steps, emit, init, after):
    length = source.ref.shape[1]
    blocks = length // 128
    for block in range(blocks):
        if block % (blocks // PIECES) == 0:
            source.wait(block // (blocks // PIECES))
        lanes = slice(block * 128, (block + 1) * 128)
        held_ref[lanes, :] = source.ref[:, lanes].T

    def step(index, carry):
        return emit(rows_at(index, CHUNKS), index, held_ref[pl.ds(index, CHUNKS, stride=steps), :], carry)

    carry = init
    for piece in range(PIECES):
        size = steps // PIECES
        carry = lax.fori_loop(piece * size, (piece + 1) * size, step, carry, unroll=4)
        after(piece)
    return carry


def to_feature_rows(load, held_ref, out, steps):
    length = out.ref.shape[1]

    def step(index, carry):
        held_ref[pl.ds(index, CHUNKS, stride=steps), :] = load(rows_at(index, CHUNKS), index)
        return carry

    lax.fori_loop(0, steps, step, 0, unroll=4)
    for block in range(length // 128):
        lanes = slice(block * 128, (block + 1) * 128)
        out.ref[:, lanes] = held_ref[lanes, :].T
    out.send()


def spread_rows(value, out):
    for group in range(out.ref.shape[0]):
        out.ref[group, :, :] = value
    out.send()


def narrowed(values, width):
    return jnp.concatenate([v[:, at : at + width] for v in values for at in range(0, v.shape[1], width)], axis=0)


def widened(rows, first, count):
    return jnp.concatenate([rows[first + place : first + place + 1, :] for place in range(count)], axis=1)


def total_rows(sums_ref):
    value = sums_ref[0, :, :]
    for other in range(1, sums_ref.shape[0]):
        value += sums_ref[other, :, :]
    return value


def assemble_states(parts, whole_ref):
    half = parts[0].shape[0] // 2
    states = half * len(parts)
    for place, part in enumerate(parts):
        whole_ref[place * half : (place + 1) * half, :] = part[:half, :]
        whole_ref[states + place * half : states + (place + 1) * half, :] = part[half:, :]


def assemble_output(parts, whole_ref):
    half = parts[0].shape[0] // 2
    states = half * len(parts)
    for place, part in enumerate(parts):
        whole_ref[place * half : (place + 1) * half, :] = part[:half, :]
        whole_ref[states + place * half : states + (place + 1) * half, :] = -part[half:, :]


def assemble_glu(parts, whole_ref, quarter):
    half = parts[0].shape[0] // 2
    width = half * len(parts)
    for place, part in enumerate(parts):
        whole_ref[lanes_at(quarter ^ place, half), :] = part[:half, :]
        whole_ref[pl.ds(pl.multiple_of(width + (quarter ^ place) * half, half), half), :] = part[half:, :]


def norm_rows(sums, counted):
    centre = sums[0:1, :] / counted
    meansq = sums[1:2, :] / counted
    return centre, lax.rsqrt(meansq - centre * centre + EPSILON)


def drive_phase(normed_ref, b_ref, drive_ref, gamma):
    drive_ref[...] = dot(normed_ref[...], b_ref[...], NT) * jnp.concatenate([gamma, gamma], axis=1)


def store_states(low_ref, drive_own_ref):
    def emit(rows, step, re, im, drive_re, drive_im, held):
        states = re.shape[1]
        low_ref[rows, :states] = re.astype(LOW)
        low_ref[rows, states:] = im.astype(LOW)
        drive_own_ref[rows, :128] = drive_re[:, :128].astype(drive_own_ref.dtype)
        drive_own_ref[rows, 128:] = drive_im[:, :128].astype(drive_own_ref.dtype)
        return held

    return emit


def pre_phase(low_ref, c_ref, normed_ref, skip, active_ref, slope_ref, held_ref, after=None):
    total, full = normed_ref.shape
    held_ref[:, :full] = dot(low_ref[...], c_ref[...], NN)

    def inner(rows, index, carry):
        value = held_ref[rows, :full] + skip * normed_ref[rows, :].astype(F32)
        cdf, density = gelu_parts(value)
        active_ref[rows, :] = (value * cdf).astype(LOW)
        slope_ref[rows, :] = (cdf + value * density).astype(slope_ref.dtype)
        return carry

    for piece in range(PIECES):
        for_rows(piece * total // PIECES, (piece + 1) * total // PIECES, 16, inner, unroll=4)
        if after is not None:
            after(piece)


def pre_grad_phase(grad_gated_ref, w_ref, slope_ref, normed_ref, quarter, pre_grad_ref, held_ref, small_ref):
    total, full = normed_ref.shape
    own = lanes_at(quarter, 128)
    held_ref[:, :full] = dot(grad_gated_ref[...], w_ref[...], NN)

    def inner(rows, index, carry):
        pre_grad_ref[rows, :] = (held_ref[rows, :full] * slope_ref[rows, :].astype(F32)).astype(LOW)
        return carry + folded(pre_grad_ref[rows, own].astype(F32) * normed_ref[rows, own].astype(F32))

    small_ref[3:4, 0:128] = column_sum(for_rows(0, total, 16, inner, jnp.zeros((8, 128), F32), unroll=4))


def adjoint_phase(pre_grad_ref, c_ref, low_ref, im_lane, drive_own_ref, state, first_row, length, grad_state_ref, grad_driven_ref, small_ref, reverse):
    total = pre_grad_ref.shape[0]
    steps = total // CHUNKS
    states = state.shape[1]
    grad_state_ref[...] = dot(pre_grad_ref[...], c_ref[...], NT)
    rate_re = state[first_row : first_row + 1, :]
    rate_im = state[first_row + 1 : first_row + 2, :]
    gamma = jnp.broadcast_to(state[first_row + 2 : first_row + 3, :], (CHUNKS, states))

    def emit(rows, step, re, im, drive_re, drive_im, held):
        out_re, out_im = gamma * re, gamma * im
        if not reverse:
            keep = keep_rows(step, CHUNKS, steps, length)
            out_re, out_im = jnp.where(keep, out_re, 0.0), jnp.where(keep, out_im, 0.0)
        grad_driven_ref[rows, :states] = out_re.astype(LOW)
        grad_driven_ref[rows, states:] = out_im.astype(LOW)
        one, two, three = held
        own_re, own_im = re[:, :128], im[:, :128]
        late_re, late_im = own_re - drive_re[:, :128], own_im - drive_im[:, :128]
        low_re = low_ref[rows, :128].astype(F32)
        low_im = low_ref[rows, im_lane : im_lane + 128].astype(F32)
        one = one + folded(late_re * low_re + late_im * low_im)
        two = two + folded(late_im * low_re - late_re * low_im)
        three = three + folded(
            own_re * drive_own_ref[rows, :128].astype(F32) + own_im * drive_own_ref[rows, 128:].astype(F32)
        )
        return one, two, three

    zero = jnp.zeros((8, 128), F32)
    one, two, three = sweep(grad_state_ref, rate_re, -rate_im, steps, reverse, emit, (zero, zero, zero))
    small_ref[0:1, 0:128] = column_sum(one)
    small_ref[1:2, 0:128] = column_sum(two)
    small_ref[2:3, 0:128] = column_sum(three)


def glu_grads(grads_ref, first, grad_gated_ref, active_ref, quarter):
    full = active_ref.shape[1]
    for place in range(2):
        lanes = pl.ds(pl.multiple_of(place * full + quarter * 128, 128), 128)
        got = dot(grad_gated_ref[:, lanes], active_ref[...], TN)
        grads_ref[first + place * 128 : first + (place + 1) * 128, :] = got.astype(LOW)


def state_grads(grads_ref, grad_driven_ref, normed_ref, low_re, low_im, pre_grad_ref, states):
    half = states // 4
    for place, low in enumerate((low_re, low_im)):
        lanes = slice(place * states, place * states + 128)
        got = dot(grad_driven_ref[:, lanes], normed_ref[...], TN)[:half, :]
        grads_ref[place * half : (place + 1) * half, :] = got.astype(LOW)
        got = dot(low, pre_grad_ref[...], TN)[:half, :]
        got = got if place == 0 else -got
        grads_ref[2 * half + place * half : 2 * half + (place + 1) * half, :] = got.astype(LOW)


def enter_kernel(length_ref, ins, outs, held_ref):
    x, gain, shift, skip, bias, nu, theta, gamma, b, c, w = ins
    tokens, spread, params, first_out = outs
    length = length_ref[0]
    width, total = x.ref.shape
    steps = total // CHUNKS

    def emit(rows, index, value, carry):
        tokens.ref[rows, :] = value
        kept = jnp.where(keep_rows(index, CHUNKS, steps, length), value, 0.0)
        return carry[0] + folded(kept), carry[1] + folded(kept * kept)

    zero = jnp.zeros((8, width), F32)
    plain, square = from_feature_rows(x, held_ref, steps, emit, (zero, zero), tokens.send_piece)
    plain = column_sum(plain)
    counted = jnp.full((1, width), length, jnp.int32).astype(F32)
    spread_rows(jnp.concatenate([plain, column_sum(square), counted, jnp.zeros((5, width), F32)], axis=0), spread)
    mean = plain / counted

    each = total // PIECES

    def centred(rows, index, carry):
        place = pl.ds(pl.multiple_of(4 * width + index * 32 % each, 32), 32)
        first_out.ref[place, lanes_at(index * 32 // each, width)] = (tokens.ref[rows, :] - mean).astype(LOW)
        return carry

    for_rows(0, total, 32, centred, unroll=4)
    first_out.send(4 * width, each)
    for value in (gain, shift, skip, bias, nu, theta, gamma):
        value.wait()
    params.ref[...] = jnp.zeros((PARAM_ROWS, width), F32)
    for layer in range(LAYERS):
        first = 5 * layer
        params.ref[first + GAIN : first + GAIN + 1, :] = gain.ref[layer : layer + 1, :]
        params.ref[first + SHIFT : first + SHIFT + 1, :] = shift.ref[layer : layer + 1, :]
        params.ref[first + SKIP : first + SKIP + 1, :] = skip.ref[layer : layer + 1, :]
        params.ref[first + BIAS_LINEAR : first + BIAS_GATE + 1, :] = bias.ref[layer, :, :]
        first = 10 + 3 * layer
        for row, source in enumerate((nu, theta, gamma)):
            params.ref[first + row : first + row + 1, : source.ref.shape[1]] = source.ref[layer : layer + 1, :]
    params.ref[OWN_MEAN : OWN_MEAN + 1, :] = mean
    params.send()
    b.wait()
    first_out.send(0, width, source=b.ref.at[0])
    c.wait()
    first_out.send(width, width, source=c.ref.at[0])
    w.wait()
    first_out.send(2 * width, 2 * width, source=w.ref.at[0])


def cotangent_kernel(length_ref, ins, outs, held_ref):
    x, b, c, w = ins
    whole, later = outs
    width, total = x.ref.shape
    steps = total // CHUNKS
    each = steps // PIECES

    def emit(rows, index, value, carry):
        whole.ref[rows, :] = value
        place = pl.ds(pl.multiple_of(4 * width + index % each * CHUNKS, CHUNKS), CHUNKS)
        later.ref[place, lanes_at(index // each, width)] = value.astype(LOW)
        return carry

    def after(piece):
        whole.send_piece(piece)
        if piece == 1:
            b.wait()
            later.send(0, width, source=b.ref.at[1])
            c.wait()
            later.send(width, width, source=c.ref.at[1])
            w.wait()
            later.send(2 * width, 2 * width, source=w.ref.at[1])

    from_feature_rows(x, held_ref, steps, emit, 0, after)
    later.send(4 * width, total // PIECES)


def start_kernel(length_ref, ins, outs, stats_ref, stream_ref, drive_ref, held_ref, b_ref, c_ref, w_ref, low_ref):
    sums, params, tokens = ins[0], ins[1:5], ins[5]
    weights = ins[6:10]
    feature, state_out, norm, normed, drive_own, low_own, stream, linear_out, gate_out, slope, active, b_out, c_out, w_out, spread = outs
    length, quarter = length_ref[0], own_quarter()
    total, full = active.ref.shape
    steps = total // CHUNKS
    width = full // 4
    lane = lax.broadcasted_iota(jnp.int32, (8, width), 1)
    tails = [part.wait() for part in params]
    for place, value in enumerate(tails):
        feature.ref[:, lanes_at(quarter ^ place, width)] = value[...]
    for pair in range(2):
        early, late = (value[8:16, :] for value in tails[2 * pair : 2 * pair + 2])
        logs = jnp.where(lane < 64, early, pltpu.roll(late, 64, 1))
        lanes = slice(pair * width, (pair + 1) * width)
        for layer in range(LAYERS):
            first = 2 + 3 * layer
            modulus = jnp.exp(-jnp.exp(logs[first : first + 1, :]))
            angle = jnp.exp(logs[first + 1 : first + 2, :])
            state_out.ref[first : first + 1, lanes] = modulus * jnp.cos(angle)
            state_out.ref[first + 1 : first + 2, lanes] = modulus * jnp.sin(angle)
            state_out.ref[first + 2 : first + 3, lanes] = jnp.exp(logs[first + 2 : first + 3, :])
    sums_ref = sums.wait()
    for place in range(4):
        value = sums_ref[place, :, :]
        for other in range(1, sums_ref.shape[0] // 4):
            value += sums_ref[other * 4 + place, :, :]
        stats_ref[:, place * width : (place + 1) * width] = value
    centre, inv_dev = norm_rows(stats_ref[0:2, :], stats_ref[2:3, :])
    norm.ref[...] = jnp.zeros_like(norm.ref)
    norm.ref[0:1, :] = centre
    norm.ref[1:2, :] = inv_dev
    norm.ref[2:3, :] = stats_ref[2:3, :]
    for out in (feature, state_out, norm):
        out.send()

    each = total // PIECES

    def normal(rows, index, carry):
        keep = keep_rows(index, 16, steps, length)
        there = pl.ds(pl.multiple_of(4 * width + index * 16 % each, 16), 16)
        for place, part in enumerate(weights):
            lanes = lanes_at(quarter ^ place, width)
            if place == 0:
                value = tokens.ref[rows, :]
            else:
                value = part.ref[there, lanes_at(index * 16 // each, width)].astype(F32)
                value = value + feature.ref[OWN_MEAN : OWN_MEAN + 1, lanes]
            stream_ref[rows, lanes] = value
            z = (value - norm.ref[0:1, lanes]) * norm.ref[1:2, lanes]
            z = z * feature.ref[GAIN : GAIN + 1, lanes] + feature.ref[SHIFT : SHIFT + 1, lanes]
            normed.ref[rows, lanes] = jnp.where(keep, z, 0.0).astype(LOW)
        return carry

    for part in weights[1:]:
        part.wait(4)
        part.wait(5)
    for piece in range(PIECES):
        tokens.wait(piece)
        for_rows(piece * total // PIECES, (piece + 1) * total // PIECES, 16, normal)
        normed.send_piece(piece)
    for part in weights:
        part.wait(0)
    assemble_states([part.ref.at[0:width] for part in weights], b_ref)
    b_out.send(source=b_ref)
    state = state_out.ref[...]
    states = state.shape[1]
    drive_phase(normed.ref, b_ref, drive_ref, state[2 + GAMMA : 3 + GAMMA, :])
    for part in weights:
        part.wait(1)
    assemble_output([part.ref.at[width : 2 * width] for part in weights], c_ref)
    c_out.send(source=c_ref)
    store = store_states(low_ref, drive_own.ref)

    def emit(rows, step, re, im, drive_re, drive_im, held):
        low_own.ref[rows, :128] = re[:, :128].astype(LOW)
        low_own.ref[rows, 128:] = im[:, :128].astype(LOW)
        return store(rows, step, re, im, drive_re, drive_im, held)

    sweep(drive_ref, state[2:3, :], state[3:4, :], steps, False, emit, 0)
    drive_own.send()
    low_own.send()

    def after(piece):
        active.send_piece(piece)
        slope.send_piece(piece)

    pre_phase(low_ref, c_ref, normed.ref, feature.ref[SKIP : SKIP + 1, :], active.ref, slope.ref, held_ref, after)
    assemble_glu([part.wait().at[2 * width : 4 * width] for part in weights], w_ref, quarter)
    w_out.send(source=w_ref)
    held_ref[...] = dot(active.ref[...], w_ref[...], NT)

    def inner(rows, index, carry):
        keep = keep_rows(index, 16, steps, length)
        linear = held_ref[rows, :full] + feature.ref[BIAS_LINEAR : BIAS_LINEAR + 1, :]
        gate = jax.nn.sigmoid(held_ref[rows, full:] + feature.ref[BIAS_GATE : BIAS_GATE + 1, :])
        mixed = linear * gate
        gate_out.ref[rows, :] = gate.astype(LOW)
        linear_out.ref[rows, :] = (mixed * (1.0 - gate)).astype(LOW)
        moved = stream_ref[rows, :] + jnp.where(keep, mixed, 0.0)
        stream.ref[rows, :] = moved
        kept = jnp.where(keep, moved, 0.0)
        return carry[0] + folded(kept), carry[1] + folded(kept * kept)

    zero = jnp.zeros((8, full), F32)
    carry = (zero, zero)
    for piece in range(PIECES):
        carry = for_rows(piece * total // PIECES, (piece + 1) * total // PIECES, 16, inner, carry)
        for out in (stream, linear_out, gate_out):
            out.send_piece(piece)
    spread_rows(narrowed([column_sum(carry[0]), column_sum(carry[1])], width), spread)


def middle_kernel(
    length_ref, ins, outs,
    small_ref, b_ref, c_ref, w_ref, normed_ref, drive_ref, drive_own_ref, low_ref, slope_ref, active_ref, held_ref,
    order_ref, up_ref, grad_gated_ref, pre_grad_ref, grad_driven_ref, grads_ref,
):
    sums, norm0, feature_in, state_in, stream, up_own = ins[:6]
    weights = ins[6:]
    result, base, spread, norm, *shares = outs
    length, quarter = length_ref[0], own_quarter()
    total, full = stream.ref.shape
    steps = total // CHUNKS
    width = 128
    counted = norm0.wait()[2:3, :]
    feature = feature_in.wait()
    state = state_in.wait()[...]
    states = state.shape[1]
    whole = total_rows(sums.wait())
    whole = jnp.concatenate([widened(whole, 0, 4), widened(whole, 4, 4)], axis=0)
    centre, inv_dev = norm_rows(whole, counted)
    norm.ref[...] = jnp.zeros_like(norm.ref)
    norm.ref[0:1, :] = centre
    norm.ref[1:2, :] = inv_dev
    norm.ref[2:3, :] = counted
    norm.send()
    gain = feature[5 + GAIN : 6 + GAIN, :]
    shift = feature[5 + SHIFT : 6 + SHIFT, :]
    skip = feature[5 + SKIP : 6 + SKIP, :]

    def normal(rows, index, carry):
        keep = keep_rows(index, 16, steps, length)
        z = (stream.ref[rows, :] - centre) * inv_dev
        normed_ref[rows, :] = jnp.where(keep, z * gain + shift, 0.0).astype(LOW)
        return carry

    for piece in range(PIECES):
        stream.wait(piece)
        for_rows(piece * total // PIECES, (piece + 1) * total // PIECES, 16, normal, unroll=4)
    for part in weights:
        part.wait()
    assemble_states([part.ref.at[0:width] for part in weights], b_ref)
    assemble_output([part.ref.at[width : 2 * width] for part in weights], c_ref)
    assemble_glu([part.ref.at[2 * width : 4 * width] for part in weights], w_ref, quarter)
    drive_phase(normed_ref, b_ref, drive_ref, state[5 + GAMMA : 6 + GAMMA, :])
    sweep(drive_ref, state[5:6, :], state[6:7, :], steps, True, store_states(low_ref, drive_own_ref), 0)
    pre_phase(low_ref, c_ref, normed_ref, skip, active_ref, slope_ref, held_ref)
    held_ref[...] = dot(active_ref[...], w_ref[...], NT)
    up_own.wait()
    own, own_far = lanes_at(quarter, width), lanes_at(quarter + 4, width)

    def spread_up(rows, index, carry):
        up_ref[rows, own] = up_own.ref[rows, :]
        return carry

    for_rows(0, total, 16, spread_up, unroll=4)
    for piece in range(PIECES):
        for place, part in enumerate(weights[1:], 1):
            lanes = lanes_at(quarter ^ place, width)
            size = total // PIECES
            up_ref[piece * size : (piece + 1) * size, lanes] = part.ref[4 * width :, piece * width : (piece + 1) * width].astype(F32)

    def inner(rows, index, carry):
        keep = keep_rows(index, 16, steps, length)
        linear = held_ref[rows, :full] + feature[5 + BIAS_LINEAR : 6 + BIAS_LINEAR, :]
        gate = jax.nn.sigmoid(held_ref[rows, full:] + feature[5 + BIAS_GATE : 6 + BIAS_GATE, :])
        mixed = linear * gate
        up = jnp.where(keep, up_ref[rows, :], 0.0)
        grad_gated_ref[rows, :full] = (up * gate).astype(LOW)
        grad_gated_ref[rows, full:] = (up * mixed * (1.0 - gate)).astype(LOW)
        held_ref[rows, :full] = jnp.where(keep, mixed, 0.0)
        return (
            carry[0] + folded(grad_gated_ref[rows, own].astype(F32)),
            carry[1] + folded(grad_gated_ref[rows, own_far].astype(F32)),
        )

    zero = jnp.zeros((8, width), F32)
    one, two = for_rows(0, total, 16, inner, (zero, zero))
    small_ref[...] = jnp.zeros_like(small_ref)
    small_ref[4:5, 0:128] = column_sum(one)
    small_ref[5:6, 0:128] = column_sum(two)
    to_feature_rows(lambda rows, index: stream.ref[rows, own] + held_ref[rows, own], order_ref, result, steps)
    pre_grad_phase(grad_gated_ref, w_ref, slope_ref, normed_ref, quarter, pre_grad_ref, held_ref, small_ref)
    adjoint_phase(
        pre_grad_ref, c_ref, low_ref, states, drive_own_ref, state, 5, length, drive_ref, grad_driven_ref, small_ref, False
    )
    held_ref[:, :full] = dot(grad_driven_ref[...], b_ref[...], NN)
    scale = inv_dev * gain

    def back(rows, index, carry):
        grad = held_ref[rows, :full] + skip * pre_grad_ref[rows, :].astype(F32)
        z = (stream.ref[rows, :] - centre) * inv_dev
        base.ref[rows, :] = scale * grad + up_ref[rows, :]
        return carry[0] + folded(grad), carry[1] + folded(grad * z)

    zero = jnp.zeros((8, full), F32)
    carry = (zero, zero)
    for piece in range(PIECES):
        carry = for_rows(piece * total // PIECES, (piece + 1) * total // PIECES, 16, back, carry)
        base.send_piece(piece)
    sent = narrowed([column_sum(carry[0]), column_sum(carry[1])], width)
    spread_rows(jnp.concatenate([sent, small_ref[:, 0:width]], axis=0), spread)
    glu_grads(grads_ref, 2 * width, grad_gated_ref, active_ref, quarter)
    state_grads(grads_ref, grad_driven_ref, normed_ref, low_ref[:, 0:128], low_ref[:, states : states + 128], pre_grad_ref, states)
    send_halves(grads_ref, shares, 0)


def last_kernel(
    length_ref, ins, outs, held_ref, grad_state_ref, grad_gated_ref, pre_grad_ref, grad_driven_ref, small_ref, row_ref, grads_ref, pack_ref, low_ref
):
    (sums, norm1, feature_in, state_in, norm0, stream, base, gate, linear, w, slope, normed, active, c, low, drive_own, b, x) = ins
    kept, sent, up_out, grad_out = outs
    length, quarter = length_ref[0], own_quarter()
    total, full = stream.ref.shape
    steps = total // CHUNKS
    width = 128
    own = lanes_at(quarter, width)
    feature, norm_ref = feature_in.wait(), norm1.wait()
    state = state_in.wait()[...]
    counted = norm_ref[2:3, :]
    whole = total_rows(sums.wait())
    whole = jnp.concatenate([widened(whole, 0, 4), widened(whole, 4, 4)], axis=0)
    centre, inv_dev = norm_ref[0:1, :], norm_ref[1:2, :]
    scale = inv_dev * feature[5 + GAIN : 6 + GAIN, :]
    level = scale * whole[0:1, :] / counted
    tilt = scale * inv_dev * whole[1:2, :] / counted

    def top(rows, index, carry):
        keep = keep_rows(index, 16, steps, length)
        up = base.ref[rows, :] - jnp.where(keep, level + (stream.ref[rows, :] - centre) * tilt, 0.0)
        row_ref[...] = up
        up_out.ref[rows, :] = row_ref[:, own]
        up = jnp.where(keep, up, 0.0)
        grad_gated_ref[rows, :full] = (up * gate.ref[rows, :].astype(F32)).astype(LOW)
        grad_gated_ref[rows, full:] = (up * linear.ref[rows, :].astype(F32)).astype(LOW)
        far = pl.ds(pl.multiple_of(full + quarter * width, width), width)
        return (
            carry[0] + folded(grad_gated_ref[rows, own].astype(F32)),
            carry[1] + folded(grad_gated_ref[rows, far].astype(F32)),
        )

    zero = jnp.zeros((8, width), F32)
    carry = (zero, zero)
    for piece in range(PIECES):
        for value in (stream, base, gate, linear):
            value.wait(piece)
        carry = for_rows(piece * total // PIECES, (piece + 1) * total // PIECES, 16, top, carry)
        up_out.send_piece(piece)
    small_ref[...] = jnp.zeros_like(small_ref)
    small_ref[4:5, 0:128] = column_sum(carry[0])
    small_ref[5:6, 0:128] = column_sum(carry[1])
    for value in (w, slope, normed):
        value.wait()
    pre_grad_phase(grad_gated_ref, w.ref, slope.ref, normed.ref, quarter, pre_grad_ref, held_ref, small_ref)
    for value in (active, c, low, drive_own):
        value.wait()
    glu_grads(grads_ref, 2 * width, grad_gated_ref, active.ref, quarter)
    adjoint_phase(
        pre_grad_ref, c.ref, low.ref, 128, drive_own.ref, state, 2, length, grad_state_ref, grad_driven_ref, small_ref, True
    )
    b.wait()
    x.wait()
    held_ref[:, :width] = dot(grad_driven_ref[...], b.ref[:, own], NN)
    centre0, inv_dev0 = norm0.wait()[0:1, own], norm0.ref[1:2, own]
    skip = feature[SKIP : SKIP + 1, own]

    def back(rows, index, carry):
        grad = held_ref[rows, :width] + skip * pre_grad_ref[rows, own].astype(F32)
        grad_out.ref[rows, :] = grad
        z = (x.ref[rows, :] - centre0) * inv_dev0
        return carry[0] + folded(grad), carry[1] + folded(grad * z)

    plain, scaled = for_rows(0, total, 16, back, (zero, zero), unroll=4)
    grad_out.send()
    small_ref[6:7, 0:width] = column_sum(plain)
    small_ref[7:8, 0:width] = column_sum(scaled)
    state_grads(grads_ref, grad_driven_ref, normed.ref, low.ref[:, :128], low.ref[:, 128:], pre_grad_ref, state.shape[1])
    pack_ref[...] = jnp.zeros_like(pack_ref)
    for place in range(8):
        pack_ref[place // 4 : place // 4 + 1, place % 4 * width : (place % 4 + 1) * width] = small_ref[place : place + 1, 0:width]
    exact = pack_ref[0:8, :]
    pack_ref[8:16, :] = exact - exact.astype(LOW).astype(F32)
    half = grads_ref.shape[0] // 2
    low_ref[...] = pack_ref[...].astype(LOW)
    mine = lax.axis_index("dp") & 1
    for out, which in ((kept, mine), (sent, 1 - mine)):
        out.send(0, half, source=grads_ref.at[rows_at(which, half)])
        out.send(half, 16, source=low_ref)


def send_halves(source_ref, outs, stage):
    kept = lax.axis_index("dp") >> stage & 1
    half = source_ref.shape[0] // 2
    for out, which in zip(outs, (kept, 1 - kept)):
        out.send(source=source_ref.at[rows_at(which, half)])


def add_kernel(length_ref, ins, outs, sum_ref, stage):
    kept, other = ins
    kept.wait()
    other.wait()
    for piece in range(0, kept.ref.shape[0], 16):
        at = slice(piece, piece + 16)
        sum_ref[at, :] = (kept.ref[at, :].astype(F32) + other.ref[at, :].astype(F32)).astype(LOW)
    send_halves(sum_ref, outs, stage)


def pair_kernel(length_ref, ins, outs, sum_ref, pack_ref):
    kept, other = ins
    kept.wait()
    other.wait()
    half = kept.ref.shape[0] - 16
    share = half // len(outs)
    small = kept.ref[half:, :].astype(F32) + other.ref[half:, :].astype(F32)
    small = small[0:8, :] + small[8:16, :]
    pack_ref[...] = jnp.concatenate([small, small - small.astype(LOW).astype(F32)], axis=0).astype(LOW)
    for piece in range(0, half, 16):
        at = slice(piece, piece + 16)
        sum_ref[at, :] = (kept.ref[at, :].astype(F32) + other.ref[at, :].astype(F32)).astype(LOW)
    for place, out in enumerate(outs):
        out.send(0, share, source=sum_ref.at[rows_at((lax.axis_index("dp") >> 1) ^ place, share)])
        out.send(share, 16, source=pack_ref)


def share_kernel(length_ref, ins, outs):
    *blocks, kept, other = ins
    out, small = outs
    share = kept.ref.shape[0]
    for value in ins:
        value.wait()
    for piece in range(0, share, 16):
        at = slice(piece, piece + 16)
        value = blocks[0].ref[at, :].astype(F32)
        for block in blocks[1:]:
            value += block.ref[at, :].astype(F32)
        out.ref[at, :] = value.astype(LOW)
        value = kept.ref[at, :].astype(F32) + other.ref[at, :].astype(F32)
        out.ref[share + piece : share + piece + 16, :] = value.astype(LOW)
    out.send()
    value = blocks[0].ref[share:, :].astype(F32)
    for block in blocks[1:]:
        value += block.ref[share:, :].astype(F32)
    small.ref[...] = value[0:8, :] + value[8:16, :]


def finish_kernel(length_ref, ins, outs, held_ref, order_ref):
    small0, bn1, norm0, feature, nu, theta, up, grad, x = ins
    nu_out, theta_out, gamma_out, skip_out, bias_out, gain_out, shift_out, out = outs
    length, quarter = length_ref[0], own_quarter()
    total, width = up.ref.shape
    steps = total // CHUNKS
    own = lanes_at(quarter, width)
    states = nu_out.ref.shape[1]
    for value in ins:
        value.wait()
    whole = total_rows(bn1.ref)
    held_ref[0:1, :] = widened(whole, 0, 4)
    held_ref[1:2, :] = widened(whole, 4, 4)
    held_ref[16:32, :width] = whole
    for place in range(8):
        held_ref[8 + place : 9 + place, :width] = small0.ref[place // 4 : place // 4 + 1, place % 4 * width : (place % 4 + 1) * width]
    for layer, first in ((0, 8), (1, 24)):
        at = slice(layer, layer + 1)
        nu_out.ref[at, :] = -jnp.exp(nu.ref[at, :]) * held_ref[first : first + 1, :states]
        theta_out.ref[at, :] = jnp.exp(theta.ref[at, :]) * held_ref[first + 1 : first + 2, :states]
        gamma_out.ref[at, :] = held_ref[first + 2 : first + 3, :states]
        skip_out.ref[at, :] = held_ref[first + 3 : first + 4, :width]
        bias_out.ref[layer, 0:1, :] = held_ref[first + 4 : first + 5, :width]
        bias_out.ref[layer, 1:2, :] = held_ref[first + 5 : first + 6, :width]
    shift_out.ref[0:1, :] = held_ref[14:15, :width]
    gain_out.ref[0:1, :] = held_ref[15:16, :width]
    shift_out.ref[1:2, :] = held_ref[0:1, own]
    gain_out.ref[1:2, :] = held_ref[1:2, own]
    counted = norm0.ref[2:3, own]
    centre, inv_dev = norm0.ref[0:1, own], norm0.ref[1:2, own]
    level = held_ref[14:15, :width] / counted
    tilt = held_ref[15:16, :width] * inv_dev / counted
    scale = inv_dev * feature.ref[GAIN : GAIN + 1, own]

    def load(rows, index):
        keep = keep_rows(index, CHUNKS, steps, length)
        inner = grad.ref[rows, :] - level - (x.ref[rows, :] - centre) * tilt
        return up.ref[rows, :] + jnp.where(keep, scale * inner, 0.0)

    to_feature_rows(load, order_ref, out, steps)


def widen_kernel(length_ref, ins, outs, held_ref):
    half = outs[0].ref.shape[1]
    groups = len(ins)
    share = ins[0].ref.shape[0] // 2
    stages = groups.bit_length() - 1
    for place, value in enumerate(ins):
        value.wait()
        owner = lax.axis_index("dp") ^ place
        index = sum((owner >> stage & 1) << (stages - 1 - stage) for stage in range(stages))
        for layer, at in ((0, (owner & 1) * (groups // 2) + (owner >> 1)), (1, index)):
            held_ref[layer, rows_at(at, share), :] = value.ref[layer * share : (layer + 1) * share, :].astype(F32)
    for layer in range(LAYERS):
        for out, first, size in zip(outs, (0, half, 2 * half), (half, half, 2 * half)):
            out.send(layer, 1, source=held_ref.at[pl.ds(layer, 1), pl.ds(first, size)])


def shape(*dims, dtype=F32):
    return jax.ShapeDtypeStruct(dims, dtype)


def swap(value, bit, sharers):
    pairs = [(q * sharers + r, (q ^ bit) * sharers + r) for q in range(4) for r in range(sharers)]
    return lax.ppermute(value, "state", pairs)


def across(value, axes):
    return lax.all_to_all(value, axes, 0, 0, tiled=True)


def local(
    inputs, lengths, cotangent, bn_gain, bn_bias, b_weight, c_weight, nu_log, theta_log, gamma_log, skip_weight,
    glu_weight, glu_bias, dp_size, state_size,
):
    sharers = state_size // 4
    place = lax.axis_index("state").astype(jnp.int32)

    def joined(value, axis):
        if sharers == 1:
            return value
        groups = [[q * sharers + r for r in range(sharers)] for q in range(4)]
        return lax.all_gather(value, "state", axis=axis, axis_index_groups=groups, tiled=True)

    def own(value, axis):
        if sharers == 1:
            return value
        size = value.shape[axis] // sharers
        return lax.dynamic_slice_in_dim(value, place % sharers * size, size, axis)

    inputs, cotangent = joined(inputs, 1), joined(cotangent, 1)
    bn_gain, bn_bias, skip_weight = joined(bn_gain, 1), joined(bn_bias, 1), joined(skip_weight, 1)
    nu_log, theta_log, gamma_log = joined(nu_log, 1), joined(theta_log, 1), joined(gamma_log, 1)
    b_weight, c_weight = joined(b_weight, 2), joined(c_weight, 2)
    glu_weight, glu_bias = joined(glu_weight, 2), joined(glu_bias, 2)
    width, total = inputs.shape[1:]
    full = b_weight.shape[3]
    states = b_weight.shape[2] * 4
    own_states = b_weight.shape[2]
    share = 4 * width // dp_size
    piece = total // PIECES

    stages = dp_size.bit_length() - 1

    def exchange(value, bit):
        return lax.ppermute(value, "dp", [(i, i ^ bit) for i in range(dp_size)])

    def add(halves, stage):
        kept, other = halves
        rows = kept.shape[0]
        return call(
            functools.partial(add_kernel, stage=stage + 1),
            (shape(rows // 2, full, dtype=LOW),) * 2,
            [pltpu.VMEM((rows, full), LOW)],
            (lengths, kept, other),
            "add",
            bare=(0, 1),
        )


    b_weight, c_weight = b_weight.reshape(LAYERS, width, full), c_weight.reshape(LAYERS, width, full)
    glu_weight = glu_weight.reshape(LAYERS, 2 * width, full)
    tokens, sums, params, first = call(
        enter_kernel,
        (
            shape(total, width),
            shape(dp_size * state_size, 8, width),
            shape(PARAM_ROWS, width),
            shape(6 * width, full, dtype=LOW),
        ),
        [pltpu.VMEM((total, width), F32)],
        (lengths, inputs[0], bn_gain, bn_bias, skip_weight, glu_bias, nu_log, theta_log, gamma_log, b_weight, c_weight, glu_weight),
        "enter",
        pieces={1: piece},
        axes={1: 1},
        late=(9, 10, 11),
    )
    near = [swap(value, 1, sharers) for value in (params, first)]
    far = [swap(value, 2, sharers) for value in (params, first)]
    sums = across(sums, ("dp", "state"))
    if sharers > 1:
        sums = sums.reshape(dp_size * 4, sharers, 8, width)[:, 0]
    cotangent, tokens = lax.optimization_barrier((cotangent, tokens))
    up_own, later = call(
        cotangent_kernel,
        (shape(total, width), shape(6 * width, full, dtype=LOW)),
        [pltpu.VMEM((total, width), F32)],
        (lengths, cotangent[0], b_weight, c_weight, glu_weight),
        "cotangent",
        pieces={1: piece},
        axes={1: 1},
        late=(2, 3, 4),
    )
    *far, near[0], near[1], sums, later = lax.optimization_barrier((*far, *near, sums, later))
    diagonal = [swap(value, 1, sharers) for value in far]
    later_far = swap(later, 2, sharers)
    parts = list(zip((params, first), near, far, diagonal))
    feature, state, norm0, normed0, drive0, low0, stream1, linear0, gate0, slope0, active0, b_all, c_all, w_all, sums1 = call(
        start_kernel,
        (
            shape(PARAM_ROWS, full),
            shape(8, states),
            shape(8, full),
            shape(total, full, dtype=LOW),
            shape(total, 256),
            shape(total, 256, dtype=LOW),
            shape(total, full),
            shape(total, full, dtype=LOW),
            shape(total, full, dtype=LOW),
            shape(total, full, dtype=LOW),
            shape(total, full, dtype=LOW),
            shape(2 * states, full, dtype=LOW),
            shape(2 * states, full, dtype=LOW),
            shape(2 * full, full, dtype=LOW),
            shape(dp_size, 8, width),
        ),
        [
            pltpu.VMEM((8, full), F32),
            pltpu.VMEM((total, full), F32),
            pltpu.VMEM((total, 2 * states), F32),
            pltpu.VMEM((total, 2 * full), F32),
            pltpu.VMEM((2 * states, full), LOW),
            pltpu.VMEM((2 * states, full), LOW),
            pltpu.VMEM((2 * full, full), LOW),
            pltpu.VMEM((total, 2 * states), LOW),
        ],
        (lengths, sums, *parts[0], tokens, *parts[1]),
        "start",
        pieces={6: piece} | {place: width for place in (7, 8, 9, 10)},
        order=(4, 5),
        bare=(11, 12, 13),
        flops=1e9,
    )
    sums1 = across(sums1, "dp")
    later_far, sums1 = lax.optimization_barrier((later_far, sums1))
    result, base, bn1, norm1, *halves1 = call(
        middle_kernel,
        (
            shape(width, total),
            shape(total, full),
            shape(dp_size, 16, width),
            shape(8, full),
            shape(2 * width, full, dtype=LOW),
            shape(2 * width, full, dtype=LOW),
        ),
        [
            pltpu.VMEM((8, full), F32),
            pltpu.VMEM((2 * states, full), LOW),
            pltpu.VMEM((2 * states, full), LOW),
            pltpu.VMEM((2 * full, full), LOW),
            pltpu.VMEM((total, full), LOW),
            pltpu.VMEM((total, 2 * states), F32),
            pltpu.VMEM((total, 256), F32),
            pltpu.VMEM((total, 2 * states), LOW),
            pltpu.VMEM((total, full), F32),
            pltpu.VMEM((total, full), LOW),
            pltpu.VMEM((total, 2 * full), F32),
            pltpu.VMEM((total, width), F32),
            pltpu.VMEM((total, full), F32),
            pltpu.VMEM((total, 2 * full), LOW),
            pltpu.VMEM((total, full), LOW),
            pltpu.VMEM((total, 2 * states), LOW),
            pltpu.VMEM((4 * width, full), LOW),
        ],
        (lengths, sums1, norm0, feature, state, stream1, up_own, later, swap(later, 1, sharers), later_far,
         swap(later_far, 1, sharers)),
        "middle",
        pieces={5: piece},
        late=(6, 7, 8, 9, 10),
        bare=(4, 5),
        flops=1e9,
    )
    bn1 = across(bn1, "dp")
    halves1[1] = exchange(halves1[1], 1)
    halves1 = list(add(halves1, 0))
    bn1, *halves1 = lax.optimization_barrier((bn1, *halves1))
    halves1[1] = exchange(halves1[1], 2)
    kept0, sent0, up0, grad0 = call(
        last_kernel,
        (
            shape(2 * width + 16, full, dtype=LOW),
            shape(2 * width + 16, full, dtype=LOW),
            shape(total, width),
            shape(total, width),
        ),
        [
            pltpu.VMEM((total, full), F32),
            pltpu.VMEM((total, 2 * states), F32),
            pltpu.VMEM((total, 2 * full), LOW),
            pltpu.VMEM((total, full), LOW),
            pltpu.VMEM((total, 2 * states), LOW),
            pltpu.VMEM((8, full), F32),
            pltpu.VMEM((16, full), F32),
            pltpu.VMEM((4 * width, full), LOW),
            pltpu.VMEM((16, full), F32),
            pltpu.VMEM((16, full), LOW),
        ],
        (lengths, bn1, norm1, feature, state, norm0, stream1, base, gate0, linear0, w_all, slope0, normed0, active0, c_all, low0,
         drive0, b_all, tokens),
        "last",
        bare=(0, 1),
        pieces={6: piece, 7: piece, 8: piece, 9: piece},
        late=tuple(range(10, 19)),
        flops=1e11,
    )
    sent0 = exchange(sent0, 1)
    *halves1, kept0 = lax.optimization_barrier((*halves1, kept0))
    for stage in range(1, stages):
        if stage > 1:
            halves1[1] = exchange(halves1[1], 1 << stage)
        if stage < stages - 1:
            halves1 = list(add(halves1, stage))
    blocks = call(
        pair_kernel,
        (shape(share + 16, full, dtype=LOW),) * (dp_size // 2),
        [pltpu.VMEM((2 * width, full), LOW), pltpu.VMEM((16, full), LOW)],
        (lengths, kept0, sent0),
        "pair",
        bare=tuple(range(dp_size // 2)),
    )
    blocks = [blocks[0]] + [exchange(blocks[place], 2 * place) for place in range(1, dp_size // 2)]
    halves1[1], *blocks = lax.optimization_barrier((halves1[1], *blocks))
    back, small0 = call(
        share_kernel,
        (shape(2 * share, full, dtype=LOW), shape(8, full)),
        [],
        (lengths, *blocks, *halves1),
        "share",
    )
    backs = {0: back, 1: exchange(back, 1)}
    for place in range(2, dp_size, 2):
        backs[place] = exchange(back, place)
        backs[place + 1] = exchange(backs[place], 1)
    grad_nu, grad_theta, grad_gamma, grad_skip, grad_bias, grad_gain, grad_shift, grad_inputs = call(
        finish_kernel,
        (
            shape(LAYERS, own_states),
            shape(LAYERS, own_states),
            shape(LAYERS, own_states),
            shape(LAYERS, width),
            shape(LAYERS, 2, width),
            shape(LAYERS, width),
            shape(LAYERS, width),
            shape(width, total),
        ),
        [pltpu.VMEM((32, full), F32), pltpu.VMEM((total, width), F32)],
        (lengths, small0, bn1, norm0, feature, nu_log, theta_log, up0, grad0, tokens),
        "finish",
    )
    grad_b, grad_c, grad_glu = call(
        widen_kernel,
        (shape(LAYERS, width, full), shape(LAYERS, width, full), shape(LAYERS, 2 * width, full)),
        [pltpu.VMEM((LAYERS, 4 * width, full), F32)],
        (lengths, *(backs[place] for place in range(dp_size))),
        "widen",
        bare=(0, 1, 2),
    )
    grad_b = grad_b.reshape(LAYERS, 2, own_states, full)
    grad_c = grad_c.reshape(LAYERS, 2, own_states, full)
    grad_glu = grad_glu.reshape(LAYERS, 2, width, full)
    return (
        own(result[None], 1),
        own(grad_inputs[None], 1),
        own(grad_gain, 1),
        own(grad_shift, 1),
        own(grad_b, 2),
        own(grad_c, 2),
        own(grad_nu, 1),
        own(grad_theta, 1),
        own(grad_gamma, 1),
        own(grad_skip, 1),
        own(grad_glu, 2),
        own(grad_bias, 2),
    )


def solution(mesh):
    in_specs = (
        P("dp", "state", None),
        P("dp"),
        P("dp", "state", None),
        P(None, "state"),
        P(None, "state"),
        P(None, None, "state", None),
        P(None, None, "state", None),
        P(None, "state"),
        P(None, "state"),
        P(None, "state"),
        P(None, "state"),
        P(None, None, "state", None),
        P(None, None, "state"),
    )
    out_specs = (
        P("dp", "state", None),
        P("dp", "state", None),
        P(None, "state"),
        P(None, "state"),
        P(None, None, "state", None),
        P(None, None, "state", None),
        P(None, "state"),
        P(None, "state"),
        P(None, "state"),
        P(None, "state"),
        P(None, None, "state", None),
        P(None, None, "state"),
    )
    step = functools.partial(local, dp_size=mesh.shape["dp"], state_size=mesh.shape["state"])
    return jax.shard_map(step, mesh=mesh, in_specs=in_specs, out_specs=out_specs, check_vma=False)
```

```python
import functools

import jax
import jax.numpy as jnp
from jax import lax
from jax.experimental import pallas as pl
from jax.experimental.pallas import tpu as pltpu
from jax.sharding import PartitionSpec as P

LAYERS = 2
CHUNKS = 16
PIECES = 4
EPSILON = 1e-05
F32 = jnp.float32
LOW = jnp.bfloat16
PARAM_ROWS = 32
OWN_MEAN = 16
VMEM_BYTES = 64 * 1024 * 1024

GAIN, SHIFT, SKIP, BIAS_LINEAR, BIAS_GATE = range(5)
RATE_RE, RATE_IM, GAMMA = range(3)

NN = (((1,), (0,)), ((), ()))
NT = (((1,), (1,)), ((), ()))
TN = (((0,), (0,)), ((), ()))


def dot(left, right, dims):
    return lax.dot_general(left, right, dims, preferred_element_type=F32)


def rows_at(index, size):
    return pl.ds(pl.multiple_of(index * size, size), size)


def lanes_at(quarter, width):
    return pl.ds(pl.multiple_of(quarter * width, width), width)


def for_rows(first, last, size, body, init=0, unroll=2):
    def step(index, carry):
        return body(rows_at(index, size), index, carry)

    return lax.fori_loop(first // size, last // size, step, init, unroll=unroll)


def blocks_of(first, last, size=16):
    return [(slice(at, at + size), at // size) for at in range(first, last, size)]


def pieces_of(total):
    size = total // PIECES
    return [slice(at, at + size) for at in range(0, total, size)]


def own_quarter():
    return (lax.axis_index("state") // (lax.axis_size("state") // 4)).astype(jnp.int32)


def keep_rows(first_step, rows, steps, length):
    row = lax.broadcasted_iota(jnp.int32, (rows, 1), 0)
    position = (row % CHUNKS) * steps + row // CHUNKS + first_step
    return position < length


def gelu_parts(value):
    return 0.5 + 0.5 * lax.erf(value * 0.7071067811865476), jnp.exp(value * value * -0.5) * 0.3989422804014327


def squared(re, im, times):
    for _ in range(times):
        re, im = re * re - im * im, 2.0 * re * im
    return re, im


def folded(value):
    return value[0:8, :] + value[8:16, :]


def column_sum(value):
    return jnp.sum(value, axis=0, keepdims=True)


def chunk_starts(re, im, rate_re, rate_im, reverse):
    row = lax.broadcasted_iota(jnp.int32, re.shape, 0)

    def moved(value, by):
        if reverse:
            return jnp.where(row < CHUNKS - by, pltpu.roll(value, CHUNKS - by, 0), 0.0)
        return jnp.where(row >= by, pltpu.roll(value, by, 0), 0.0)

    by = 1
    while by < CHUNKS:
        past_re, past_im = moved(re, by), moved(im, by)
        re, im = (
            re + rate_re * past_re - rate_im * past_im,
            im + rate_re * past_im + rate_im * past_re,
        )
        rate_re, rate_im = squared(rate_re, rate_im, 1)
        by *= 2
    return moved(re, 1), moved(im, 1)


def sweep(drive_ref, rate_re, rate_im, steps, reverse, emit, extra, after=None, beside=None, unroll=4):
    states = rate_re.shape[1]
    shape = (CHUNKS, states)
    wide_re = jnp.broadcast_to(rate_re, shape)
    wide_im = jnp.broadcast_to(rate_im, shape)

    def advance(index, re, im):
        place = steps - 1 - index if reverse else index
        rows = slice(place * CHUNKS, (place + 1) * CHUNKS) if isinstance(place, int) else rows_at(place, CHUNKS)
        drive_re = drive_ref[rows, :states]
        drive_im = drive_ref[rows, states:]
        new_re = (wide_re * re + drive_re) - wide_im * im
        new_im = (wide_re * im + drive_im) + wide_im * re
        return rows, place, new_re, new_im, drive_re, drive_im

    def first(index, carry):
        _, _, re, im, _, _ = advance(index, *carry)
        return re, im

    def second(index, carry):
        re, im, held = carry
        rows, place, re, im, drive_re, drive_im = advance(index, re, im)
        return re, im, emit(rows, place, re, im, drive_re, drive_im, held)

    zero = jnp.zeros(shape, F32)
    re, im = lax.fori_loop(0, steps, first, (zero, zero), unroll=unroll)
    far_re, far_im = rate_re, rate_im
    power = 1
    while power < steps:
        far_re, far_im = squared(far_re, far_im, 1)
        power *= 2
    re, im = chunk_starts(re, im, far_re, far_im, reverse)
    carry = (re, im, extra)
    for piece in range(PIECES):
        size = steps // PIECES
        if beside is not None:
            beside[piece]()
            for index in range(piece * size, (piece + 1) * size):
                carry = second(index, carry)
        else:
            carry = lax.fori_loop(piece * size, (piece + 1) * size, second, carry, unroll=unroll)
        if after is not None:
            after(PIECES - 1 - piece if reverse else piece)
    return carry[2]


class Arrival:
    def __init__(self, source, ref, done, first, size, axis):
        self.ref = ref
        self.copies = []
        whole = ref.shape[axis]
        for piece, start in enumerate(range(0, whole, size)):
            where = (slice(None),) * axis + (pl.ds(start, min(size, whole - start)),)
            self.copies.append(
                pltpu.make_async_copy(source.at[where], ref.at[where], done.at[first + piece])
                if size < whole
                else pltpu.make_async_copy(source, ref, done.at[first])
            )
        self.short = whole % size > 0
        self.waited = set()

    def start(self, piece):
        last = len(self.copies) - self.short
        if piece < 0 and self.short:
            self.copies[-1].start()
        if 0 <= piece < last:
            self.copies[piece].start()

    def wait(self, piece=None):
        for place in range(len(self.copies)) if piece is None else (piece,):
            if place not in self.waited:
                self.copies[place].wait()
                self.waited.add(place)
        return self.ref


class Departure:
    def __init__(self, target, ref, done, first):
        self.target, self.ref, self.done, self.first = target, ref, done, first
        self.copies = []

    def send(self, start=None, size=None, source=None):
        place = self.done.at[self.first + len(self.copies)]
        where = self.target if start is None else self.target.at[pl.ds(start, size)]
        if source is None:
            source = self.ref if start is None else self.ref.at[pl.ds(start, size)]
        self.copies.append(pltpu.make_async_copy(source, where, place))
        self.copies[-1].start()

    def send_piece(self, piece):
        size = self.target.shape[0] // PIECES
        self.send(piece * size, size)

    def send_unsent(self):
        if not self.copies:
            self.send()

    def finish(self):
        for copy in self.copies:
            copy.wait()


def call(kernel, outs, scratch, args, name, pieces=None, axes=None, bare=(), late=(), order=None, flops=0):
    pieces, axes = pieces or {}, axes or {}
    along = [axes.get(place, 0) for place in range(1, len(args))]
    sizes = [pieces.get(place, args[place].shape[axis]) for place, axis in enumerate(along, 1)]
    counts = [-(-args[place].shape[axis] // size) for place, (axis, size) in enumerate(zip(along, sizes), 1)]
    slots = 6
    copies_in = [pltpu.VMEM(a.shape, a.dtype) for a in args[1:]]
    copies_out = [pltpu.VMEM((8, 128) if place in bare else o.shape, o.dtype if place not in bare else F32) for place, o in enumerate(outs)]

    def body(*refs):
        refs = list(refs)

        def take(count):
            got = refs[:count]
            del refs[:count]
            return got

        (length_ref,) = take(1)
        sources = take(len(args) - 1)
        targets = take(len(outs))
        in_refs, out_refs = take(len(args) - 1), take(len(outs))
        arrived, sent = take(2)
        arrivals, first = [], 0
        for source, ref, size, count, axis in zip(sources, in_refs, sizes, counts, along):
            arrivals.append(Arrival(source, ref, arrived, first, size, axis))
            first += count
        for group in (False, True):
            for piece in (-1, *(order or ()), *(piece for piece in range(max(counts)) if piece not in (order or ()))):
                for place, arrival in enumerate(arrivals, 1):
                    if (place in late) is group:
                        arrival.start(piece)
        departures = [
            Departure(target, ref, sent, place * slots) for place, (target, ref) in enumerate(zip(targets, out_refs))
        ]
        kernel(length_ref, arrivals, departures, *refs)
        for arrival in arrivals:
            arrival.wait()
        for departure in departures:
            departure.send_unsent()
        for departure in departures:
            departure.finish()

    return pl.pallas_call(
        body,
        out_shape=tuple(outs),
        in_specs=[pl.BlockSpec(memory_space=pltpu.SMEM if place == 0 else pl.ANY) for place in range(len(args))],
        out_specs=tuple(pl.BlockSpec(memory_space=pl.ANY) for _ in outs),
        scratch_shapes=[
            *copies_in,
            *copies_out,
            pltpu.SemaphoreType.DMA((sum(counts),)),
            pltpu.SemaphoreType.DMA((slots * len(outs),)),
            *scratch,
        ],
        compiler_params=pltpu.CompilerParams(vmem_limit_bytes=VMEM_BYTES),
        cost_estimate=pl.CostEstimate(flops=int(flops), bytes_accessed=0, transcendentals=0),
        name=name,
    )(*args)


def from_feature_rows(source, held_ref, steps, emit, init, after):
    length = source.ref.shape[1]
    blocks = length // 128
    for block in range(blocks):
        if block % (blocks // PIECES) == 0:
            source.wait(block // (blocks // PIECES))
        lanes = slice(block * 128, (block + 1) * 128)
        held_ref[lanes, :] = source.ref[:, lanes].T

    def step(index, carry):
        return emit(rows_at(index, CHUNKS), index, held_ref[pl.ds(index, CHUNKS, stride=steps), :], carry)

    carry = init
    for piece in range(PIECES):
        size = steps // PIECES
        carry = lax.fori_loop(piece * size, (piece + 1) * size, step, carry, unroll=4)
        after(piece)
    return carry


def to_feature_rows(load, held_ref, out, steps):
    length = out.ref.shape[1]

    def step(index, carry):
        held_ref[pl.ds(index, CHUNKS, stride=steps), :] = load(rows_at(index, CHUNKS), index)
        return carry

    lax.fori_loop(0, steps, step, 0, unroll=4)
    for block in range(length // 128):
        lanes = slice(block * 128, (block + 1) * 128)
        out.ref[:, lanes] = held_ref[lanes, :].T
    out.send()


def spread_rows(value, out):
    for group in range(out.ref.shape[0]):
        out.ref[group, :, :] = value
    out.send()


def narrowed(values, width):
    return jnp.concatenate([v[:, at : at + width] for v in values for at in range(0, v.shape[1], width)], axis=0)


def widened(rows, first, count):
    return jnp.concatenate([rows[first + place : first + place + 1, :] for place in range(count)], axis=1)


def total_rows(sums_ref):
    value = sums_ref[0, :, :]
    for other in range(1, sums_ref.shape[0]):
        value += sums_ref[other, :, :]
    return value


def assemble_states(parts, whole_ref):
    half = parts[0].shape[0] // 2
    states = half * len(parts)
    for place, part in enumerate(parts):
        whole_ref[place * half : (place + 1) * half, :] = part[:half, :]
        whole_ref[states + place * half : states + (place + 1) * half, :] = part[half:, :]


def assemble_output(parts, whole_ref):
    half = parts[0].shape[0] // 2
    states = half * len(parts)
    for place, part in enumerate(parts):
        whole_ref[place * half : (place + 1) * half, :] = part[:half, :]
        whole_ref[states + place * half : states + (place + 1) * half, :] = -part[half:, :]


def assemble_glu(parts, whole_ref, quarter):
    half = parts[0].shape[0] // 2
    width = half * len(parts)
    for place, part in enumerate(parts):
        whole_ref[lanes_at(quarter ^ place, half), :] = part[:half, :]
        whole_ref[pl.ds(pl.multiple_of(width + (quarter ^ place) * half, half), half), :] = part[half:, :]


def norm_rows(sums, counted):
    centre = sums[0:1, :] / counted
    meansq = sums[1:2, :] / counted
    return centre, lax.rsqrt(meansq - centre * centre + EPSILON)


def drive_phase(normed_ref, b_ref, drive_ref, gamma):
    drive_ref[...] = dot(normed_ref[...], b_ref[...], NT) * jnp.concatenate([gamma, gamma], axis=1)


def store_states(low_ref, drive_own_ref):
    def emit(rows, step, re, im, drive_re, drive_im, held):
        states = re.shape[1]
        low_ref[rows, :states] = re.astype(LOW)
        low_ref[rows, states:] = im.astype(LOW)
        drive_own_ref[rows, :128] = drive_re[:, :128].astype(drive_own_ref.dtype)
        drive_own_ref[rows, 128:] = drive_im[:, :128].astype(drive_own_ref.dtype)
        return held

    return emit


def pre_products(low_ref, c_ref, held_ref):
    total, full = low_ref.shape[0], c_ref.shape[1]
    for piece in pieces_of(total):
        held_ref[piece, :full] = dot(low_ref[piece, :], c_ref[...], NN)


def pre_piece(piece, held_ref, normed_ref, skip, active_ref, slope_ref):
    full = normed_ref.shape[1]
    for rows, _ in blocks_of(piece.start, piece.stop):
        value = held_ref[rows, :full] + skip * normed_ref[rows, :].astype(F32)
        cdf, density = gelu_parts(value)
        active_ref[rows, :] = (value * cdf).astype(LOW)
        slope_ref[rows, :] = (cdf + value * density).astype(slope_ref.dtype)


def pre_grad_piece(piece, held_ref, slope_ref, pre_grad_ref):
    full = slope_ref.shape[1]
    for rows, _ in blocks_of(piece.start, piece.stop):
        pre_grad_ref[rows, :] = (held_ref[rows, :full] * slope_ref[rows, :].astype(F32)).astype(LOW)


def skip_sums(pre_grad_ref, normed_ref, quarter, small_ref):
    own = lanes_at(quarter, 128)

    def inner(rows, index, carry):
        return carry + folded(pre_grad_ref[rows, own].astype(F32) * normed_ref[rows, own].astype(F32))

    small_ref[3:4, 0:128] = column_sum(for_rows(0, pre_grad_ref.shape[0], 16, inner, jnp.zeros((8, 128), F32), unroll=4))


def bias_sums(grad_gated_ref, quarter, small_ref):
    own, far = lanes_at(quarter, 128), lanes_at(quarter + 4, 128)

    def inner(rows, index, carry):
        return (
            carry[0] + folded(grad_gated_ref[rows, own].astype(F32)),
            carry[1] + folded(grad_gated_ref[rows, far].astype(F32)),
        )

    zero = jnp.zeros((8, 128), F32)
    one, two = for_rows(0, grad_gated_ref.shape[0], 16, inner, (zero, zero), unroll=4)
    small_ref[4:5, 0:128] = column_sum(one)
    small_ref[5:6, 0:128] = column_sum(two)


def adjoint_phase(low_ref, im_lane, drive_own_ref, state, first_row, length, grad_state_ref, grad_driven_ref, small_ref, reverse, beside):
    total = grad_state_ref.shape[0]
    steps = total // CHUNKS
    states = state.shape[1]
    rate_re = state[first_row : first_row + 1, :]
    rate_im = state[first_row + 1 : first_row + 2, :]
    gamma = jnp.broadcast_to(state[first_row + 2 : first_row + 3, :], (CHUNKS, states))

    def emit(rows, step, re, im, drive_re, drive_im, held):
        out_re, out_im = gamma * re, gamma * im
        if not reverse:
            keep = keep_rows(step, CHUNKS, steps, length)
            out_re, out_im = jnp.where(keep, out_re, 0.0), jnp.where(keep, out_im, 0.0)
        grad_driven_ref[rows, :states] = out_re.astype(LOW)
        grad_driven_ref[rows, states:] = out_im.astype(LOW)
        one, two, three = held
        own_re, own_im = re[:, :128], im[:, :128]
        late_re, late_im = own_re - drive_re[:, :128], own_im - drive_im[:, :128]
        low_re = low_ref[rows, :128].astype(F32)
        low_im = low_ref[rows, im_lane : im_lane + 128].astype(F32)
        one = one + folded(late_re * low_re + late_im * low_im)
        two = two + folded(late_im * low_re - late_re * low_im)
        three = three + folded(
            own_re * drive_own_ref[rows, :128].astype(F32) + own_im * drive_own_ref[rows, 128:].astype(F32)
        )
        return one, two, three

    zero = jnp.zeros((8, 128), F32)
    one, two, three = sweep(grad_state_ref, rate_re, -rate_im, steps, reverse, emit, (zero, zero, zero), beside=beside)
    small_ref[0:1, 0:128] = column_sum(one)
    small_ref[1:2, 0:128] = column_sum(two)
    small_ref[2:3, 0:128] = column_sum(three)


def glu_products(grads_ref, first, grad_gated_ref, active_ref, quarter):
    full = active_ref.shape[1]

    def product(place):
        lanes = pl.ds(pl.multiple_of(place * full + quarter * 128, 128), 128)
        got = dot(grad_gated_ref[:, lanes], active_ref[...], TN)
        grads_ref[first + place * 128 : first + (place + 1) * 128, :] = got.astype(LOW)

    return [functools.partial(product, place) for place in range(2)]


def output_products(grads_ref, low_re, low_im, pre_grad_ref, states):
    half = states // 4

    def product(place, low, sign):
        got = sign * dot(low(), pre_grad_ref[...], TN)[:half, :]
        grads_ref[2 * half + place * half : 2 * half + (place + 1) * half, :] = got.astype(LOW)

    return [functools.partial(product, 0, low_re, 1.0), functools.partial(product, 1, low_im, -1.0)]


def input_products(grads_ref, grad_driven_ref, normed_ref, states):
    half = states // 4
    for place in range(2):
        lanes = slice(place * states, place * states + 128)
        got = dot(grad_driven_ref[:, lanes], normed_ref[...], TN)[:half, :]
        grads_ref[place * half : (place + 1) * half, :] = got.astype(LOW)


def enter_kernel(length_ref, ins, outs, held_ref, params_ref):
    x, gain, shift, skip, bias, nu, theta, gamma, b, c, w = ins
    tokens, spread, first_out = outs
    length = length_ref[0]
    width, total = x.ref.shape
    steps = total // CHUNKS

    def emit(rows, index, value, carry):
        tokens.ref[rows, :] = value
        kept = jnp.where(keep_rows(index, CHUNKS, steps, length), value, 0.0)
        return carry[0] + folded(kept), carry[1] + folded(kept * kept)

    zero = jnp.zeros((8, width), F32)
    plain, square = from_feature_rows(x, held_ref, steps, emit, (zero, zero), tokens.send_piece)
    plain = column_sum(plain)
    counted = jnp.full((1, width), length, jnp.int32).astype(F32)
    spread_rows(jnp.concatenate([plain, column_sum(square), counted, jnp.zeros((5, width), F32)], axis=0), spread)
    mean = plain / counted

    each = total // PIECES

    def centred(rows, index, carry):
        place = pl.ds(pl.multiple_of(4 * width + index * 32 % each, 32), 32)
        first_out.ref[place, lanes_at(index * 32 // each, width)] = (tokens.ref[rows, :] - mean).astype(LOW)
        return carry

    for_rows(0, total, 32, centred, unroll=4)
    for value in (gain, shift, skip, bias, nu, theta, gamma):
        value.wait()
    params_ref[...] = jnp.zeros(params_ref.shape, F32)
    for layer in range(LAYERS):
        first = 5 * layer
        params_ref[first + GAIN : first + GAIN + 1, :] = gain.ref[layer : layer + 1, :]
        params_ref[first + SHIFT : first + SHIFT + 1, :] = shift.ref[layer : layer + 1, :]
        params_ref[first + SKIP : first + SKIP + 1, :] = skip.ref[layer : layer + 1, :]
        params_ref[first + BIAS_LINEAR : first + BIAS_GATE + 1, :] = bias.ref[layer, :, :]
        first = 10 + 3 * layer
        for row, source in enumerate((nu, theta, gamma)):
            params_ref[first + row : first + row + 1, : source.ref.shape[1]] = source.ref[layer : layer + 1, :]
    params_ref[OWN_MEAN : OWN_MEAN + 1, :] = mean
    rest = params_ref[...]
    first_out.ref[6 * width :, :] = jnp.zeros((32, 4 * width), LOW)
    for place in range(3):
        high = rest.astype(LOW)
        first_out.ref[6 * width : 6 * width + PARAM_ROWS, place * width : (place + 1) * width] = high
        rest = rest - high.astype(F32)
    first_out.send(4 * width, 2 * width + 32)
    send_weights(0, b, c, w, first_out)


def send_weights(layer, b, c, w, whole):
    width = b.ref.shape[1]
    for value, first, size in ((b, 0, width), (c, width, width), (w, 2 * width, 2 * width)):
        value.wait()
        whole.send(first, size, source=value.ref.at[layer])


def cotangent_kernel(length_ref, ins, outs, held_ref):
    x, b, c, w = ins
    whole, later = outs
    width, total = x.ref.shape
    steps = total // CHUNKS
    each = steps // PIECES

    def emit(rows, index, value, carry):
        whole.ref[rows, :] = value
        place = pl.ds(pl.multiple_of(4 * width + index % each * CHUNKS, CHUNKS), CHUNKS)
        later.ref[place, lanes_at(index // each, width)] = value.astype(LOW)
        return carry

    def after(piece):
        whole.send_piece(piece)
        if piece == 1:
            send_weights(1, b, c, w, later)

    from_feature_rows(x, held_ref, steps, emit, 0, after)
    later.send(4 * width, total // PIECES)


def start_kernel(length_ref, ins, outs, stats_ref, stream_ref, drive_ref, pre_ref, held_ref, b_ref, c_ref, w_ref, low_ref):
    sums, tokens, *parts = ins
    feature, state_out, norm, normed, drive_own, low_own, stream, linear_out, gate_out, slope, active, b_out, c_out, w_out, spread = outs
    length, quarter = length_ref[0], own_quarter()
    total, full = active.ref.shape
    steps = total // CHUNKS
    width = full // 4
    lane = lax.broadcasted_iota(jnp.int32, (8, width), 1)
    tails = []
    rows_refs = []
    for part in parts:
        for piece in (6, 4, 5):
            part.wait(piece)
        rows_refs.append(part.ref.at[pl.ds(4 * width, 2 * width + PARAM_ROWS)])
    for place, part_ref in enumerate(rows_refs):
        value = sum(part_ref[2 * width :, at * width : (at + 1) * width].astype(F32) for at in range(3))
        feature.ref[:, lanes_at(quarter ^ place, width)] = value
        tails.append(value[8:16, :])
    for pair in range(2):
        early, late = tails[2 * pair : 2 * pair + 2]
        logs = jnp.where(lane < 64, early, pltpu.roll(late, 64, 1))
        lanes = slice(pair * width, (pair + 1) * width)
        for layer in range(LAYERS):
            first = 2 + 3 * layer
            modulus = jnp.exp(-jnp.exp(logs[first : first + 1, :]))
            angle = jnp.exp(logs[first + 1 : first + 2, :])
            state_out.ref[first : first + 1, lanes] = modulus * jnp.cos(angle)
            state_out.ref[first + 1 : first + 2, lanes] = modulus * jnp.sin(angle)
            state_out.ref[first + 2 : first + 3, lanes] = jnp.exp(logs[first + 2 : first + 3, :])
    sums_ref = sums.wait()
    for place in range(4):
        value = sums_ref[place, :, :]
        for other in range(1, sums_ref.shape[0] // 4):
            value += sums_ref[other * 4 + place, :, :]
        stats_ref[:, place * width : (place + 1) * width] = value
    centre, inv_dev = norm_rows(stats_ref[0:2, :], stats_ref[2:3, :])
    norm.ref[...] = jnp.zeros_like(norm.ref)
    norm.ref[0:1, :] = centre
    norm.ref[1:2, :] = inv_dev
    norm.ref[2:3, :] = stats_ref[2:3, :]
    for out in (feature, state_out, norm):
        out.send()

    each = total // PIECES

    def normal(rows, index, carry):
        keep = keep_rows(index, 16, steps, length)
        there = pl.ds(pl.multiple_of(index * 16 % each, 16), 16)
        for place, part_ref in enumerate(rows_refs):
            lanes = lanes_at(quarter ^ place, width)
            if place == 0:
                value = tokens.ref[rows, :]
            else:
                value = part_ref[there, lanes_at(index * 16 // each, width)].astype(F32)
                value = value + feature.ref[OWN_MEAN : OWN_MEAN + 1, lanes]
            stream_ref[rows, lanes] = value
            z = (value - norm.ref[0:1, lanes]) * norm.ref[1:2, lanes]
            z = z * feature.ref[GAIN : GAIN + 1, lanes] + feature.ref[SHIFT : SHIFT + 1, lanes]
            normed.ref[rows, lanes] = jnp.where(keep, z, 0.0).astype(LOW)
        return carry

    for piece in range(PIECES):
        tokens.wait(piece)
        for_rows(piece * total // PIECES, (piece + 1) * total // PIECES, 16, normal)
        normed.send_piece(piece)
    assemble_states([part.wait(0).at[0:width] for part in parts], b_ref)
    b_out.send(source=b_ref)
    state = state_out.ref[...]
    states = state.shape[1]
    drive_phase(normed.ref, b_ref, drive_ref, state[2 + GAMMA : 3 + GAMMA, :])
    assemble_output([part.wait(1).at[width : 2 * width] for part in parts], c_ref)
    c_out.send(source=c_ref)
    store = store_states(low_ref, drive_own.ref)

    def emit(rows, step, re, im, drive_re, drive_im, held):
        low_own.ref[rows, :128] = re[:, :128].astype(LOW)
        low_own.ref[rows, 128:] = im[:, :128].astype(LOW)
        return store(rows, step, re, im, drive_re, drive_im, held)

    sweep(drive_ref, state[2:3, :], state[3:4, :], steps, False, emit, 0)
    drive_own.send()
    low_own.send()

    assemble_glu([part.wait().at[2 * width : 4 * width] for part in parts], w_ref, quarter)
    w_out.send(source=w_ref)
    skip = feature.ref[SKIP : SKIP + 1, :]
    bias_linear = feature.ref[BIAS_LINEAR : BIAS_LINEAR + 1, :]
    bias_gate = feature.ref[BIAS_GATE : BIAS_GATE + 1, :]
    pre_products(low_ref, c_ref, pre_ref)
    for piece in pieces_of(total):
        pre_piece(piece, pre_ref, normed.ref, skip, active.ref, slope.ref)
        held_ref[piece, :] = dot(active.ref[piece, :], w_ref[...], NT)
    active.send()
    slope.send()
    plain, square = jnp.zeros((8, full), F32), jnp.zeros((8, full), F32)
    for place, piece in enumerate(pieces_of(total)):
        for rows, index in blocks_of(piece.start, piece.stop):
            keep = keep_rows(index, 16, steps, length)
            linear = held_ref[rows, :full] + bias_linear
            gate = jax.nn.sigmoid(held_ref[rows, full:] + bias_gate)
            mixed = linear * gate
            gate_out.ref[rows, :] = gate.astype(LOW)
            linear_out.ref[rows, :] = (mixed * (1.0 - gate)).astype(LOW)
            moved = stream_ref[rows, :] + jnp.where(keep, mixed, 0.0)
            stream.ref[rows, :] = moved
            kept = jnp.where(keep, moved, 0.0)
            plain += folded(kept)
            square += folded(kept * kept)
        for out in (stream, linear_out, gate_out):
            out.send_piece(place)
    carry = plain, square
    spread_rows(narrowed([column_sum(carry[0]), column_sum(carry[1])], width), spread)


def middle_kernel(
    length_ref, ins, outs,
    small_ref, b_ref, c_ref, w_ref, normed_ref, drive_ref, drive_own_ref, low_ref, slope_ref, active_ref, held_ref, pre_ref, mixed_ref,
    order_ref, up_ref, grad_gated_ref, pre_grad_ref, grad_driven_ref, grads_ref,
):
    sums, norm0, feature_in, state_in, stream, up_own = ins[:6]
    parts = ins[6:]
    result, base, spread, norm, *shares = outs
    length, quarter = length_ref[0], own_quarter()
    total, full = stream.ref.shape
    steps = total // CHUNKS
    width = 128
    counted = norm0.wait()[2:3, :]
    feature = feature_in.wait()
    state = state_in.wait()[...]
    states = state.shape[1]
    whole = total_rows(sums.wait())
    whole = jnp.concatenate([widened(whole, 0, 4), widened(whole, 4, 4)], axis=0)
    centre, inv_dev = norm_rows(whole, counted)
    norm.ref[...] = jnp.zeros_like(norm.ref)
    norm.ref[0:1, :] = centre
    norm.ref[1:2, :] = inv_dev
    norm.ref[2:3, :] = counted
    norm.send()
    gain = feature[5 + GAIN : 6 + GAIN, :]
    shift = feature[5 + SHIFT : 6 + SHIFT, :]
    skip = feature[5 + SKIP : 6 + SKIP, :]

    for part in parts:
        part.wait(0)
    assemble_states([part.ref.at[0:width] for part in parts], b_ref)
    gamma = state[5 + GAMMA : 6 + GAMMA, :]
    gammas = jnp.concatenate([gamma, gamma], axis=1)
    for place, piece in enumerate(pieces_of(total)):
        stream.wait(place)
        for rows, index in blocks_of(piece.start, piece.stop):
            z = (stream.ref[rows, :] - centre) * inv_dev
            normed_ref[rows, :] = jnp.where(keep_rows(index, 16, steps, length), z * gain + shift, 0.0).astype(LOW)
        drive_ref[piece, :] = dot(normed_ref[piece, :], b_ref[...], NT) * gammas
    sweep(drive_ref, state[5:6, :], state[6:7, :], steps, True, store_states(low_ref, drive_own_ref), 0)
    for part in parts:
        part.wait()
    assemble_output([part.ref.at[width : 2 * width] for part in parts], c_ref)
    assemble_glu([part.ref.at[2 * width : 4 * width] for part in parts], w_ref, quarter)
    up_own.wait()
    own = lanes_at(quarter, width)

    def spread_up(rows, index, carry):
        up_ref[rows, own] = up_own.ref[rows, :]
        return carry

    for_rows(0, total, 16, spread_up, unroll=4)
    for place, piece in enumerate(pieces_of(total)):
        for other in range(1, 4):
            lanes = lanes_at(quarter ^ other, width)
            up_ref[piece, lanes] = parts[other].ref[4 * width :, place * width : (place + 1) * width].astype(F32)
    bias_linear = feature[5 + BIAS_LINEAR : 6 + BIAS_LINEAR, :]
    bias_gate = feature[5 + BIAS_GATE : 6 + BIAS_GATE, :]
    pre_products(low_ref, c_ref, pre_ref)
    for piece in pieces_of(total):
        pre_piece(piece, pre_ref, normed_ref, skip, active_ref, slope_ref)
        held_ref[piece, :] = dot(active_ref[piece, :], w_ref[...], NT)
    for piece in pieces_of(total):
        for rows, index in blocks_of(piece.start, piece.stop):
            keep = keep_rows(index, 16, steps, length)
            linear = held_ref[rows, :full] + bias_linear
            gate = jax.nn.sigmoid(held_ref[rows, full:] + bias_gate)
            mixed = linear * gate
            up = jnp.where(keep, up_ref[rows, :], 0.0)
            grad_gated_ref[rows, :full] = (up * gate).astype(LOW)
            grad_gated_ref[rows, full:] = (up * mixed * (1.0 - gate)).astype(LOW)
            mixed_ref[rows, :] = jnp.where(keep, mixed, 0.0)
        pre_ref[piece, :] = dot(grad_gated_ref[piece, :], w_ref[...], NN)
    for piece in pieces_of(total):
        pre_grad_piece(piece, pre_ref, slope_ref, pre_grad_ref)
        drive_ref[piece, :] = dot(pre_grad_ref[piece, :], c_ref[...], NT)
    small_ref[...] = jnp.zeros_like(small_ref)
    bias_sums(grad_gated_ref, quarter, small_ref)
    skip_sums(pre_grad_ref, normed_ref, quarter, small_ref)
    to_feature_rows(lambda rows, index: stream.ref[rows, own] + mixed_ref[rows, own], order_ref, result, steps)
    adjoint_phase(
        low_ref, states, drive_own_ref, state, 5, length, drive_ref, grad_driven_ref, small_ref, False,
        glu_products(grads_ref, 2 * width, grad_gated_ref, active_ref, quarter)
        + output_products(grads_ref, lambda: low_ref[:, 0:128], lambda: low_ref[:, states : states + 128], pre_grad_ref, states),
    )
    scale = inv_dev * gain
    for piece in pieces_of(total):
        pre_ref[piece, :] = dot(grad_driven_ref[piece, :], b_ref[...], NN)
    plain, scaled = jnp.zeros((8, full), F32), jnp.zeros((8, full), F32)
    for place, piece in enumerate(pieces_of(total)):
        for rows, _ in blocks_of(piece.start, piece.stop):
            grad = pre_ref[rows, :] + skip * pre_grad_ref[rows, :].astype(F32)
            z = (stream.ref[rows, :] - centre) * inv_dev
            base.ref[rows, :] = scale * grad + up_ref[rows, :]
            plain += folded(grad)
            scaled += folded(grad * z)
        base.send_piece(place)
    input_products(grads_ref, grad_driven_ref, normed_ref, states)
    sent = narrowed([column_sum(plain), column_sum(scaled)], width)
    spread_rows(jnp.concatenate([sent, small_ref[:, 0:width]], axis=0), spread)
    send_halves(grads_ref, shares, 0)


def last_kernel(
    length_ref, ins, outs, held_ref, grad_state_ref, grad_gated_ref, pre_grad_ref, grad_driven_ref, small_ref, up_ref, grads_ref, pack_ref, low_ref
):
    (sums, norm1, feature_in, state_in, norm0, stream, base, gate, linear, w, slope, c, normed, active, low, drive_own, b, x) = ins
    kept, sent, up_out, grad_out = outs
    length, quarter = length_ref[0], own_quarter()
    total, full = stream.ref.shape
    steps = total // CHUNKS
    width = 128
    own = lanes_at(quarter, width)
    feature, norm_ref = feature_in.wait(), norm1.wait()
    state = state_in.wait()[...]
    counted = norm_ref[2:3, :]
    whole = total_rows(sums.wait())
    whole = jnp.concatenate([widened(whole, 0, 4), widened(whole, 4, 4)], axis=0)
    centre, inv_dev = norm_ref[0:1, :], norm_ref[1:2, :]
    scale = inv_dev * feature[5 + GAIN : 6 + GAIN, :]
    level = scale * whole[0:1, :] / counted
    tilt = scale * inv_dev * whole[1:2, :] / counted

    for place, piece in enumerate(pieces_of(total)):
        for value in (stream, base, gate, linear):
            value.wait(place)
        if place == 0:
            w.wait()
        for rows, index in blocks_of(piece.start, piece.stop):
            keep = keep_rows(index, 16, steps, length)
            up = base.ref[rows, :] - jnp.where(keep, level + (stream.ref[rows, :] - centre) * tilt, 0.0)
            up_ref[rows, :] = up
            up = jnp.where(keep, up, 0.0)
            grad_gated_ref[rows, :full] = (up * gate.ref[rows, :].astype(F32)).astype(LOW)
            grad_gated_ref[rows, full:] = (up * linear.ref[rows, :].astype(F32)).astype(LOW)
        held_ref[piece, :] = dot(grad_gated_ref[piece, :], w.ref[...], NN)
    for value in (slope, c):
        value.wait()
    for piece in pieces_of(total):
        pre_grad_piece(piece, held_ref, slope.ref, pre_grad_ref)
        grad_state_ref[piece, :] = dot(pre_grad_ref[piece, :], c.ref[...], NT)
    small_ref[...] = jnp.zeros_like(small_ref)

    def own_up(rows, index, carry):
        up_out.ref[rows, :] = up_ref[rows, own]
        return carry

    for_rows(0, total, 16, own_up, unroll=4)
    up_out.send()
    for value in (normed, active, low, drive_own):
        value.wait()
    bias_sums(grad_gated_ref, quarter, small_ref)
    skip_sums(pre_grad_ref, normed.ref, quarter, small_ref)
    adjoint_phase(
        low.ref, 128, drive_own.ref, state, 2, length, grad_state_ref, grad_driven_ref, small_ref, True,
        glu_products(grads_ref, 2 * width, grad_gated_ref, active.ref, quarter)
        + output_products(grads_ref, lambda: low.ref[:, :128], lambda: low.ref[:, 128:], pre_grad_ref, state.shape[1]),
    )
    b.wait()
    x.wait()
    held_ref[:, :width] = dot(grad_driven_ref[...], b.ref[:, own], NN)
    input_products(grads_ref, grad_driven_ref, normed.ref, state.shape[1])
    zero = jnp.zeros((8, width), F32)
    centre0, inv_dev0 = norm0.wait()[0:1, own], norm0.ref[1:2, own]
    skip = feature[SKIP : SKIP + 1, own]

    def back(rows, index, carry):
        grad = held_ref[rows, :width] + skip * pre_grad_ref[rows, own].astype(F32)
        grad_out.ref[rows, :] = grad
        z = (x.ref[rows, :] - centre0) * inv_dev0
        return carry[0] + folded(grad), carry[1] + folded(grad * z)

    plain, scaled = for_rows(0, total, 16, back, (zero, zero), unroll=4)
    grad_out.send()
    small_ref[6:7, 0:width] = column_sum(plain)
    small_ref[7:8, 0:width] = column_sum(scaled)
    pack_ref[...] = jnp.zeros_like(pack_ref)
    for place in range(8):
        pack_ref[place // 4 : place // 4 + 1, place % 4 * width : (place % 4 + 1) * width] = small_ref[place : place + 1, 0:width]
    exact = pack_ref[0:8, :]
    pack_ref[8:16, :] = exact - exact.astype(LOW).astype(F32)
    half = grads_ref.shape[0] // 2
    low_ref[...] = pack_ref[...].astype(LOW)
    mine = lax.axis_index("dp") & 1
    for out, which in ((kept, mine), (sent, 1 - mine)):
        out.send(0, half, source=grads_ref.at[rows_at(which, half)])
        out.send(half, 16, source=low_ref)


def send_halves(source_ref, outs, stage):
    kept = lax.axis_index("dp") >> stage & 1
    half = source_ref.shape[0] // 2
    for out, which in zip(outs, (kept, 1 - kept)):
        out.send(source=source_ref.at[rows_at(which, half)])


def add_kernel(length_ref, ins, outs, sum_ref, stage):
    kept, other = ins
    kept.wait()
    other.wait()
    for piece in range(0, kept.ref.shape[0], 16):
        at = slice(piece, piece + 16)
        sum_ref[at, :] = (kept.ref[at, :].astype(F32) + other.ref[at, :].astype(F32)).astype(LOW)
    send_halves(sum_ref, outs, stage)


def pair_kernel(length_ref, ins, outs, sum_ref, pack_ref):
    kept, other, *last = ins
    back, *outs = outs
    for value in ins:
        value.wait()
    half = kept.ref.shape[0] - 16
    share = half // len(outs)
    small = kept.ref[half:, :].astype(F32) + other.ref[half:, :].astype(F32)
    small = small[0:8, :] + small[8:16, :]
    pack_ref[...] = jnp.concatenate([small, small - small.astype(LOW).astype(F32)], axis=0).astype(LOW)
    for piece in range(0, half, 16):
        at = slice(piece, piece + 16)
        sum_ref[at, :] = (kept.ref[at, :].astype(F32) + other.ref[at, :].astype(F32)).astype(LOW)
    for place, out in enumerate(outs):
        out.send(0, share, source=sum_ref.at[rows_at((lax.axis_index("dp") >> 1) ^ place, share)])
        out.send(share, 16, source=pack_ref)
    for piece in range(0, share, 16):
        at = slice(piece, piece + 16)
        back.ref[at, :] = (last[0].ref[at, :].astype(F32) + last[1].ref[at, :].astype(F32)).astype(LOW)


def share_kernel(length_ref, ins, outs):
    out, small = outs
    share = out.ref.shape[0]
    for value in ins:
        value.wait()
    for piece in range(0, share, 16):
        at = slice(piece, piece + 16)
        value = ins[0].ref[at, :].astype(F32)
        for block in ins[1:]:
            value += block.ref[at, :].astype(F32)
        out.ref[at, :] = value.astype(LOW)
    out.send()
    value = ins[0].ref[share:, :].astype(F32)
    for block in ins[1:]:
        value += block.ref[share:, :].astype(F32)
    small.ref[...] = value[0:8, :] + value[8:16, :]


def finish_kernel(length_ref, ins, outs, held_ref, order_ref):
    small0, bn1, norm0, feature, nu, theta, up, grad, x = ins
    nu_out, theta_out, gamma_out, skip_out, bias_out, gain_out, shift_out, out = outs
    length, quarter = length_ref[0], own_quarter()
    total, width = up.ref.shape
    steps = total // CHUNKS
    own = lanes_at(quarter, width)
    states = nu_out.ref.shape[1]
    for value in ins:
        value.wait()
    whole = total_rows(bn1.ref)
    held_ref[0:1, :] = widened(whole, 0, 4)
    held_ref[1:2, :] = widened(whole, 4, 4)
    held_ref[16:32, :width] = whole
    for place in range(8):
        held_ref[8 + place : 9 + place, :width] = small0.ref[place // 4 : place // 4 + 1, place % 4 * width : (place % 4 + 1) * width]
    for layer, first in ((0, 8), (1, 24)):
        at = slice(layer, layer + 1)
        nu_out.ref[at, :] = -jnp.exp(nu.ref[at, :]) * held_ref[first : first + 1, :states]
        theta_out.ref[at, :] = jnp.exp(theta.ref[at, :]) * held_ref[first + 1 : first + 2, :states]
        gamma_out.ref[at, :] = held_ref[first + 2 : first + 3, :states]
        skip_out.ref[at, :] = held_ref[first + 3 : first + 4, :width]
        bias_out.ref[layer, 0:1, :] = held_ref[first + 4 : first + 5, :width]
        bias_out.ref[layer, 1:2, :] = held_ref[first + 5 : first + 6, :width]
    shift_out.ref[0:1, :] = held_ref[14:15, :width]
    gain_out.ref[0:1, :] = held_ref[15:16, :width]
    shift_out.ref[1:2, :] = held_ref[0:1, own]
    gain_out.ref[1:2, :] = held_ref[1:2, own]
    counted = norm0.ref[2:3, own]
    centre, inv_dev = norm0.ref[0:1, own], norm0.ref[1:2, own]
    level = held_ref[14:15, :width] / counted
    tilt = held_ref[15:16, :width] * inv_dev / counted
    scale = inv_dev * feature.ref[GAIN : GAIN + 1, own]

    def load(rows, index):
        keep = keep_rows(index, CHUNKS, steps, length)
        inner = grad.ref[rows, :] - level - (x.ref[rows, :] - centre) * tilt
        return up.ref[rows, :] + jnp.where(keep, scale * inner, 0.0)

    to_feature_rows(load, order_ref, out, steps)


def widen_kernel(length_ref, ins, outs, held_ref):
    half = outs[0].ref.shape[1]
    groups = len(ins) // 2
    share = ins[0].ref.shape[0]
    stages = groups.bit_length() - 1
    for layer, values in ((1, ins[:groups]), (0, ins[groups:])):
        for place, value in enumerate(values):
            value.wait()
            owner = lax.axis_index("dp") ^ place
            at = (owner & 1) * (groups // 2) + (owner >> 1)
            if layer == 1:
                at = sum((owner >> stage & 1) << (stages - 1 - stage) for stage in range(stages))
            held_ref[layer, rows_at(at, share), :] = value.ref[...].astype(F32)
        for out, first, size in zip(outs, (0, half, 2 * half), (half, half, 2 * half)):
            out.send(layer, 1, source=held_ref.at[pl.ds(layer, 1), pl.ds(first, size)])


def shape(*dims, dtype=F32):
    return jax.ShapeDtypeStruct(dims, dtype)


def swap(value, bit, sharers):
    pairs = [(q * sharers + r, (q ^ bit) * sharers + r) for q in range(4) for r in range(sharers)]
    return lax.ppermute(value, "state", pairs)


def across(value, axes):
    return lax.all_to_all(value, axes, 0, 0, tiled=True)


def local(
    inputs, lengths, cotangent, bn_gain, bn_bias, b_weight, c_weight, nu_log, theta_log, gamma_log, skip_weight,
    glu_weight, glu_bias, dp_size, state_size,
):
    sharers = state_size // 4
    place = lax.axis_index("state").astype(jnp.int32)

    def joined(value, axis):
        if sharers == 1:
            return value
        groups = [[q * sharers + r for r in range(sharers)] for q in range(4)]
        return lax.all_gather(value, "state", axis=axis, axis_index_groups=groups, tiled=True)

    def own(value, axis):
        if sharers == 1:
            return value
        size = value.shape[axis] // sharers
        return lax.dynamic_slice_in_dim(value, place % sharers * size, size, axis)

    inputs, cotangent = joined(inputs, 1), joined(cotangent, 1)
    bn_gain, bn_bias, skip_weight = joined(bn_gain, 1), joined(bn_bias, 1), joined(skip_weight, 1)
    nu_log, theta_log, gamma_log = joined(nu_log, 1), joined(theta_log, 1), joined(gamma_log, 1)
    b_weight, c_weight = joined(b_weight, 2), joined(c_weight, 2)
    glu_weight, glu_bias = joined(glu_weight, 2), joined(glu_bias, 2)
    width, total = inputs.shape[1:]
    full = b_weight.shape[3]
    states = b_weight.shape[2] * 4
    own_states = b_weight.shape[2]
    share = 4 * width // dp_size
    piece = total // PIECES

    stages = dp_size.bit_length() - 1

    def exchange(value, bit):
        return lax.ppermute(value, "dp", [(i, i ^ bit) for i in range(dp_size)])

    def add(halves, stage):
        kept, other = halves
        rows = kept.shape[0]
        return call(
            functools.partial(add_kernel, stage=stage + 1),
            (shape(rows // 2, full, dtype=LOW),) * 2,
            [pltpu.VMEM((rows, full), LOW)],
            (lengths, kept, other),
            "add",
            bare=(0, 1),
        )


    b_weight, c_weight = b_weight.reshape(LAYERS, width, full), c_weight.reshape(LAYERS, width, full)
    glu_weight = glu_weight.reshape(LAYERS, 2 * width, full)
    tokens, sums, first = call(
        enter_kernel,
        (
            shape(total, width),
            shape(dp_size * state_size, 8, width),
            shape(6 * width + PARAM_ROWS, full, dtype=LOW),
        ),
        [pltpu.VMEM((total, width), F32), pltpu.VMEM((PARAM_ROWS, width), F32)],
        (lengths, inputs[0], bn_gain, bn_bias, skip_weight, glu_bias, nu_log, theta_log, gamma_log, b_weight, c_weight, glu_weight),
        "enter",
        pieces={1: piece},
        axes={1: 1},
        late=(9, 10, 11),
    )
    near, far = swap(first, 1, sharers), swap(first, 2, sharers)
    sums = across(sums, ("dp", "state"))
    if sharers > 1:
        sums = sums.reshape(dp_size * 4, sharers, 8, width)[:, 0]
    cotangent, tokens = lax.optimization_barrier((cotangent, tokens))
    up_own, later = call(
        cotangent_kernel,
        (
            shape(total, width),
            shape(6 * width, full, dtype=LOW),
        ),
        [pltpu.VMEM((total, width), F32)],
        (lengths, cotangent[0], b_weight, c_weight, glu_weight),
        "cotangent",
        pieces={1: piece},
        axes={1: 1},
        late=(2, 3, 4),
    )
    near, far, sums, later = lax.optimization_barrier((near, far, sums, later))
    parts = (first, near, far, swap(far, 1, sharers))
    later_far = swap(later, 2, sharers)
    feature, state, norm0, normed0, drive0, low0, stream1, linear0, gate0, slope0, active0, b_all, c_all, w_all, sums1 = call(
        start_kernel,
        (
            shape(PARAM_ROWS, full),
            shape(8, states),
            shape(8, full),
            shape(total, full, dtype=LOW),
            shape(total, 256),
            shape(total, 256, dtype=LOW),
            shape(total, full),
            shape(total, full, dtype=LOW),
            shape(total, full, dtype=LOW),
            shape(total, full, dtype=LOW),
            shape(total, full, dtype=LOW),
            shape(2 * states, full, dtype=LOW),
            shape(2 * states, full, dtype=LOW),
            shape(2 * full, full, dtype=LOW),
            shape(dp_size, 8, width),
        ),
        [
            pltpu.VMEM((8, full), F32),
            pltpu.VMEM((total, full), F32),
            pltpu.VMEM((total, 2 * states), F32),
            pltpu.VMEM((total, full), F32),
            pltpu.VMEM((total, 2 * full), F32),
            pltpu.VMEM((2 * states, full), LOW),
            pltpu.VMEM((2 * states, full), LOW),
            pltpu.VMEM((2 * full, full), LOW),
            pltpu.VMEM((total, 2 * states), LOW),
        ],
        (lengths, sums, tokens, *parts),
        "start",
        pieces={2: piece} | {place: width for place in (3, 4, 5, 6)},
        order=(4, 5),
        bare=(11, 12, 13),
        flops=1e9,
    )
    sums1 = across(sums1, "dp")
    later_far, sums1 = lax.optimization_barrier((later_far, sums1))
    later_parts = (later, swap(later, 1, sharers), later_far, swap(later_far, 1, sharers))
    result, base, bn1, norm1, *halves1 = call(
        middle_kernel,
        (
            shape(width, total),
            shape(total, full),
            shape(dp_size, 16, width),
            shape(8, full),
            shape(2 * width, full, dtype=LOW),
            shape(2 * width, full, dtype=LOW),
        ),
        [
            pltpu.VMEM((8, full), F32),
            pltpu.VMEM((2 * states, full), LOW),
            pltpu.VMEM((2 * states, full), LOW),
            pltpu.VMEM((2 * full, full), LOW),
            pltpu.VMEM((total, full), LOW),
            pltpu.VMEM((total, 2 * states), F32),
            pltpu.VMEM((total, 256), F32),
            pltpu.VMEM((total, 2 * states), LOW),
            pltpu.VMEM((total, full), F32),
            pltpu.VMEM((total, full), LOW),
            pltpu.VMEM((total, 2 * full), F32),
            pltpu.VMEM((total, full), F32),
            pltpu.VMEM((total, full), F32),
            pltpu.VMEM((total, width), F32),
            pltpu.VMEM((total, full), F32),
            pltpu.VMEM((total, 2 * full), LOW),
            pltpu.VMEM((total, full), LOW),
            pltpu.VMEM((total, 2 * states), LOW),
            pltpu.VMEM((4 * width, full), LOW),
        ],
        (lengths, sums1, norm0, feature, state, stream1, up_own, *later_parts),
        "middle",
        pieces={5: piece} | {place: width for place in (7, 8, 9, 10)},
        late=(6, 7, 8, 9, 10),
        bare=(4, 5),
        flops=1e9,
    )
    bn1 = across(bn1, "dp")
    halves1[1] = exchange(halves1[1], 1)
    halves1 = list(add(halves1, 0))
    bn1, *halves1 = lax.optimization_barrier((bn1, *halves1))
    halves1[1] = exchange(halves1[1], 2)
    kept0, sent0, up0, grad0 = call(
        last_kernel,
        (
            shape(2 * width + 16, full, dtype=LOW),
            shape(2 * width + 16, full, dtype=LOW),
            shape(total, width),
            shape(total, width),
        ),
        [
            pltpu.VMEM((total, full), F32),
            pltpu.VMEM((total, 2 * states), F32),
            pltpu.VMEM((total, 2 * full), LOW),
            pltpu.VMEM((total, full), LOW),
            pltpu.VMEM((total, 2 * states), LOW),
            pltpu.VMEM((8, full), F32),
            pltpu.VMEM((total, full), F32),
            pltpu.VMEM((4 * width, full), LOW),
            pltpu.VMEM((16, full), F32),
            pltpu.VMEM((16, full), LOW),
        ],
        (lengths, bn1, norm1, feature, state, norm0, stream1, base, gate0, linear0, w_all, slope0, c_all, normed0, active0, low0,
         drive0, b_all, tokens),
        "last",
        bare=(0, 1),
        pieces={6: piece, 7: piece, 8: piece, 9: piece},
        late=tuple(range(11, 19)),
        flops=1e11,
    )
    *halves1, kept0, sent0 = lax.optimization_barrier((*halves1, kept0, sent0))
    sent0 = exchange(sent0, 1)
    for stage in range(1, stages):
        if stage > 1:
            halves1[1] = exchange(halves1[1], 1 << stage)
        if stage < stages - 1:
            halves1 = list(add(halves1, stage))
    back1, *blocks = call(
        pair_kernel,
        (shape(share, full, dtype=LOW),) + (shape(share + 16, full, dtype=LOW),) * (dp_size // 2),
        [pltpu.VMEM((2 * width, full), LOW), pltpu.VMEM((16, full), LOW)],
        (lengths, kept0, sent0, *halves1),
        "pair",
        bare=tuple(range(1, 1 + dp_size // 2)),
    )
    blocks = [blocks[0]] + [exchange(blocks[place], 2 * place) for place in range(1, dp_size // 2)]
    back0, small0 = call(
        share_kernel,
        (shape(share, full, dtype=LOW), shape(8, full)),
        [],
        (lengths, *blocks),
        "share",
    )

    def to_all(value):
        got = [value] + [exchange(value, place) for place in range(2, dp_size, 2)]
        return [each for first in got for each in (first, exchange(first, 1))]

    backs = to_all(back1) + to_all(back0)
    grad_nu, grad_theta, grad_gamma, grad_skip, grad_bias, grad_gain, grad_shift, grad_inputs = call(
        finish_kernel,
        (
            shape(LAYERS, own_states),
            shape(LAYERS, own_states),
            shape(LAYERS, own_states),
            shape(LAYERS, width),
            shape(LAYERS, 2, width),
            shape(LAYERS, width),
            shape(LAYERS, width),
            shape(width, total),
        ),
        [pltpu.VMEM((32, full), F32), pltpu.VMEM((total, width), F32)],
        (lengths, small0, bn1, norm0, feature, nu_log, theta_log, up0, grad0, tokens),
        "finish",
    )
    grad_b, grad_c, grad_glu = call(
        widen_kernel,
        (shape(LAYERS, width, full), shape(LAYERS, width, full), shape(LAYERS, 2 * width, full)),
        [pltpu.VMEM((LAYERS, 4 * width, full), F32)],
        (lengths, *backs),
        "widen",
        bare=(0, 1, 2),
    )
    grad_b = grad_b.reshape(LAYERS, 2, own_states, full)
    grad_c = grad_c.reshape(LAYERS, 2, own_states, full)
    grad_glu = grad_glu.reshape(LAYERS, 2, width, full)
    return (
        own(result[None], 1),
        own(grad_inputs[None], 1),
        own(grad_gain, 1),
        own(grad_shift, 1),
        own(grad_b, 2),
        own(grad_c, 2),
        own(grad_nu, 1),
        own(grad_theta, 1),
        own(grad_gamma, 1),
        own(grad_skip, 1),
        own(grad_glu, 2),
        own(grad_bias, 2),
    )


def solution(mesh):
    in_specs = (
        P("dp", "state", None),
        P("dp"),
        P("dp", "state", None),
        P(None, "state"),
        P(None, "state"),
        P(None, None, "state", None),
        P(None, None, "state", None),
        P(None, "state"),
        P(None, "state"),
        P(None, "state"),
        P(None, "state"),
        P(None, None, "state", None),
        P(None, None, "state"),
    )
    out_specs = (
        P("dp", "state", None),
        P("dp", "state", None),
        P(None, "state"),
        P(None, "state"),
        P(None, None, "state", None),
        P(None, None, "state", None),
        P(None, "state"),
        P(None, "state"),
        P(None, "state"),
        P(None, "state"),
        P(None, None, "state", None),
        P(None, None, "state"),
    )
    step = functools.partial(local, dp_size=mesh.shape["dp"], state_size=mesh.shape["state"])
    return jax.shard_map(step, mesh=mesh, in_specs=in_specs, out_specs=out_specs, check_vma=False)
```

```python
import functools

import jax
import jax.numpy as jnp
from jax import lax
from jax.experimental import pallas as pl
from jax.experimental.pallas import tpu as pltpu
from jax.sharding import PartitionSpec as P

LAYERS = 2
CHUNKS = 16
PIECES = 4
EPSILON = 1e-05
F32 = jnp.float32
LOW = jnp.bfloat16
PARAM_ROWS = 32
OWN_MEAN = 16
VMEM_BYTES = 64 * 1024 * 1024
SMALL_VMEM_BYTES = 24 * 1024 * 1024

GAIN, SHIFT, SKIP, BIAS_LINEAR, BIAS_GATE = range(5)
RATE_RE, RATE_IM, GAMMA = range(3)

NN = (((1,), (0,)), ((), ()))
NT = (((1,), (1,)), ((), ()))
TN = (((0,), (0,)), ((), ()))


def dot(left, right, dims):
    return lax.dot_general(left, right, dims, preferred_element_type=F32)


def rows_at(index, size):
    return pl.ds(pl.multiple_of(index * size, size), size)


def lanes_at(quarter, width):
    return pl.ds(pl.multiple_of(quarter * width, width), width)


def for_rows(first, last, size, body, init=0, unroll=2):
    def step(index, carry):
        return body(rows_at(index, size), index, carry)

    return lax.fori_loop(first // size, last // size, step, init, unroll=unroll)


def blocks_of(first, last, size=16):
    return [(slice(at, at + size), at // size) for at in range(first, last, size)]


def pieces_of(total):
    size = total // PIECES
    return [slice(at, at + size) for at in range(0, total, size)]


def own_quarter():
    return (lax.axis_index("state") // (lax.axis_size("state") // 4)).astype(jnp.int32)


def keep_rows(first_step, rows, steps, length):
    row = lax.broadcasted_iota(jnp.int32, (rows, 1), 0)
    position = (row % CHUNKS) * steps + row // CHUNKS + first_step
    return position < length


def gelu_parts(value):
    return 0.5 + 0.5 * lax.erf(value * 0.7071067811865476), jnp.exp(value * value * -0.5) * 0.3989422804014327


def squared(re, im, times):
    for _ in range(times):
        re, im = re * re - im * im, 2.0 * re * im
    return re, im


def folded(value):
    return value[0:8, :] + value[8:16, :]


def column_sum(value):
    return jnp.sum(value, axis=0, keepdims=True)


def chunk_starts(re, im, rate_re, rate_im, reverse):
    row = lax.broadcasted_iota(jnp.int32, re.shape, 0)

    def moved(value, by):
        if reverse:
            return jnp.where(row < CHUNKS - by, pltpu.roll(value, CHUNKS - by, 0), 0.0)
        return jnp.where(row >= by, pltpu.roll(value, by, 0), 0.0)

    by = 1
    while by < CHUNKS:
        past_re, past_im = moved(re, by), moved(im, by)
        re, im = (
            re + rate_re * past_re - rate_im * past_im,
            im + rate_re * past_im + rate_im * past_re,
        )
        rate_re, rate_im = squared(rate_re, rate_im, 1)
        by *= 2
    return moved(re, 1), moved(im, 1)


def sweep(drive_ref, rate_re, rate_im, steps, reverse, emit, extra, after=None, beside=None, unroll=4):
    states = rate_re.shape[1]
    shape = (CHUNKS, states)
    wide_re = jnp.broadcast_to(rate_re, shape)
    wide_im = jnp.broadcast_to(rate_im, shape)

    def advance(index, re, im):
        place = steps - 1 - index if reverse else index
        rows = slice(place * CHUNKS, (place + 1) * CHUNKS) if isinstance(place, int) else rows_at(place, CHUNKS)
        drive_re = drive_ref[rows, :states]
        drive_im = drive_ref[rows, states:]
        new_re = (wide_re * re + drive_re) - wide_im * im
        new_im = (wide_re * im + drive_im) + wide_im * re
        return rows, place, new_re, new_im, drive_re, drive_im

    def first(index, carry):
        _, _, re, im, _, _ = advance(index, *carry)
        return re, im

    def second(index, carry):
        re, im, held = carry
        rows, place, re, im, drive_re, drive_im = advance(index, re, im)
        return re, im, emit(rows, place, re, im, drive_re, drive_im, held)

    zero = jnp.zeros(shape, F32)
    re, im = lax.fori_loop(0, steps, first, (zero, zero), unroll=unroll)
    far_re, far_im = rate_re, rate_im
    power = 1
    while power < steps:
        far_re, far_im = squared(far_re, far_im, 1)
        power *= 2
    re, im = chunk_starts(re, im, far_re, far_im, reverse)
    carry = (re, im, extra)
    for piece in range(PIECES):
        size = steps // PIECES
        if beside is not None:
            beside[piece]()
            for index in range(piece * size, (piece + 1) * size):
                carry = second(index, carry)
        else:
            carry = lax.fori_loop(piece * size, (piece + 1) * size, second, carry, unroll=unroll)
        if after is not None:
            after(PIECES - 1 - piece if reverse else piece)
    return carry[2]


class Arrival:
    def __init__(self, source, ref, done, first, size, axis):
        self.ref = ref
        self.copies = []
        whole = ref.shape[axis]
        for piece, start in enumerate(range(0, whole, size)):
            where = (slice(None),) * axis + (pl.ds(start, min(size, whole - start)),)
            self.copies.append(
                pltpu.make_async_copy(source.at[where], ref.at[where], done.at[first + piece])
                if size < whole
                else pltpu.make_async_copy(source, ref, done.at[first])
            )
        self.short = whole % size > 0
        self.waited = set()

    def start(self, piece):
        last = len(self.copies) - self.short
        if piece < 0 and self.short:
            self.copies[-1].start()
        if 0 <= piece < last:
            self.copies[piece].start()

    def wait(self, piece=None):
        for place in range(len(self.copies)) if piece is None else (piece,):
            if place not in self.waited:
                self.copies[place].wait()
                self.waited.add(place)
        return self.ref


class Departure:
    def __init__(self, target, ref, done, first):
        self.target, self.ref, self.done, self.first = target, ref, done, first
        self.copies = []

    def send(self, start=None, size=None, source=None):
        place = self.done.at[self.first + len(self.copies)]
        where = self.target if start is None else self.target.at[pl.ds(start, size)]
        if source is None:
            source = self.ref if start is None else self.ref.at[pl.ds(start, size)]
        self.copies.append(pltpu.make_async_copy(source, where, place))
        self.copies[-1].start()

    def send_piece(self, piece):
        size = self.target.shape[0] // PIECES
        self.send(piece * size, size)

    def send_unsent(self):
        if not self.copies:
            self.send()

    def finish(self):
        for copy in self.copies:
            copy.wait()


class Resident:
    def __init__(self, ref):
        self.ref = ref

    def wait(self, piece=None):
        return self.ref

    def send(self, start=None, size=None, source=None):
        if source is not None and start is None:
            self.ref[...] = source[...]
        elif source is not None:
            self.ref[start : start + size, :] = source[...]


def call_small(kernel, outs, scratch, args, name, sent=False):
    def body(*refs):
        count, results = len(args), len(outs)
        ins, refs = [Resident(ref) for ref in refs[:count]], refs[count:]
        if not sent:
            kernel(None, ins, [Resident(ref) for ref in refs[:results]], *refs[results:])
            return
        targets, copied, scratch_refs = refs[:results], refs[results], refs[results + 1 :]
        departures = [Departure(target, None, copied, place * LAYERS) for place, target in enumerate(targets)]
        kernel(None, ins, departures, *scratch_refs)
        for departure in departures:
            departure.finish()

    return pl.pallas_call(
        body,
        out_shape=tuple(outs),
        in_specs=[pl.BlockSpec(memory_space=pltpu.VMEM)] * len(args),
        out_specs=tuple(pl.BlockSpec(memory_space=pl.ANY if sent else pltpu.VMEM) for _ in outs),
        scratch_shapes=([pltpu.SemaphoreType.DMA((LAYERS * len(outs),))] if sent else []) + list(scratch),
        compiler_params=pltpu.CompilerParams(vmem_limit_bytes=SMALL_VMEM_BYTES),
        cost_estimate=pl.CostEstimate(flops=0, bytes_accessed=0, transcendentals=0),
        name=name,
    )(*args)


def call(kernel, outs, scratch, args, name, pieces=None, axes=None, bare=(), late=(), order=None, flops=0):
    pieces, axes = pieces or {}, axes or {}
    along = [axes.get(place, 0) for place in range(1, len(args))]
    sizes = [pieces.get(place, args[place].shape[axis]) for place, axis in enumerate(along, 1)]
    counts = [-(-args[place].shape[axis] // size) for place, (axis, size) in enumerate(zip(along, sizes), 1)]
    slots = 6
    copies_in = [pltpu.VMEM(a.shape, a.dtype) for a in args[1:]]
    copies_out = [pltpu.VMEM((8, 128) if place in bare else o.shape, o.dtype if place not in bare else F32) for place, o in enumerate(outs)]

    def body(*refs):
        refs = list(refs)

        def take(count):
            got = refs[:count]
            del refs[:count]
            return got

        (length_ref,) = take(1)
        sources = take(len(args) - 1)
        targets = take(len(outs))
        in_refs, out_refs = take(len(args) - 1), take(len(outs))
        arrived, sent = take(2)
        arrivals, first = [], 0
        for source, ref, size, count, axis in zip(sources, in_refs, sizes, counts, along):
            arrivals.append(Arrival(source, ref, arrived, first, size, axis))
            first += count
        for group in (False, True):
            for piece in (-1, *(order or ()), *(piece for piece in range(max(counts)) if piece not in (order or ()))):
                for place, arrival in enumerate(arrivals, 1):
                    if (place in late) is group:
                        arrival.start(piece)
        departures = [
            Departure(target, ref, sent, place * slots) for place, (target, ref) in enumerate(zip(targets, out_refs))
        ]
        kernel(length_ref, arrivals, departures, *refs)
        for arrival in arrivals:
            arrival.wait()
        for departure in departures:
            departure.send_unsent()
        for departure in departures:
            departure.finish()

    return pl.pallas_call(
        body,
        out_shape=tuple(outs),
        in_specs=[pl.BlockSpec(memory_space=pltpu.SMEM if place == 0 else pl.ANY) for place in range(len(args))],
        out_specs=tuple(pl.BlockSpec(memory_space=pl.ANY) for _ in outs),
        scratch_shapes=[
            *copies_in,
            *copies_out,
            pltpu.SemaphoreType.DMA((sum(counts),)),
            pltpu.SemaphoreType.DMA((slots * len(outs),)),
            *scratch,
        ],
        compiler_params=pltpu.CompilerParams(vmem_limit_bytes=VMEM_BYTES),
        cost_estimate=pl.CostEstimate(flops=int(flops), bytes_accessed=0, transcendentals=0),
        name=name,
    )(*args)


def from_feature_rows(source, held_ref, steps, emit, init, after):
    length = source.ref.shape[1]
    blocks = length // 128
    for block in range(blocks):
        if block % (blocks // PIECES) == 0:
            source.wait(block // (blocks // PIECES))
        lanes = slice(block * 128, (block + 1) * 128)
        held_ref[lanes, :] = source.ref[:, lanes].T

    def step(index, carry):
        return emit(rows_at(index, CHUNKS), index, held_ref[pl.ds(index, CHUNKS, stride=steps), :], carry)

    carry = init
    for piece in range(PIECES):
        size = steps // PIECES
        carry = lax.fori_loop(piece * size, (piece + 1) * size, step, carry, unroll=4)
        after(piece)
    return carry


def to_feature_rows(load, held_ref, out, steps):
    length = out.ref.shape[1]

    def step(index, carry):
        held_ref[pl.ds(index, CHUNKS, stride=steps), :] = load(rows_at(index, CHUNKS), index)
        return carry

    lax.fori_loop(0, steps, step, 0, unroll=4)
    for block in range(length // 128):
        lanes = slice(block * 128, (block + 1) * 128)
        out.ref[:, lanes] = held_ref[lanes, :].T
    out.send()


def spread_rows(value, out):
    for group in range(out.ref.shape[0]):
        out.ref[group, :, :] = value
    out.send()


def narrowed(values, width):
    return jnp.concatenate([v[:, at : at + width] for v in values for at in range(0, v.shape[1], width)], axis=0)


def widened(rows, first, count):
    return jnp.concatenate([rows[first + place : first + place + 1, :] for place in range(count)], axis=1)


def total_rows(sums_ref):
    value = sums_ref[0, :, :]
    for other in range(1, sums_ref.shape[0]):
        value += sums_ref[other, :, :]
    return value


def assemble_states(parts, whole_ref):
    half = parts[0].shape[0] // 2
    states = half * len(parts)
    for place, part in enumerate(parts):
        whole_ref[place * half : (place + 1) * half, :] = part[:half, :]
        whole_ref[states + place * half : states + (place + 1) * half, :] = part[half:, :]


def assemble_output(parts, whole_ref):
    half = parts[0].shape[0] // 2
    states = half * len(parts)
    for place, part in enumerate(parts):
        whole_ref[place * half : (place + 1) * half, :] = part[:half, :]
        whole_ref[states + place * half : states + (place + 1) * half, :] = -part[half:, :]


def assemble_glu(parts, whole_ref, quarter):
    half = parts[0].shape[0] // 2
    width = half * len(parts)
    for place, part in enumerate(parts):
        whole_ref[lanes_at(quarter ^ place, half), :] = part[:half, :]
        whole_ref[pl.ds(pl.multiple_of(width + (quarter ^ place) * half, half), half), :] = part[half:, :]


def norm_rows(sums, counted):
    centre = sums[0:1, :] / counted
    meansq = sums[1:2, :] / counted
    return centre, lax.rsqrt(meansq - centre * centre + EPSILON)


def drive_phase(normed_ref, b_ref, drive_ref, gamma):
    drive_ref[...] = dot(normed_ref[...], b_ref[...], NT) * jnp.concatenate([gamma, gamma], axis=1)


def store_states(low_ref, drive_own_ref):
    def emit(rows, step, re, im, drive_re, drive_im, held):
        states = re.shape[1]
        low_ref[rows, :states] = re.astype(LOW)
        low_ref[rows, states:] = im.astype(LOW)
        drive_own_ref[rows, :128] = drive_re[:, :128].astype(drive_own_ref.dtype)
        drive_own_ref[rows, 128:] = drive_im[:, :128].astype(drive_own_ref.dtype)
        return held

    return emit


def pre_products(low_ref, c_ref, held_ref):
    total, full = low_ref.shape[0], c_ref.shape[1]
    for piece in pieces_of(total):
        held_ref[piece, :full] = dot(low_ref[piece, :], c_ref[...], NN)


def pre_piece(piece, held_ref, normed_ref, skip, active_ref, slope_ref):
    full = normed_ref.shape[1]
    for rows, _ in blocks_of(piece.start, piece.stop):
        value = held_ref[rows, :full] + skip * normed_ref[rows, :].astype(F32)
        cdf, density = gelu_parts(value)
        active_ref[rows, :] = (value * cdf).astype(LOW)
        slope_ref[rows, :] = (cdf + value * density).astype(slope_ref.dtype)


def pre_grad_piece(piece, held_ref, slope_ref, pre_grad_ref):
    full = slope_ref.shape[1]
    for rows, _ in blocks_of(piece.start, piece.stop):
        pre_grad_ref[rows, :] = (held_ref[rows, :full] * slope_ref[rows, :].astype(F32)).astype(LOW)


def skip_sums(pre_grad_ref, normed_ref, quarter, small_ref):
    own = lanes_at(quarter, 128)
    value = jnp.zeros((8, 128), F32)
    for rows, _ in blocks_of(0, pre_grad_ref.shape[0]):
        value += folded(pre_grad_ref[rows, own].astype(F32) * normed_ref[rows, own].astype(F32))
    small_ref[3:4, 0:128] = column_sum(value)


def bias_sums(grad_gated_ref, quarter, small_ref):
    for place in range(2):
        lanes = lanes_at(quarter + 4 * place, 128)
        value = jnp.zeros((8, 128), F32)
        for rows, _ in blocks_of(0, grad_gated_ref.shape[0]):
            value += folded(grad_gated_ref[rows, lanes].astype(F32))
        small_ref[4 + place : 5 + place, 0:128] = column_sum(value)


def together(*parts):
    def run():
        for part in parts:
            part()

    return run


def adjoint_phase(low_ref, im_lane, drive_own_ref, state, first_row, length, grad_state_ref, grad_driven_ref, small_ref, reverse, beside):
    total = grad_state_ref.shape[0]
    steps = total // CHUNKS
    states = state.shape[1]
    rate_re = state[first_row : first_row + 1, :]
    rate_im = state[first_row + 1 : first_row + 2, :]
    gamma = jnp.broadcast_to(state[first_row + 2 : first_row + 3, :], (CHUNKS, states))

    def emit(rows, step, re, im, drive_re, drive_im, held):
        out_re, out_im = gamma * re, gamma * im
        if not reverse:
            keep = keep_rows(step, CHUNKS, steps, length)
            out_re, out_im = jnp.where(keep, out_re, 0.0), jnp.where(keep, out_im, 0.0)
        grad_driven_ref[rows, :states] = out_re.astype(LOW)
        grad_driven_ref[rows, states:] = out_im.astype(LOW)
        one, two, three = held
        own_re, own_im = re[:, :128], im[:, :128]
        late_re, late_im = own_re - drive_re[:, :128], own_im - drive_im[:, :128]
        low_re = low_ref[rows, :128].astype(F32)
        low_im = low_ref[rows, im_lane : im_lane + 128].astype(F32)
        one = one + folded(late_re * low_re + late_im * low_im)
        two = two + folded(late_im * low_re - late_re * low_im)
        three = three + folded(
            own_re * drive_own_ref[rows, :128].astype(F32) + own_im * drive_own_ref[rows, 128:].astype(F32)
        )
        return one, two, three

    zero = jnp.zeros((8, 128), F32)
    one, two, three = sweep(grad_state_ref, rate_re, -rate_im, steps, reverse, emit, (zero, zero, zero), beside=beside)
    small_ref[0:1, 0:128] = column_sum(one)
    small_ref[1:2, 0:128] = column_sum(two)
    small_ref[2:3, 0:128] = column_sum(three)


def glu_products(grads_ref, first, grad_gated_ref, active_ref, quarter):
    full = active_ref.shape[1]

    def product(place):
        lanes = pl.ds(pl.multiple_of(place * full + quarter * 128, 128), 128)
        got = dot(grad_gated_ref[:, lanes], active_ref[...], TN)
        grads_ref[first + place * 128 : first + (place + 1) * 128, :] = got.astype(LOW)

    return [functools.partial(product, place) for place in range(2)]


def output_products(grads_ref, low_re, low_im, pre_grad_ref, states):
    half = states // 4

    def product(place, low, sign):
        got = sign * dot(low(), pre_grad_ref[...], TN)[:half, :]
        grads_ref[2 * half + place * half : 2 * half + (place + 1) * half, :] = got.astype(LOW)

    return [functools.partial(product, 0, low_re, 1.0), functools.partial(product, 1, low_im, -1.0)]


def beside_sweep(products, grad_gated_ref, pre_grad_ref, normed_ref, quarter, small_ref):
    first, second, third, fourth = products
    return (
        together(first, functools.partial(bias_sums, grad_gated_ref, quarter, small_ref)),
        together(second, functools.partial(skip_sums, pre_grad_ref, normed_ref, quarter, small_ref)),
        third,
        fourth,
    )


def input_products(grads_ref, grad_driven_ref, normed_ref, states):
    half = states // 4
    for place in range(2):
        lanes = slice(place * states, place * states + 128)
        got = dot(grad_driven_ref[:, lanes], normed_ref[...], TN)[:half, :]
        grads_ref[place * half : (place + 1) * half, :] = got.astype(LOW)


def enter_kernel(length_ref, ins, outs, held_ref, params_ref):
    x, gain, shift, skip, bias, nu, theta, gamma, b, c, w = ins
    tokens, spread, first_out = outs
    length = length_ref[0]
    width, total = x.ref.shape
    steps = total // CHUNKS

    def emit(rows, index, value, carry):
        tokens.ref[rows, :] = value
        kept = jnp.where(keep_rows(index, CHUNKS, steps, length), value, 0.0)
        return carry[0] + folded(kept), carry[1] + folded(kept * kept)

    zero = jnp.zeros((8, width), F32)
    plain, square = from_feature_rows(x, held_ref, steps, emit, (zero, zero), tokens.send_piece)
    plain = column_sum(plain)
    counted = jnp.full((1, width), length, jnp.int32).astype(F32)
    spread_rows(jnp.concatenate([plain, column_sum(square), counted, jnp.zeros((5, width), F32)], axis=0), spread)
    mean = plain / counted

    each = total // PIECES

    def centred(rows, index, carry):
        place = pl.ds(pl.multiple_of(4 * width + index * 32 % each, 32), 32)
        first_out.ref[place, lanes_at(index * 32 // each, width)] = (tokens.ref[rows, :] - mean).astype(LOW)
        return carry

    for_rows(0, total, 32, centred, unroll=4)
    for value in (gain, shift, skip, bias, nu, theta, gamma):
        value.wait()
    params_ref[...] = jnp.zeros(params_ref.shape, F32)
    for layer in range(LAYERS):
        first = 5 * layer
        params_ref[first + GAIN : first + GAIN + 1, :] = gain.ref[layer : layer + 1, :]
        params_ref[first + SHIFT : first + SHIFT + 1, :] = shift.ref[layer : layer + 1, :]
        params_ref[first + SKIP : first + SKIP + 1, :] = skip.ref[layer : layer + 1, :]
        params_ref[first + BIAS_LINEAR : first + BIAS_GATE + 1, :] = bias.ref[layer, :, :]
        first = 10 + 3 * layer
        for row, source in enumerate((nu, theta, gamma)):
            params_ref[first + row : first + row + 1, : source.ref.shape[1]] = source.ref[layer : layer + 1, :]
    params_ref[OWN_MEAN : OWN_MEAN + 1, :] = mean
    rest = params_ref[...]
    first_out.ref[6 * width :, :] = jnp.zeros((32, 4 * width), LOW)
    for place in range(3):
        high = rest.astype(LOW)
        first_out.ref[6 * width : 6 * width + PARAM_ROWS, place * width : (place + 1) * width] = high
        rest = rest - high.astype(F32)
    first_out.send(4 * width, 2 * width + 32)
    send_weights(0, b, c, w, first_out)


def send_weights(layer, b, c, w, whole):
    width = b.ref.shape[1]
    for value, first, size in ((b, 0, width), (c, width, width), (w, 2 * width, 2 * width)):
        value.wait()
        whole.send(first, size, source=value.ref.at[layer])


def total_kernel(length_ref, ins, outs):
    outs[0].ref[...] = total_rows(ins[0].ref)


def cotangent_kernel(length_ref, ins, outs, held_ref):
    x, b, c, w = ins
    whole, later = outs
    width, total = x.ref.shape
    steps = total // CHUNKS
    each = steps // PIECES

    def emit(rows, index, value, carry):
        whole.ref[rows, :] = value
        place = pl.ds(pl.multiple_of(4 * width + index % each * CHUNKS, CHUNKS), CHUNKS)
        later.ref[place, lanes_at(index // each, width)] = value.astype(LOW)
        return carry

    def after(piece):
        whole.send_piece(piece)
        if piece == 1:
            send_weights(1, b, c, w, later)

    from_feature_rows(x, held_ref, steps, emit, 0, after)
    later.send(4 * width, total // PIECES)


def start_kernel(length_ref, ins, outs, stats_ref, stream_ref, drive_ref, pre_ref, held_ref, b_ref, c_ref, w_ref, low_ref):
    all_stats, tokens, parts = ins[:4], ins[4], ins[5:]
    feature, state_out, norm, normed, drive_own, low_own, stream, linear_out, gate_out, slope, active, b_out, c_out, w_out, spread = outs
    length, quarter = length_ref[0], own_quarter()
    total, full = active.ref.shape
    steps = total // CHUNKS
    width = full // 4
    lane = lax.broadcasted_iota(jnp.int32, (8, width), 1)
    tails = []
    rows_refs = []
    for part in parts:
        for piece in (6, 4, 5):
            part.wait(piece)
        rows_refs.append(part.ref.at[pl.ds(4 * width, 2 * width + PARAM_ROWS)])
    for place, part_ref in enumerate(rows_refs):
        value = sum(part_ref[2 * width :, at * width : (at + 1) * width].astype(F32) for at in range(3))
        feature.ref[:, lanes_at(quarter ^ place, width)] = value
        tails.append(value[8:16, :])
    for pair in range(2):
        early, late = tails[2 * pair : 2 * pair + 2]
        logs = jnp.where(lane < 64, early, pltpu.roll(late, 64, 1))
        lanes = slice(pair * width, (pair + 1) * width)
        for layer in range(LAYERS):
            first = 2 + 3 * layer
            modulus = jnp.exp(-jnp.exp(logs[first : first + 1, :]))
            angle = jnp.exp(logs[first + 1 : first + 2, :])
            state_out.ref[first : first + 1, lanes] = modulus * jnp.cos(angle)
            state_out.ref[first + 1 : first + 2, lanes] = modulus * jnp.sin(angle)
            state_out.ref[first + 2 : first + 3, lanes] = jnp.exp(logs[first + 2 : first + 3, :])
    for place, stats in enumerate(all_stats):
        stats_ref[:, lanes_at(quarter ^ place, width)] = stats.wait()[...]
    centre, inv_dev = norm_rows(stats_ref[0:2, :], stats_ref[2:3, :])
    norm.ref[...] = jnp.zeros_like(norm.ref)
    norm.ref[0:1, :] = centre
    norm.ref[1:2, :] = inv_dev
    norm.ref[2:3, :] = stats_ref[2:3, :]
    for out in (feature, state_out, norm):
        out.send()

    each = total // PIECES

    def normal(rows, index, carry):
        keep = keep_rows(index, 16, steps, length)
        there = pl.ds(pl.multiple_of(index * 16 % each, 16), 16)
        for place, part_ref in enumerate(rows_refs):
            lanes = lanes_at(quarter ^ place, width)
            if place == 0:
                value = tokens.ref[rows, :]
            else:
                value = part_ref[there, lanes_at(index * 16 // each, width)].astype(F32)
                value = value + feature.ref[OWN_MEAN : OWN_MEAN + 1, lanes]
            stream_ref[rows, lanes] = value
            z = (value - norm.ref[0:1, lanes]) * norm.ref[1:2, lanes]
            z = z * feature.ref[GAIN : GAIN + 1, lanes] + feature.ref[SHIFT : SHIFT + 1, lanes]
            normed.ref[rows, lanes] = jnp.where(keep, z, 0.0).astype(LOW)
        return carry

    for piece in range(PIECES):
        tokens.wait(piece)
        for_rows(piece * total // PIECES, (piece + 1) * total // PIECES, 16, normal)
        normed.send_piece(piece)
    assemble_states([part.wait(0).at[0:width] for part in parts], b_ref)
    b_out.send(source=b_ref)
    state = state_out.ref[...]
    states = state.shape[1]
    drive_phase(normed.ref, b_ref, drive_ref, state[2 + GAMMA : 3 + GAMMA, :])
    assemble_output([part.wait(1).at[width : 2 * width] for part in parts], c_ref)
    c_out.send(source=c_ref)
    store = store_states(low_ref, drive_own.ref)

    def emit(rows, step, re, im, drive_re, drive_im, held):
        low_own.ref[rows, :128] = re[:, :128].astype(LOW)
        low_own.ref[rows, 128:] = im[:, :128].astype(LOW)
        return store(rows, step, re, im, drive_re, drive_im, held)

    sweep(drive_ref, state[2:3, :], state[3:4, :], steps, False, emit, 0)
    drive_own.send()
    low_own.send()

    assemble_glu([part.wait().at[2 * width : 4 * width] for part in parts], w_ref, quarter)
    w_out.send(source=w_ref)
    skip = feature.ref[SKIP : SKIP + 1, :]
    bias_linear = feature.ref[BIAS_LINEAR : BIAS_LINEAR + 1, :]
    bias_gate = feature.ref[BIAS_GATE : BIAS_GATE + 1, :]
    pre_products(low_ref, c_ref, pre_ref)
    for piece in pieces_of(total):
        pre_piece(piece, pre_ref, normed.ref, skip, active.ref, slope.ref)
        held_ref[piece, :] = dot(active.ref[piece, :], w_ref[...], NT)
    active.send()
    slope.send()
    plain, square = jnp.zeros((8, full), F32), jnp.zeros((8, full), F32)
    for place, piece in enumerate(pieces_of(total)):
        for rows, index in blocks_of(piece.start, piece.stop):
            keep = keep_rows(index, 16, steps, length)
            linear = held_ref[rows, :full] + bias_linear
            gate = jax.nn.sigmoid(held_ref[rows, full:] + bias_gate)
            mixed = linear * gate
            gate_out.ref[rows, :] = gate.astype(LOW)
            linear_out.ref[rows, :] = (mixed * (1.0 - gate)).astype(LOW)
            moved = stream_ref[rows, :] + jnp.where(keep, mixed, 0.0)
            stream.ref[rows, :] = moved
            kept = jnp.where(keep, moved, 0.0)
            plain += folded(kept)
            square += folded(kept * kept)
        for out in (stream, linear_out, gate_out):
            out.send_piece(place)
    carry = plain, square
    spread_rows(narrowed([column_sum(carry[0]), column_sum(carry[1])], width), spread)


def middle_kernel(
    length_ref, ins, outs,
    small_ref, b_ref, c_ref, w_ref, normed_ref, drive_ref, drive_own_ref, low_ref, slope_ref, active_ref, held_ref, pre_ref, mixed_ref,
    order_ref, up_ref, grad_gated_ref, pre_grad_ref, grad_driven_ref, grads_ref,
):
    sums, norm0, feature_in, state_in, stream, up_own = ins[:6]
    parts = ins[6:]
    result, base, spread, norm, *shares = outs
    length, quarter = length_ref[0], own_quarter()
    total, full = stream.ref.shape
    steps = total // CHUNKS
    width = 128
    counted = norm0.wait()[2:3, :]
    feature = feature_in.wait()
    state = state_in.wait()[...]
    states = state.shape[1]
    whole = total_rows(sums.wait())
    whole = jnp.concatenate([widened(whole, 0, 4), widened(whole, 4, 4)], axis=0)
    centre, inv_dev = norm_rows(whole, counted)
    norm.ref[...] = jnp.zeros_like(norm.ref)
    norm.ref[0:1, :] = centre
    norm.ref[1:2, :] = inv_dev
    norm.ref[2:3, :] = counted
    norm.send()
    gain = feature[5 + GAIN : 6 + GAIN, :]
    shift = feature[5 + SHIFT : 6 + SHIFT, :]
    skip = feature[5 + SKIP : 6 + SKIP, :]

    for part in parts:
        part.wait(0)
    assemble_states([part.ref.at[0:width] for part in parts], b_ref)
    gamma = state[5 + GAMMA : 6 + GAMMA, :]
    gammas = jnp.concatenate([gamma, gamma], axis=1)
    for place, piece in enumerate(pieces_of(total)):
        stream.wait(place)
        for rows, index in blocks_of(piece.start, piece.stop):
            z = (stream.ref[rows, :] - centre) * inv_dev
            normed_ref[rows, :] = jnp.where(keep_rows(index, 16, steps, length), z * gain + shift, 0.0).astype(LOW)
        drive_ref[piece, :] = dot(normed_ref[piece, :], b_ref[...], NT) * gammas
    sweep(drive_ref, state[5:6, :], state[6:7, :], steps, True, store_states(low_ref, drive_own_ref), 0)
    for part in parts:
        part.wait()
    assemble_output([part.ref.at[width : 2 * width] for part in parts], c_ref)
    assemble_glu([part.ref.at[2 * width : 4 * width] for part in parts], w_ref, quarter)
    up_own.wait()
    own = lanes_at(quarter, width)

    def spread_up(rows, index, carry):
        up_ref[rows, own] = up_own.ref[rows, :]
        return carry

    for_rows(0, total, 16, spread_up, unroll=4)
    for place, piece in enumerate(pieces_of(total)):
        for other in range(1, 4):
            lanes = lanes_at(quarter ^ other, width)
            up_ref[piece, lanes] = parts[other].ref[4 * width :, place * width : (place + 1) * width].astype(F32)
    bias_linear = feature[5 + BIAS_LINEAR : 6 + BIAS_LINEAR, :]
    bias_gate = feature[5 + BIAS_GATE : 6 + BIAS_GATE, :]
    pre_products(low_ref, c_ref, pre_ref)
    for piece in pieces_of(total):
        pre_piece(piece, pre_ref, normed_ref, skip, active_ref, slope_ref)
        held_ref[piece, :] = dot(active_ref[piece, :], w_ref[...], NT)
    for piece in pieces_of(total):
        for rows, index in blocks_of(piece.start, piece.stop):
            keep = keep_rows(index, 16, steps, length)
            linear = held_ref[rows, :full] + bias_linear
            gate = jax.nn.sigmoid(held_ref[rows, full:] + bias_gate)
            mixed = linear * gate
            up = jnp.where(keep, up_ref[rows, :], 0.0)
            grad_gated_ref[rows, :full] = (up * gate).astype(LOW)
            grad_gated_ref[rows, full:] = (up * mixed * (1.0 - gate)).astype(LOW)
            mixed_ref[rows, :] = jnp.where(keep, mixed, 0.0)
        pre_ref[piece, :] = dot(grad_gated_ref[piece, :], w_ref[...], NN)
    for piece in pieces_of(total):
        pre_grad_piece(piece, pre_ref, slope_ref, pre_grad_ref)
        drive_ref[piece, :] = dot(pre_grad_ref[piece, :], c_ref[...], NT)
    small_ref[...] = jnp.zeros_like(small_ref)
    to_feature_rows(lambda rows, index: stream.ref[rows, own] + mixed_ref[rows, own], order_ref, result, steps)
    adjoint_phase(
        low_ref, states, drive_own_ref, state, 5, length, drive_ref, grad_driven_ref, small_ref, False,
        beside_sweep(
            glu_products(grads_ref, 2 * width, grad_gated_ref, active_ref, quarter)
            + output_products(grads_ref, lambda: low_ref[:, 0:128], lambda: low_ref[:, states : states + 128], pre_grad_ref, states),
            grad_gated_ref, pre_grad_ref, normed_ref, quarter, small_ref,
        ),
    )
    scale = inv_dev * gain
    for piece in pieces_of(total):
        pre_ref[piece, :] = dot(grad_driven_ref[piece, :], b_ref[...], NN)
    plain, scaled = jnp.zeros((8, full), F32), jnp.zeros((8, full), F32)
    for place, piece in enumerate(pieces_of(total)):
        for rows, _ in blocks_of(piece.start, piece.stop):
            grad = pre_ref[rows, :] + skip * pre_grad_ref[rows, :].astype(F32)
            z = (stream.ref[rows, :] - centre) * inv_dev
            base.ref[rows, :] = scale * grad + up_ref[rows, :]
            plain += folded(grad)
            scaled += folded(grad * z)
        base.send_piece(place)
    input_products(grads_ref, grad_driven_ref, normed_ref, states)
    sent = narrowed([column_sum(plain), column_sum(scaled)], width)
    spread_rows(jnp.concatenate([sent, small_ref[:, 0:width]], axis=0), spread)
    send_halves(grads_ref, shares, 0)


def last_kernel(
    length_ref, ins, outs, held_ref, grad_state_ref, grad_gated_ref, pre_grad_ref, grad_driven_ref, small_ref, up_ref, grads_ref, pack_ref, low_ref
):
    (sums, norm1, feature_in, state_in, norm0, stream, base, gate, linear, w, slope, c, normed, active, low, drive_own, b, x) = ins
    kept, sent, up_out, grad_out = outs
    length, quarter = length_ref[0], own_quarter()
    total, full = stream.ref.shape
    steps = total // CHUNKS
    width = 128
    own = lanes_at(quarter, width)
    feature, norm_ref = feature_in.wait(), norm1.wait()
    state = state_in.wait()[...]
    counted = norm_ref[2:3, :]
    whole = total_rows(sums.wait())
    whole = jnp.concatenate([widened(whole, 0, 4), widened(whole, 4, 4)], axis=0)
    centre, inv_dev = norm_ref[0:1, :], norm_ref[1:2, :]
    scale = inv_dev * feature[5 + GAIN : 6 + GAIN, :]
    level = scale * whole[0:1, :] / counted
    tilt = scale * inv_dev * whole[1:2, :] / counted

    for place, piece in enumerate(pieces_of(total)):
        for value in (stream, base, gate, linear):
            value.wait(place)
        if place == 0:
            w.wait()
        for rows, index in blocks_of(piece.start, piece.stop):
            keep = keep_rows(index, 16, steps, length)
            up = base.ref[rows, :] - jnp.where(keep, level + (stream.ref[rows, :] - centre) * tilt, 0.0)
            up_ref[rows, :] = up
            up = jnp.where(keep, up, 0.0)
            grad_gated_ref[rows, :full] = (up * gate.ref[rows, :].astype(F32)).astype(LOW)
            grad_gated_ref[rows, full:] = (up * linear.ref[rows, :].astype(F32)).astype(LOW)
        held_ref[piece, :] = dot(grad_gated_ref[piece, :], w.ref[...], NN)
    for value in (slope, c):
        value.wait()
    for piece in pieces_of(total):
        pre_grad_piece(piece, held_ref, slope.ref, pre_grad_ref)
        grad_state_ref[piece, :] = dot(pre_grad_ref[piece, :], c.ref[...], NT)
    small_ref[...] = jnp.zeros_like(small_ref)

    def own_up(rows, index, carry):
        up_out.ref[rows, :] = up_ref[rows, own]
        return carry

    for_rows(0, total, 16, own_up, unroll=4)
    up_out.send()
    for value in (normed, active, low, drive_own):
        value.wait()
    adjoint_phase(
        low.ref, 128, drive_own.ref, state, 2, length, grad_state_ref, grad_driven_ref, small_ref, True,
        beside_sweep(
            glu_products(grads_ref, 2 * width, grad_gated_ref, active.ref, quarter)
            + output_products(grads_ref, lambda: low.ref[:, :128], lambda: low.ref[:, 128:], pre_grad_ref, state.shape[1]),
            grad_gated_ref, pre_grad_ref, normed.ref, quarter, small_ref,
        ),
    )
    b.wait()
    x.wait()
    held_ref[:, :width] = dot(grad_driven_ref[...], b.ref[:, own], NN)
    input_products(grads_ref, grad_driven_ref, normed.ref, state.shape[1])
    zero = jnp.zeros((8, width), F32)
    centre0, inv_dev0 = norm0.wait()[0:1, own], norm0.ref[1:2, own]
    skip = feature[SKIP : SKIP + 1, own]

    def back(rows, index, carry):
        grad = held_ref[rows, :width] + skip * pre_grad_ref[rows, own].astype(F32)
        grad_out.ref[rows, :] = grad
        z = (x.ref[rows, :] - centre0) * inv_dev0
        return carry[0] + folded(grad), carry[1] + folded(grad * z)

    plain, scaled = for_rows(0, total, 16, back, (zero, zero), unroll=4)
    grad_out.send()
    small_ref[6:7, 0:width] = column_sum(plain)
    small_ref[7:8, 0:width] = column_sum(scaled)
    pack_ref[...] = jnp.zeros_like(pack_ref)
    for place in range(8):
        pack_ref[place // 4 : place // 4 + 1, place % 4 * width : (place % 4 + 1) * width] = small_ref[place : place + 1, 0:width]
    exact = pack_ref[0:8, :]
    pack_ref[8:16, :] = exact - exact.astype(LOW).astype(F32)
    half = grads_ref.shape[0] // 2
    low_ref[...] = pack_ref[...].astype(LOW)
    mine = lax.axis_index("dp") & 1
    for out, which in ((kept, mine), (sent, 1 - mine)):
        out.send(0, half, source=grads_ref.at[rows_at(which, half)])
        out.send(half, 16, source=low_ref)


def send_halves(source_ref, outs, stage):
    kept = lax.axis_index("dp") >> stage & 1
    half = source_ref.shape[0] // 2
    for out, which in zip(outs, (kept, 1 - kept)):
        out.send(source=source_ref.at[rows_at(which, half)])


def add_kernel(length_ref, ins, outs, sum_ref, stage):
    kept, other = ins
    kept.wait()
    other.wait()
    for piece in range(0, kept.ref.shape[0], 16):
        at = slice(piece, piece + 16)
        sum_ref[at, :] = (kept.ref[at, :].astype(F32) + other.ref[at, :].astype(F32)).astype(LOW)
    send_halves(sum_ref, outs, stage)


def pair_kernel(length_ref, ins, outs, sum_ref, pack_ref):
    kept, other = ins
    for value in ins:
        value.wait()
    half = kept.ref.shape[0] - 16
    share = half // len(outs)
    small = kept.ref[half:, :].astype(F32) + other.ref[half:, :].astype(F32)
    small = small[0:8, :] + small[8:16, :]
    pack_ref[...] = jnp.concatenate([small, small - small.astype(LOW).astype(F32)], axis=0).astype(LOW)
    for piece in range(0, half, 16):
        at = slice(piece, piece + 16)
        sum_ref[at, :] = (kept.ref[at, :].astype(F32) + other.ref[at, :].astype(F32)).astype(LOW)
    for place, out in enumerate(outs):
        out.send(0, share, source=sum_ref.at[rows_at((lax.axis_index("dp") >> 1) ^ place, share)])
        out.send(share, 16, source=pack_ref)


def share_kernel(length_ref, ins, outs):
    *blocks, kept, other = ins
    out, small = outs
    share = kept.ref.shape[0]
    for value in ins:
        value.wait()
    for piece in range(0, share, 16):
        at = slice(piece, piece + 16)
        value = blocks[0].ref[at, :].astype(F32)
        for block in blocks[1:]:
            value += block.ref[at, :].astype(F32)
        out.ref[at, :] = value.astype(LOW)
        value = kept.ref[at, :].astype(F32) + other.ref[at, :].astype(F32)
        out.ref[share + piece : share + piece + 16, :] = value.astype(LOW)
    value = blocks[0].ref[share:, :].astype(F32)
    for block in blocks[1:]:
        value += block.ref[share:, :].astype(F32)
    small.ref[...] = value[0:8, :] + value[8:16, :]


def finish_kernel(length_ref, ins, outs, held_ref, order_ref):
    small0, bn1, norm0, feature, nu, theta, up, grad, x = ins
    nu_out, theta_out, gamma_out, skip_out, bias_out, gain_out, shift_out, out = outs
    length, quarter = length_ref[0], own_quarter()
    total, width = up.ref.shape
    steps = total // CHUNKS
    own = lanes_at(quarter, width)
    states = nu_out.ref.shape[1]
    for value in ins:
        value.wait()
    whole = total_rows(bn1.ref)
    held_ref[0:1, :] = widened(whole, 0, 4)
    held_ref[1:2, :] = widened(whole, 4, 4)
    held_ref[16:32, :width] = whole
    for place in range(8):
        held_ref[8 + place : 9 + place, :width] = small0.ref[place // 4 : place // 4 + 1, place % 4 * width : (place % 4 + 1) * width]
    for layer, first in ((0, 8), (1, 24)):
        at = slice(layer, layer + 1)
        nu_out.ref[at, :] = -jnp.exp(nu.ref[at, :]) * held_ref[first : first + 1, :states]
        theta_out.ref[at, :] = jnp.exp(theta.ref[at, :]) * held_ref[first + 1 : first + 2, :states]
        gamma_out.ref[at, :] = held_ref[first + 2 : first + 3, :states]
        skip_out.ref[at, :] = held_ref[first + 3 : first + 4, :width]
        bias_out.ref[layer, 0:1, :] = held_ref[first + 4 : first + 5, :width]
        bias_out.ref[layer, 1:2, :] = held_ref[first + 5 : first + 6, :width]
    shift_out.ref[0:1, :] = held_ref[14:15, :width]
    gain_out.ref[0:1, :] = held_ref[15:16, :width]
    shift_out.ref[1:2, :] = held_ref[0:1, own]
    gain_out.ref[1:2, :] = held_ref[1:2, own]
    counted = norm0.ref[2:3, own]
    centre, inv_dev = norm0.ref[0:1, own], norm0.ref[1:2, own]
    level = held_ref[14:15, :width] / counted
    tilt = held_ref[15:16, :width] * inv_dev / counted
    scale = inv_dev * feature.ref[GAIN : GAIN + 1, own]

    def load(rows, index):
        keep = keep_rows(index, CHUNKS, steps, length)
        inner = grad.ref[rows, :] - level - (x.ref[rows, :] - centre) * tilt
        return up.ref[rows, :] + jnp.where(keep, scale * inner, 0.0)

    to_feature_rows(load, order_ref, out, steps)


def widen_kernel(length_ref, ins, outs, held_ref):
    half = outs[0].target.shape[1]
    groups = len(ins)
    share = ins[0].ref.shape[0] // 2
    stages = groups.bit_length() - 1
    for layer in (1, 0):
        for place, value in enumerate(ins):
            owner = lax.axis_index("dp") ^ place
            at = (owner & 1) * (groups // 2) + (owner >> 1)
            if layer == 1:
                at = sum((owner >> stage & 1) << (stages - 1 - stage) for stage in range(stages))
            held_ref[layer, rows_at(at, share), :] = value.ref[layer * share : (layer + 1) * share, :].astype(F32)
        for out, first, size in zip(outs, (0, half, 2 * half), (half, half, 2 * half)):
            out.send(layer, 1, source=held_ref.at[pl.ds(layer, 1), pl.ds(first, size)])


def shape(*dims, dtype=F32):
    return jax.ShapeDtypeStruct(dims, dtype)


def swap(value, bit, sharers):
    pairs = [(q * sharers + r, (q ^ bit) * sharers + r) for q in range(4) for r in range(sharers)]
    return lax.ppermute(value, "state", pairs)


def across(value, axes):
    return lax.all_to_all(value, axes, 0, 0, tiled=True)


def local(
    inputs, lengths, cotangent, bn_gain, bn_bias, b_weight, c_weight, nu_log, theta_log, gamma_log, skip_weight,
    glu_weight, glu_bias, dp_size, state_size,
):
    sharers = state_size // 4
    place = lax.axis_index("state").astype(jnp.int32)

    def joined(value, axis):
        if sharers == 1:
            return value
        groups = [[q * sharers + r for r in range(sharers)] for q in range(4)]
        return lax.all_gather(value, "state", axis=axis, axis_index_groups=groups, tiled=True)

    def own(value, axis):
        if sharers == 1:
            return value
        size = value.shape[axis] // sharers
        return lax.dynamic_slice_in_dim(value, place % sharers * size, size, axis)

    inputs, cotangent = joined(inputs, 1), joined(cotangent, 1)
    bn_gain, bn_bias, skip_weight = joined(bn_gain, 1), joined(bn_bias, 1), joined(skip_weight, 1)
    nu_log, theta_log, gamma_log = joined(nu_log, 1), joined(theta_log, 1), joined(gamma_log, 1)
    b_weight, c_weight = joined(b_weight, 2), joined(c_weight, 2)
    glu_weight, glu_bias = joined(glu_weight, 2), joined(glu_bias, 2)
    width, total = inputs.shape[1:]
    full = b_weight.shape[3]
    states = b_weight.shape[2] * 4
    own_states = b_weight.shape[2]
    share = 4 * width // dp_size
    piece = total // PIECES

    stages = dp_size.bit_length() - 1

    def exchange(value, bit):
        return lax.ppermute(value, "dp", [(i, i ^ bit) for i in range(dp_size)])

    def add(halves, stage):
        kept, other = halves
        rows = kept.shape[0]
        return call_small(
            functools.partial(add_kernel, stage=stage + 1),
            (shape(rows // 2, full, dtype=LOW),) * 2,
            [pltpu.VMEM((rows, full), LOW)],
            (kept, other),
            "add",
        )


    b_weight, c_weight = b_weight.reshape(LAYERS, width, full), c_weight.reshape(LAYERS, width, full)
    glu_weight = glu_weight.reshape(LAYERS, 2 * width, full)
    tokens, sums, first = call(
        enter_kernel,
        (
            shape(total, width),
            shape(dp_size, 8, width),
            shape(6 * width + PARAM_ROWS, full, dtype=LOW),
        ),
        [pltpu.VMEM((total, width), F32), pltpu.VMEM((PARAM_ROWS, width), F32)],
        (lengths, inputs[0], bn_gain, bn_bias, skip_weight, glu_bias, nu_log, theta_log, gamma_log, b_weight, c_weight, glu_weight),
        "enter",
        pieces={1: piece},
        axes={1: 1},
        late=(9, 10, 11),
    )
    near, far = swap(first, 1, sharers), swap(first, 2, sharers)
    (stats,) = call_small(total_kernel, (shape(8, width),), [], (across(sums, "dp"),), "total")
    stats_near, stats_far = swap(stats, 1, sharers), swap(stats, 2, sharers)
    cotangent, tokens = lax.optimization_barrier((cotangent, tokens))
    up_own, later = call(
        cotangent_kernel,
        (
            shape(total, width),
            shape(6 * width, full, dtype=LOW),
        ),
        [pltpu.VMEM((total, width), F32)],
        (lengths, cotangent[0], b_weight, c_weight, glu_weight),
        "cotangent",
        pieces={1: piece},
        axes={1: 1},
        late=(2, 3, 4),
    )
    near, far, stats_near, stats_far, later = lax.optimization_barrier((near, far, stats_near, stats_far, later))
    parts = (first, near, far, swap(far, 1, sharers))
    all_stats = (stats, stats_near, stats_far, swap(stats_far, 1, sharers))
    later_far = swap(later, 2, sharers)
    feature, state, norm0, normed0, drive0, low0, stream1, linear0, gate0, slope0, active0, b_all, c_all, w_all, sums1 = call(
        start_kernel,
        (
            shape(PARAM_ROWS, full),
            shape(8, states),
            shape(8, full),
            shape(total, full, dtype=LOW),
            shape(total, 256),
            shape(total, 256, dtype=LOW),
            shape(total, full),
            shape(total, full, dtype=LOW),
            shape(total, full, dtype=LOW),
            shape(total, full, dtype=LOW),
            shape(total, full, dtype=LOW),
            shape(2 * states, full, dtype=LOW),
            shape(2 * states, full, dtype=LOW),
            shape(2 * full, full, dtype=LOW),
            shape(dp_size, 8, width),
        ),
        [
            pltpu.VMEM((8, full), F32),
            pltpu.VMEM((total, full), F32),
            pltpu.VMEM((total, 2 * states), F32),
            pltpu.VMEM((total, full), F32),
            pltpu.VMEM((total, 2 * full), F32),
            pltpu.VMEM((2 * states, full), LOW),
            pltpu.VMEM((2 * states, full), LOW),
            pltpu.VMEM((2 * full, full), LOW),
            pltpu.VMEM((total, 2 * states), LOW),
        ],
        (lengths, *all_stats, tokens, *parts),
        "start",
        pieces={5: piece} | {place: width for place in (6, 7, 8, 9)},
        order=(4, 5),
        bare=(11, 12, 13),
        flops=1e9,
    )
    sums1 = across(sums1, "dp")
    later_far, sums1 = lax.optimization_barrier((later_far, sums1))
    later_parts = (later, swap(later, 1, sharers), later_far, swap(later_far, 1, sharers))
    result, base, bn1, norm1, *halves1 = call(
        middle_kernel,
        (
            shape(width, total),
            shape(total, full),
            shape(dp_size, 16, width),
            shape(8, full),
            shape(2 * width, full, dtype=LOW),
            shape(2 * width, full, dtype=LOW),
        ),
        [
            pltpu.VMEM((8, full), F32),
            pltpu.VMEM((2 * states, full), LOW),
            pltpu.VMEM((2 * states, full), LOW),
            pltpu.VMEM((2 * full, full), LOW),
            pltpu.VMEM((total, full), LOW),
            pltpu.VMEM((total, 2 * states), F32),
            pltpu.VMEM((total, 256), F32),
            pltpu.VMEM((total, 2 * states), LOW),
            pltpu.VMEM((total, full), F32),
            pltpu.VMEM((total, full), LOW),
            pltpu.VMEM((total, 2 * full), F32),
            pltpu.VMEM((total, full), F32),
            pltpu.VMEM((total, full), F32),
            pltpu.VMEM((total, width), F32),
            pltpu.VMEM((total, full), F32),
            pltpu.VMEM((total, 2 * full), LOW),
            pltpu.VMEM((total, full), LOW),
            pltpu.VMEM((total, 2 * states), LOW),
            pltpu.VMEM((4 * width, full), LOW),
        ],
        (lengths, sums1, norm0, feature, state, stream1, up_own, *later_parts),
        "middle",
        pieces={5: piece} | {place: width for place in (7, 8, 9, 10)},
        late=(6,),
        bare=(4, 5),
        flops=1e9,
    )
    bn1 = across(bn1, "dp")
    halves1[1] = exchange(halves1[1], 1)
    halves1 = list(add(halves1, 0))
    bn1, *halves1 = lax.optimization_barrier((bn1, *halves1))
    halves1[1] = exchange(halves1[1], 2)
    kept0, sent0, up0, grad0 = call(
        last_kernel,
        (
            shape(2 * width + 16, full, dtype=LOW),
            shape(2 * width + 16, full, dtype=LOW),
            shape(total, width),
            shape(total, width),
        ),
        [
            pltpu.VMEM((total, full), F32),
            pltpu.VMEM((total, 2 * states), F32),
            pltpu.VMEM((total, 2 * full), LOW),
            pltpu.VMEM((total, full), LOW),
            pltpu.VMEM((total, 2 * states), LOW),
            pltpu.VMEM((8, full), F32),
            pltpu.VMEM((total, full), F32),
            pltpu.VMEM((4 * width, full), LOW),
            pltpu.VMEM((16, full), F32),
            pltpu.VMEM((16, full), LOW),
        ],
        (lengths, bn1, norm1, feature, state, norm0, stream1, base, gate0, linear0, w_all, slope0, c_all, normed0, active0, low0,
         drive0, b_all, tokens),
        "last",
        bare=(0, 1),
        pieces={6: piece, 7: piece, 8: piece, 9: piece},
        late=tuple(range(11, 19)),
        flops=1e11,
    )
    *halves1, kept0, sent0 = lax.optimization_barrier((*halves1, kept0, sent0))
    sent0 = exchange(sent0, 1)
    for stage in range(1, stages):
        if stage > 1:
            halves1[1] = exchange(halves1[1], 1 << stage)
        if stage < stages - 1:
            halves1 = list(add(halves1, stage))
    kept0, *halves1 = lax.optimization_barrier((kept0, *halves1))
    blocks = call_small(
        pair_kernel,
        (shape(share + 16, full, dtype=LOW),) * (dp_size // 2),
        [pltpu.VMEM((2 * width, full), LOW), pltpu.VMEM((16, full), LOW)],
        (kept0, sent0),
        "pair",
    )
    blocks = [blocks[0]] + [exchange(blocks[place], 2 * place) for place in range(1, dp_size // 2)]
    back, small0 = call_small(
        share_kernel,
        (shape(2 * share, full, dtype=LOW), shape(8, full)),
        [],
        (*blocks, *halves1),
        "share",
    )
    backs = [back] + [exchange(back, place) for place in range(2, dp_size, 2)]
    backs = [each for first in backs for each in (first, exchange(first, 1))]
    grad_nu, grad_theta, grad_gamma, grad_skip, grad_bias, grad_gain, grad_shift, grad_inputs = call(
        finish_kernel,
        (
            shape(LAYERS, own_states),
            shape(LAYERS, own_states),
            shape(LAYERS, own_states),
            shape(LAYERS, width),
            shape(LAYERS, 2, width),
            shape(LAYERS, width),
            shape(LAYERS, width),
            shape(width, total),
        ),
        [pltpu.VMEM((32, full), F32), pltpu.VMEM((total, width), F32)],
        (lengths, small0, bn1, norm0, feature, nu_log, theta_log, up0, grad0, tokens),
        "finish",
    )
    grad_b, grad_c, grad_glu = call_small(
        widen_kernel,
        (shape(LAYERS, width, full), shape(LAYERS, width, full), shape(LAYERS, 2 * width, full)),
        [pltpu.VMEM((LAYERS, 4 * width, full), F32)],
        tuple(backs),
        "widen",
        sent=True,
    )
    grad_b = grad_b.reshape(LAYERS, 2, own_states, full)
    grad_c = grad_c.reshape(LAYERS, 2, own_states, full)
    grad_glu = grad_glu.reshape(LAYERS, 2, width, full)
    return (
        own(result[None], 1),
        own(grad_inputs[None], 1),
        own(grad_gain, 1),
        own(grad_shift, 1),
        own(grad_b, 2),
        own(grad_c, 2),
        own(grad_nu, 1),
        own(grad_theta, 1),
        own(grad_gamma, 1),
        own(grad_skip, 1),
        own(grad_glu, 2),
        own(grad_bias, 2),
    )


def solution(mesh):
    in_specs = (
        P("dp", "state", None),
        P("dp"),
        P("dp", "state", None),
        P(None, "state"),
        P(None, "state"),
        P(None, None, "state", None),
        P(None, None, "state", None),
        P(None, "state"),
        P(None, "state"),
        P(None, "state"),
        P(None, "state"),
        P(None, None, "state", None),
        P(None, None, "state"),
    )
    out_specs = (
        P("dp", "state", None),
        P("dp", "state", None),
        P(None, "state"),
        P(None, "state"),
        P(None, None, "state", None),
        P(None, None, "state", None),
        P(None, "state"),
        P(None, "state"),
        P(None, "state"),
        P(None, "state"),
        P(None, None, "state", None),
        P(None, None, "state"),
    )
    step = functools.partial(local, dp_size=mesh.shape["dp"], state_size=mesh.shape["state"])
    return jax.shard_map(step, mesh=mesh, in_specs=in_specs, out_specs=out_specs, check_vma=False)
```

```python
import functools

import jax
import jax.numpy as jnp
from jax import lax
from jax.experimental import pallas as pl
from jax.experimental.pallas import tpu as pltpu
from jax.sharding import PartitionSpec as P

LAYERS = 2
CHUNKS = 16
PIECES = 4
EPSILON = 1e-05
F32 = jnp.float32
LOW = jnp.bfloat16
PARAM_ROWS = 32
OWN_MEAN = 16
VMEM_BYTES = 64 * 1024 * 1024
SMALL_VMEM_BYTES = 8 * 1024 * 1024

GAIN, SHIFT, SKIP, BIAS_LINEAR, BIAS_GATE = range(5)
RATE_RE, RATE_IM, GAMMA = range(3)

NN = (((1,), (0,)), ((), ()))
NT = (((1,), (1,)), ((), ()))
TN = (((0,), (0,)), ((), ()))


def dot(left, right, dims):
    return lax.dot_general(left, right, dims, preferred_element_type=F32)


def rows_at(index, size):
    return pl.ds(pl.multiple_of(index * size, size), size)


def lanes_at(quarter, width):
    return pl.ds(pl.multiple_of(quarter * width, width), width)


def for_rows(first, last, size, body, init=0, unroll=2):
    def step(index, carry):
        return body(rows_at(index, size), index, carry)

    return lax.fori_loop(first // size, last // size, step, init, unroll=unroll)


def blocks_of(first, last, size=16):
    return [(slice(at, at + size), at // size) for at in range(first, last, size)]


def pieces_of(total):
    size = total // PIECES
    return [slice(at, at + size) for at in range(0, total, size)]


def own_quarter():
    return (lax.axis_index("state") // (lax.axis_size("state") // 4)).astype(jnp.int32)


def keep_rows(first_step, rows, steps, length):
    row = lax.broadcasted_iota(jnp.int32, (rows, 1), 0)
    position = (row % CHUNKS) * steps + row // CHUNKS + first_step
    return position < length


def gelu_parts(value):
    return 0.5 + 0.5 * lax.erf(value * 0.7071067811865476), jnp.exp(value * value * -0.5) * 0.3989422804014327


def squared(re, im, times):
    for _ in range(times):
        re, im = re * re - im * im, 2.0 * re * im
    return re, im


def folded(value):
    return value[0:8, :] + value[8:16, :]


def column_sum(value):
    return jnp.sum(value, axis=0, keepdims=True)


def chunk_starts(re, im, rate_re, rate_im, reverse):
    row = lax.broadcasted_iota(jnp.int32, re.shape, 0)

    def moved(value, by):
        if reverse:
            return jnp.where(row < CHUNKS - by, pltpu.roll(value, CHUNKS - by, 0), 0.0)
        return jnp.where(row >= by, pltpu.roll(value, by, 0), 0.0)

    by = 1
    while by < CHUNKS:
        past_re, past_im = moved(re, by), moved(im, by)
        re, im = (
            re + rate_re * past_re - rate_im * past_im,
            im + rate_re * past_im + rate_im * past_re,
        )
        rate_re, rate_im = squared(rate_re, rate_im, 1)
        by *= 2
    return moved(re, 1), moved(im, 1)


def sweep(drive_ref, rate_re, rate_im, steps, reverse, emit, extra, after=None, beside=None, unroll=4):
    states = rate_re.shape[1]
    shape = (CHUNKS, states)
    wide_re = jnp.broadcast_to(rate_re, shape)
    wide_im = jnp.broadcast_to(rate_im, shape)

    def advance(index, re, im):
        place = steps - 1 - index if reverse else index
        rows = slice(place * CHUNKS, (place + 1) * CHUNKS) if isinstance(place, int) else rows_at(place, CHUNKS)
        drive_re = drive_ref[rows, :states]
        drive_im = drive_ref[rows, states:]
        new_re = (wide_re * re + drive_re) - wide_im * im
        new_im = (wide_re * im + drive_im) + wide_im * re
        return rows, place, new_re, new_im, drive_re, drive_im

    def first(index, carry):
        _, _, re, im, _, _ = advance(index, *carry)
        return re, im

    def second(index, carry):
        re, im, held = carry
        rows, place, re, im, drive_re, drive_im = advance(index, re, im)
        return re, im, emit(rows, place, re, im, drive_re, drive_im, held)

    zero = jnp.zeros(shape, F32)
    re, im = lax.fori_loop(0, steps, first, (zero, zero), unroll=unroll)
    far_re, far_im = rate_re, rate_im
    power = 1
    while power < steps:
        far_re, far_im = squared(far_re, far_im, 1)
        power *= 2
    re, im = chunk_starts(re, im, far_re, far_im, reverse)
    carry = (re, im, extra)
    for piece in range(PIECES):
        size = steps // PIECES
        if beside is not None:
            beside[piece]()
            for index in range(piece * size, (piece + 1) * size):
                carry = second(index, carry)
        else:
            carry = lax.fori_loop(piece * size, (piece + 1) * size, second, carry, unroll=unroll)
        if after is not None:
            after(PIECES - 1 - piece if reverse else piece)
    return carry[2]


class Arrival:
    def __init__(self, source, ref, done, first, size, axis):
        self.ref = ref
        self.copies = []
        whole = ref.shape[axis]
        for piece, start in enumerate(range(0, whole, size)):
            where = (slice(None),) * axis + (pl.ds(start, min(size, whole - start)),)
            self.copies.append(
                pltpu.make_async_copy(source.at[where], ref.at[where], done.at[first + piece])
                if size < whole
                else pltpu.make_async_copy(source, ref, done.at[first])
            )
        self.short = whole % size > 0
        self.waited = set()

    def start(self, piece):
        last = len(self.copies) - self.short
        if piece < 0 and self.short:
            self.copies[-1].start()
        if 0 <= piece < last:
            self.copies[piece].start()

    def wait(self, piece=None):
        for place in range(len(self.copies)) if piece is None else (piece,):
            if place not in self.waited:
                self.copies[place].wait()
                self.waited.add(place)
        return self.ref


class Departure:
    def __init__(self, target, ref, done, first):
        self.target, self.ref, self.done, self.first = target, ref, done, first
        self.copies = []

    def send(self, start=None, size=None, source=None):
        place = self.done.at[self.first + len(self.copies)]
        where = self.target if start is None else self.target.at[pl.ds(start, size)]
        if source is None:
            source = self.ref if start is None else self.ref.at[pl.ds(start, size)]
        self.copies.append(pltpu.make_async_copy(source, where, place))
        self.copies[-1].start()

    def send_piece(self, piece):
        size = self.target.shape[0] // PIECES
        self.send(piece * size, size)

    def send_unsent(self):
        if not self.copies:
            self.send()

    def finish(self):
        for copy in self.copies:
            copy.wait()


class Resident:
    def __init__(self, ref):
        self.ref = ref

    def wait(self, piece=None):
        return self.ref

    def send(self, start=None, size=None, source=None):
        if source is not None and start is None:
            self.ref[...] = source[...]
        elif source is not None:
            self.ref[start : start + size, :] = source[...]


def call_small(kernel, outs, scratch, args, name, sent=False, into=()):
    def body(*refs):
        count, results = len(args), len(outs)
        ins, refs = [Resident(ref) for ref in refs[:count]], refs[count + len(into) :]
        if not sent:
            kernel(None, ins, [Resident(ref) for ref in refs[:results]], *refs[results:])
            return
        targets, copied, scratch_refs = refs[:results], refs[results], refs[results + 1 :]
        departures = [Departure(target, None, copied, place * LAYERS) for place, target in enumerate(targets)]
        kernel(None, ins, departures, *scratch_refs)
        for departure in departures:
            departure.finish()

    return pl.pallas_call(
        body,
        out_shape=tuple(outs),
        in_specs=[pl.BlockSpec(memory_space=pltpu.VMEM)] * len(args) + [pl.BlockSpec(memory_space=pl.ANY)] * len(into),
        out_specs=tuple(pl.BlockSpec(memory_space=pl.ANY if sent else pltpu.VMEM) for _ in outs),
        input_output_aliases={len(args) + place: place for place in range(len(into))},
        scratch_shapes=([pltpu.SemaphoreType.DMA((LAYERS * len(outs),))] if sent else []) + list(scratch),
        compiler_params=pltpu.CompilerParams(vmem_limit_bytes=SMALL_VMEM_BYTES),
        cost_estimate=pl.CostEstimate(flops=0, bytes_accessed=0, transcendentals=0),
        name=name,
    )(*args, *into)


def call(kernel, outs, scratch, args, name, pieces=None, axes=None, bare=(), late=(), order=None, flops=0):
    pieces, axes = pieces or {}, axes or {}
    along = [axes.get(place, 0) for place in range(1, len(args))]
    sizes = [pieces.get(place, args[place].shape[axis]) for place, axis in enumerate(along, 1)]
    counts = [-(-args[place].shape[axis] // size) for place, (axis, size) in enumerate(zip(along, sizes), 1)]
    slots = 6
    copies_in = [pltpu.VMEM(a.shape, a.dtype) for a in args[1:]]
    copies_out = [pltpu.VMEM((8, 128) if place in bare else o.shape, o.dtype if place not in bare else F32) for place, o in enumerate(outs)]

    def body(*refs):
        refs = list(refs)

        def take(count):
            got = refs[:count]
            del refs[:count]
            return got

        (length_ref,) = take(1)
        sources = take(len(args) - 1)
        targets = take(len(outs))
        in_refs, out_refs = take(len(args) - 1), take(len(outs))
        arrived, sent = take(2)
        arrivals, first = [], 0
        for source, ref, size, count, axis in zip(sources, in_refs, sizes, counts, along):
            arrivals.append(Arrival(source, ref, arrived, first, size, axis))
            first += count
        for group in (False, True):
            for piece in (-1, *(order or ()), *(piece for piece in range(max(counts)) if piece not in (order or ()))):
                for place, arrival in enumerate(arrivals, 1):
                    if (place in late) is group:
                        arrival.start(piece)
        departures = [
            Departure(target, ref, sent, place * slots) for place, (target, ref) in enumerate(zip(targets, out_refs))
        ]
        kernel(length_ref, arrivals, departures, *refs)
        for arrival in arrivals:
            arrival.wait()
        for departure in departures:
            departure.send_unsent()
        for departure in departures:
            departure.finish()

    return pl.pallas_call(
        body,
        out_shape=tuple(outs),
        in_specs=[pl.BlockSpec(memory_space=pltpu.SMEM if place == 0 else pl.ANY) for place in range(len(args))],
        out_specs=tuple(pl.BlockSpec(memory_space=pl.ANY) for _ in outs),
        scratch_shapes=[
            *copies_in,
            *copies_out,
            pltpu.SemaphoreType.DMA((sum(counts),)),
            pltpu.SemaphoreType.DMA((slots * len(outs),)),
            *scratch,
        ],
        compiler_params=pltpu.CompilerParams(vmem_limit_bytes=VMEM_BYTES),
        cost_estimate=pl.CostEstimate(flops=int(flops), bytes_accessed=0, transcendentals=0),
        name=name,
    )(*args)


def from_feature_rows(source, held_ref, steps, emit, init, after):
    length = source.ref.shape[1]
    blocks = length // 128
    for block in range(blocks):
        if block % (blocks // PIECES) == 0:
            source.wait(block // (blocks // PIECES))
        lanes = slice(block * 128, (block + 1) * 128)
        held_ref[lanes, :] = source.ref[:, lanes].T

    def step(index, carry):
        return emit(rows_at(index, CHUNKS), index, held_ref[pl.ds(index, CHUNKS, stride=steps), :], carry)

    carry = init
    for piece in range(PIECES):
        size = steps // PIECES
        carry = lax.fori_loop(piece * size, (piece + 1) * size, step, carry, unroll=4)
        after(piece)
    return carry


def to_feature_rows(load, held_ref, out, steps):
    length = out.ref.shape[1]

    def step(index, carry):
        held_ref[pl.ds(index, CHUNKS, stride=steps), :] = load(rows_at(index, CHUNKS), index)
        return carry

    lax.fori_loop(0, steps, step, 0, unroll=4)
    for block in range(length // 128):
        lanes = slice(block * 128, (block + 1) * 128)
        out.ref[:, lanes] = held_ref[lanes, :].T
    out.send()


def spread_rows(value, out):
    for group in range(out.ref.shape[0]):
        out.ref[group, :, :] = value
    out.send()


def narrowed(values, width):
    return jnp.concatenate([v[:, at : at + width] for v in values for at in range(0, v.shape[1], width)], axis=0)


def widened(rows, first, count):
    return jnp.concatenate([rows[first + place : first + place + 1, :] for place in range(count)], axis=1)


def total_rows(sums_ref):
    value = sums_ref[0, :, :]
    for other in range(1, sums_ref.shape[0]):
        value += sums_ref[other, :, :]
    return value


def assemble_states(parts, whole_ref):
    half = parts[0].shape[0] // 2
    states = half * len(parts)
    for place, part in enumerate(parts):
        whole_ref[place * half : (place + 1) * half, :] = part[:half, :]
        whole_ref[states + place * half : states + (place + 1) * half, :] = part[half:, :]


def assemble_output(parts, whole_ref):
    half = parts[0].shape[0] // 2
    states = half * len(parts)
    for place, part in enumerate(parts):
        whole_ref[place * half : (place + 1) * half, :] = part[:half, :]
        whole_ref[states + place * half : states + (place + 1) * half, :] = -part[half:, :]


def assemble_glu(parts, whole_ref, quarter):
    half = parts[0].shape[0] // 2
    width = half * len(parts)
    for place, part in enumerate(parts):
        whole_ref[lanes_at(quarter ^ place, half), :] = part[:half, :]
        whole_ref[pl.ds(pl.multiple_of(width + (quarter ^ place) * half, half), half), :] = part[half:, :]


def norm_rows(sums, counted):
    centre = sums[0:1, :] / counted
    meansq = sums[1:2, :] / counted
    return centre, lax.rsqrt(meansq - centre * centre + EPSILON)


def drive_phase(normed_ref, b_ref, drive_ref, gamma):
    drive_ref[...] = dot(normed_ref[...], b_ref[...], NT) * jnp.concatenate([gamma, gamma], axis=1)


def store_states(low_ref, drive_own_ref):
    def emit(rows, step, re, im, drive_re, drive_im, held):
        states = re.shape[1]
        low_ref[rows, :states] = re.astype(LOW)
        low_ref[rows, states:] = im.astype(LOW)
        drive_own_ref[rows, :128] = drive_re[:, :128].astype(drive_own_ref.dtype)
        drive_own_ref[rows, 128:] = drive_im[:, :128].astype(drive_own_ref.dtype)
        return held

    return emit


def pre_products(low_ref, c_ref, held_ref):
    total, full = low_ref.shape[0], c_ref.shape[1]
    for piece in pieces_of(total):
        held_ref[piece, :full] = dot(low_ref[piece, :], c_ref[...], NN)


def pre_piece(piece, held_ref, normed_ref, skip, active_ref, slope_ref):
    full = normed_ref.shape[1]
    for rows, _ in blocks_of(piece.start, piece.stop):
        value = held_ref[rows, :full] + skip * normed_ref[rows, :].astype(F32)
        cdf, density = gelu_parts(value)
        active_ref[rows, :] = (value * cdf).astype(LOW)
        slope_ref[rows, :] = (cdf + value * density).astype(slope_ref.dtype)


def pre_grad_piece(piece, held_ref, slope_ref, pre_grad_ref):
    full = slope_ref.shape[1]
    for rows, _ in blocks_of(piece.start, piece.stop):
        pre_grad_ref[rows, :] = (held_ref[rows, :full] * slope_ref[rows, :].astype(F32)).astype(LOW)


def skip_sums(pre_grad_ref, normed_ref, quarter, small_ref):
    own = lanes_at(quarter, 128)
    value = jnp.zeros((8, 128), F32)
    for rows, _ in blocks_of(0, pre_grad_ref.shape[0]):
        value += folded(pre_grad_ref[rows, own].astype(F32) * normed_ref[rows, own].astype(F32))
    small_ref[3:4, 0:128] = column_sum(value)


def bias_sums(grad_gated_ref, quarter, small_ref):
    for place in range(2):
        lanes = lanes_at(quarter + 4 * place, 128)
        value = jnp.zeros((8, 128), F32)
        for rows, _ in blocks_of(0, grad_gated_ref.shape[0]):
            value += folded(grad_gated_ref[rows, lanes].astype(F32))
        small_ref[4 + place : 5 + place, 0:128] = column_sum(value)


def together(*parts):
    def run():
        for part in parts:
            part()

    return run


def adjoint_phase(low_ref, im_lane, drive_own_ref, state, first_row, length, grad_state_ref, grad_driven_ref, small_ref, reverse, beside):
    total = grad_state_ref.shape[0]
    steps = total // CHUNKS
    states = state.shape[1]
    rate_re = state[first_row : first_row + 1, :]
    rate_im = state[first_row + 1 : first_row + 2, :]
    gamma = jnp.broadcast_to(state[first_row + 2 : first_row + 3, :], (CHUNKS, states))

    def emit(rows, step, re, im, drive_re, drive_im, held):
        out_re, out_im = gamma * re, gamma * im
        if not reverse:
            keep = keep_rows(step, CHUNKS, steps, length)
            out_re, out_im = jnp.where(keep, out_re, 0.0), jnp.where(keep, out_im, 0.0)
        grad_driven_ref[rows, :states] = out_re.astype(LOW)
        grad_driven_ref[rows, states:] = out_im.astype(LOW)
        one, two, three = held
        own_re, own_im = re[:, :128], im[:, :128]
        late_re, late_im = own_re - drive_re[:, :128], own_im - drive_im[:, :128]
        low_re = low_ref[rows, :128].astype(F32)
        low_im = low_ref[rows, im_lane : im_lane + 128].astype(F32)
        one = one + folded(late_re * low_re + late_im * low_im)
        two = two + folded(late_im * low_re - late_re * low_im)
        three = three + folded(
            own_re * drive_own_ref[rows, :128].astype(F32) + own_im * drive_own_ref[rows, 128:].astype(F32)
        )
        return one, two, three

    zero = jnp.zeros((8, 128), F32)
    one, two, three = sweep(grad_state_ref, rate_re, -rate_im, steps, reverse, emit, (zero, zero, zero), beside=beside)
    small_ref[0:1, 0:128] = column_sum(one)
    small_ref[1:2, 0:128] = column_sum(two)
    small_ref[2:3, 0:128] = column_sum(three)


def glu_products(grads_ref, first, grad_gated_ref, active_ref, quarter):
    full = active_ref.shape[1]

    def product(place):
        lanes = pl.ds(pl.multiple_of(place * full + quarter * 128, 128), 128)
        got = dot(grad_gated_ref[:, lanes], active_ref[...], TN)
        grads_ref[first + place * 128 : first + (place + 1) * 128, :] = got.astype(LOW)

    return [functools.partial(product, place) for place in range(2)]


def output_products(grads_ref, low_re, low_im, pre_grad_ref, states):
    half = states // 4

    def product(place, low, sign):
        got = sign * dot(low(), pre_grad_ref[...], TN)[:half, :]
        grads_ref[2 * half + place * half : 2 * half + (place + 1) * half, :] = got.astype(LOW)

    return [functools.partial(product, 0, low_re, 1.0), functools.partial(product, 1, low_im, -1.0)]


def beside_sweep(products, grad_gated_ref, pre_grad_ref, normed_ref, quarter, small_ref):
    first, second, third, fourth = products
    return (
        together(first, functools.partial(bias_sums, grad_gated_ref, quarter, small_ref)),
        together(second, functools.partial(skip_sums, pre_grad_ref, normed_ref, quarter, small_ref)),
        third,
        fourth,
    )


def input_products(grads_ref, grad_driven_ref, normed_ref, states):
    half = states // 4
    for place in range(2):
        lanes = slice(place * states, place * states + 128)
        got = dot(grad_driven_ref[:, lanes], normed_ref[...], TN)[:half, :]
        grads_ref[place * half : (place + 1) * half, :] = got.astype(LOW)


def enter_kernel(length_ref, ins, outs, held_ref, params_ref):
    x, gain, shift, skip, bias, nu, theta, gamma, b, c, w = ins
    tokens, spread, first_out = outs
    length = length_ref[0]
    width, total = x.ref.shape
    steps = total // CHUNKS

    def emit(rows, index, value, carry):
        tokens.ref[rows, :] = value
        kept = jnp.where(keep_rows(index, CHUNKS, steps, length), value, 0.0)
        return carry[0] + folded(kept), carry[1] + folded(kept * kept)

    zero = jnp.zeros((8, width), F32)
    plain, square = from_feature_rows(x, held_ref, steps, emit, (zero, zero), tokens.send_piece)
    plain = column_sum(plain)
    counted = jnp.full((1, width), length, jnp.int32).astype(F32)
    spread_rows(jnp.concatenate([plain, column_sum(square), counted, jnp.zeros((5, width), F32)], axis=0), spread)
    mean = plain / counted

    each = total // PIECES

    def centred(rows, index, carry):
        place = pl.ds(pl.multiple_of(4 * width + index * 32 % each, 32), 32)
        first_out.ref[place, lanes_at(index * 32 // each, width)] = (tokens.ref[rows, :] - mean).astype(LOW)
        return carry

    for_rows(0, total, 32, centred, unroll=4)
    for value in (gain, shift, skip, bias, nu, theta, gamma):
        value.wait()
    params_ref[...] = jnp.zeros(params_ref.shape, F32)
    for layer in range(LAYERS):
        first = 5 * layer
        params_ref[first + GAIN : first + GAIN + 1, :] = gain.ref[layer : layer + 1, :]
        params_ref[first + SHIFT : first + SHIFT + 1, :] = shift.ref[layer : layer + 1, :]
        params_ref[first + SKIP : first + SKIP + 1, :] = skip.ref[layer : layer + 1, :]
        params_ref[first + BIAS_LINEAR : first + BIAS_GATE + 1, :] = bias.ref[layer, :, :]
        first = 10 + 3 * layer
        for row, source in enumerate((nu, theta, gamma)):
            params_ref[first + row : first + row + 1, : source.ref.shape[1]] = source.ref[layer : layer + 1, :]
    params_ref[OWN_MEAN : OWN_MEAN + 1, :] = mean
    rest = params_ref[...]
    first_out.ref[6 * width :, :] = jnp.zeros((32, 4 * width), LOW)
    for place in range(3):
        high = rest.astype(LOW)
        first_out.ref[6 * width : 6 * width + PARAM_ROWS, place * width : (place + 1) * width] = high
        rest = rest - high.astype(F32)
    first_out.send(4 * width, 2 * width + 32)
    send_weights(0, b, c, w, first_out)


def send_weights(layer, b, c, w, whole):
    width = b.ref.shape[1]
    for value, first, size in ((b, 0, width), (c, width, width), (w, 2 * width, 2 * width)):
        value.wait()
        whole.send(first, size, source=value.ref.at[layer])


def total_kernel(length_ref, ins, outs):
    outs[0].ref[...] = total_rows(ins[0].ref)


def cotangent_kernel(length_ref, ins, outs, held_ref):
    x, b, c, w = ins
    whole, later = outs
    width, total = x.ref.shape
    steps = total // CHUNKS
    each = steps // PIECES

    def emit(rows, index, value, carry):
        whole.ref[rows, :] = value
        place = pl.ds(pl.multiple_of(4 * width + index % each * CHUNKS, CHUNKS), CHUNKS)
        later.ref[place, lanes_at(index // each, width)] = value.astype(LOW)
        return carry

    def after(piece):
        whole.send_piece(piece)
        if piece == 1:
            send_weights(1, b, c, w, later)

    from_feature_rows(x, held_ref, steps, emit, 0, after)
    later.send(4 * width, total // PIECES)


def start_kernel(length_ref, ins, outs, stats_ref, stream_ref, drive_ref, pre_ref, held_ref, b_ref, c_ref, w_ref, low_ref):
    all_stats, tokens, parts = ins[:4], ins[4], ins[5:]
    feature, state_out, norm, normed, drive_own, low_own, stream, linear_out, gate_out, slope, active, b_out, c_out, w_out, spread = outs
    length, quarter = length_ref[0], own_quarter()
    total, full = active.ref.shape
    steps = total // CHUNKS
    width = full // 4
    lane = lax.broadcasted_iota(jnp.int32, (8, width), 1)
    tails = []
    rows_refs = []
    for part in parts:
        for piece in (6, 4, 5):
            part.wait(piece)
        rows_refs.append(part.ref.at[pl.ds(4 * width, 2 * width + PARAM_ROWS)])
    for place, part_ref in enumerate(rows_refs):
        value = sum(part_ref[2 * width :, at * width : (at + 1) * width].astype(F32) for at in range(3))
        feature.ref[:, lanes_at(quarter ^ place, width)] = value
        tails.append(value[8:16, :])
    for pair in range(2):
        early, late = tails[2 * pair : 2 * pair + 2]
        logs = jnp.where(lane < 64, early, pltpu.roll(late, 64, 1))
        lanes = slice(pair * width, (pair + 1) * width)
        for layer in range(LAYERS):
            first = 2 + 3 * layer
            modulus = jnp.exp(-jnp.exp(logs[first : first + 1, :]))
            angle = jnp.exp(logs[first + 1 : first + 2, :])
            state_out.ref[first : first + 1, lanes] = modulus * jnp.cos(angle)
            state_out.ref[first + 1 : first + 2, lanes] = modulus * jnp.sin(angle)
            state_out.ref[first + 2 : first + 3, lanes] = jnp.exp(logs[first + 2 : first + 3, :])
    for place, stats in enumerate(all_stats):
        stats_ref[:, lanes_at(quarter ^ place, width)] = stats.wait()[...]
    centre, inv_dev = norm_rows(stats_ref[0:2, :], stats_ref[2:3, :])
    norm.ref[...] = jnp.zeros_like(norm.ref)
    norm.ref[0:1, :] = centre
    norm.ref[1:2, :] = inv_dev
    norm.ref[2:3, :] = stats_ref[2:3, :]
    for out in (feature, state_out, norm):
        out.send()

    each = total // PIECES
    assemble_states([part.wait(0).at[0:width] for part in parts], b_ref)
    b_out.send(source=b_ref)
    state = state_out.ref[...]
    states = state.shape[1]
    gamma = state[2 + GAMMA : 3 + GAMMA, :]
    gammas = jnp.concatenate([gamma, gamma], axis=1)
    rows_of = []
    for place in range(4):
        lanes = lanes_at(quarter ^ place, width)
        rows_of.append((lanes, feature.ref[OWN_MEAN : OWN_MEAN + 1, lanes], norm.ref[0:1, lanes], norm.ref[1:2, lanes],
                        feature.ref[GAIN : GAIN + 1, lanes], feature.ref[SHIFT : SHIFT + 1, lanes]))
    for at, piece in enumerate(pieces_of(total)):
        tokens.wait(at)
        for rows, index in blocks_of(piece.start, piece.stop):
            keep = keep_rows(index, 16, steps, length)
            there = slice(rows.start % each, rows.start % each + 16)
            for place, (lanes, mean, middle, inverse, gain, shift) in enumerate(rows_of):
                if place == 0:
                    value = tokens.ref[rows, :]
                else:
                    value = rows_refs[place][there, at * width : (at + 1) * width].astype(F32) + mean
                stream_ref[rows, lanes] = value
                z = (value - middle) * inverse * gain + shift
                normed.ref[rows, lanes] = jnp.where(keep, z, 0.0).astype(LOW)
        normed.send_piece(at)
        drive_ref[piece, :] = dot(normed.ref[piece, :], b_ref[...], NT) * gammas
    assemble_output([part.wait(1).at[width : 2 * width] for part in parts], c_ref)
    c_out.send(source=c_ref)
    store = store_states(low_ref, drive_own.ref)

    def emit(rows, step, re, im, drive_re, drive_im, held):
        low_own.ref[rows, :128] = re[:, :128].astype(LOW)
        low_own.ref[rows, 128:] = im[:, :128].astype(LOW)
        return store(rows, step, re, im, drive_re, drive_im, held)

    sweep(drive_ref, state[2:3, :], state[3:4, :], steps, False, emit, 0)
    drive_own.send()
    low_own.send()

    assemble_glu([part.wait().at[2 * width : 4 * width] for part in parts], w_ref, quarter)
    w_out.send(source=w_ref)
    skip = feature.ref[SKIP : SKIP + 1, :]
    bias_linear = feature.ref[BIAS_LINEAR : BIAS_LINEAR + 1, :]
    bias_gate = feature.ref[BIAS_GATE : BIAS_GATE + 1, :]
    pre_products(low_ref, c_ref, pre_ref)
    for piece in pieces_of(total):
        pre_piece(piece, pre_ref, normed.ref, skip, active.ref, slope.ref)
        held_ref[piece, :] = dot(active.ref[piece, :], w_ref[...], NT)
    active.send()
    slope.send()
    plain, square = jnp.zeros((8, full), F32), jnp.zeros((8, full), F32)
    for place, piece in enumerate(pieces_of(total)):
        for rows, index in blocks_of(piece.start, piece.stop):
            keep = keep_rows(index, 16, steps, length)
            linear = held_ref[rows, :full] + bias_linear
            gate = jax.nn.sigmoid(held_ref[rows, full:] + bias_gate)
            mixed = linear * gate
            gate_out.ref[rows, :] = gate.astype(LOW)
            linear_out.ref[rows, :] = (mixed * (1.0 - gate)).astype(LOW)
            moved = stream_ref[rows, :] + jnp.where(keep, mixed, 0.0)
            stream.ref[rows, :] = moved
            kept = jnp.where(keep, moved, 0.0)
            plain += folded(kept)
            square += folded(kept * kept)
        for out in (stream, linear_out, gate_out):
            out.send_piece(place)
    carry = plain, square
    spread_rows(narrowed([column_sum(carry[0]), column_sum(carry[1])], width), spread)


def middle_kernel(
    length_ref, ins, outs,
    small_ref, b_ref, c_ref, w_ref, normed_ref, drive_ref, drive_own_ref, low_ref, slope_ref, active_ref, held_ref, pre_ref, mixed_ref,
    up_ref, grad_gated_ref, pre_grad_ref, grad_driven_ref, grads_ref,
):
    sums, norm0, feature_in, state_in, stream, up_own = ins[:6]
    parts = ins[6:]
    result, base, spread, norm, *shares = outs
    length, quarter = length_ref[0], own_quarter()
    total, full = stream.ref.shape
    steps = total // CHUNKS
    width = 128
    counted = norm0.wait()[2:3, :]
    feature = feature_in.wait()
    state = state_in.wait()[...]
    states = state.shape[1]
    whole = total_rows(sums.wait())
    whole = jnp.concatenate([widened(whole, 0, 4), widened(whole, 4, 4)], axis=0)
    centre, inv_dev = norm_rows(whole, counted)
    norm.ref[...] = jnp.zeros_like(norm.ref)
    norm.ref[0:1, :] = centre
    norm.ref[1:2, :] = inv_dev
    norm.ref[2:3, :] = counted
    norm.send()
    gain = feature[5 + GAIN : 6 + GAIN, :]
    shift = feature[5 + SHIFT : 6 + SHIFT, :]
    skip = feature[5 + SKIP : 6 + SKIP, :]

    for part in parts:
        part.wait(0)
    assemble_states([part.ref.at[0:width] for part in parts], b_ref)
    gamma = state[5 + GAMMA : 6 + GAMMA, :]
    gammas = jnp.concatenate([gamma, gamma], axis=1)
    for place, piece in enumerate(pieces_of(total)):
        stream.wait(place)
        for rows, index in blocks_of(piece.start, piece.stop):
            z = (stream.ref[rows, :] - centre) * inv_dev
            normed_ref[rows, :] = jnp.where(keep_rows(index, 16, steps, length), z * gain + shift, 0.0).astype(LOW)
        drive_ref[piece, :] = dot(normed_ref[piece, :], b_ref[...], NT) * gammas
    sweep(drive_ref, state[5:6, :], state[6:7, :], steps, True, store_states(low_ref, drive_own_ref), 0)
    for part in parts:
        part.wait()
    assemble_output([part.ref.at[width : 2 * width] for part in parts], c_ref)
    assemble_glu([part.ref.at[2 * width : 4 * width] for part in parts], w_ref, quarter)
    up_own.wait()
    own = lanes_at(quarter, width)

    for rows, _ in blocks_of(0, total):
        up_ref[rows, own] = up_own.ref[rows, :]
    for place, piece in enumerate(pieces_of(total)):
        for other in range(1, 4):
            lanes = lanes_at(quarter ^ other, width)
            up_ref[piece, lanes] = parts[other].ref[4 * width :, place * width : (place + 1) * width].astype(F32)
    bias_linear = feature[5 + BIAS_LINEAR : 6 + BIAS_LINEAR, :]
    bias_gate = feature[5 + BIAS_GATE : 6 + BIAS_GATE, :]
    pre_products(low_ref, c_ref, pre_ref)
    for piece in pieces_of(total):
        pre_piece(piece, pre_ref, normed_ref, skip, active_ref, slope_ref)
        held_ref[piece, :] = dot(active_ref[piece, :], w_ref[...], NT)
    for piece in pieces_of(total):
        for rows, index in blocks_of(piece.start, piece.stop):
            keep = keep_rows(index, 16, steps, length)
            linear = held_ref[rows, :full] + bias_linear
            gate = jax.nn.sigmoid(held_ref[rows, full:] + bias_gate)
            mixed = linear * gate
            up = jnp.where(keep, up_ref[rows, :], 0.0)
            grad_gated_ref[rows, :full] = (up * gate).astype(LOW)
            grad_gated_ref[rows, full:] = (up * mixed * (1.0 - gate)).astype(LOW)
            mixed_ref[rows, :] = jnp.where(keep, mixed, 0.0)
        pre_ref[piece, :] = dot(grad_gated_ref[piece, :], w_ref[...], NN)
    for piece in pieces_of(total):
        pre_grad_piece(piece, pre_ref, slope_ref, pre_grad_ref)
        drive_ref[piece, :] = dot(pre_grad_ref[piece, :], c_ref[...], NT)
    small_ref[...] = jnp.zeros_like(small_ref)
    for rows, _ in blocks_of(0, total):
        result.ref[rows, :] = stream.ref[rows, own] + mixed_ref[rows, own]
    result.send()
    adjoint_phase(
        low_ref, states, drive_own_ref, state, 5, length, drive_ref, grad_driven_ref, small_ref, False,
        beside_sweep(
            glu_products(grads_ref, 2 * width, grad_gated_ref, active_ref, quarter)
            + output_products(grads_ref, lambda: low_ref[:, 0:128], lambda: low_ref[:, states : states + 128], pre_grad_ref, states),
            grad_gated_ref, pre_grad_ref, normed_ref, quarter, small_ref,
        ),
    )
    scale = inv_dev * gain
    for piece in pieces_of(total):
        pre_ref[piece, :] = dot(grad_driven_ref[piece, :], b_ref[...], NN)
    plain, scaled = jnp.zeros((8, full), F32), jnp.zeros((8, full), F32)
    for place, piece in enumerate(pieces_of(total)):
        for rows, _ in blocks_of(piece.start, piece.stop):
            grad = pre_ref[rows, :] + skip * pre_grad_ref[rows, :].astype(F32)
            z = (stream.ref[rows, :] - centre) * inv_dev
            base.ref[rows, :] = scale * grad + up_ref[rows, :]
            plain += folded(grad)
            scaled += folded(grad * z)
        base.send_piece(place)
    input_products(grads_ref, grad_driven_ref, normed_ref, states)
    sent = narrowed([column_sum(plain), column_sum(scaled)], width)
    spread_rows(jnp.concatenate([sent, small_ref[:, 0:width]], axis=0), spread)
    send_halves(grads_ref, shares, 0)


def last_kernel(
    length_ref, ins, outs, held_ref, grad_state_ref, grad_gated_ref, pre_grad_ref, grad_driven_ref, small_ref, up_ref, grads_ref, pack_ref, low_ref
):
    (sums, norm1, feature_in, state_in, norm0, stream, base, gate, linear, w, slope, c, normed, active, low, drive_own, b, x) = ins
    kept, sent, up_out, grad_out = outs
    length, quarter = length_ref[0], own_quarter()
    total, full = stream.ref.shape
    steps = total // CHUNKS
    width = 128
    own = lanes_at(quarter, width)
    feature, norm_ref = feature_in.wait(), norm1.wait()
    state = state_in.wait()[...]
    counted = norm_ref[2:3, :]
    whole = total_rows(sums.wait())
    whole = jnp.concatenate([widened(whole, 0, 4), widened(whole, 4, 4)], axis=0)
    centre, inv_dev = norm_ref[0:1, :], norm_ref[1:2, :]
    scale = inv_dev * feature[5 + GAIN : 6 + GAIN, :]
    level = scale * whole[0:1, :] / counted
    tilt = scale * inv_dev * whole[1:2, :] / counted

    for place, piece in enumerate(pieces_of(total)):
        for value in (stream, base, gate, linear):
            value.wait(place)
        for rows, index in blocks_of(piece.start, piece.stop):
            keep = keep_rows(index, 16, steps, length)
            up = base.ref[rows, :] - jnp.where(keep, level + (stream.ref[rows, :] - centre) * tilt, 0.0)
            up_ref[rows, :] = up
            up = jnp.where(keep, up, 0.0)
            grad_gated_ref[rows, :full] = (up * gate.ref[rows, :].astype(F32)).astype(LOW)
            grad_gated_ref[rows, full:] = (up * linear.ref[rows, :].astype(F32)).astype(LOW)
        if place == 0:
            w.wait()
        held_ref[piece, :] = dot(grad_gated_ref[piece, :], w.ref[...], NN)
    for value in (slope, c):
        value.wait()
    for piece in pieces_of(total):
        pre_grad_piece(piece, held_ref, slope.ref, pre_grad_ref)
        grad_state_ref[piece, :] = dot(pre_grad_ref[piece, :], c.ref[...], NT)
    small_ref[...] = jnp.zeros_like(small_ref)

    def own_up(rows, index, carry):
        up_out.ref[rows, :] = up_ref[rows, own]
        return carry

    for_rows(0, total, 16, own_up, unroll=4)
    up_out.send()
    for value in (normed, active, low, drive_own):
        value.wait()
    adjoint_phase(
        low.ref, 128, drive_own.ref, state, 2, length, grad_state_ref, grad_driven_ref, small_ref, True,
        beside_sweep(
            glu_products(grads_ref, 2 * width, grad_gated_ref, active.ref, quarter)
            + output_products(grads_ref, lambda: low.ref[:, :128], lambda: low.ref[:, 128:], pre_grad_ref, state.shape[1]),
            grad_gated_ref, pre_grad_ref, normed.ref, quarter, small_ref,
        ),
    )
    b.wait()
    x.wait()
    held_ref[:, :width] = dot(grad_driven_ref[...], b.ref[:, own], NN)
    input_products(grads_ref, grad_driven_ref, normed.ref, state.shape[1])
    zero = jnp.zeros((8, width), F32)
    centre0, inv_dev0 = norm0.wait()[0:1, own], norm0.ref[1:2, own]
    skip = feature[SKIP : SKIP + 1, own]

    def back(rows, index, carry):
        grad = held_ref[rows, :width] + skip * pre_grad_ref[rows, own].astype(F32)
        grad_out.ref[rows, :] = grad
        z = (x.ref[rows, :] - centre0) * inv_dev0
        return carry[0] + folded(grad), carry[1] + folded(grad * z)

    plain, scaled = for_rows(0, total, 16, back, (zero, zero), unroll=4)
    grad_out.send()
    small_ref[6:7, 0:width] = column_sum(plain)
    small_ref[7:8, 0:width] = column_sum(scaled)
    pack_ref[...] = jnp.zeros_like(pack_ref)
    for place in range(8):
        pack_ref[place // 4 : place // 4 + 1, place % 4 * width : (place % 4 + 1) * width] = small_ref[place : place + 1, 0:width]
    exact = pack_ref[0:8, :]
    pack_ref[8:16, :] = exact - exact.astype(LOW).astype(F32)
    half = grads_ref.shape[0] // 2
    low_ref[...] = pack_ref[...].astype(LOW)
    mine = lax.axis_index("dp") & 1
    for out, which in ((kept, mine), (sent, 1 - mine)):
        out.send(0, half, source=grads_ref.at[rows_at(which, half)])
        out.send(half, 16, source=low_ref)


def send_halves(source_ref, outs, stage):
    kept = lax.axis_index("dp") >> stage & 1
    half = source_ref.shape[0] // 2
    for out, which in zip(outs, (kept, 1 - kept)):
        out.send(source=source_ref.at[rows_at(which, half)])


def add_kernel(length_ref, ins, outs):
    outs[0].ref[...] = (ins[0].ref[...].astype(F32) + ins[1].ref[...].astype(F32)).astype(LOW)


def pair_kernel(length_ref, ins, outs, sum_ref, pack_ref):
    kept, other = ins
    for value in ins:
        value.wait()
    half = kept.ref.shape[0] - 16
    share = half // len(outs)
    small = kept.ref[half:, :].astype(F32) + other.ref[half:, :].astype(F32)
    small = small[0:8, :] + small[8:16, :]
    pack_ref[...] = jnp.concatenate([small, small - small.astype(LOW).astype(F32)], axis=0).astype(LOW)
    for piece in range(0, half, 16):
        at = slice(piece, piece + 16)
        sum_ref[at, :] = (kept.ref[at, :].astype(F32) + other.ref[at, :].astype(F32)).astype(LOW)
    for place, out in enumerate(outs):
        out.send(0, share, source=sum_ref.at[rows_at((lax.axis_index("dp") >> 1) ^ place, share)])
        out.send(share, 16, source=pack_ref)


def share_kernel(length_ref, ins, outs):
    out, small = outs
    share = out.ref.shape[0]
    value = ins[0].ref[...].astype(F32)
    for block in ins[1:]:
        value += block.ref[...].astype(F32)
    out.ref[...] = value[:share, :].astype(LOW)
    small.ref[...] = value[share : share + 8, :] + value[share + 8 :, :]


def finish_kernel(length_ref, ins, outs, held_ref, order_ref):
    small0, bn1, norm0, feature, nu, theta, result, up, grad, x = ins
    nu_out, theta_out, gamma_out, skip_out, bias_out, gain_out, shift_out, result_out, out = outs
    length, quarter = length_ref[0], own_quarter()
    total, width = up.ref.shape
    steps = total // CHUNKS
    own = lanes_at(quarter, width)
    states = nu_out.ref.shape[1]
    result.wait()
    to_feature_rows(lambda rows, index: result.ref[rows, :], order_ref, result_out, steps)
    for value in ins:
        value.wait()
    whole = total_rows(bn1.ref)
    held_ref[0:1, :] = widened(whole, 0, 4)
    held_ref[1:2, :] = widened(whole, 4, 4)
    held_ref[16:32, :width] = whole
    for place in range(8):
        held_ref[8 + place : 9 + place, :width] = small0.ref[place // 4 : place // 4 + 1, place % 4 * width : (place % 4 + 1) * width]
    for layer, first in ((0, 8), (1, 24)):
        at = slice(layer, layer + 1)
        nu_out.ref[at, :] = -jnp.exp(nu.ref[at, :]) * held_ref[first : first + 1, :states]
        theta_out.ref[at, :] = jnp.exp(theta.ref[at, :]) * held_ref[first + 1 : first + 2, :states]
        gamma_out.ref[at, :] = held_ref[first + 2 : first + 3, :states]
        skip_out.ref[at, :] = held_ref[first + 3 : first + 4, :width]
        bias_out.ref[layer, 0:1, :] = held_ref[first + 4 : first + 5, :width]
        bias_out.ref[layer, 1:2, :] = held_ref[first + 5 : first + 6, :width]
    shift_out.ref[0:1, :] = held_ref[14:15, :width]
    gain_out.ref[0:1, :] = held_ref[15:16, :width]
    shift_out.ref[1:2, :] = held_ref[0:1, own]
    gain_out.ref[1:2, :] = held_ref[1:2, own]
    counted = norm0.ref[2:3, own]
    centre, inv_dev = norm0.ref[0:1, own], norm0.ref[1:2, own]
    level = held_ref[14:15, :width] / counted
    tilt = held_ref[15:16, :width] * inv_dev / counted
    scale = inv_dev * feature.ref[GAIN : GAIN + 1, own]

    def load(rows, index):
        keep = keep_rows(index, CHUNKS, steps, length)
        inner = grad.ref[rows, :] - level - (x.ref[rows, :] - centre) * tilt
        return up.ref[rows, :] + jnp.where(keep, scale * inner, 0.0)

    to_feature_rows(load, order_ref, out, steps)


def send_wide(layer, outs, held_ref):
    half = outs[0].target.shape[1]
    for out, first, size in zip(outs, (0, half, 2 * half), (half, half, 2 * half)):
        out.send(layer, 1, source=held_ref.at[pl.ds(0, 1), pl.ds(first, size)])


def widen1_kernel(length_ref, ins, outs, held_ref):
    half = ins[0].ref.shape[0]
    mine = lax.axis_index("dp") & 1
    for which, value in ((mine, ins[0]), (1 - mine, ins[1])):
        held_ref[0, rows_at(which, half), :] = value.ref[...].astype(F32)
    send_wide(1, outs, held_ref)


def widen0_kernel(length_ref, ins, outs, held_ref):
    groups = len(ins)
    share = ins[0].ref.shape[0]
    for place, value in enumerate(ins):
        owner = lax.axis_index("dp") ^ place
        held_ref[0, rows_at((owner & 1) * (groups // 2) + (owner >> 1), share), :] = value.ref[...].astype(F32)
    send_wide(0, outs, held_ref)


def shape(*dims, dtype=F32):
    return jax.ShapeDtypeStruct(dims, dtype)


def swap(value, bit, sharers):
    pairs = [(q * sharers + r, (q ^ bit) * sharers + r) for q in range(4) for r in range(sharers)]
    return lax.ppermute(value, "state", pairs)


def across(value, axes):
    return lax.all_to_all(value, axes, 0, 0, tiled=True)


def local(
    inputs, lengths, cotangent, bn_gain, bn_bias, b_weight, c_weight, nu_log, theta_log, gamma_log, skip_weight,
    glu_weight, glu_bias, dp_size, state_size,
):
    sharers = state_size // 4
    place = lax.axis_index("state").astype(jnp.int32)

    def joined(value, axis):
        if sharers == 1:
            return value
        groups = [[q * sharers + r for r in range(sharers)] for q in range(4)]
        return lax.all_gather(value, "state", axis=axis, axis_index_groups=groups, tiled=True)

    def own(value, axis):
        if sharers == 1:
            return value
        size = value.shape[axis] // sharers
        return lax.dynamic_slice_in_dim(value, place % sharers * size, size, axis)

    inputs, cotangent = joined(inputs, 1), joined(cotangent, 1)
    bn_gain, bn_bias, skip_weight = joined(bn_gain, 1), joined(bn_bias, 1), joined(skip_weight, 1)
    nu_log, theta_log, gamma_log = joined(nu_log, 1), joined(theta_log, 1), joined(gamma_log, 1)
    b_weight, c_weight = joined(b_weight, 2), joined(c_weight, 2)
    glu_weight, glu_bias = joined(glu_weight, 2), joined(glu_bias, 2)
    width, total = inputs.shape[1:]
    full = b_weight.shape[3]
    states = b_weight.shape[2] * 4
    own_states = b_weight.shape[2]
    share = 4 * width // dp_size
    piece = total // PIECES

    stages = dp_size.bit_length() - 1

    def exchange(value, bit):
        return lax.ppermute(value, "dp", [(i, i ^ bit) for i in range(dp_size)])

    def add(one, other):
        return call_small(add_kernel, (shape(*one.shape, dtype=LOW),), [], (one, other), "add")[0]

    b_weight, c_weight = b_weight.reshape(LAYERS, width, full), c_weight.reshape(LAYERS, width, full)
    glu_weight = glu_weight.reshape(LAYERS, 2 * width, full)
    tokens, sums, first = call(
        enter_kernel,
        (
            shape(total, width),
            shape(dp_size, 8, width),
            shape(6 * width + PARAM_ROWS, full, dtype=LOW),
        ),
        [pltpu.VMEM((total, width), F32), pltpu.VMEM((PARAM_ROWS, width), F32)],
        (lengths, inputs[0], bn_gain, bn_bias, skip_weight, glu_bias, nu_log, theta_log, gamma_log, b_weight, c_weight, glu_weight),
        "enter",
        pieces={1: piece},
        axes={1: 1},
        late=(9, 10, 11),
    )
    near, far = swap(first, 1, sharers), swap(first, 2, sharers)
    (stats,) = call_small(total_kernel, (shape(8, width),), [], (across(sums, "dp"),), "total")
    stats_near, stats_far = swap(stats, 1, sharers), swap(stats, 2, sharers)
    cotangent, tokens = lax.optimization_barrier((cotangent, tokens))
    up_own, later = call(
        cotangent_kernel,
        (
            shape(total, width),
            shape(6 * width, full, dtype=LOW),
        ),
        [pltpu.VMEM((total, width), F32)],
        (lengths, cotangent[0], b_weight, c_weight, glu_weight),
        "cotangent",
        pieces={1: piece},
        axes={1: 1},
        late=(2, 3, 4),
    )
    later_far = swap(later, 2, sharers)
    near, far, stats_near, stats_far, later = lax.optimization_barrier((near, far, stats_near, stats_far, later))
    parts = (first, near, far, swap(far, 1, sharers))
    all_stats = (stats, stats_near, stats_far, swap(stats_far, 1, sharers))
    feature, state, norm0, normed0, drive0, low0, stream1, linear0, gate0, slope0, active0, b_all, c_all, w_all, sums1 = call(
        start_kernel,
        (
            shape(PARAM_ROWS, full),
            shape(8, states),
            shape(8, full),
            shape(total, full, dtype=LOW),
            shape(total, 256),
            shape(total, 256, dtype=LOW),
            shape(total, full),
            shape(total, full, dtype=LOW),
            shape(total, full, dtype=LOW),
            shape(total, full, dtype=LOW),
            shape(total, full, dtype=LOW),
            shape(2 * states, full, dtype=LOW),
            shape(2 * states, full, dtype=LOW),
            shape(2 * full, full, dtype=LOW),
            shape(dp_size, 8, width),
        ),
        [
            pltpu.VMEM((8, full), F32),
            pltpu.VMEM((total, full), F32),
            pltpu.VMEM((total, 2 * states), F32),
            pltpu.VMEM((total, full), F32),
            pltpu.VMEM((total, 2 * full), F32),
            pltpu.VMEM((2 * states, full), LOW),
            pltpu.VMEM((2 * states, full), LOW),
            pltpu.VMEM((2 * full, full), LOW),
            pltpu.VMEM((total, 2 * states), LOW),
        ],
        (lengths, *all_stats, tokens, *parts),
        "start",
        pieces={5: piece} | {place: width for place in (6, 7, 8, 9)},
        order=(4, 5),
        bare=(11, 12, 13),
        flops=0,
    )
    sums1 = across(sums1, "dp")
    later_far, sums1 = lax.optimization_barrier((later_far, sums1))
    later_parts = (later, swap(later, 1, sharers), later_far, swap(later_far, 1, sharers))
    result_rows, base, bn1, norm1, *halves1 = call(
        middle_kernel,
        (
            shape(total, width),
            shape(total, full),
            shape(dp_size, 16, width),
            shape(8, full),
            shape(2 * width, full, dtype=LOW),
            shape(2 * width, full, dtype=LOW),
        ),
        [
            pltpu.VMEM((8, full), F32),
            pltpu.VMEM((2 * states, full), LOW),
            pltpu.VMEM((2 * states, full), LOW),
            pltpu.VMEM((2 * full, full), LOW),
            pltpu.VMEM((total, full), LOW),
            pltpu.VMEM((total, 2 * states), F32),
            pltpu.VMEM((total, 256), F32),
            pltpu.VMEM((total, 2 * states), LOW),
            pltpu.VMEM((total, full), F32),
            pltpu.VMEM((total, full), LOW),
            pltpu.VMEM((total, 2 * full), F32),
            pltpu.VMEM((total, full), F32),
            pltpu.VMEM((total, full), F32),
            pltpu.VMEM((total, full), F32),
            pltpu.VMEM((total, 2 * full), LOW),
            pltpu.VMEM((total, full), LOW),
            pltpu.VMEM((total, 2 * states), LOW),
            pltpu.VMEM((4 * width, full), LOW),
        ],
        (lengths, sums1, norm0, feature, state, stream1, up_own, *later_parts),
        "middle",
        pieces={5: piece} | {place: width for place in (7, 8, 9, 10)},
        late=(6,),
        bare=(4, 5),
        flops=1e9,
    )
    bn1 = across(bn1, "dp")
    half1 = add(halves1[0], exchange(halves1[1], 1))
    bn1, half1 = lax.optimization_barrier((bn1, half1))
    other1 = exchange(half1, 1 << (stages - 1))
    kept0, sent0, up0, grad0 = call(
        last_kernel,
        (
            shape(2 * width + 16, full, dtype=LOW),
            shape(2 * width + 16, full, dtype=LOW),
            shape(total, width),
            shape(total, width),
        ),
        [
            pltpu.VMEM((total, full), F32),
            pltpu.VMEM((total, 2 * states), F32),
            pltpu.VMEM((total, 2 * full), LOW),
            pltpu.VMEM((total, full), LOW),
            pltpu.VMEM((total, 2 * states), LOW),
            pltpu.VMEM((8, full), F32),
            pltpu.VMEM((total, full), F32),
            pltpu.VMEM((4 * width, full), LOW),
            pltpu.VMEM((16, full), F32),
            pltpu.VMEM((16, full), LOW),
        ],
        (lengths, bn1, norm1, feature, state, norm0, stream1, base, gate0, linear0, w_all, slope0, c_all, normed0, active0, low0,
         drive0, b_all, tokens),
        "last",
        bare=(0, 1),
        pieces={6: piece, 7: piece, 8: piece, 9: piece},
        late=tuple(range(11, 19)),
        flops=1e11,
    )
    other1, kept0 = lax.optimization_barrier((other1, kept0))
    sent0 = exchange(sent0, 1)
    half1 = add(half1, other1)
    kept0, half1 = lax.optimization_barrier((kept0, half1))
    for stage in reversed(range(2, stages - 1)):
        half1 = add(half1, exchange(half1, 1 << stage))
    other1 = exchange(half1, 2)
    blocks = call_small(
        pair_kernel,
        (shape(share + 16, full, dtype=LOW),) * (dp_size // 2),
        [pltpu.VMEM((2 * width, full), LOW), pltpu.VMEM((16, full), LOW)],
        (kept0, sent0),
        "pair",
    )
    blocks = [blocks[0]] + [exchange(blocks[place], 2 * place) for place in range(1, dp_size // 2)]
    other1, *blocks = lax.optimization_barrier((other1, *blocks))
    half1 = add(half1, other1)
    blocks[0], half1 = lax.optimization_barrier((blocks[0], half1))
    other1 = exchange(half1, 1)
    back, small0 = call_small(
        share_kernel, (shape(share, full, dtype=LOW), shape(8, full)), [], tuple(blocks), "share"
    )
    small0, other1 = lax.optimization_barrier((small0, other1))
    backs = [back] + [exchange(back, place) for place in range(2, dp_size, 2)]
    backs = [each for first in backs for each in (first, exchange(first, 1))]
    grad_nu, grad_theta, grad_gamma, grad_skip, grad_bias, grad_gain, grad_shift, result, grad_inputs = call(
        finish_kernel,
        (
            shape(LAYERS, own_states),
            shape(LAYERS, own_states),
            shape(LAYERS, own_states),
            shape(LAYERS, width),
            shape(LAYERS, 2, width),
            shape(LAYERS, width),
            shape(LAYERS, width),
            shape(width, total),
            shape(width, total),
        ),
        [pltpu.VMEM((32, full), F32), pltpu.VMEM((total, width), F32)],
        (lengths, small0, bn1, norm0, feature, nu_log, theta_log, result_rows, up0, grad0, tokens),
        "finish",
    )
    wide = (shape(LAYERS, width, full), shape(LAYERS, width, full), shape(LAYERS, 2 * width, full))
    held = [pltpu.VMEM((1, 4 * width, full), F32)]
    grads = call_small(widen1_kernel, wide, held, (half1, other1), "widen1", sent=True)
    grad_b, grad_c, grad_glu = call_small(widen0_kernel, wide, held, tuple(backs), "widen0", sent=True, into=tuple(grads))
    grad_b = grad_b.reshape(LAYERS, 2, own_states, full)
    grad_c = grad_c.reshape(LAYERS, 2, own_states, full)
    grad_glu = grad_glu.reshape(LAYERS, 2, width, full)
    return (
        own(result[None], 1),
        own(grad_inputs[None], 1),
        own(grad_gain, 1),
        own(grad_shift, 1),
        own(grad_b, 2),
        own(grad_c, 2),
        own(grad_nu, 1),
        own(grad_theta, 1),
        own(grad_gamma, 1),
        own(grad_skip, 1),
        own(grad_glu, 2),
        own(grad_bias, 2),
    )


def solution(mesh):
    in_specs = (
        P("dp", "state", None),
        P("dp"),
        P("dp", "state", None),
        P(None, "state"),
        P(None, "state"),
        P(None, None, "state", None),
        P(None, None, "state", None),
        P(None, "state"),
        P(None, "state"),
        P(None, "state"),
        P(None, "state"),
        P(None, None, "state", None),
        P(None, None, "state"),
    )
    out_specs = (
        P("dp", "state", None),
        P("dp", "state", None),
        P(None, "state"),
        P(None, "state"),
        P(None, None, "state", None),
        P(None, None, "state", None),
        P(None, "state"),
        P(None, "state"),
        P(None, "state"),
        P(None, "state"),
        P(None, None, "state", None),
        P(None, None, "state"),
    )
    step = functools.partial(local, dp_size=mesh.shape["dp"], state_size=mesh.shape["state"])
    return jax.shard_map(step, mesh=mesh, in_specs=in_specs, out_specs=out_specs, check_vma=False)
```

```python
import functools

import jax
import jax.numpy as jnp
from jax import lax
from jax.experimental import pallas as pl
from jax.experimental.pallas import tpu as pltpu
from jax.sharding import PartitionSpec as P

LAYERS = 2
CHUNKS = 16
PIECES = 4
EPSILON = 1e-05
F32 = jnp.float32
LOW = jnp.bfloat16
PARAM_ROWS = 32
OWN_MEAN = 16
VMEM_BYTES = 64 * 1024 * 1024
SMALL_VMEM_BYTES = 8 * 1024 * 1024

GAIN, SHIFT, SKIP, BIAS_LINEAR, BIAS_GATE = range(5)
RATE_RE, RATE_IM, GAMMA = range(3)

NN = (((1,), (0,)), ((), ()))
NT = (((1,), (1,)), ((), ()))
TN = (((0,), (0,)), ((), ()))


def dot(left, right, dims):
    return lax.dot_general(left, right, dims, preferred_element_type=F32)


def rows_at(index, size):
    return pl.ds(pl.multiple_of(index * size, size), size)


def lanes_at(quarter, width):
    return pl.ds(pl.multiple_of(quarter * width, width), width)


def for_rows(first, last, size, body, init=0, unroll=2):
    def step(index, carry):
        return body(rows_at(index, size), index, carry)

    return lax.fori_loop(first // size, last // size, step, init, unroll=unroll)


def blocks_of(first, last, size=16):
    return [(slice(at, at + size), at // size) for at in range(first, last, size)]


def pieces_of(total):
    size = total // PIECES
    return [slice(at, at + size) for at in range(0, total, size)]


def own_quarter():
    return (lax.axis_index("state") // (lax.axis_size("state") // 4)).astype(jnp.int32)


def keep_rows(first_step, rows, steps, length):
    row = lax.broadcasted_iota(jnp.int32, (rows, 1), 0)
    position = (row % CHUNKS) * steps + row // CHUNKS + first_step
    return position < length


def gelu_parts(value):
    return 0.5 + 0.5 * lax.erf(value * 0.7071067811865476), jnp.exp(value * value * -0.5) * 0.3989422804014327


def squared(re, im, times):
    for _ in range(times):
        re, im = re * re - im * im, 2.0 * re * im
    return re, im


def folded(value):
    return value[0:8, :] + value[8:16, :]


def column_sum(value):
    return jnp.sum(value, axis=0, keepdims=True)


def chunk_starts(re, im, rate_re, rate_im, reverse):
    row = lax.broadcasted_iota(jnp.int32, re.shape, 0)

    def moved(value, by):
        if reverse:
            return jnp.where(row < CHUNKS - by, pltpu.roll(value, CHUNKS - by, 0), 0.0)
        return jnp.where(row >= by, pltpu.roll(value, by, 0), 0.0)

    by = 1
    while by < CHUNKS:
        past_re, past_im = moved(re, by), moved(im, by)
        re, im = (
            re + rate_re * past_re - rate_im * past_im,
            im + rate_re * past_im + rate_im * past_re,
        )
        rate_re, rate_im = squared(rate_re, rate_im, 1)
        by *= 2
    return moved(re, 1), moved(im, 1)


def sweep(drive_ref, rate_re, rate_im, steps, reverse, emit, extra, after=None, beside=None, unroll=4):
    states = rate_re.shape[1]
    shape = (CHUNKS, states)
    wide_re = jnp.broadcast_to(rate_re, shape)
    wide_im = jnp.broadcast_to(rate_im, shape)

    def advance(index, re, im):
        place = steps - 1 - index if reverse else index
        rows = slice(place * CHUNKS, (place + 1) * CHUNKS) if isinstance(place, int) else rows_at(place, CHUNKS)
        drive_re = drive_ref[rows, :states]
        drive_im = drive_ref[rows, states:]
        new_re = (wide_re * re + drive_re) - wide_im * im
        new_im = (wide_re * im + drive_im) + wide_im * re
        return rows, place, new_re, new_im, drive_re, drive_im

    def first(index, carry):
        _, _, re, im, _, _ = advance(index, *carry)
        return re, im

    def second(index, carry):
        re, im, held = carry
        rows, place, re, im, drive_re, drive_im = advance(index, re, im)
        return re, im, emit(rows, place, re, im, drive_re, drive_im, held)

    zero = jnp.zeros(shape, F32)
    re, im = lax.fori_loop(0, steps, first, (zero, zero), unroll=unroll)
    far_re, far_im = rate_re, rate_im
    power = 1
    while power < steps:
        far_re, far_im = squared(far_re, far_im, 1)
        power *= 2
    re, im = chunk_starts(re, im, far_re, far_im, reverse)
    carry = (re, im, extra)
    for piece in range(PIECES):
        size = steps // PIECES
        if beside is not None:
            beside[piece]()
            for index in range(piece * size, (piece + 1) * size):
                carry = second(index, carry)
        else:
            carry = lax.fori_loop(piece * size, (piece + 1) * size, second, carry, unroll=unroll)
        if after is not None:
            after(PIECES - 1 - piece if reverse else piece)
    return carry[2]


class Arrival:
    def __init__(self, source, ref, done, first, size, axis):
        self.ref = ref
        self.copies = []
        whole = ref.shape[axis]
        for piece, start in enumerate(range(0, whole, size)):
            where = (slice(None),) * axis + (pl.ds(start, min(size, whole - start)),)
            self.copies.append(
                pltpu.make_async_copy(source.at[where], ref.at[where], done.at[first + piece])
                if size < whole
                else pltpu.make_async_copy(source, ref, done.at[first])
            )
        self.short = whole % size > 0
        self.waited = set()

    def start(self, piece):
        last = len(self.copies) - self.short
        if piece < 0 and self.short:
            self.copies[-1].start()
        if 0 <= piece < last:
            self.copies[piece].start()

    def wait(self, piece=None):
        for place in range(len(self.copies)) if piece is None else (piece,):
            if place not in self.waited:
                self.copies[place].wait()
                self.waited.add(place)
        return self.ref


class Departure:
    def __init__(self, target, ref, done, first):
        self.target, self.ref, self.done, self.first = target, ref, done, first
        self.copies = []

    def send(self, start=None, size=None, source=None):
        place = self.done.at[self.first + len(self.copies)]
        where = self.target if start is None else self.target.at[pl.ds(start, size)]
        if source is None:
            source = self.ref if start is None else self.ref.at[pl.ds(start, size)]
        self.copies.append(pltpu.make_async_copy(source, where, place))
        self.copies[-1].start()

    def send_piece(self, piece):
        size = self.target.shape[0] // PIECES
        self.send(piece * size, size)

    def send_unsent(self):
        if not self.copies:
            self.send()

    def finish(self):
        for copy in self.copies:
            copy.wait()


class Resident:
    def __init__(self, ref):
        self.ref = ref

    def wait(self, piece=None):
        return self.ref

    def send(self, start=None, size=None, source=None):
        if source is not None and start is None:
            self.ref[...] = source[...]
        elif source is not None:
            self.ref[start : start + size, :] = source[...]


def call_small(kernel, outs, scratch, args, name, sent=False, into=()):
    def body(*refs):
        count, results = len(args), len(outs)
        ins, refs = [Resident(ref) for ref in refs[:count]], refs[count + len(into) :]
        if not sent:
            kernel(None, ins, [Resident(ref) for ref in refs[:results]], *refs[results:])
            return
        targets, copied, scratch_refs = refs[:results], refs[results], refs[results + 1 :]
        departures = [Departure(target, None, copied, place * LAYERS) for place, target in enumerate(targets)]
        kernel(None, ins, departures, *scratch_refs)
        for departure in departures:
            departure.finish()

    return pl.pallas_call(
        body,
        out_shape=tuple(outs),
        in_specs=[pl.BlockSpec(memory_space=pltpu.VMEM)] * len(args) + [pl.BlockSpec(memory_space=pl.ANY)] * len(into),
        out_specs=tuple(pl.BlockSpec(memory_space=pl.ANY if sent else pltpu.VMEM) for _ in outs),
        input_output_aliases={len(args) + place: place for place in range(len(into))},
        scratch_shapes=([pltpu.SemaphoreType.DMA((LAYERS * len(outs),))] if sent else []) + list(scratch),
        compiler_params=pltpu.CompilerParams(vmem_limit_bytes=SMALL_VMEM_BYTES),
        cost_estimate=pl.CostEstimate(flops=0, bytes_accessed=0, transcendentals=0),
        name=name,
    )(*args, *into)


def call(kernel, outs, scratch, args, name, pieces=None, axes=None, bare=(), late=(), order=None, flops=0, vmem=VMEM_BYTES):
    pieces, axes = pieces or {}, axes or {}
    along = [axes.get(place, 0) for place in range(1, len(args))]
    sizes = [pieces.get(place, args[place].shape[axis]) for place, axis in enumerate(along, 1)]
    counts = [-(-args[place].shape[axis] // size) for place, (axis, size) in enumerate(zip(along, sizes), 1)]
    slots = 6
    copies_in = [pltpu.VMEM(a.shape, a.dtype) for a in args[1:]]
    copies_out = [pltpu.VMEM((8, 128) if place in bare else o.shape, o.dtype if place not in bare else F32) for place, o in enumerate(outs)]

    def body(*refs):
        refs = list(refs)

        def take(count):
            got = refs[:count]
            del refs[:count]
            return got

        (length_ref,) = take(1)
        sources = take(len(args) - 1)
        targets = take(len(outs))
        in_refs, out_refs = take(len(args) - 1), take(len(outs))
        arrived, sent = take(2)
        arrivals, first = [], 0
        for source, ref, size, count, axis in zip(sources, in_refs, sizes, counts, along):
            arrivals.append(Arrival(source, ref, arrived, first, size, axis))
            first += count
        for group in (False, True):
            for piece in (-1, *(order or ()), *(piece for piece in range(max(counts)) if piece not in (order or ()))):
                for place, arrival in enumerate(arrivals, 1):
                    if (place in late) is group:
                        arrival.start(piece)
        departures = [
            Departure(target, ref, sent, place * slots) for place, (target, ref) in enumerate(zip(targets, out_refs))
        ]
        kernel(length_ref, arrivals, departures, *refs)
        for arrival in arrivals:
            arrival.wait()
        for departure in departures:
            departure.send_unsent()
        for departure in departures:
            departure.finish()

    return pl.pallas_call(
        body,
        out_shape=tuple(outs),
        in_specs=[pl.BlockSpec(memory_space=pltpu.SMEM if place == 0 else pl.ANY) for place in range(len(args))],
        out_specs=tuple(pl.BlockSpec(memory_space=pl.ANY) for _ in outs),
        scratch_shapes=[
            *copies_in,
            *copies_out,
            pltpu.SemaphoreType.DMA((sum(counts),)),
            pltpu.SemaphoreType.DMA((slots * len(outs),)),
            *scratch,
        ],
        compiler_params=pltpu.CompilerParams(vmem_limit_bytes=vmem),
        cost_estimate=pl.CostEstimate(flops=int(flops), bytes_accessed=0, transcendentals=0),
        name=name,
    )(*args)


def from_feature_rows(source, held_ref, steps, emit, init, after):
    length = source.ref.shape[1]
    blocks = length // 128
    for block in range(blocks):
        if block % (blocks // PIECES) == 0:
            source.wait(block // (blocks // PIECES))
        lanes = slice(block * 128, (block + 1) * 128)
        held_ref[lanes, :] = source.ref[:, lanes].T

    def step(index, carry):
        return emit(rows_at(index, CHUNKS), index, held_ref[pl.ds(index, CHUNKS, stride=steps), :], carry)

    carry = init
    for piece in range(PIECES):
        size = steps // PIECES
        carry = lax.fori_loop(piece * size, (piece + 1) * size, step, carry, unroll=4)
        after(piece)
    return carry


def to_feature_rows(load, held_ref, out, steps):
    length = out.ref.shape[1]

    def step(index, carry):
        held_ref[pl.ds(index, CHUNKS, stride=steps), :] = load(rows_at(index, CHUNKS), index)
        return carry

    lax.fori_loop(0, steps, step, 0, unroll=4)
    for block in range(length // 128):
        lanes = slice(block * 128, (block + 1) * 128)
        out.ref[:, lanes] = held_ref[lanes, :].T
    out.send()


def spread_rows(value, out):
    for group in range(out.ref.shape[0]):
        out.ref[group, :, :] = value
    out.send()


def narrowed(values, width):
    return jnp.concatenate([v[:, at : at + width] for v in values for at in range(0, v.shape[1], width)], axis=0)


def widened(rows, first, count):
    return jnp.concatenate([rows[first + place : first + place + 1, :] for place in range(count)], axis=1)


def total_rows(sums_ref):
    value = sums_ref[0, :, :]
    for other in range(1, sums_ref.shape[0]):
        value += sums_ref[other, :, :]
    return value


def assemble_states(parts, whole_ref):
    half = parts[0].shape[0] // 2
    states = half * len(parts)
    for place, part in enumerate(parts):
        whole_ref[place * half : (place + 1) * half, :] = part[:half, :]
        whole_ref[states + place * half : states + (place + 1) * half, :] = part[half:, :]


def assemble_output(parts, whole_ref):
    half = parts[0].shape[0] // 2
    states = half * len(parts)
    for place, part in enumerate(parts):
        whole_ref[place * half : (place + 1) * half, :] = part[:half, :]
        whole_ref[states + place * half : states + (place + 1) * half, :] = -part[half:, :]


def assemble_glu(parts, whole_ref, quarter):
    half = parts[0].shape[0] // 2
    width = half * len(parts)
    for place, part in enumerate(parts):
        whole_ref[lanes_at(quarter ^ place, half), :] = part[:half, :]
        whole_ref[pl.ds(pl.multiple_of(width + (quarter ^ place) * half, half), half), :] = part[half:, :]


def norm_rows(sums, counted):
    centre = sums[0:1, :] / counted
    meansq = sums[1:2, :] / counted
    return centre, lax.rsqrt(meansq - centre * centre + EPSILON)


def drive_phase(normed_ref, b_ref, drive_ref, gamma):
    drive_ref[...] = dot(normed_ref[...], b_ref[...], NT) * jnp.concatenate([gamma, gamma], axis=1)


def store_states(low_ref, drive_own_ref):
    def emit(rows, step, re, im, drive_re, drive_im, held):
        states = re.shape[1]
        low_ref[rows, :states] = re.astype(LOW)
        low_ref[rows, states:] = im.astype(LOW)
        drive_own_ref[rows, :128] = drive_re[:, :128].astype(drive_own_ref.dtype)
        drive_own_ref[rows, 128:] = drive_im[:, :128].astype(drive_own_ref.dtype)
        return held

    return emit


def pre_products(low_ref, c_ref, held_ref):
    total, full = low_ref.shape[0], c_ref.shape[1]
    for piece in pieces_of(total):
        held_ref[piece, :full] = dot(low_ref[piece, :], c_ref[...], NN)


def pre_piece(piece, held_ref, normed_ref, skip, active_ref, slope_ref):
    full = normed_ref.shape[1]
    for rows, _ in blocks_of(piece.start, piece.stop):
        value = held_ref[rows, :full] + skip * normed_ref[rows, :].astype(F32)
        cdf, density = gelu_parts(value)
        active_ref[rows, :] = (value * cdf).astype(LOW)
        slope_ref[rows, :] = (cdf + value * density).astype(slope_ref.dtype)


def pre_grad_piece(piece, held_ref, slope_ref, pre_grad_ref):
    full = slope_ref.shape[1]
    for rows, _ in blocks_of(piece.start, piece.stop):
        pre_grad_ref[rows, :] = (held_ref[rows, :full] * slope_ref[rows, :].astype(F32)).astype(LOW)


def skip_sums(pre_grad_ref, normed_ref, quarter, small_ref):
    own = lanes_at(quarter, 128)
    value = jnp.zeros((8, 128), F32)
    for rows, _ in blocks_of(0, pre_grad_ref.shape[0]):
        value += folded(pre_grad_ref[rows, own].astype(F32) * normed_ref[rows, own].astype(F32))
    small_ref[3:4, 0:128] = column_sum(value)


def bias_sums(grad_gated_ref, quarter, small_ref):
    for place in range(2):
        lanes = lanes_at(quarter + 4 * place, 128)
        value = jnp.zeros((8, 128), F32)
        for rows, _ in blocks_of(0, grad_gated_ref.shape[0]):
            value += folded(grad_gated_ref[rows, lanes].astype(F32))
        small_ref[4 + place : 5 + place, 0:128] = column_sum(value)


def together(*parts):
    def run():
        for part in parts:
            part()

    return run


def adjoint_phase(low_ref, im_lane, drive_own_ref, state, first_row, length, grad_state_ref, grad_driven_ref, small_ref, reverse, beside):
    total = grad_state_ref.shape[0]
    steps = total // CHUNKS
    states = state.shape[1]
    rate_re = state[first_row : first_row + 1, :]
    rate_im = state[first_row + 1 : first_row + 2, :]
    gamma = jnp.broadcast_to(state[first_row + 2 : first_row + 3, :], (CHUNKS, states))

    def emit(rows, step, re, im, drive_re, drive_im, held):
        out_re, out_im = gamma * re, gamma * im
        if not reverse:
            keep = keep_rows(step, CHUNKS, steps, length)
            out_re, out_im = jnp.where(keep, out_re, 0.0), jnp.where(keep, out_im, 0.0)
        grad_driven_ref[rows, :states] = out_re.astype(LOW)
        grad_driven_ref[rows, states:] = out_im.astype(LOW)
        one, two, three = held
        own_re, own_im = re[:, :128], im[:, :128]
        late_re, late_im = own_re - drive_re[:, :128], own_im - drive_im[:, :128]
        low_re = low_ref[rows, :128].astype(F32)
        low_im = low_ref[rows, im_lane : im_lane + 128].astype(F32)
        one = one + folded(late_re * low_re + late_im * low_im)
        two = two + folded(late_im * low_re - late_re * low_im)
        three = three + folded(
            own_re * drive_own_ref[rows, :128].astype(F32) + own_im * drive_own_ref[rows, 128:].astype(F32)
        )
        return one, two, three

    zero = jnp.zeros((8, 128), F32)
    one, two, three = sweep(grad_state_ref, rate_re, -rate_im, steps, reverse, emit, (zero, zero, zero), beside=beside)
    small_ref[0:1, 0:128] = column_sum(one)
    small_ref[1:2, 0:128] = column_sum(two)
    small_ref[2:3, 0:128] = column_sum(three)


def glu_products(grads_ref, first, grad_gated_ref, active_ref, quarter):
    full = active_ref.shape[1]

    def product(place):
        lanes = pl.ds(pl.multiple_of(place * full + quarter * 128, 128), 128)
        got = dot(grad_gated_ref[:, lanes], active_ref[...], TN)
        grads_ref[first + place * 128 : first + (place + 1) * 128, :] = got.astype(LOW)

    return [functools.partial(product, place) for place in range(2)]


def output_products(grads_ref, low_re, low_im, pre_grad_ref, states):
    half = states // 4

    def product(place, low, sign):
        got = sign * dot(low(), pre_grad_ref[...], TN)[:half, :]
        grads_ref[2 * half + place * half : 2 * half + (place + 1) * half, :] = got.astype(LOW)

    return [functools.partial(product, 0, low_re, 1.0), functools.partial(product, 1, low_im, -1.0)]


def beside_sweep(products, grad_gated_ref, pre_grad_ref, normed_ref, quarter, small_ref):
    first, second, third, fourth = products
    return (
        together(first, functools.partial(bias_sums, grad_gated_ref, quarter, small_ref)),
        together(second, functools.partial(skip_sums, pre_grad_ref, normed_ref, quarter, small_ref)),
        third,
        fourth,
    )


def input_products(grads_ref, grad_driven_ref, normed_ref, states):
    half = states // 4
    for place in range(2):
        lanes = slice(place * states, place * states + 128)
        got = dot(grad_driven_ref[:, lanes], normed_ref[...], TN)[:half, :]
        grads_ref[place * half : (place + 1) * half, :] = got.astype(LOW)


def enter_kernel(length_ref, ins, outs, held_ref, params_ref):
    x, gain, shift, skip, bias, nu, theta, gamma, b, c, w = ins
    tokens, spread, first_out = outs
    length = length_ref[0]
    width, total = x.ref.shape
    steps = total // CHUNKS

    def emit(rows, index, value, carry):
        tokens.ref[rows, :] = value
        kept = jnp.where(keep_rows(index, CHUNKS, steps, length), value, 0.0)
        return carry[0] + folded(kept), carry[1] + folded(kept * kept)

    zero = jnp.zeros((8, width), F32)
    plain, square = from_feature_rows(x, held_ref, steps, emit, (zero, zero), tokens.send_piece)
    plain = column_sum(plain)
    counted = jnp.full((1, width), length, jnp.int32).astype(F32)
    spread_rows(jnp.concatenate([plain, column_sum(square), counted, jnp.zeros((5, width), F32)], axis=0), spread)
    mean = plain / counted

    each = total // PIECES

    def centred(rows, index, carry):
        place = pl.ds(pl.multiple_of(4 * width + index * 32 % each, 32), 32)
        first_out.ref[place, lanes_at(index * 32 // each, width)] = (tokens.ref[rows, :] - mean).astype(LOW)
        return carry

    for_rows(0, total, 32, centred, unroll=4)
    for value in (gain, shift, skip, bias, nu, theta, gamma):
        value.wait()
    params_ref[...] = jnp.zeros(params_ref.shape, F32)
    for layer in range(LAYERS):
        first = 5 * layer
        params_ref[first + GAIN : first + GAIN + 1, :] = gain.ref[layer : layer + 1, :]
        params_ref[first + SHIFT : first + SHIFT + 1, :] = shift.ref[layer : layer + 1, :]
        params_ref[first + SKIP : first + SKIP + 1, :] = skip.ref[layer : layer + 1, :]
        params_ref[first + BIAS_LINEAR : first + BIAS_GATE + 1, :] = bias.ref[layer, :, :]
        first = 10 + 3 * layer
        for row, source in enumerate((nu, theta, gamma)):
            params_ref[first + row : first + row + 1, : source.ref.shape[1]] = source.ref[layer : layer + 1, :]
    params_ref[OWN_MEAN : OWN_MEAN + 1, :] = mean
    rest = params_ref[...]
    first_out.ref[6 * width :, :] = jnp.zeros((32, 4 * width), LOW)
    for place in range(3):
        high = rest.astype(LOW)
        first_out.ref[6 * width : 6 * width + PARAM_ROWS, place * width : (place + 1) * width] = high
        rest = rest - high.astype(F32)
    first_out.send(4 * width, 2 * width + 32)
    send_weights(0, b, c, w, first_out)


def send_weights(layer, b, c, w, whole):
    width = b.ref.shape[1]
    for value, first, size in ((b, 0, width), (c, width, width), (w, 2 * width, 2 * width)):
        value.wait()
        whole.send(first, size, source=value.ref.at[layer])


def total_kernel(length_ref, ins, outs):
    outs[0].ref[...] = total_rows(ins[0].ref)


def cotangent_kernel(length_ref, ins, outs, held_ref):
    x, b, c, w = ins
    whole, later = outs
    width, total = x.ref.shape
    steps = total // CHUNKS
    each = steps // PIECES

    def emit(rows, index, value, carry):
        whole.ref[rows, :] = value
        place = pl.ds(pl.multiple_of(4 * width + index % each * CHUNKS, CHUNKS), CHUNKS)
        later.ref[place, lanes_at(index // each, width)] = value.astype(LOW)
        return carry

    def after(piece):
        whole.send_piece(piece)
        if piece == 1:
            send_weights(1, b, c, w, later)

    from_feature_rows(x, held_ref, steps, emit, 0, after)
    later.send(4 * width, total // PIECES)


def start_kernel(length_ref, ins, outs, stats_ref, stream_ref, drive_ref, pre_ref, held_ref, b_ref, c_ref, w_ref, low_ref):
    all_stats, tokens, parts = ins[:4], ins[4], ins[5:]
    feature, state_out, norm, normed, drive_own, low_own, stream, linear_out, gate_out, slope, active, b_out, c_out, w_out, spread = outs
    length, quarter = length_ref[0], own_quarter()
    total, full = active.ref.shape
    steps = total // CHUNKS
    width = full // 4
    lane = lax.broadcasted_iota(jnp.int32, (8, width), 1)
    tails = []
    rows_refs = []
    for part in parts:
        for piece in (6, 4, 5):
            part.wait(piece)
        rows_refs.append(part.ref.at[pl.ds(4 * width, 2 * width + PARAM_ROWS)])
    for place, part_ref in enumerate(rows_refs):
        value = sum(part_ref[2 * width :, at * width : (at + 1) * width].astype(F32) for at in range(3))
        feature.ref[:, lanes_at(quarter ^ place, width)] = value
        tails.append(value[8:16, :])
    for pair in range(2):
        early, late = tails[2 * pair : 2 * pair + 2]
        logs = jnp.where(lane < 64, early, pltpu.roll(late, 64, 1))
        lanes = slice(pair * width, (pair + 1) * width)
        for layer in range(LAYERS):
            first = 2 + 3 * layer
            modulus = jnp.exp(-jnp.exp(logs[first : first + 1, :]))
            angle = jnp.exp(logs[first + 1 : first + 2, :])
            state_out.ref[first : first + 1, lanes] = modulus * jnp.cos(angle)
            state_out.ref[first + 1 : first + 2, lanes] = modulus * jnp.sin(angle)
            state_out.ref[first + 2 : first + 3, lanes] = jnp.exp(logs[first + 2 : first + 3, :])
    for place, stats in enumerate(all_stats):
        stats_ref[:, lanes_at(quarter ^ place, width)] = stats.wait()[...]
    centre, inv_dev = norm_rows(stats_ref[0:2, :], stats_ref[2:3, :])
    norm.ref[...] = jnp.zeros_like(norm.ref)
    norm.ref[0:1, :] = centre
    norm.ref[1:2, :] = inv_dev
    norm.ref[2:3, :] = stats_ref[2:3, :]
    for out in (feature, state_out, norm):
        out.send()

    each = total // PIECES
    assemble_states([part.wait(0).at[0:width] for part in parts], b_ref)
    b_out.send(source=b_ref)
    state = state_out.ref[...]
    states = state.shape[1]
    gamma = state[2 + GAMMA : 3 + GAMMA, :]
    gammas = jnp.concatenate([gamma, gamma], axis=1)
    rows_of = []
    for place in range(4):
        lanes = lanes_at(quarter ^ place, width)
        rows_of.append((lanes, feature.ref[OWN_MEAN : OWN_MEAN + 1, lanes], norm.ref[0:1, lanes], norm.ref[1:2, lanes],
                        feature.ref[GAIN : GAIN + 1, lanes], feature.ref[SHIFT : SHIFT + 1, lanes]))
    for at, piece in enumerate(pieces_of(total)):
        tokens.wait(at)
        for rows, index in blocks_of(piece.start, piece.stop):
            keep = keep_rows(index, 16, steps, length)
            there = slice(rows.start % each, rows.start % each + 16)
            for place, (lanes, mean, middle, inverse, gain, shift) in enumerate(rows_of):
                if place == 0:
                    value = tokens.ref[rows, :]
                else:
                    value = rows_refs[place][there, at * width : (at + 1) * width].astype(F32) + mean
                stream_ref[rows, lanes] = value
                z = (value - middle) * inverse * gain + shift
                normed.ref[rows, lanes] = jnp.where(keep, z, 0.0).astype(LOW)
        normed.send_piece(at)
        drive_ref[piece, :] = dot(normed.ref[piece, :], b_ref[...], NT) * gammas
    assemble_output([part.wait(1).at[width : 2 * width] for part in parts], c_ref)
    c_out.send(source=c_ref)
    store = store_states(low_ref, drive_own.ref)

    def emit(rows, step, re, im, drive_re, drive_im, held):
        low_own.ref[rows, :128] = re[:, :128].astype(LOW)
        low_own.ref[rows, 128:] = im[:, :128].astype(LOW)
        return store(rows, step, re, im, drive_re, drive_im, held)

    sweep(drive_ref, state[2:3, :], state[3:4, :], steps, False, emit, 0)
    drive_own.send()
    low_own.send()

    assemble_glu([part.wait().at[2 * width : 4 * width] for part in parts], w_ref, quarter)
    w_out.send(source=w_ref)
    skip = feature.ref[SKIP : SKIP + 1, :]
    bias_linear = feature.ref[BIAS_LINEAR : BIAS_LINEAR + 1, :]
    bias_gate = feature.ref[BIAS_GATE : BIAS_GATE + 1, :]
    pre_products(low_ref, c_ref, pre_ref)
    for piece in pieces_of(total):
        pre_piece(piece, pre_ref, normed.ref, skip, active.ref, slope.ref)
        held_ref[piece, :] = dot(active.ref[piece, :], w_ref[...], NT)
    active.send()
    slope.send()
    plain, square = jnp.zeros((8, full), F32), jnp.zeros((8, full), F32)
    for place, piece in enumerate(pieces_of(total)):
        for rows, index in blocks_of(piece.start, piece.stop):
            keep = keep_rows(index, 16, steps, length)
            linear = held_ref[rows, :full] + bias_linear
            gate = jax.nn.sigmoid(held_ref[rows, full:] + bias_gate)
            mixed = linear * gate
            gate_out.ref[rows, :] = gate.astype(LOW)
            linear_out.ref[rows, :] = (mixed * (1.0 - gate)).astype(LOW)
            moved = stream_ref[rows, :] + jnp.where(keep, mixed, 0.0)
            stream.ref[rows, :] = moved
            kept = jnp.where(keep, moved, 0.0)
            plain += folded(kept)
            square += folded(kept * kept)
        for out in (stream, linear_out, gate_out):
            out.send_piece(place)
    carry = plain, square
    spread_rows(narrowed([column_sum(carry[0]), column_sum(carry[1])], width), spread)


def middle_kernel(
    length_ref, ins, outs,
    small_ref, b_ref, c_ref, w_ref, normed_ref, drive_ref, drive_own_ref, low_ref, slope_ref, active_ref, held_ref, pre_ref, mixed_ref,
    up_ref, grad_gated_ref, pre_grad_ref, grad_driven_ref, grads_ref,
):
    sums, norm0, feature_in, state_in, stream, up_own = ins[:6]
    parts = ins[6:]
    result, base, spread, norm, *shares = outs
    length, quarter = length_ref[0], own_quarter()
    total, full = stream.ref.shape
    steps = total // CHUNKS
    width = 128
    counted = norm0.wait()[2:3, :]
    feature = feature_in.wait()
    state = state_in.wait()[...]
    states = state.shape[1]
    whole = total_rows(sums.wait())
    whole = jnp.concatenate([widened(whole, 0, 4), widened(whole, 4, 4)], axis=0)
    centre, inv_dev = norm_rows(whole, counted)
    norm.ref[...] = jnp.zeros_like(norm.ref)
    norm.ref[0:1, :] = centre
    norm.ref[1:2, :] = inv_dev
    norm.ref[2:3, :] = counted
    norm.send()
    gain = feature[5 + GAIN : 6 + GAIN, :]
    shift = feature[5 + SHIFT : 6 + SHIFT, :]
    skip = feature[5 + SKIP : 6 + SKIP, :]

    for part in parts:
        part.wait(0)
    assemble_states([part.ref.at[0:width] for part in parts], b_ref)
    gamma = state[5 + GAMMA : 6 + GAMMA, :]
    gammas = jnp.concatenate([gamma, gamma], axis=1)
    for place, piece in enumerate(pieces_of(total)):
        stream.wait(place)
        for rows, index in blocks_of(piece.start, piece.stop):
            z = (stream.ref[rows, :] - centre) * inv_dev
            normed_ref[rows, :] = jnp.where(keep_rows(index, 16, steps, length), z * gain + shift, 0.0).astype(LOW)
        drive_ref[piece, :] = dot(normed_ref[piece, :], b_ref[...], NT) * gammas
    sweep(drive_ref, state[5:6, :], state[6:7, :], steps, True, store_states(low_ref, drive_own_ref), 0)
    for part in parts:
        part.wait()
    assemble_output([part.ref.at[width : 2 * width] for part in parts], c_ref)
    assemble_glu([part.ref.at[2 * width : 4 * width] for part in parts], w_ref, quarter)
    up_own.wait()
    own = lanes_at(quarter, width)

    for rows, _ in blocks_of(0, total):
        up_ref[rows, own] = up_own.ref[rows, :]
    for place, piece in enumerate(pieces_of(total)):
        for other in range(1, 4):
            lanes = lanes_at(quarter ^ other, width)
            up_ref[piece, lanes] = parts[other].ref[4 * width :, place * width : (place + 1) * width].astype(F32)
    bias_linear = feature[5 + BIAS_LINEAR : 6 + BIAS_LINEAR, :]
    bias_gate = feature[5 + BIAS_GATE : 6 + BIAS_GATE, :]
    pre_products(low_ref, c_ref, pre_ref)
    for piece in pieces_of(total):
        pre_piece(piece, pre_ref, normed_ref, skip, active_ref, slope_ref)
        held_ref[piece, :] = dot(active_ref[piece, :], w_ref[...], NT)
    for piece in pieces_of(total):
        for rows, index in blocks_of(piece.start, piece.stop):
            keep = keep_rows(index, 16, steps, length)
            linear = held_ref[rows, :full] + bias_linear
            gate = jax.nn.sigmoid(held_ref[rows, full:] + bias_gate)
            mixed = linear * gate
            up = jnp.where(keep, up_ref[rows, :], 0.0)
            grad_gated_ref[rows, :full] = (up * gate).astype(LOW)
            grad_gated_ref[rows, full:] = (up * mixed * (1.0 - gate)).astype(LOW)
            mixed_ref[rows, :] = jnp.where(keep, mixed, 0.0)
        pre_ref[piece, :] = dot(grad_gated_ref[piece, :], w_ref[...], NN)
    for piece in pieces_of(total):
        pre_grad_piece(piece, pre_ref, slope_ref, pre_grad_ref)
        drive_ref[piece, :] = dot(pre_grad_ref[piece, :], c_ref[...], NT)
    small_ref[...] = jnp.zeros_like(small_ref)
    for rows, _ in blocks_of(0, total):
        result.ref[rows, :] = stream.ref[rows, own] + mixed_ref[rows, own]
    result.send()
    adjoint_phase(
        low_ref, states, drive_own_ref, state, 5, length, drive_ref, grad_driven_ref, small_ref, False,
        beside_sweep(
            glu_products(grads_ref, 2 * width, grad_gated_ref, active_ref, quarter)
            + output_products(grads_ref, lambda: low_ref[:, 0:128], lambda: low_ref[:, states : states + 128], pre_grad_ref, states),
            grad_gated_ref, pre_grad_ref, normed_ref, quarter, small_ref,
        ),
    )
    scale = inv_dev * gain
    for piece in pieces_of(total):
        pre_ref[piece, :] = dot(grad_driven_ref[piece, :], b_ref[...], NN)
    plain, scaled = jnp.zeros((8, full), F32), jnp.zeros((8, full), F32)
    for place, piece in enumerate(pieces_of(total)):
        for rows, _ in blocks_of(piece.start, piece.stop):
            grad = pre_ref[rows, :] + skip * pre_grad_ref[rows, :].astype(F32)
            z = (stream.ref[rows, :] - centre) * inv_dev
            base.ref[rows, :] = scale * grad + up_ref[rows, :]
            plain += folded(grad)
            scaled += folded(grad * z)
        base.send_piece(place)
    input_products(grads_ref, grad_driven_ref, normed_ref, states)
    sent = narrowed([column_sum(plain), column_sum(scaled)], width)
    spread_rows(jnp.concatenate([sent, small_ref[:, 0:width]], axis=0), spread)
    send_halves(grads_ref, shares, 0)


def last_kernel(
    length_ref, ins, outs, held_ref, grad_state_ref, grad_gated_ref, pre_grad_ref, grad_driven_ref, small_ref, up_ref, grads_ref, pack_ref, low_ref
):
    (sums, norm1, feature_in, state_in, norm0, stream, base, gate, linear, w, slope, c, normed, active, low, drive_own, b, x) = ins
    kept, sent, up_out, grad_out = outs
    length, quarter = length_ref[0], own_quarter()
    total, full = stream.ref.shape
    steps = total // CHUNKS
    width = 128
    own = lanes_at(quarter, width)
    feature, norm_ref = feature_in.wait(), norm1.wait()
    state = state_in.wait()[...]
    counted = norm_ref[2:3, :]
    whole = total_rows(sums.wait())
    whole = jnp.concatenate([widened(whole, 0, 4), widened(whole, 4, 4)], axis=0)
    centre, inv_dev = norm_ref[0:1, :], norm_ref[1:2, :]
    scale = inv_dev * feature[5 + GAIN : 6 + GAIN, :]
    level = scale * whole[0:1, :] / counted
    tilt = scale * inv_dev * whole[1:2, :] / counted

    for place, piece in enumerate(pieces_of(total)):
        for value in (stream, base, gate, linear):
            value.wait(place)
        for rows, index in blocks_of(piece.start, piece.stop):
            keep = keep_rows(index, 16, steps, length)
            up = base.ref[rows, :] - jnp.where(keep, level + (stream.ref[rows, :] - centre) * tilt, 0.0)
            up_ref[rows, :] = up
            up = jnp.where(keep, up, 0.0)
            grad_gated_ref[rows, :full] = (up * gate.ref[rows, :].astype(F32)).astype(LOW)
            grad_gated_ref[rows, full:] = (up * linear.ref[rows, :].astype(F32)).astype(LOW)
        if place == 0:
            w.wait()
        held_ref[piece, :] = dot(grad_gated_ref[piece, :], w.ref[...], NN)
    for value in (slope, c):
        value.wait()
    for piece in pieces_of(total):
        pre_grad_piece(piece, held_ref, slope.ref, pre_grad_ref)
        grad_state_ref[piece, :] = dot(pre_grad_ref[piece, :], c.ref[...], NT)
    small_ref[...] = jnp.zeros_like(small_ref)

    def own_up(rows, index, carry):
        up_out.ref[rows, :] = up_ref[rows, own]
        return carry

    for_rows(0, total, 16, own_up, unroll=4)
    up_out.send()
    for value in (normed, active, low, drive_own):
        value.wait()
    adjoint_phase(
        low.ref, 128, drive_own.ref, state, 2, length, grad_state_ref, grad_driven_ref, small_ref, True,
        beside_sweep(
            glu_products(grads_ref, 2 * width, grad_gated_ref, active.ref, quarter)
            + output_products(grads_ref, lambda: low.ref[:, :128], lambda: low.ref[:, 128:], pre_grad_ref, state.shape[1]),
            grad_gated_ref, pre_grad_ref, normed.ref, quarter, small_ref,
        ),
    )
    b.wait()
    x.wait()
    held_ref[:, :width] = dot(grad_driven_ref[...], b.ref[:, own], NN)
    input_products(grads_ref, grad_driven_ref, normed.ref, state.shape[1])
    zero = jnp.zeros((8, width), F32)
    centre0, inv_dev0 = norm0.wait()[0:1, own], norm0.ref[1:2, own]
    skip = feature[SKIP : SKIP + 1, own]

    def back(rows, index, carry):
        grad = held_ref[rows, :width] + skip * pre_grad_ref[rows, own].astype(F32)
        grad_out.ref[rows, :] = grad
        z = (x.ref[rows, :] - centre0) * inv_dev0
        return carry[0] + folded(grad), carry[1] + folded(grad * z)

    plain, scaled = for_rows(0, total, 16, back, (zero, zero), unroll=4)
    grad_out.send()
    small_ref[6:7, 0:width] = column_sum(plain)
    small_ref[7:8, 0:width] = column_sum(scaled)
    pack_ref[...] = jnp.zeros_like(pack_ref)
    for place in range(8):
        pack_ref[place // 4 : place // 4 + 1, place % 4 * width : (place % 4 + 1) * width] = small_ref[place : place + 1, 0:width]
    exact = pack_ref[0:8, :]
    pack_ref[8:16, :] = exact - exact.astype(LOW).astype(F32)
    half = grads_ref.shape[0] // 2
    low_ref[...] = pack_ref[...].astype(LOW)
    mine = lax.axis_index("dp") & 1
    for out, which in ((kept, mine), (sent, 1 - mine)):
        out.send(0, half, source=grads_ref.at[rows_at(which, half)])
        out.send(half, 16, source=low_ref)


def send_halves(source_ref, outs, stage):
    kept = lax.axis_index("dp") >> stage & 1
    half = source_ref.shape[0] // 2
    for out, which in zip(outs, (kept, 1 - kept)):
        out.send(source=source_ref.at[rows_at(which, half)])


def add_kernel(length_ref, ins, outs):
    outs[0].ref[...] = (ins[0].ref[...].astype(F32) + ins[1].ref[...].astype(F32)).astype(LOW)


def pair_kernel(length_ref, ins, outs, sum_ref, pack_ref):
    kept, other = ins
    for value in ins:
        value.wait()
    half = kept.ref.shape[0] - 16
    share = half // len(outs)
    small = kept.ref[half:, :].astype(F32) + other.ref[half:, :].astype(F32)
    small = small[0:8, :] + small[8:16, :]
    pack_ref[...] = jnp.concatenate([small, small - small.astype(LOW).astype(F32)], axis=0).astype(LOW)
    for piece in range(0, half, 16):
        at = slice(piece, piece + 16)
        sum_ref[at, :] = (kept.ref[at, :].astype(F32) + other.ref[at, :].astype(F32)).astype(LOW)
    for place, out in enumerate(outs):
        out.send(0, share, source=sum_ref.at[rows_at((lax.axis_index("dp") >> 1) ^ place, share)])
        out.send(share, 16, source=pack_ref)


def share_kernel(length_ref, ins, outs):
    half, *blocks = ins
    out, both, small = outs
    share, rows = out.ref.shape[0], half.ref.shape[0]
    value = blocks[0].ref[...].astype(F32)
    for block in blocks[1:]:
        value += block.ref[...].astype(F32)
    out.ref[...] = value[:share, :].astype(LOW)
    both.ref[0:rows, :] = half.ref[...]
    both.ref[rows:, :] = value[:share, :].astype(LOW)
    small.ref[...] = value[share : share + 8, :] + value[share + 8 :, :]


def finish_kernel(length_ref, ins, outs, held_ref, order_ref):
    small0, bn1, norm0, feature, nu, theta, result, up, grad, x = ins
    nu_out, theta_out, gamma_out, skip_out, bias_out, gain_out, shift_out, result_out, out = outs
    length, quarter = length_ref[0], own_quarter()
    total, width = up.ref.shape
    steps = total // CHUNKS
    own = lanes_at(quarter, width)
    states = nu_out.ref.shape[1]
    result.wait()
    to_feature_rows(lambda rows, index: result.ref[rows, :], order_ref, result_out, steps)
    for value in ins:
        value.wait()
    whole = total_rows(bn1.ref)
    held_ref[0:1, :] = widened(whole, 0, 4)
    held_ref[1:2, :] = widened(whole, 4, 4)
    held_ref[16:32, :width] = whole
    for place in range(8):
        held_ref[8 + place : 9 + place, :width] = small0.ref[place // 4 : place // 4 + 1, place % 4 * width : (place % 4 + 1) * width]
    for layer, first in ((0, 8), (1, 24)):
        at = slice(layer, layer + 1)
        nu_out.ref[at, :] = -jnp.exp(nu.ref[at, :]) * held_ref[first : first + 1, :states]
        theta_out.ref[at, :] = jnp.exp(theta.ref[at, :]) * held_ref[first + 1 : first + 2, :states]
        gamma_out.ref[at, :] = held_ref[first + 2 : first + 3, :states]
        skip_out.ref[at, :] = held_ref[first + 3 : first + 4, :width]
        bias_out.ref[layer, 0:1, :] = held_ref[first + 4 : first + 5, :width]
        bias_out.ref[layer, 1:2, :] = held_ref[first + 5 : first + 6, :width]
    shift_out.ref[0:1, :] = held_ref[14:15, :width]
    gain_out.ref[0:1, :] = held_ref[15:16, :width]
    shift_out.ref[1:2, :] = held_ref[0:1, own]
    gain_out.ref[1:2, :] = held_ref[1:2, own]
    counted = norm0.ref[2:3, own]
    centre, inv_dev = norm0.ref[0:1, own], norm0.ref[1:2, own]
    level = held_ref[14:15, :width] / counted
    tilt = held_ref[15:16, :width] * inv_dev / counted
    scale = inv_dev * feature.ref[GAIN : GAIN + 1, own]

    def load(rows, index):
        keep = keep_rows(index, CHUNKS, steps, length)
        inner = grad.ref[rows, :] - level - (x.ref[rows, :] - centre) * tilt
        return up.ref[rows, :] + jnp.where(keep, scale * inner, 0.0)

    to_feature_rows(load, order_ref, out, steps)


def send_wide(layer, outs, held_ref):
    half = outs[0].target.shape[1]
    for out, first, size in zip(outs, (0, half, 2 * half), (half, half, 2 * half)):
        out.send(layer, 1, source=held_ref.at[pl.ds(0, 1), pl.ds(first, size)])


def widen1_kernel(length_ref, ins, outs, held_ref):
    half = ins[0].ref.shape[0]
    mine = lax.axis_index("dp") & 1
    for which, value in ((mine, ins[0]), (1 - mine, ins[1])):
        held_ref[0, rows_at(which, half), :] = value.ref[0:half, :].astype(F32)
    send_wide(1, outs, held_ref)


def widen0_kernel(length_ref, ins, outs, held_ref):
    groups = len(ins)
    share = ins[0].ref.shape[0]
    for place, value in enumerate(ins):
        owner = lax.axis_index("dp") ^ place
        first = value.ref.shape[0] - share
        held_ref[0, rows_at((owner & 1) * (groups // 2) + (owner >> 1), share), :] = value.ref[first:, :].astype(F32)
    send_wide(0, outs, held_ref)


def shape(*dims, dtype=F32):
    return jax.ShapeDtypeStruct(dims, dtype)


def swap(value, bit, sharers):
    pairs = [(q * sharers + r, (q ^ bit) * sharers + r) for q in range(4) for r in range(sharers)]
    return lax.ppermute(value, "state", pairs)


def across(value, axes):
    return lax.all_to_all(value, axes, 0, 0, tiled=True)


def local(
    inputs, lengths, cotangent, bn_gain, bn_bias, b_weight, c_weight, nu_log, theta_log, gamma_log, skip_weight,
    glu_weight, glu_bias, dp_size, state_size,
):
    sharers = state_size // 4
    place = lax.axis_index("state").astype(jnp.int32)

    def joined(value, axis):
        if sharers == 1:
            return value
        groups = [[q * sharers + r for r in range(sharers)] for q in range(4)]
        return lax.all_gather(value, "state", axis=axis, axis_index_groups=groups, tiled=True)

    def own(value, axis):
        if sharers == 1:
            return value
        size = value.shape[axis] // sharers
        return lax.dynamic_slice_in_dim(value, place % sharers * size, size, axis)

    inputs, cotangent = joined(inputs, 1), joined(cotangent, 1)
    bn_gain, bn_bias, skip_weight = joined(bn_gain, 1), joined(bn_bias, 1), joined(skip_weight, 1)
    nu_log, theta_log, gamma_log = joined(nu_log, 1), joined(theta_log, 1), joined(gamma_log, 1)
    b_weight, c_weight = joined(b_weight, 2), joined(c_weight, 2)
    glu_weight, glu_bias = joined(glu_weight, 2), joined(glu_bias, 2)
    width, total = inputs.shape[1:]
    full = b_weight.shape[3]
    states = b_weight.shape[2] * 4
    own_states = b_weight.shape[2]
    share = 4 * width // dp_size
    piece = total // PIECES

    stages = dp_size.bit_length() - 1

    def exchange(value, bit):
        return lax.ppermute(value, "dp", [(i, i ^ bit) for i in range(dp_size)])

    def add(one, other):
        return call_small(add_kernel, (shape(*one.shape, dtype=LOW),), [], (one, other), "add")[0]

    b_weight, c_weight = b_weight.reshape(LAYERS, width, full), c_weight.reshape(LAYERS, width, full)
    glu_weight = glu_weight.reshape(LAYERS, 2 * width, full)
    tokens, sums, first = call(
        enter_kernel,
        (
            shape(total, width),
            shape(dp_size, 8, width),
            shape(6 * width + PARAM_ROWS, full, dtype=LOW),
        ),
        [pltpu.VMEM((total, width), F32), pltpu.VMEM((PARAM_ROWS, width), F32)],
        (lengths, inputs[0], bn_gain, bn_bias, skip_weight, glu_bias, nu_log, theta_log, gamma_log, b_weight, c_weight, glu_weight),
        "enter",
        pieces={1: piece},
        axes={1: 1},
        late=(9, 10, 11),
    )
    near, far = swap(first, 1, sharers), swap(first, 2, sharers)
    (stats,) = call_small(total_kernel, (shape(8, width),), [], (across(sums, "dp"),), "total")
    stats_near, stats_far = swap(stats, 1, sharers), swap(stats, 2, sharers)
    cotangent, tokens = lax.optimization_barrier((cotangent, tokens))
    up_own, later = call(
        cotangent_kernel,
        (
            shape(total, width),
            shape(6 * width, full, dtype=LOW),
        ),
        [pltpu.VMEM((total, width), F32)],
        (lengths, cotangent[0], b_weight, c_weight, glu_weight),
        "cotangent",
        pieces={1: piece},
        axes={1: 1},
        late=(2, 3, 4),
    )
    later_far = swap(later, 2, sharers)
    near, far, stats_near, stats_far, later = lax.optimization_barrier((near, far, stats_near, stats_far, later))
    parts = (first, near, far, swap(far, 1, sharers))
    all_stats = (stats, stats_near, stats_far, swap(stats_far, 1, sharers))
    feature, state, norm0, normed0, drive0, low0, stream1, linear0, gate0, slope0, active0, b_all, c_all, w_all, sums1 = call(
        start_kernel,
        (
            shape(PARAM_ROWS, full),
            shape(8, states),
            shape(8, full),
            shape(total, full, dtype=LOW),
            shape(total, 256),
            shape(total, 256, dtype=LOW),
            shape(total, full),
            shape(total, full, dtype=LOW),
            shape(total, full, dtype=LOW),
            shape(total, full, dtype=LOW),
            shape(total, full, dtype=LOW),
            shape(2 * states, full, dtype=LOW),
            shape(2 * states, full, dtype=LOW),
            shape(2 * full, full, dtype=LOW),
            shape(dp_size, 8, width),
        ),
        [
            pltpu.VMEM((8, full), F32),
            pltpu.VMEM((total, full), F32),
            pltpu.VMEM((total, 2 * states), F32),
            pltpu.VMEM((total, full), F32),
            pltpu.VMEM((total, 2 * full), F32),
            pltpu.VMEM((2 * states, full), LOW),
            pltpu.VMEM((2 * states, full), LOW),
            pltpu.VMEM((2 * full, full), LOW),
            pltpu.VMEM((total, 2 * states), LOW),
        ],
        (lengths, *all_stats, tokens, *parts),
        "start",
        pieces={5: piece} | {place: width for place in (6, 7, 8, 9)},
        order=(4, 5),
        bare=(11, 12, 13),
        flops=0,
    )
    sums1 = across(sums1, "dp")
    later_far, sums1 = lax.optimization_barrier((later_far, sums1))
    later_parts = (later, swap(later, 1, sharers), later_far, swap(later_far, 1, sharers))
    result_rows, base, bn1, norm1, *halves1 = call(
        middle_kernel,
        (
            shape(total, width),
            shape(total, full),
            shape(dp_size, 16, width),
            shape(8, full),
            shape(2 * width, full, dtype=LOW),
            shape(2 * width, full, dtype=LOW),
        ),
        [
            pltpu.VMEM((8, full), F32),
            pltpu.VMEM((2 * states, full), LOW),
            pltpu.VMEM((2 * states, full), LOW),
            pltpu.VMEM((2 * full, full), LOW),
            pltpu.VMEM((total, full), LOW),
            pltpu.VMEM((total, 2 * states), F32),
            pltpu.VMEM((total, 256), F32),
            pltpu.VMEM((total, 2 * states), LOW),
            pltpu.VMEM((total, full), F32),
            pltpu.VMEM((total, full), LOW),
            pltpu.VMEM((total, 2 * full), F32),
            pltpu.VMEM((total, full), F32),
            pltpu.VMEM((total, full), F32),
            pltpu.VMEM((total, full), F32),
            pltpu.VMEM((total, 2 * full), LOW),
            pltpu.VMEM((total, full), LOW),
            pltpu.VMEM((total, 2 * states), LOW),
            pltpu.VMEM((4 * width, full), LOW),
        ],
        (lengths, sums1, norm0, feature, state, stream1, up_own, *later_parts),
        "middle",
        pieces={5: piece} | {place: width for place in (7, 8, 9, 10)},
        late=(6,),
        bare=(4, 5),
        flops=1e9,
    )
    bn1 = across(bn1, "dp")
    half1 = add(halves1[0], exchange(halves1[1], 1))
    bn1, half1 = lax.optimization_barrier((bn1, half1))
    other1 = exchange(half1, 1 << (stages - 1))
    kept0, sent0, up0, grad0 = call(
        last_kernel,
        (
            shape(2 * width + 16, full, dtype=LOW),
            shape(2 * width + 16, full, dtype=LOW),
            shape(total, width),
            shape(total, width),
        ),
        [
            pltpu.VMEM((total, full), F32),
            pltpu.VMEM((total, 2 * states), F32),
            pltpu.VMEM((total, 2 * full), LOW),
            pltpu.VMEM((total, full), LOW),
            pltpu.VMEM((total, 2 * states), LOW),
            pltpu.VMEM((8, full), F32),
            pltpu.VMEM((total, full), F32),
            pltpu.VMEM((4 * width, full), LOW),
            pltpu.VMEM((16, full), F32),
            pltpu.VMEM((16, full), LOW),
        ],
        (lengths, bn1, norm1, feature, state, norm0, stream1, base, gate0, linear0, w_all, slope0, c_all, normed0, active0, low0,
         drive0, b_all, tokens),
        "last",
        bare=(0, 1),
        pieces={6: piece, 7: piece, 8: piece, 9: piece},
        late=tuple(range(11, 19)),
        flops=1e11,
    )
    other1, kept0 = lax.optimization_barrier((other1, kept0))
    sent0 = exchange(sent0, 1)
    half1 = add(half1, other1)
    kept0, half1 = lax.optimization_barrier((kept0, half1))
    for stage in reversed(range(2, stages - 1)):
        half1 = add(half1, exchange(half1, 1 << stage))
    other1 = exchange(half1, 2)
    blocks = call_small(
        pair_kernel,
        (shape(share + 16, full, dtype=LOW),) * (dp_size // 2),
        [pltpu.VMEM((2 * width, full), LOW), pltpu.VMEM((16, full), LOW)],
        (kept0, sent0),
        "pair",
    )
    blocks = [blocks[0]] + [exchange(blocks[place], 2 * place) for place in range(1, dp_size // 2)]
    other1, *blocks = lax.optimization_barrier((other1, *blocks))
    half1 = add(half1, other1)
    back, both, small0 = call_small(
        share_kernel,
        (shape(share, full, dtype=LOW), shape(2 * width + share, full, dtype=LOW), shape(8, full)),
        [],
        (half1, *blocks),
        "share",
    )
    neighbour = exchange(both, 1)
    small0, neighbour = lax.optimization_barrier((small0, neighbour))
    backs = [back, neighbour]
    for place in range(2, dp_size, 2):
        backs += [exchange(back, place)]
        backs += [exchange(backs[-1], 1)]
    grad_nu, grad_theta, grad_gamma, grad_skip, grad_bias, grad_gain, grad_shift, result, grad_inputs = call(
        finish_kernel,
        (
            shape(LAYERS, own_states),
            shape(LAYERS, own_states),
            shape(LAYERS, own_states),
            shape(LAYERS, width),
            shape(LAYERS, 2, width),
            shape(LAYERS, width),
            shape(LAYERS, width),
            shape(width, total),
            shape(width, total),
        ),
        [pltpu.VMEM((32, full), F32), pltpu.VMEM((total, width), F32)],
        (lengths, small0, bn1, norm0, feature, nu_log, theta_log, result_rows, up0, grad0, tokens),
        "finish",
        late=(1, 2, 3, 4, 5, 6),
        vmem=16 * 1024 * 1024,
    )
    wide = (shape(LAYERS, width, full), shape(LAYERS, width, full), shape(LAYERS, 2 * width, full))
    held = [pltpu.VMEM((1, 4 * width, full), F32)]
    grads = call_small(widen1_kernel, wide, held, (half1, neighbour), "widen1", sent=True)
    grad_b, grad_c, grad_glu = call_small(widen0_kernel, wide, held, tuple(backs), "widen0", sent=True, into=tuple(grads))
    grad_b = grad_b.reshape(LAYERS, 2, own_states, full)
    grad_c = grad_c.reshape(LAYERS, 2, own_states, full)
    grad_glu = grad_glu.reshape(LAYERS, 2, width, full)
    return (
        own(result[None], 1),
        own(grad_inputs[None], 1),
        own(grad_gain, 1),
        own(grad_shift, 1),
        own(grad_b, 2),
        own(grad_c, 2),
        own(grad_nu, 1),
        own(grad_theta, 1),
        own(grad_gamma, 1),
        own(grad_skip, 1),
        own(grad_glu, 2),
        own(grad_bias, 2),
    )


def solution(mesh):
    in_specs = (
        P("dp", "state", None),
        P("dp"),
        P("dp", "state", None),
        P(None, "state"),
        P(None, "state"),
        P(None, None, "state", None),
        P(None, None, "state", None),
        P(None, "state"),
        P(None, "state"),
        P(None, "state"),
        P(None, "state"),
        P(None, None, "state", None),
        P(None, None, "state"),
    )
    out_specs = (
        P("dp", "state", None),
        P("dp", "state", None),
        P(None, "state"),
        P(None, "state"),
        P(None, None, "state", None),
        P(None, None, "state", None),
        P(None, "state"),
        P(None, "state"),
        P(None, "state"),
        P(None, "state"),
        P(None, None, "state", None),
        P(None, None, "state"),
    )
    step = functools.partial(local, dp_size=mesh.shape["dp"], state_size=mesh.shape["state"])
    return jax.shard_map(step, mesh=mesh, in_specs=in_specs, out_specs=out_specs, check_vma=False)
```

```python
import functools

import jax
import jax.numpy as jnp
from jax import lax
from jax.experimental import pallas as pl
from jax.experimental.pallas import tpu as pltpu
from jax.sharding import PartitionSpec as P

LAYERS = 2
CHUNKS = 16
PIECES = 4
EPSILON = 1e-05
F32 = jnp.float32
LOW = jnp.bfloat16
PARAM_ROWS = 32
OWN_MEAN = 16
VMEM_BYTES = 64 * 1024 * 1024
SMALL_VMEM_BYTES = 8 * 1024 * 1024

GAIN, SHIFT, SKIP, BIAS_LINEAR, BIAS_GATE = range(5)
RATE_RE, RATE_IM, GAMMA = range(3)

NN = (((1,), (0,)), ((), ()))
NT = (((1,), (1,)), ((), ()))
TN = (((0,), (0,)), ((), ()))


def dot(left, right, dims):
    return lax.dot_general(left, right, dims, preferred_element_type=F32)


def rows_at(index, size):
    return pl.ds(pl.multiple_of(index * size, size), size)


def lanes_at(quarter, width):
    return pl.ds(pl.multiple_of(quarter * width, width), width)


def for_rows(first, last, size, body, init=0, unroll=2):
    def step(index, carry):
        return body(rows_at(index, size), index, carry)

    return lax.fori_loop(first // size, last // size, step, init, unroll=unroll)


def blocks_of(first, last, size=16):
    return [(slice(at, at + size), at // size) for at in range(first, last, size)]


def pieces_of(total):
    size = total // PIECES
    return [slice(at, at + size) for at in range(0, total, size)]


def own_quarter():
    return (lax.axis_index("state") // (lax.axis_size("state") // 4)).astype(jnp.int32)


def keep_rows(first_step, rows, steps, length):
    row = lax.broadcasted_iota(jnp.int32, (rows, 1), 0)
    position = (row % CHUNKS) * steps + row // CHUNKS + first_step
    return position < length


def gelu_parts(value):
    return 0.5 + 0.5 * lax.erf(value * 0.7071067811865476), jnp.exp(value * value * -0.5) * 0.3989422804014327


def squared(re, im, times):
    for _ in range(times):
        re, im = re * re - im * im, 2.0 * re * im
    return re, im


def folded(value):
    return value[0:8, :] + value[8:16, :]


def column_sum(value):
    return jnp.sum(value, axis=0, keepdims=True)


def chunk_starts(re, im, rate_re, rate_im, reverse):
    row = lax.broadcasted_iota(jnp.int32, re.shape, 0)

    def moved(value, by):
        if reverse:
            return jnp.where(row < CHUNKS - by, pltpu.roll(value, CHUNKS - by, 0), 0.0)
        return jnp.where(row >= by, pltpu.roll(value, by, 0), 0.0)

    by = 1
    while by < CHUNKS:
        past_re, past_im = moved(re, by), moved(im, by)
        re, im = (
            re + rate_re * past_re - rate_im * past_im,
            im + rate_re * past_im + rate_im * past_re,
        )
        rate_re, rate_im = squared(rate_re, rate_im, 1)
        by *= 2
    return moved(re, 1), moved(im, 1)


def sweep(drive_ref, rate_re, rate_im, steps, reverse, emit, extra, after=None, beside=None, unroll=4):
    states = rate_re.shape[1]
    shape = (CHUNKS, states)
    wide_re = jnp.broadcast_to(rate_re, shape)
    wide_im = jnp.broadcast_to(rate_im, shape)

    def advance(index, re, im):
        place = steps - 1 - index if reverse else index
        rows = slice(place * CHUNKS, (place + 1) * CHUNKS) if isinstance(place, int) else rows_at(place, CHUNKS)
        drive_re = drive_ref[rows, :states]
        drive_im = drive_ref[rows, states:]
        new_re = (wide_re * re + drive_re) - wide_im * im
        new_im = (wide_re * im + drive_im) + wide_im * re
        return rows, place, new_re, new_im, drive_re, drive_im

    def first(index, carry):
        _, _, re, im, _, _ = advance(index, *carry)
        return re, im

    def second(index, carry):
        re, im, held = carry
        rows, place, re, im, drive_re, drive_im = advance(index, re, im)
        return re, im, emit(rows, place, re, im, drive_re, drive_im, held)

    zero = jnp.zeros(shape, F32)
    re, im = lax.fori_loop(0, steps, first, (zero, zero), unroll=unroll)
    far_re, far_im = rate_re, rate_im
    power = 1
    while power < steps:
        far_re, far_im = squared(far_re, far_im, 1)
        power *= 2
    re, im = chunk_starts(re, im, far_re, far_im, reverse)
    carry = (re, im, extra)
    for piece in range(PIECES):
        size = steps // PIECES
        if beside is not None:
            beside[piece]()
            for index in range(piece * size, (piece + 1) * size):
                carry = second(index, carry)
        else:
            carry = lax.fori_loop(piece * size, (piece + 1) * size, second, carry, unroll=unroll)
        if after is not None:
            after(PIECES - 1 - piece if reverse else piece)
    return carry[2]


class Arrival:
    def __init__(self, source, ref, done, first, size, axis):
        self.ref = ref
        self.copies = []
        whole = ref.shape[axis]
        for piece, start in enumerate(range(0, whole, size)):
            where = (slice(None),) * axis + (pl.ds(start, min(size, whole - start)),)
            self.copies.append(
                pltpu.make_async_copy(source.at[where], ref.at[where], done.at[first + piece])
                if size < whole
                else pltpu.make_async_copy(source, ref, done.at[first])
            )
        self.short = whole % size > 0
        self.waited = set()

    def start(self, piece):
        last = len(self.copies) - self.short
        if piece < 0 and self.short:
            self.copies[-1].start()
        if 0 <= piece < last:
            self.copies[piece].start()

    def wait(self, piece=None):
        for place in range(len(self.copies)) if piece is None else (piece,):
            if place not in self.waited:
                self.copies[place].wait()
                self.waited.add(place)
        return self.ref


class Departure:
    def __init__(self, target, ref, done, first):
        self.target, self.ref, self.done, self.first = target, ref, done, first
        self.copies = []

    def send(self, start=None, size=None, source=None):
        place = self.done.at[self.first + len(self.copies)]
        where = self.target if start is None else self.target.at[pl.ds(start, size)]
        if source is None:
            source = self.ref if start is None else self.ref.at[pl.ds(start, size)]
        self.copies.append(pltpu.make_async_copy(source, where, place))
        self.copies[-1].start()

    def send_piece(self, piece):
        size = self.target.shape[0] // PIECES
        self.send(piece * size, size)

    def send_unsent(self):
        if not self.copies:
            self.send()

    def finish(self):
        for copy in self.copies:
            copy.wait()


class Resident:
    def __init__(self, ref):
        self.ref = ref

    def wait(self, piece=None):
        return self.ref

    def send(self, start=None, size=None, source=None):
        if source is not None and start is None:
            self.ref[...] = source[...]
        elif source is not None:
            self.ref[start : start + size, :] = source[...]


def call_small(kernel, outs, scratch, args, name, sent=False, into=()):
    def body(*refs):
        count, results = len(args), len(outs)
        ins, refs = [Resident(ref) for ref in refs[:count]], refs[count + len(into) :]
        if not sent:
            kernel(None, ins, [Resident(ref) for ref in refs[:results]], *refs[results:])
            return
        targets, copied, scratch_refs = refs[:results], refs[results], refs[results + 1 :]
        departures = [Departure(target, None, copied, place * LAYERS) for place, target in enumerate(targets)]
        kernel(None, ins, departures, *scratch_refs)
        for departure in departures:
            departure.finish()

    return pl.pallas_call(
        body,
        out_shape=tuple(outs),
        in_specs=[pl.BlockSpec(memory_space=pltpu.VMEM)] * len(args) + [pl.BlockSpec(memory_space=pl.ANY)] * len(into),
        out_specs=tuple(pl.BlockSpec(memory_space=pl.ANY if sent else pltpu.VMEM) for _ in outs),
        input_output_aliases={len(args) + place: place for place in range(len(into))},
        scratch_shapes=([pltpu.SemaphoreType.DMA((LAYERS * len(outs),))] if sent else []) + list(scratch),
        compiler_params=pltpu.CompilerParams(vmem_limit_bytes=SMALL_VMEM_BYTES),
        cost_estimate=pl.CostEstimate(flops=0, bytes_accessed=0, transcendentals=0),
        name=name,
    )(*args, *into)


def call(kernel, outs, scratch, args, name, pieces=None, axes=None, bare=(), late=(), order=None, flops=0, vmem=VMEM_BYTES):
    pieces, axes = pieces or {}, axes or {}
    along = [axes.get(place, 0) for place in range(1, len(args))]
    sizes = [pieces.get(place, args[place].shape[axis]) for place, axis in enumerate(along, 1)]
    counts = [-(-args[place].shape[axis] // size) for place, (axis, size) in enumerate(zip(along, sizes), 1)]
    slots = 6
    copies_in = [pltpu.VMEM(a.shape, a.dtype) for a in args[1:]]
    copies_out = [pltpu.VMEM((8, 128) if place in bare else o.shape, o.dtype if place not in bare else F32) for place, o in enumerate(outs)]

    def body(*refs):
        refs = list(refs)

        def take(count):
            got = refs[:count]
            del refs[:count]
            return got

        (length_ref,) = take(1)
        sources = take(len(args) - 1)
        targets = take(len(outs))
        in_refs, out_refs = take(len(args) - 1), take(len(outs))
        arrived, sent = take(2)
        arrivals, first = [], 0
        for source, ref, size, count, axis in zip(sources, in_refs, sizes, counts, along):
            arrivals.append(Arrival(source, ref, arrived, first, size, axis))
            first += count
        for group in (False, True):
            for piece in (-1, *(order or ()), *(piece for piece in range(max(counts)) if piece not in (order or ()))):
                for place, arrival in enumerate(arrivals, 1):
                    if (place in late) is group:
                        arrival.start(piece)
        departures = [
            Departure(target, ref, sent, place * slots) for place, (target, ref) in enumerate(zip(targets, out_refs))
        ]
        kernel(length_ref, arrivals, departures, *refs)
        for arrival in arrivals:
            arrival.wait()
        for departure in departures:
            departure.send_unsent()
        for departure in departures:
            departure.finish()

    return pl.pallas_call(
        body,
        out_shape=tuple(outs),
        in_specs=[pl.BlockSpec(memory_space=pltpu.SMEM if place == 0 else pl.ANY) for place in range(len(args))],
        out_specs=tuple(pl.BlockSpec(memory_space=pl.ANY) for _ in outs),
        scratch_shapes=[
            *copies_in,
            *copies_out,
            pltpu.SemaphoreType.DMA((sum(counts),)),
            pltpu.SemaphoreType.DMA((slots * len(outs),)),
            *scratch,
        ],
        compiler_params=pltpu.CompilerParams(vmem_limit_bytes=vmem),
        cost_estimate=pl.CostEstimate(flops=int(flops), bytes_accessed=0, transcendentals=0),
        name=name,
    )(*args)


def from_feature_rows(source, held_ref, steps, emit, init, after):
    length = source.ref.shape[1]
    blocks = length // 128
    for block in range(blocks):
        if block % (blocks // PIECES) == 0:
            source.wait(block // (blocks // PIECES))
        lanes = slice(block * 128, (block + 1) * 128)
        held_ref[lanes, :] = source.ref[:, lanes].T

    def step(index, carry):
        return emit(rows_at(index, CHUNKS), index, held_ref[pl.ds(index, CHUNKS, stride=steps), :], carry)

    carry = init
    for piece in range(PIECES):
        size = steps // PIECES
        carry = lax.fori_loop(piece * size, (piece + 1) * size, step, carry, unroll=4)
        after(piece)
    return carry


def to_feature_rows(load, held_ref, out, steps):
    length = out.ref.shape[1]

    def step(index, carry):
        held_ref[pl.ds(index, CHUNKS, stride=steps), :] = load(rows_at(index, CHUNKS), index)
        return carry

    lax.fori_loop(0, steps, step, 0, unroll=4)
    for block in range(length // 128):
        lanes = slice(block * 128, (block + 1) * 128)
        out.ref[:, lanes] = held_ref[lanes, :].T
    out.send()


def spread_rows(value, out):
    for group in range(out.ref.shape[0]):
        out.ref[group, :, :] = value
    out.send()


def narrowed(values, width):
    return jnp.concatenate([v[:, at : at + width] for v in values for at in range(0, v.shape[1], width)], axis=0)


def widened(rows, first, count):
    return jnp.concatenate([rows[first + place : first + place + 1, :] for place in range(count)], axis=1)


def total_rows(sums_ref):
    value = sums_ref[0, :, :]
    for other in range(1, sums_ref.shape[0]):
        value += sums_ref[other, :, :]
    return value


def assemble_states(parts, whole_ref):
    half = parts[0].shape[0] // 2
    states = half * len(parts)
    for place, part in enumerate(parts):
        whole_ref[place * half : (place + 1) * half, :] = part[:half, :]
        whole_ref[states + place * half : states + (place + 1) * half, :] = part[half:, :]


def assemble_output(parts, whole_ref):
    half = parts[0].shape[0] // 2
    states = half * len(parts)
    for place, part in enumerate(parts):
        whole_ref[place * half : (place + 1) * half, :] = part[:half, :]
        whole_ref[states + place * half : states + (place + 1) * half, :] = -part[half:, :]


def assemble_glu(parts, whole_ref, quarter):
    half = parts[0].shape[0] // 2
    width = half * len(parts)
    for place, part in enumerate(parts):
        whole_ref[lanes_at(quarter ^ place, half), :] = part[:half, :]
        whole_ref[pl.ds(pl.multiple_of(width + (quarter ^ place) * half, half), half), :] = part[half:, :]


def norm_rows(sums, counted):
    centre = sums[0:1, :] / counted
    meansq = sums[1:2, :] / counted
    return centre, lax.rsqrt(meansq - centre * centre + EPSILON)


def drive_phase(normed_ref, b_ref, drive_ref, gamma):
    drive_ref[...] = dot(normed_ref[...], b_ref[...], NT) * jnp.concatenate([gamma, gamma], axis=1)


def store_states(low_ref, drive_own_ref):
    def emit(rows, step, re, im, drive_re, drive_im, held):
        states = re.shape[1]
        low_ref[rows, :states] = re.astype(LOW)
        low_ref[rows, states:] = im.astype(LOW)
        drive_own_ref[rows, :128] = drive_re[:, :128].astype(drive_own_ref.dtype)
        drive_own_ref[rows, 128:] = drive_im[:, :128].astype(drive_own_ref.dtype)
        return held

    return emit


def pre_products(low_ref, c_ref, held_ref):
    total, full = low_ref.shape[0], c_ref.shape[1]
    for piece in pieces_of(total):
        held_ref[piece, :full] = dot(low_ref[piece, :], c_ref[...], NN)


def pre_piece(piece, held_ref, normed_ref, skip, active_ref, slope_ref):
    full = normed_ref.shape[1]
    for rows, _ in blocks_of(piece.start, piece.stop):
        value = held_ref[rows, :full] + skip * normed_ref[rows, :].astype(F32)
        cdf, density = gelu_parts(value)
        active_ref[rows, :] = (value * cdf).astype(LOW)
        slope_ref[rows, :] = (cdf + value * density).astype(slope_ref.dtype)


def pre_grad_piece(piece, held_ref, slope_ref, pre_grad_ref):
    full = slope_ref.shape[1]
    for rows, _ in blocks_of(piece.start, piece.stop):
        pre_grad_ref[rows, :] = (held_ref[rows, :full] * slope_ref[rows, :].astype(F32)).astype(LOW)


def skip_sums(pre_grad_ref, normed_ref, quarter, small_ref):
    own = lanes_at(quarter, 128)
    value = jnp.zeros((8, 128), F32)
    for rows, _ in blocks_of(0, pre_grad_ref.shape[0]):
        value += folded(pre_grad_ref[rows, own].astype(F32) * normed_ref[rows, own].astype(F32))
    small_ref[3:4, 0:128] = column_sum(value)


def bias_sums(grad_gated_ref, quarter, small_ref):
    for place in range(2):
        lanes = lanes_at(quarter + 4 * place, 128)
        value = jnp.zeros((8, 128), F32)
        for rows, _ in blocks_of(0, grad_gated_ref.shape[0]):
            value += folded(grad_gated_ref[rows, lanes].astype(F32))
        small_ref[4 + place : 5 + place, 0:128] = column_sum(value)


def together(*parts):
    def run():
        for part in parts:
            part()

    return run


def adjoint_phase(low_ref, im_lane, drive_own_ref, state, first_row, length, grad_state_ref, grad_driven_ref, small_ref, reverse, beside):
    total = grad_state_ref.shape[0]
    steps = total // CHUNKS
    states = state.shape[1]
    rate_re = state[first_row : first_row + 1, :]
    rate_im = state[first_row + 1 : first_row + 2, :]
    gamma = jnp.broadcast_to(state[first_row + 2 : first_row + 3, :], (CHUNKS, states))

    def emit(rows, step, re, im, drive_re, drive_im, held):
        out_re, out_im = gamma * re, gamma * im
        if not reverse:
            keep = keep_rows(step, CHUNKS, steps, length)
            out_re, out_im = jnp.where(keep, out_re, 0.0), jnp.where(keep, out_im, 0.0)
        grad_driven_ref[rows, :states] = out_re.astype(LOW)
        grad_driven_ref[rows, states:] = out_im.astype(LOW)
        one, two, three = held
        own_re, own_im = re[:, :128], im[:, :128]
        late_re, late_im = own_re - drive_re[:, :128], own_im - drive_im[:, :128]
        low_re = low_ref[rows, :128].astype(F32)
        low_im = low_ref[rows, im_lane : im_lane + 128].astype(F32)
        one = one + folded(late_re * low_re + late_im * low_im)
        two = two + folded(late_im * low_re - late_re * low_im)
        three = three + folded(
            own_re * drive_own_ref[rows, :128].astype(F32) + own_im * drive_own_ref[rows, 128:].astype(F32)
        )
        return one, two, three

    zero = jnp.zeros((8, 128), F32)
    one, two, three = sweep(grad_state_ref, rate_re, -rate_im, steps, reverse, emit, (zero, zero, zero), beside=beside)
    small_ref[0:1, 0:128] = column_sum(one)
    small_ref[1:2, 0:128] = column_sum(two)
    small_ref[2:3, 0:128] = column_sum(three)


def glu_products(grads_ref, first, grad_gated_ref, active_ref, quarter):
    full = active_ref.shape[1]

    def product(place):
        lanes = pl.ds(pl.multiple_of(place * full + quarter * 128, 128), 128)
        got = dot(grad_gated_ref[:, lanes], active_ref[...], TN)
        grads_ref[first + place * 128 : first + (place + 1) * 128, :] = got.astype(LOW)

    return [functools.partial(product, place) for place in range(2)]


def pack_own(source_ref, im_lane, packed_ref):
    lane = lax.broadcasted_iota(jnp.int32, (16, 128), 1)
    for rows, _ in blocks_of(0, source_ref.shape[0]):
        re = source_ref[rows, 0:128].astype(F32)
        im = source_ref[rows, im_lane : im_lane + 128].astype(F32)
        packed_ref[rows, :] = jnp.where(lane < 64, re, pltpu.roll(im, 64, 1)).astype(LOW)


def output_product(grads_ref, packed_ref, pre_grad_ref):
    got = dot(packed_ref[...], pre_grad_ref[...], TN)
    half = got.shape[0] // 2
    grads_ref[2 * half : 3 * half, :] = got[:half, :].astype(LOW)
    grads_ref[3 * half : 4 * half, :] = -got[half:, :].astype(LOW)


def beside_sweep(products, grad_gated_ref, pre_grad_ref, normed_ref, quarter, small_ref):
    return (
        *products,
        together(
            functools.partial(bias_sums, grad_gated_ref, quarter, small_ref),
            functools.partial(skip_sums, pre_grad_ref, normed_ref, quarter, small_ref),
        ),
    )


def input_product(grads_ref, packed_ref, normed_ref):
    got = dot(packed_ref[...], normed_ref[...], TN)
    grads_ref[0 : got.shape[0], :] = got.astype(LOW)


def enter_kernel(length_ref, ins, outs, held_ref, params_ref):
    x, gain, shift, skip, bias, nu, theta, gamma, b, c, w = ins
    tokens, spread, first_out = outs
    length = length_ref[0]
    width, total = x.ref.shape
    steps = total // CHUNKS

    def emit(rows, index, value, carry):
        tokens.ref[rows, :] = value
        kept = jnp.where(keep_rows(index, CHUNKS, steps, length), value, 0.0)
        return carry[0] + folded(kept), carry[1] + folded(kept * kept)

    zero = jnp.zeros((8, width), F32)
    plain, square = from_feature_rows(x, held_ref, steps, emit, (zero, zero), tokens.send_piece)
    plain = column_sum(plain)
    counted = jnp.full((1, width), length, jnp.int32).astype(F32)
    spread_rows(jnp.concatenate([plain, column_sum(square), counted, jnp.zeros((5, width), F32)], axis=0), spread)
    mean = plain / counted

    each = total // PIECES

    def centred(rows, index, carry):
        place = pl.ds(pl.multiple_of(4 * width + index * 32 % each, 32), 32)
        first_out.ref[place, lanes_at(index * 32 // each, width)] = (tokens.ref[rows, :] - mean).astype(LOW)
        return carry

    for_rows(0, total, 32, centred, unroll=4)
    for value in (gain, shift, skip, bias, nu, theta, gamma):
        value.wait()
    params_ref[...] = jnp.zeros(params_ref.shape, F32)
    for layer in range(LAYERS):
        first = 5 * layer
        params_ref[first + GAIN : first + GAIN + 1, :] = gain.ref[layer : layer + 1, :]
        params_ref[first + SHIFT : first + SHIFT + 1, :] = shift.ref[layer : layer + 1, :]
        params_ref[first + SKIP : first + SKIP + 1, :] = skip.ref[layer : layer + 1, :]
        params_ref[first + BIAS_LINEAR : first + BIAS_GATE + 1, :] = bias.ref[layer, :, :]
        first = 10 + 3 * layer
        for row, source in enumerate((nu, theta, gamma)):
            params_ref[first + row : first + row + 1, : source.ref.shape[1]] = source.ref[layer : layer + 1, :]
    params_ref[OWN_MEAN : OWN_MEAN + 1, :] = mean
    rest = params_ref[...]
    first_out.ref[6 * width :, :] = jnp.zeros((32, 4 * width), LOW)
    for place in range(3):
        high = rest.astype(LOW)
        first_out.ref[6 * width : 6 * width + PARAM_ROWS, place * width : (place + 1) * width] = high
        rest = rest - high.astype(F32)
    first_out.send(4 * width, 2 * width + 32)
    send_weights(0, b, c, w, first_out)


def send_weights(layer, b, c, w, whole):
    width = b.ref.shape[1]
    for value, first, size in ((b, 0, width), (c, width, width), (w, 2 * width, 2 * width)):
        value.wait()
        whole.send(first, size, source=value.ref.at[layer])


def total_kernel(length_ref, ins, outs):
    outs[0].ref[...] = total_rows(ins[0].ref)


def cotangent_kernel(length_ref, ins, outs, held_ref):
    x, b, c, w = ins
    whole, later = outs
    width, total = x.ref.shape
    steps = total // CHUNKS
    each = steps // PIECES

    def emit(rows, index, value, carry):
        whole.ref[rows, :] = value
        place = pl.ds(pl.multiple_of(4 * width + index % each * CHUNKS, CHUNKS), CHUNKS)
        later.ref[place, lanes_at(index // each, width)] = value.astype(LOW)
        return carry

    def after(piece):
        whole.send_piece(piece)
        if piece == 1:
            send_weights(1, b, c, w, later)

    from_feature_rows(x, held_ref, steps, emit, 0, after)
    later.send(4 * width, total // PIECES)


def start_kernel(length_ref, ins, outs, stats_ref, stream_ref, drive_ref, pre_ref, held_ref, b_ref, c_ref, w_ref, low_ref):
    all_stats, tokens, parts = ins[:4], ins[4], ins[5:]
    feature, state_out, norm, normed, drive_own, low_own, stream, linear_out, gate_out, slope, active, b_out, c_out, w_out, spread = outs
    length, quarter = length_ref[0], own_quarter()
    total, full = active.ref.shape
    steps = total // CHUNKS
    width = full // 4
    lane = lax.broadcasted_iota(jnp.int32, (8, width), 1)
    tails = []
    rows_refs = []
    for part in parts:
        for piece in (6, 4, 5):
            part.wait(piece)
        rows_refs.append(part.ref.at[pl.ds(4 * width, 2 * width + PARAM_ROWS)])
    for place, part_ref in enumerate(rows_refs):
        value = sum(part_ref[2 * width :, at * width : (at + 1) * width].astype(F32) for at in range(3))
        feature.ref[:, lanes_at(quarter ^ place, width)] = value
        tails.append(value[8:16, :])
    for pair in range(2):
        early, late = tails[2 * pair : 2 * pair + 2]
        logs = jnp.where(lane < 64, early, pltpu.roll(late, 64, 1))
        lanes = slice(pair * width, (pair + 1) * width)
        for layer in range(LAYERS):
            first = 2 + 3 * layer
            modulus = jnp.exp(-jnp.exp(logs[first : first + 1, :]))
            angle = jnp.exp(logs[first + 1 : first + 2, :])
            state_out.ref[first : first + 1, lanes] = modulus * jnp.cos(angle)
            state_out.ref[first + 1 : first + 2, lanes] = modulus * jnp.sin(angle)
            state_out.ref[first + 2 : first + 3, lanes] = jnp.exp(logs[first + 2 : first + 3, :])
    for place, stats in enumerate(all_stats):
        stats_ref[:, lanes_at(quarter ^ place, width)] = stats.wait()[...]
    centre, inv_dev = norm_rows(stats_ref[0:2, :], stats_ref[2:3, :])
    norm.ref[...] = jnp.zeros_like(norm.ref)
    norm.ref[0:1, :] = centre
    norm.ref[1:2, :] = inv_dev
    norm.ref[2:3, :] = stats_ref[2:3, :]
    for out in (feature, state_out, norm):
        out.send()

    each = total // PIECES
    assemble_states([part.wait(0).at[0:width] for part in parts], b_ref)
    b_out.send(source=b_ref)
    state = state_out.ref[...]
    states = state.shape[1]
    gamma = state[2 + GAMMA : 3 + GAMMA, :]
    gammas = jnp.concatenate([gamma, gamma], axis=1)
    rows_of = []
    for place in range(4):
        lanes = lanes_at(quarter ^ place, width)
        rows_of.append((lanes, feature.ref[OWN_MEAN : OWN_MEAN + 1, lanes], norm.ref[0:1, lanes], norm.ref[1:2, lanes],
                        feature.ref[GAIN : GAIN + 1, lanes], feature.ref[SHIFT : SHIFT + 1, lanes]))
    for at, piece in enumerate(pieces_of(total)):
        tokens.wait(at)
        for rows, index in blocks_of(piece.start, piece.stop):
            keep = keep_rows(index, 16, steps, length)
            there = slice(rows.start % each, rows.start % each + 16)
            for place, (lanes, mean, middle, inverse, gain, shift) in enumerate(rows_of):
                if place == 0:
                    value = tokens.ref[rows, :]
                else:
                    value = rows_refs[place][there, at * width : (at + 1) * width].astype(F32) + mean
                stream_ref[rows, lanes] = value
                z = (value - middle) * inverse * gain + shift
                normed.ref[rows, lanes] = jnp.where(keep, z, 0.0).astype(LOW)
        normed.send_piece(at)
        drive_ref[piece, :] = dot(normed.ref[piece, :], b_ref[...], NT) * gammas
    assemble_output([part.wait(1).at[width : 2 * width] for part in parts], c_ref)
    c_out.send(source=c_ref)
    store = store_states(low_ref, drive_own.ref)

    def emit(rows, step, re, im, drive_re, drive_im, held):
        low_own.ref[rows, :128] = re[:, :128].astype(LOW)
        low_own.ref[rows, 128:] = im[:, :128].astype(LOW)
        return store(rows, step, re, im, drive_re, drive_im, held)

    sweep(drive_ref, state[2:3, :], state[3:4, :], steps, False, emit, 0)
    drive_own.send()
    low_own.send()

    assemble_glu([part.wait().at[2 * width : 4 * width] for part in parts], w_ref, quarter)
    w_out.send(source=w_ref)
    skip = feature.ref[SKIP : SKIP + 1, :]
    bias_linear = feature.ref[BIAS_LINEAR : BIAS_LINEAR + 1, :]
    bias_gate = feature.ref[BIAS_GATE : BIAS_GATE + 1, :]
    pre_products(low_ref, c_ref, pre_ref)
    for piece in pieces_of(total):
        pre_piece(piece, pre_ref, normed.ref, skip, active.ref, slope.ref)
        held_ref[piece, :] = dot(active.ref[piece, :], w_ref[...], NT)
    active.send()
    slope.send()
    plain, square = jnp.zeros((8, full), F32), jnp.zeros((8, full), F32)
    for place, piece in enumerate(pieces_of(total)):
        for rows, index in blocks_of(piece.start, piece.stop):
            keep = keep_rows(index, 16, steps, length)
            linear = held_ref[rows, :full] + bias_linear
            gate = jax.nn.sigmoid(held_ref[rows, full:] + bias_gate)
            mixed = linear * gate
            gate_out.ref[rows, :] = gate.astype(LOW)
            linear_out.ref[rows, :] = (mixed * (1.0 - gate)).astype(LOW)
            moved = stream_ref[rows, :] + jnp.where(keep, mixed, 0.0)
            stream.ref[rows, :] = moved
            kept = jnp.where(keep, moved, 0.0)
            plain += folded(kept)
            square += folded(kept * kept)
        for out in (stream, linear_out, gate_out):
            out.send_piece(place)
    carry = plain, square
    spread_rows(narrowed([column_sum(carry[0]), column_sum(carry[1])], width), spread)


def middle_kernel(
    length_ref, ins, outs,
    small_ref, b_ref, c_ref, w_ref, normed_ref, drive_ref, drive_own_ref, low_ref, slope_ref, active_ref, held_ref, pre_ref, mixed_ref,
    up_ref, grad_gated_ref, pre_grad_ref, grad_driven_ref, grads_ref, packed_ref,
):
    sums, norm0, feature_in, state_in, stream, up_own = ins[:6]
    parts = ins[6:]
    result, base, spread, norm, *shares = outs
    length, quarter = length_ref[0], own_quarter()
    total, full = stream.ref.shape
    steps = total // CHUNKS
    width = 128
    counted = norm0.wait()[2:3, :]
    feature = feature_in.wait()
    state = state_in.wait()[...]
    states = state.shape[1]
    whole = total_rows(sums.wait())
    whole = jnp.concatenate([widened(whole, 0, 4), widened(whole, 4, 4)], axis=0)
    centre, inv_dev = norm_rows(whole, counted)
    norm.ref[...] = jnp.zeros_like(norm.ref)
    norm.ref[0:1, :] = centre
    norm.ref[1:2, :] = inv_dev
    norm.ref[2:3, :] = counted
    norm.send()
    gain = feature[5 + GAIN : 6 + GAIN, :]
    shift = feature[5 + SHIFT : 6 + SHIFT, :]
    skip = feature[5 + SKIP : 6 + SKIP, :]

    for part in parts:
        part.wait(0)
    assemble_states([part.ref.at[0:width] for part in parts], b_ref)
    gamma = state[5 + GAMMA : 6 + GAMMA, :]
    gammas = jnp.concatenate([gamma, gamma], axis=1)
    for place, piece in enumerate(pieces_of(total)):
        stream.wait(place)
        for rows, index in blocks_of(piece.start, piece.stop):
            z = (stream.ref[rows, :] - centre) * inv_dev
            normed_ref[rows, :] = jnp.where(keep_rows(index, 16, steps, length), z * gain + shift, 0.0).astype(LOW)
        drive_ref[piece, :] = dot(normed_ref[piece, :], b_ref[...], NT) * gammas
    sweep(drive_ref, state[5:6, :], state[6:7, :], steps, True, store_states(low_ref, drive_own_ref), 0)
    for part in parts:
        part.wait()
    assemble_output([part.ref.at[width : 2 * width] for part in parts], c_ref)
    assemble_glu([part.ref.at[2 * width : 4 * width] for part in parts], w_ref, quarter)
    up_own.wait()
    own = lanes_at(quarter, width)

    for rows, _ in blocks_of(0, total):
        up_ref[rows, own] = up_own.ref[rows, :]
    for place, piece in enumerate(pieces_of(total)):
        for other in range(1, 4):
            lanes = lanes_at(quarter ^ other, width)
            up_ref[piece, lanes] = parts[other].ref[4 * width :, place * width : (place + 1) * width].astype(F32)
    bias_linear = feature[5 + BIAS_LINEAR : 6 + BIAS_LINEAR, :]
    bias_gate = feature[5 + BIAS_GATE : 6 + BIAS_GATE, :]
    pre_products(low_ref, c_ref, pre_ref)
    pack_own(low_ref, states, packed_ref)
    for piece in pieces_of(total):
        pre_piece(piece, pre_ref, normed_ref, skip, active_ref, slope_ref)
        held_ref[piece, :] = dot(active_ref[piece, :], w_ref[...], NT)
    for piece in pieces_of(total):
        for rows, index in blocks_of(piece.start, piece.stop):
            keep = keep_rows(index, 16, steps, length)
            linear = held_ref[rows, :full] + bias_linear
            gate = jax.nn.sigmoid(held_ref[rows, full:] + bias_gate)
            mixed = linear * gate
            up = jnp.where(keep, up_ref[rows, :], 0.0)
            grad_gated_ref[rows, :full] = (up * gate).astype(LOW)
            grad_gated_ref[rows, full:] = (up * mixed * (1.0 - gate)).astype(LOW)
            mixed_ref[rows, :] = jnp.where(keep, mixed, 0.0)
        pre_ref[piece, :] = dot(grad_gated_ref[piece, :], w_ref[...], NN)
    for piece in pieces_of(total):
        pre_grad_piece(piece, pre_ref, slope_ref, pre_grad_ref)
        drive_ref[piece, :] = dot(pre_grad_ref[piece, :], c_ref[...], NT)
    small_ref[...] = jnp.zeros_like(small_ref)
    for rows, _ in blocks_of(0, total):
        result.ref[rows, :] = stream.ref[rows, own] + mixed_ref[rows, own]
    result.send()
    adjoint_phase(
        low_ref, states, drive_own_ref, state, 5, length, drive_ref, grad_driven_ref, small_ref, False,
        beside_sweep(
            glu_products(grads_ref, 2 * width, grad_gated_ref, active_ref, quarter)
            + [functools.partial(output_product, grads_ref, packed_ref, pre_grad_ref)],
            grad_gated_ref, pre_grad_ref, normed_ref, quarter, small_ref,
        ),
    )
    scale = inv_dev * gain
    for piece in pieces_of(total):
        pre_ref[piece, :] = dot(grad_driven_ref[piece, :], b_ref[...], NN)
    pack_own(grad_driven_ref, states, packed_ref)
    plain, scaled = jnp.zeros((8, full), F32), jnp.zeros((8, full), F32)
    for place, piece in enumerate(pieces_of(total)):
        for rows, _ in blocks_of(piece.start, piece.stop):
            grad = pre_ref[rows, :] + skip * pre_grad_ref[rows, :].astype(F32)
            z = (stream.ref[rows, :] - centre) * inv_dev
            base.ref[rows, :] = scale * grad + up_ref[rows, :]
            plain += folded(grad)
            scaled += folded(grad * z)
        base.send_piece(place)
    input_product(grads_ref, packed_ref, normed_ref)
    sent = narrowed([column_sum(plain), column_sum(scaled)], width)
    spread_rows(jnp.concatenate([sent, small_ref[:, 0:width]], axis=0), spread)
    send_halves(grads_ref, shares, 0)


def last_kernel(
    length_ref, ins, outs, held_ref, grad_state_ref, grad_gated_ref, pre_grad_ref, grad_driven_ref, small_ref, up_ref, grads_ref, pack_ref, low_ref, packed_ref
):
    (sums, norm1, feature_in, state_in, norm0, stream, base, gate, linear, w, slope, c, low, normed, active, drive_own, b, x) = ins
    kept, sent, up_out, grad_out = outs
    length, quarter = length_ref[0], own_quarter()
    total, full = stream.ref.shape
    steps = total // CHUNKS
    width = 128
    own = lanes_at(quarter, width)
    feature, norm_ref = feature_in.wait(), norm1.wait()
    state = state_in.wait()[...]
    counted = norm_ref[2:3, :]
    whole = total_rows(sums.wait())
    whole = jnp.concatenate([widened(whole, 0, 4), widened(whole, 4, 4)], axis=0)
    centre, inv_dev = norm_ref[0:1, :], norm_ref[1:2, :]
    scale = inv_dev * feature[5 + GAIN : 6 + GAIN, :]
    level = scale * whole[0:1, :] / counted
    tilt = scale * inv_dev * whole[1:2, :] / counted

    for place, piece in enumerate(pieces_of(total)):
        for value in (stream, base, gate, linear):
            value.wait(place)
        for rows, index in blocks_of(piece.start, piece.stop):
            keep = keep_rows(index, 16, steps, length)
            up = base.ref[rows, :] - jnp.where(keep, level + (stream.ref[rows, :] - centre) * tilt, 0.0)
            up_ref[rows, :] = up
            up = jnp.where(keep, up, 0.0)
            grad_gated_ref[rows, :full] = (up * gate.ref[rows, :].astype(F32)).astype(LOW)
            grad_gated_ref[rows, full:] = (up * linear.ref[rows, :].astype(F32)).astype(LOW)
        if place == 0:
            w.wait()
        held_ref[piece, :] = dot(grad_gated_ref[piece, :], w.ref[...], NN)
    for value in (slope, c, low):
        value.wait()
    pack_own(low.ref, 128, packed_ref)
    for piece in pieces_of(total):
        pre_grad_piece(piece, held_ref, slope.ref, pre_grad_ref)
        grad_state_ref[piece, :] = dot(pre_grad_ref[piece, :], c.ref[...], NT)
    small_ref[...] = jnp.zeros_like(small_ref)

    def own_up(rows, index, carry):
        up_out.ref[rows, :] = up_ref[rows, own]
        return carry

    for_rows(0, total, 16, own_up, unroll=4)
    up_out.send()
    for value in (normed, active, low, drive_own):
        value.wait()
    adjoint_phase(
        low.ref, 128, drive_own.ref, state, 2, length, grad_state_ref, grad_driven_ref, small_ref, True,
        beside_sweep(
            glu_products(grads_ref, 2 * width, grad_gated_ref, active.ref, quarter)
            + [functools.partial(output_product, grads_ref, packed_ref, pre_grad_ref)],
            grad_gated_ref, pre_grad_ref, normed.ref, quarter, small_ref,
        ),
    )
    b.wait()
    x.wait()
    held_ref[:, :width] = dot(grad_driven_ref[...], b.ref[:, own], NN)
    pack_own(grad_driven_ref, state.shape[1], packed_ref)
    input_product(grads_ref, packed_ref, normed.ref)
    zero = jnp.zeros((8, width), F32)
    centre0, inv_dev0 = norm0.wait()[0:1, own], norm0.ref[1:2, own]
    skip = feature[SKIP : SKIP + 1, own]

    def back(rows, index, carry):
        grad = held_ref[rows, :width] + skip * pre_grad_ref[rows, own].astype(F32)
        grad_out.ref[rows, :] = grad
        z = (x.ref[rows, :] - centre0) * inv_dev0
        return carry[0] + folded(grad), carry[1] + folded(grad * z)

    plain, scaled = for_rows(0, total, 16, back, (zero, zero), unroll=4)
    grad_out.send()
    small_ref[6:7, 0:width] = column_sum(plain)
    small_ref[7:8, 0:width] = column_sum(scaled)
    pack_ref[...] = jnp.zeros_like(pack_ref)
    for place in range(8):
        pack_ref[place // 4 : place // 4 + 1, place % 4 * width : (place % 4 + 1) * width] = small_ref[place : place + 1, 0:width]
    exact = pack_ref[0:8, :]
    pack_ref[8:16, :] = exact - exact.astype(LOW).astype(F32)
    half = grads_ref.shape[0] // 2
    low_ref[...] = pack_ref[...].astype(LOW)
    mine = lax.axis_index("dp") & 1
    for out, which in ((kept, mine), (sent, 1 - mine)):
        out.send(0, half, source=grads_ref.at[rows_at(which, half)])
        out.send(half, 16, source=low_ref)


def send_halves(source_ref, outs, stage):
    kept = lax.axis_index("dp") >> stage & 1
    half = source_ref.shape[0] // 2
    for out, which in zip(outs, (kept, 1 - kept)):
        out.send(source=source_ref.at[rows_at(which, half)])


def add_kernel(length_ref, ins, outs):
    outs[0].ref[...] = (ins[0].ref[...].astype(F32) + ins[1].ref[...].astype(F32)).astype(LOW)


def pair_kernel(length_ref, ins, outs, sum_ref, pack_ref):
    kept, other = ins
    for value in ins:
        value.wait()
    half = kept.ref.shape[0] - 16
    share = half // len(outs)
    small = kept.ref[half:, :].astype(F32) + other.ref[half:, :].astype(F32)
    small = small[0:8, :] + small[8:16, :]
    pack_ref[...] = jnp.concatenate([small, small - small.astype(LOW).astype(F32)], axis=0).astype(LOW)
    for piece in range(0, half, 16):
        at = slice(piece, piece + 16)
        sum_ref[at, :] = (kept.ref[at, :].astype(F32) + other.ref[at, :].astype(F32)).astype(LOW)
    for place, out in enumerate(outs):
        out.send(0, share, source=sum_ref.at[rows_at((lax.axis_index("dp") >> 1) ^ place, share)])
        out.send(share, 16, source=pack_ref)


def share_kernel(length_ref, ins, outs):
    half, *blocks = ins
    out, both, small = outs
    share, rows = out.ref.shape[0], half.ref.shape[0]
    value = blocks[0].ref[...].astype(F32)
    for block in blocks[1:]:
        value += block.ref[...].astype(F32)
    out.ref[...] = value[:share, :].astype(LOW)
    both.ref[0:rows, :] = half.ref[...]
    both.ref[rows:, :] = value[:share, :].astype(LOW)
    small.ref[...] = value[share : share + 8, :] + value[share + 8 :, :]


def finish_kernel(length_ref, ins, outs, held_ref, order_ref):
    small0, bn1, norm0, feature, nu, theta, result, up, grad, x = ins
    nu_out, theta_out, gamma_out, skip_out, bias_out, gain_out, shift_out, result_out, out = outs
    length, quarter = length_ref[0], own_quarter()
    total, width = up.ref.shape
    steps = total // CHUNKS
    own = lanes_at(quarter, width)
    states = nu_out.ref.shape[1]
    result.wait()
    to_feature_rows(lambda rows, index: result.ref[rows, :], order_ref, result_out, steps)
    for value in ins:
        value.wait()
    whole = total_rows(bn1.ref)
    held_ref[0:1, :] = widened(whole, 0, 4)
    held_ref[1:2, :] = widened(whole, 4, 4)
    held_ref[16:32, :width] = whole
    for place in range(8):
        held_ref[8 + place : 9 + place, :width] = small0.ref[place // 4 : place // 4 + 1, place % 4 * width : (place % 4 + 1) * width]
    for layer, first in ((0, 8), (1, 24)):
        at = slice(layer, layer + 1)
        nu_out.ref[at, :] = -jnp.exp(nu.ref[at, :]) * held_ref[first : first + 1, :states]
        theta_out.ref[at, :] = jnp.exp(theta.ref[at, :]) * held_ref[first + 1 : first + 2, :states]
        gamma_out.ref[at, :] = held_ref[first + 2 : first + 3, :states]
        skip_out.ref[at, :] = held_ref[first + 3 : first + 4, :width]
        bias_out.ref[layer, 0:1, :] = held_ref[first + 4 : first + 5, :width]
        bias_out.ref[layer, 1:2, :] = held_ref[first + 5 : first + 6, :width]
    shift_out.ref[0:1, :] = held_ref[14:15, :width]
    gain_out.ref[0:1, :] = held_ref[15:16, :width]
    shift_out.ref[1:2, :] = held_ref[0:1, own]
    gain_out.ref[1:2, :] = held_ref[1:2, own]
    counted = norm0.ref[2:3, own]
    centre, inv_dev = norm0.ref[0:1, own], norm0.ref[1:2, own]
    level = held_ref[14:15, :width] / counted
    tilt = held_ref[15:16, :width] * inv_dev / counted
    scale = inv_dev * feature.ref[GAIN : GAIN + 1, own]

    def load(rows, index):
        keep = keep_rows(index, CHUNKS, steps, length)
        inner = grad.ref[rows, :] - level - (x.ref[rows, :] - centre) * tilt
        return up.ref[rows, :] + jnp.where(keep, scale * inner, 0.0)

    to_feature_rows(load, order_ref, out, steps)


def send_wide(layer, outs, held_ref):
    half = outs[0].target.shape[1]
    for out, first, size in zip(outs, (0, half, 2 * half), (half, half, 2 * half)):
        out.send(layer, 1, source=held_ref.at[pl.ds(0, 1), pl.ds(first, size)])


def widen1_kernel(length_ref, ins, outs, held_ref):
    half = ins[0].ref.shape[0]
    mine = lax.axis_index("dp") & 1
    for which, value in ((mine, ins[0]), (1 - mine, ins[1])):
        held_ref[0, rows_at(which, half), :] = value.ref[0:half, :].astype(F32)
    send_wide(1, outs, held_ref)


def widen0_kernel(length_ref, ins, outs, held_ref):
    groups = len(ins)
    share = ins[0].ref.shape[0]
    for place, value in enumerate(ins):
        owner = lax.axis_index("dp") ^ place
        first = value.ref.shape[0] - share
        held_ref[0, rows_at((owner & 1) * (groups // 2) + (owner >> 1), share), :] = value.ref[first:, :].astype(F32)
    send_wide(0, outs, held_ref)


def shape(*dims, dtype=F32):
    return jax.ShapeDtypeStruct(dims, dtype)


def swap(value, bit, sharers):
    pairs = [(q * sharers + r, (q ^ bit) * sharers + r) for q in range(4) for r in range(sharers)]
    return lax.ppermute(value, "state", pairs)


def across(value, axes):
    return lax.all_to_all(value, axes, 0, 0, tiled=True)


def local(
    inputs, lengths, cotangent, bn_gain, bn_bias, b_weight, c_weight, nu_log, theta_log, gamma_log, skip_weight,
    glu_weight, glu_bias, dp_size, state_size,
):
    sharers = state_size // 4
    place = lax.axis_index("state").astype(jnp.int32)

    def joined(value, axis):
        if sharers == 1:
            return value
        groups = [[q * sharers + r for r in range(sharers)] for q in range(4)]
        return lax.all_gather(value, "state", axis=axis, axis_index_groups=groups, tiled=True)

    def own(value, axis):
        if sharers == 1:
            return value
        size = value.shape[axis] // sharers
        return lax.dynamic_slice_in_dim(value, place % sharers * size, size, axis)

    inputs, cotangent = joined(inputs, 1), joined(cotangent, 1)
    bn_gain, bn_bias, skip_weight = joined(bn_gain, 1), joined(bn_bias, 1), joined(skip_weight, 1)
    nu_log, theta_log, gamma_log = joined(nu_log, 1), joined(theta_log, 1), joined(gamma_log, 1)
    b_weight, c_weight = joined(b_weight, 2), joined(c_weight, 2)
    glu_weight, glu_bias = joined(glu_weight, 2), joined(glu_bias, 2)
    width, total = inputs.shape[1:]
    full = b_weight.shape[3]
    states = b_weight.shape[2] * 4
    own_states = b_weight.shape[2]
    share = 4 * width // dp_size
    piece = total // PIECES

    stages = dp_size.bit_length() - 1

    def exchange(value, bit):
        return lax.ppermute(value, "dp", [(i, i ^ bit) for i in range(dp_size)])

    def add(one, other):
        return call_small(add_kernel, (shape(*one.shape, dtype=LOW),), [], (one, other), "add")[0]

    b_weight, c_weight = b_weight.reshape(LAYERS, width, full), c_weight.reshape(LAYERS, width, full)
    glu_weight = glu_weight.reshape(LAYERS, 2 * width, full)
    tokens, sums, first = call(
        enter_kernel,
        (
            shape(total, width),
            shape(dp_size, 8, width),
            shape(6 * width + PARAM_ROWS, full, dtype=LOW),
        ),
        [pltpu.VMEM((total, width), F32), pltpu.VMEM((PARAM_ROWS, width), F32)],
        (lengths, inputs[0], bn_gain, bn_bias, skip_weight, glu_bias, nu_log, theta_log, gamma_log, b_weight, c_weight, glu_weight),
        "enter",
        pieces={1: piece},
        axes={1: 1},
        late=(9, 10, 11),
    )
    near, far = swap(first, 1, sharers), swap(first, 2, sharers)
    (stats,) = call_small(total_kernel, (shape(8, width),), [], (across(sums, "dp"),), "total")
    stats_near, stats_far = swap(stats, 1, sharers), swap(stats, 2, sharers)
    cotangent, tokens = lax.optimization_barrier((cotangent, tokens))
    up_own, later = call(
        cotangent_kernel,
        (
            shape(total, width),
            shape(6 * width, full, dtype=LOW),
        ),
        [pltpu.VMEM((total, width), F32)],
        (lengths, cotangent[0], b_weight, c_weight, glu_weight),
        "cotangent",
        pieces={1: piece},
        axes={1: 1},
        late=(2, 3, 4),
    )
    later_far = swap(later, 2, sharers)
    near, far, stats_near, stats_far, later = lax.optimization_barrier((near, far, stats_near, stats_far, later))
    parts = (first, near, far, swap(far, 1, sharers))
    all_stats = (stats, stats_near, stats_far, swap(stats_far, 1, sharers))
    feature, state, norm0, normed0, drive0, low0, stream1, linear0, gate0, slope0, active0, b_all, c_all, w_all, sums1 = call(
        start_kernel,
        (
            shape(PARAM_ROWS, full),
            shape(8, states),
            shape(8, full),
            shape(total, full, dtype=LOW),
            shape(total, 256),
            shape(total, 256, dtype=LOW),
            shape(total, full),
            shape(total, full, dtype=LOW),
            shape(total, full, dtype=LOW),
            shape(total, full, dtype=LOW),
            shape(total, full, dtype=LOW),
            shape(2 * states, full, dtype=LOW),
            shape(2 * states, full, dtype=LOW),
            shape(2 * full, full, dtype=LOW),
            shape(dp_size, 8, width),
        ),
        [
            pltpu.VMEM((8, full), F32),
            pltpu.VMEM((total, full), F32),
            pltpu.VMEM((total, 2 * states), F32),
            pltpu.VMEM((total, full), F32),
            pltpu.VMEM((total, 2 * full), F32),
            pltpu.VMEM((2 * states, full), LOW),
            pltpu.VMEM((2 * states, full), LOW),
            pltpu.VMEM((2 * full, full), LOW),
            pltpu.VMEM((total, 2 * states), LOW),
        ],
        (lengths, *all_stats, tokens, *parts),
        "start",
        pieces={5: piece} | {place: width for place in (6, 7, 8, 9)},
        order=(4, 5),
        bare=(11, 12, 13),
        flops=0,
    )
    sums1 = across(sums1, "dp")
    later_far, sums1 = lax.optimization_barrier((later_far, sums1))
    later_parts = (later, swap(later, 1, sharers), later_far, swap(later_far, 1, sharers))
    result_rows, base, bn1, norm1, *halves1 = call(
        middle_kernel,
        (
            shape(total, width),
            shape(total, full),
            shape(dp_size, 16, width),
            shape(8, full),
            shape(2 * width, full, dtype=LOW),
            shape(2 * width, full, dtype=LOW),
        ),
        [
            pltpu.VMEM((8, full), F32),
            pltpu.VMEM((2 * states, full), LOW),
            pltpu.VMEM((2 * states, full), LOW),
            pltpu.VMEM((2 * full, full), LOW),
            pltpu.VMEM((total, full), LOW),
            pltpu.VMEM((total, 2 * states), F32),
            pltpu.VMEM((total, 256), F32),
            pltpu.VMEM((total, 2 * states), LOW),
            pltpu.VMEM((total, full), F32),
            pltpu.VMEM((total, full), LOW),
            pltpu.VMEM((total, 2 * full), F32),
            pltpu.VMEM((total, full), F32),
            pltpu.VMEM((total, full), F32),
            pltpu.VMEM((total, full), F32),
            pltpu.VMEM((total, 2 * full), LOW),
            pltpu.VMEM((total, full), LOW),
            pltpu.VMEM((total, 2 * states), LOW),
            pltpu.VMEM((4 * width, full), LOW),
            pltpu.VMEM((total, width), LOW),
        ],
        (lengths, sums1, norm0, feature, state, stream1, up_own, *later_parts),
        "middle",
        pieces={5: piece} | {place: width for place in (7, 8, 9, 10)},
        late=(6,),
        bare=(4, 5),
        flops=1e9,
    )
    bn1 = across(bn1, "dp")
    half1 = add(halves1[0], exchange(halves1[1], 1))
    bn1, half1 = lax.optimization_barrier((bn1, half1))
    other1 = exchange(half1, 1 << (stages - 1))
    kept0, sent0, up0, grad0 = call(
        last_kernel,
        (
            shape(2 * width + 16, full, dtype=LOW),
            shape(2 * width + 16, full, dtype=LOW),
            shape(total, width),
            shape(total, width),
        ),
        [
            pltpu.VMEM((total, full), F32),
            pltpu.VMEM((total, 2 * states), F32),
            pltpu.VMEM((total, 2 * full), LOW),
            pltpu.VMEM((total, full), LOW),
            pltpu.VMEM((total, 2 * states), LOW),
            pltpu.VMEM((8, full), F32),
            pltpu.VMEM((total, full), F32),
            pltpu.VMEM((4 * width, full), LOW),
            pltpu.VMEM((16, full), F32),
            pltpu.VMEM((16, full), LOW),
            pltpu.VMEM((total, width), LOW),
        ],
        (lengths, bn1, norm1, feature, state, norm0, stream1, base, gate0, linear0, w_all, slope0, c_all, low0, normed0, active0,
         drive0, b_all, tokens),
        "last",
        bare=(0, 1),
        pieces={6: piece, 7: piece, 8: piece, 9: piece},
        late=tuple(range(11, 19)),
        flops=1e11,
    )
    other1, kept0 = lax.optimization_barrier((other1, kept0))
    sent0 = exchange(sent0, 1)
    half1 = add(half1, other1)
    kept0, half1 = lax.optimization_barrier((kept0, half1))
    for stage in reversed(range(2, stages - 1)):
        half1 = add(half1, exchange(half1, 1 << stage))
    other1 = exchange(half1, 2)
    blocks = call_small(
        pair_kernel,
        (shape(share + 16, full, dtype=LOW),) * (dp_size // 2),
        [pltpu.VMEM((2 * width, full), LOW), pltpu.VMEM((16, full), LOW)],
        (kept0, sent0),
        "pair",
    )
    blocks = [blocks[0]] + [exchange(blocks[place], 2 * place) for place in range(1, dp_size // 2)]
    other1, *blocks = lax.optimization_barrier((other1, *blocks))
    half1 = add(half1, other1)
    back, both, small0 = call_small(
        share_kernel,
        (shape(share, full, dtype=LOW), shape(2 * width + share, full, dtype=LOW), shape(8, full)),
        [],
        (half1, *blocks),
        "share",
    )
    neighbour = exchange(both, 1)
    small0, neighbour = lax.optimization_barrier((small0, neighbour))
    backs = [back, neighbour]
    for place in range(2, dp_size, 2):
        backs += [exchange(back, place)]
        backs += [exchange(backs[-1], 1)]
    grad_nu, grad_theta, grad_gamma, grad_skip, grad_bias, grad_gain, grad_shift, result, grad_inputs = call(
        finish_kernel,
        (
            shape(LAYERS, own_states),
            shape(LAYERS, own_states),
            shape(LAYERS, own_states),
            shape(LAYERS, width),
            shape(LAYERS, 2, width),
            shape(LAYERS, width),
            shape(LAYERS, width),
            shape(width, total),
            shape(width, total),
        ),
        [pltpu.VMEM((32, full), F32), pltpu.VMEM((total, width), F32)],
        (lengths, small0, bn1, norm0, feature, nu_log, theta_log, result_rows, up0, grad0, tokens),
        "finish",
        late=(1, 2, 3, 4, 5, 6),
        vmem=16 * 1024 * 1024,
    )
    wide = (shape(LAYERS, width, full), shape(LAYERS, width, full), shape(LAYERS, 2 * width, full))
    held = [pltpu.VMEM((1, 4 * width, full), F32)]
    grads = call_small(widen1_kernel, wide, held, (half1, neighbour), "widen1", sent=True)
    grad_b, grad_c, grad_glu = call_small(widen0_kernel, wide, held, tuple(backs), "widen0", sent=True, into=tuple(grads))
    grad_b = grad_b.reshape(LAYERS, 2, own_states, full)
    grad_c = grad_c.reshape(LAYERS, 2, own_states, full)
    grad_glu = grad_glu.reshape(LAYERS, 2, width, full)
    return (
        own(result[None], 1),
        own(grad_inputs[None], 1),
        own(grad_gain, 1),
        own(grad_shift, 1),
        own(grad_b, 2),
        own(grad_c, 2),
        own(grad_nu, 1),
        own(grad_theta, 1),
        own(grad_gamma, 1),
        own(grad_skip, 1),
        own(grad_glu, 2),
        own(grad_bias, 2),
    )


def solution(mesh):
    in_specs = (
        P("dp", "state", None),
        P("dp"),
        P("dp", "state", None),
        P(None, "state"),
        P(None, "state"),
        P(None, None, "state", None),
        P(None, None, "state", None),
        P(None, "state"),
        P(None, "state"),
        P(None, "state"),
        P(None, "state"),
        P(None, None, "state", None),
        P(None, None, "state"),
    )
    out_specs = (
        P("dp", "state", None),
        P("dp", "state", None),
        P(None, "state"),
        P(None, "state"),
        P(None, None, "state", None),
        P(None, None, "state", None),
        P(None, "state"),
        P(None, "state"),
        P(None, "state"),
        P(None, "state"),
        P(None, None, "state", None),
        P(None, None, "state"),
    )
    step = functools.partial(local, dp_size=mesh.shape["dp"], state_size=mesh.shape["state"])
    return jax.shard_map(step, mesh=mesh, in_specs=in_specs, out_specs=out_specs, check_vma=False)
```
